32 devices in a mesh: dp: 8 (over y, x, core), mp: 4 (over z).
Axes of the slice: x: 2, y: 2, z: 4, core: 2. Of those that a mesh axis runs over, the one named last changes fastest.
Arguments:
- tokens: bfloat16 [27648, 768], P(('dp', 'mp')), may hold values from -6 to 6
- scene_ids: int32 [27648], P('dp'), may hold values from -1 to 3, as said below
- gain_one: float32 [768], replicated, may hold values from 0.25 to 1.75
- shift_one: float32 [768], replicated, may hold values from -4 to 4
- w_qkv: bfloat16 [3, 768, 768], P(None, None, 'mp'), may hold values from -0.3125 to 0.3125
- w_out: bfloat16 [768, 768], P('mp'), may hold values from -0.875 to 0.875
- b_out: float32 [768], replicated, may hold values from -4 to 4
- gain_two: float32 [768], replicated, may hold values from 0.25 to 1.75
- shift_two: float32 [768], replicated, may hold values from -4 to 4
- w_up: bfloat16 [768, 1536], P(None, 'mp'), may hold values from -0.21875 to 0.21875
- b_up: float32 [1536], P('mp'), may hold values from -6 to 6
- w_down: bfloat16 [1536, 768], P('mp'), may hold values from -0.15625 to 0.15625
- b_down: float32 [768], replicated, may hold values from -4 to 4
- cotangent: bfloat16 [27648, 768], P(('dp', 'mp')), may hold values from -6 to 6
Outputs:
- layer_out: bfloat16 [27648, 768], P(('dp', 'mp'))
- tokens_grad: float32 [27648, 768], P(('dp', 'mp'))
- gain_one_grad: float32 [768], replicated
- shift_one_grad: float32 [768], replicated
- w_qkv_grad: float32 [3, 768, 768], P(None, None, 'mp')
- w_out_grad: float32 [768, 768], P('mp')
- b_out_grad: float32 [768], replicated
- gain_two_grad: float32 [768], replicated
- shift_two_grad: float32 [768], replicated
- w_up_grad: float32 [768, 1536], P(None, 'mp')
- b_up_grad: float32 [1536], P('mp')
- w_down_grad: float32 [1536, 768], P('mp')
- b_down_grad: float32 [768], replicated
The draws below stay inside these ranges and needn't reach their ends.
Inputs may be any that keep to these rules, and one draw needn't show every extreme that they name: `scene_ids`: within each packed sequence of 3456 tokens the scene numbers start at 0 and never fall, each scene is one contiguous run of at least 600 and at most 1500 tokens, a sequence holds two to four scenes, and -1 marks padding after its last scene.
All inputs are finite; a program needn't handle non-finite values.
Results may differ from the reference program's by a relative error of at most 0.018.
The reference program's roundings to bfloat16 on the way count: a program that leaves them out, or rounds other values in their place, can miss the bound.
Values may be sent and summed in bfloat16 or wider, within the bound.
A program may use at most 192 MiB of HBM per device.

```python
import jax
import jax.numpy as jnp
from jax import lax

D = 768
HEADS = 12
HEAD = 64
FF = 1536
SEQ = 3456
BLOCK_ROWS = 576
SCENE_MIN = 600
SCENE_MAX = 1500
TOKENS = 27648


def draw_scene_ids(key, part):
    key = jax.random.fold_in(key, 11)
    seq_count = TOKENS // SEQ
    shift_key, size_key = jax.random.split(key)
    offset = jax.random.randint(shift_key, (), 0, 3)
    scene_count = 2 + (jnp.arange(seq_count, dtype=jnp.int32) + offset) % 3
    largest = jnp.minimum(SCENE_MAX, SEQ // scene_count)
    scene_sizes = jax.random.randint(size_key, (seq_count, 4), SCENE_MIN, largest[:, None] + 1)
    slot_index = jnp.arange(4, dtype=jnp.int32)
    scene_sizes = jnp.where(slot_index[None, :] < scene_count[:, None], scene_sizes, 0)
    scene_ends = jnp.cumsum(scene_sizes, axis=1)
    position = jnp.arange(SEQ, dtype=jnp.int32)
    scene_number = jnp.sum((position[None, :, None] >= scene_ends[:, None, :]).astype(jnp.int32), axis=2)
    scene_number = jnp.where(position[None, :] < scene_ends[:, 3:4], scene_number, -1)
    return scene_number.reshape(TOKENS).astype(jnp.int32)


def block_levels(rng, extent, shards, smallest, top_value):
    def one(axis_at, shards_of):
        draws = jax.random.uniform(jax.random.fold_in(jax.random.fold_in(rng, 6), axis_at), (shards_of,), jnp.float32, smallest / len(shards), top_value / len(shards))
        return jnp.repeat(jnp.exp(draws), extent[axis_at] // shards_of).reshape((-1,) + (1,) * (len(extent) - axis_at - 1))

    factor_of = one(*shards[0])
    for cut in shards[1:]:
        factor_of = factor_of * one(*cut)
    return factor_of


def gaussian(own_key, shape, scale, reach, shards=(), held_as=jnp.bfloat16):
    factor_of = block_levels(own_key, shape, shards, -0.22, 0.18) if shards else 1.0
    entries = jax.random.normal(own_key, shape, jnp.float32) * scale * factor_of
    return jnp.minimum(jnp.maximum(entries, -reach), reach).astype(held_as)


def setup_inputs(seed: int = 0) -> dict:
    splits = jax.random.split(jax.random.key(seed), 15)
    tokens = gaussian(splits[0], (TOKENS, D), 1.0, 6.0, ((0, 32),))
    scene_ids = draw_scene_ids(jax.random.fold_in(splits[14], 71), 0)
    gain_one = jnp.clip(1.0 + 0.15 * jax.random.normal(splits[2], (D,), jnp.float32), 0.25, 1.75)
    shift_one = gaussian(splits[3], (D,), 0.3, 4.0, (), jnp.float32)
    w_qkv = gaussian(splits[4], (3, D, D), (D // 2) ** -0.5, 0.3125, ((2, 4),))
    w_out = gaussian(splits[5], (D, D), (D // 16) ** -0.5, 0.875, ((0, 4),))
    b_out = gaussian(splits[6], (D,), 0.3, 4.0, (), jnp.float32)
    gain_two = jnp.clip(1.0 + 0.15 * jax.random.normal(splits[7], (D,), jnp.float32), 0.25, 1.75)
    shift_two = gaussian(splits[8], (D,), 0.3, 4.0, (), jnp.float32)
    w_up = gaussian(splits[9], (D, FF), D ** -0.5, 0.21875, ((1, 4),))
    b_up = gaussian(splits[10], (FF,), 0.5, 6.0, ((0, 4),), jnp.float32)
    w_down = gaussian(splits[11], (FF, D), FF ** -0.5, 0.15625, ((0, 4),))
    b_down = gaussian(splits[12], (D,), 0.3, 4.0, (), jnp.float32)
    cotangent = gaussian(splits[13], (TOKENS, D), 1.0, 6.0, ((0, 32),))
    return dict(tokens=tokens, scene_ids=scene_ids, gain_one=gain_one, shift_one=shift_one, w_qkv=w_qkv, w_out=w_out, b_out=b_out, gain_two=gain_two, shift_two=shift_two, w_up=w_up, b_up=b_up, w_down=w_down, b_down=b_down, cotangent=cotangent)


@jax.custom_vjp
def low(v):
    return lax.optimization_barrier(v.astype(jnp.bfloat16)).astype(jnp.float32)

@jax.custom_vjp
def low_back(v):
    return v

def low_keep(v):
    return (low(v), None)

def low_pass(kept, grad):
    return (grad,)

def back_keep(v):
    return (v, None)

def back_low(kept, grad):
    return (low(grad),)
low.defvjp(low_keep, low_pass)
low_back.defvjp(back_keep, back_low)
epsilon = 1e-05
masked_value = -1e+30
precise = lax.Precision.HIGHEST

def layer_norm(values, gain_vec, shift_vec):
    average = lax.optimization_barrier(jnp.mean(values, axis=-1, keepdims=True))
    centred = values - average
    variance = lax.optimization_barrier(jnp.mean(centred * centred, axis=-1, keepdims=True))
    return centred * lax.rsqrt(variance + epsilon) * gain_vec + shift_vec

def allowed_pairs(query_ids, key_ids, query_place, key_place):
    same_scene = (query_ids[:, None] == key_ids[None, :]) & (query_ids[:, None] >= 0)
    return same_scene | (query_place[:, None] == key_place[None, :])

def attention(queries, key_rows, value_rows, scene_seq):
    position = jnp.arange(SEQ, dtype=jnp.int32)
    valid_rows = (scene_seq >= 0).astype(jnp.float32)
    block_count = SEQ // BLOCK_ROWS
    query_blocks = queries.reshape(block_count, BLOCK_ROWS, HEADS, HEAD)
    id_blocks = scene_seq.reshape(block_count, BLOCK_ROWS)
    place_blocks = position.reshape(block_count, BLOCK_ROWS)

    def one_block(pieces):
        query_blk, query_ids, query_place = pieces
        allowed = allowed_pairs(query_ids, scene_seq, query_place, position)
        raw_scores = low_back(jnp.einsum('qhd,khd->hqk', query_blk, key_rows, precision=precise) * HEAD ** (-0.5))
        shifted = jnp.where(allowed[None], raw_scores, masked_value)
        row_top = lax.optimization_barrier(jnp.max(shifted, axis=-1, keepdims=True))
        weights = jnp.exp(shifted - row_top)
        attn_probs = low(weights / lax.optimization_barrier(jnp.sum(weights, axis=-1, keepdims=True)))
        return jnp.einsum('hqk,khd->qhd', attn_probs, value_rows, precision=precise)
    mixed_rows = lax.map(jax.checkpoint(one_block), (query_blocks, id_blocks, place_blocks))
    return mixed_rows.reshape(SEQ, HEADS * HEAD) * valid_rows[:, None]

def sequence_forward(row_values, scene_seq, weight_list):
    gain_one, shift_one, w_qkv, w_out, b_out, gain_two, shift_two, w_up, b_up, w_down, b_down = weight_list
    normed_one = low(layer_norm(row_values, gain_one, shift_one))
    projected = low(low_back(jnp.einsum('td,cde->cte', normed_one, w_qkv, precision=precise)))
    shaped = projected.reshape(3, SEQ, HEADS, HEAD)
    attended = low(low_back(attention(shaped[0], shaped[1], shaped[2], scene_seq)))
    middle = row_values + low_back(jnp.dot(attended, w_out, precision=precise)) + b_out
    normed_two = low(layer_norm(middle, gain_two, shift_two))
    hidden = low_back(jnp.dot(normed_two, w_up, precision=precise) + b_up)
    active = low(jax.nn.gelu(hidden, approximate=False))
    return middle + jnp.dot(active, w_down, precision=precise) + b_down

def add_pair(first_term, second_term):
    return first_term + second_term

def reference(tokens, scene_ids, gain_one, shift_one, w_qkv, w_out, b_out, gain_two, shift_two, w_up, b_up, w_down, b_down, cotangent):
    weights_all = tuple((weight_item.astype(jnp.float32) for weight_item in (gain_one, shift_one, w_qkv, w_out, b_out, gain_two, shift_two, w_up, b_up, w_down, b_down)))
    seq_count = TOKENS // SEQ
    token_seqs = tokens.astype(jnp.float32).reshape(seq_count, SEQ, D)
    scene_seqs = scene_ids.reshape(seq_count, SEQ)
    grad_seqs = cotangent.astype(jnp.float32).reshape(seq_count, SEQ, D)

    def one_sequence(totals, pieces):
        row_values, scene_seq, grad_rows = pieces

        def forward(inputs, weight_list):
            return sequence_forward(inputs, scene_seq, weight_list)
        output_rows, pullback = jax.vjp(forward, row_values, weights_all)
        grad_inputs, grad_weights = pullback(grad_rows)
        totals = jax.tree.map(add_pair, totals, grad_weights)
        return (totals, (output_rows.astype(jnp.bfloat16), grad_inputs))
    start_totals = tuple((jnp.zeros_like(weight_item) for weight_item in weights_all))
    totals, (outputs, input_grads) = lax.scan(one_sequence, start_totals, (token_seqs, scene_seqs, grad_seqs))
    return (outputs.reshape(TOKENS, D), input_grads.reshape(TOKENS, D), totals[0], totals[1], totals[2], totals[3], totals[4], totals[5], totals[6], totals[7], totals[8], totals[9], totals[10])
```

```python
import functools

import jax
import jax.numpy as jnp
from jax import lax
from jax.experimental import pallas as pl
from jax.experimental.pallas import tpu as pltpu
from jax.sharding import PartitionSpec as P

HEAD = 64
D = 768
FF = 1536
LANES = 128
PAD = 384
EPS = 1e-05
MASKED = -1e30
MESH = pl.DeviceIdType.MESH
F32 = jnp.float32
BF16 = jnp.bfloat16
VMEM = pl.BlockSpec(memory_space=pltpu.VMEM)
SMEM = pl.BlockSpec(memory_space=pltpu.SMEM)
ANY = pl.BlockSpec(memory_space=pl.ANY)
DMA = pltpu.SemaphoreType.DMA

NN = (((1,), (0,)), ((), ()))
NT = (((1,), (1,)), ((), ()))
TN = (((0,), (0,)), ((), ()))


def dot(a, b, dims=NN):
    return lax.dot_general(a, b, dims, preferred_element_type=F32)


def limit(mib):
    return pltpu.CompilerParams(vmem_limit_bytes=mib << 20)


class Place:
    def __init__(self):
        self.d = lax.axis_index("dp")
        self.m = lax.axis_index("mp")
        self.c = lax.rem(self.d, 2)
        self.r = lax.rem(self.m, 2)
        self.hf = self.m // 2
        self.q = 2 * self.c + self.r
        self.native = self.c == self.hf
        self.sibling = (self.d + 1 - 2 * self.c, self.m)
        self.cross = (self.d, self.m + 1 - 2 * self.r)
        self.partner = (self.d + 1 - 2 * self.c, lax.rem(self.m + 2, 4))

    def member(self, quarter):
        return (self.d - self.c + quarter // 2, 2 * self.hf + quarter % 2)


def greet(others):
    barrier = pltpu.get_barrier_semaphore()
    for other in others:
        pl.semaphore_signal(barrier, inc=1, device_id=other, device_id_type=MESH)
    pl.semaphore_wait(barrier, len(others))


def remote(src, dst, send, recv, device):
    return pltpu.make_async_remote_copy(
        src_ref=src, dst_ref=dst, send_sem=send, recv_sem=recv, device_id=device, device_id_type=MESH
    )


PIECES = 3


def gather_kernel(
    tok, wq, full, wown, swap_s, swap_r, cross_s, cross_r, sib_s, sib_r, fwd_s, fwd_r, w_s, w_r, loc, wloc
):
    me = Place()
    rows = tok.shape[0]
    piece = rows // PIECES
    greet([me.sibling, me.cross, me.partner])

    def part(quarter, p):
        return full.at[pl.ds(pl.multiple_of(quarter * rows + p * piece, 16), piece)]

    def send_cross(src, p):
        return remote(src, part(me.q, p), cross_s.at[p], cross_r.at[p], me.cross)

    def send_sib(src, p):
        return remote(src, part(me.q, p), sib_s.at[p], sib_r.at[p], me.sibling)

    def tok_part(p):
        return tok.at[pl.ds(p * piece, piece)]

    partner_q = 2 * (1 - me.c) + me.r
    cross_q = 2 * me.c + 1 - me.r
    sib_cross_q = 2 * (1 - me.c) + 1 - me.r

    def swap(p):
        return remote(tok_part(p), part(partner_q, p), swap_s.at[p], swap_r.at[p], me.partner)

    def swap_in(p):
        return remote(tok_part(p), part(me.q, p), swap_s.at[p], swap_r.at[p], me.partner)

    weight = remote(wq, wown, w_s, w_r, me.partner)
    own_rows = full.at[pl.ds(pl.multiple_of(me.q * rows, 16), rows)]

    @pl.when(me.native)
    def _():
        for p in range(PIECES):
            send_cross(tok_part(p), p).start()
            send_sib(tok_part(p), p).start()
        pltpu.make_async_copy(tok, own_rows, loc).start()
        pltpu.make_async_copy(wq, wown, wloc).start()

    @pl.when(jnp.logical_not(me.native))
    def _():
        for p in range(PIECES):
            swap(p).start()
        weight.start()
        for p in range(PIECES):
            swap_in(p).wait_recv()
            send_cross(part(me.q, p), p).start()
            send_sib(part(me.q, p), p).start()

    for p in range(PIECES):
        remote(part(cross_q, p), part(cross_q, p), cross_s.at[p], cross_r.at[p], me.cross).wait_recv()
        remote(part(cross_q, p), part(cross_q, p), fwd_s.at[p], fwd_r.at[p], me.sibling).start()
    for p in range(PIECES):
        remote(part(partner_q, p), part(partner_q, p), sib_s.at[p], sib_r.at[p], me.sibling).wait_recv()
        remote(part(sib_cross_q, p), part(sib_cross_q, p), fwd_s.at[p], fwd_r.at[p], me.sibling).wait_recv()
        remote(part(cross_q, p), part(cross_q, p), fwd_s.at[p], fwd_r.at[p], me.sibling).wait_send()

    @pl.when(me.native)
    def _():
        for p in range(PIECES):
            send_cross(tok_part(p), p).wait_send()
            send_sib(tok_part(p), p).wait_send()
        pltpu.make_async_copy(tok, own_rows, loc).wait()
        pltpu.make_async_copy(wq, wown, wloc).wait()

    @pl.when(jnp.logical_not(me.native))
    def _():
        for p in range(PIECES):
            swap(p).wait_send()
            send_cross(part(me.q, p), p).wait_send()
            send_sib(part(me.q, p), p).wait_send()
        weight.wait_send()
        weight.wait_recv()


def gather_sequence(tokens, w_qkv):
    rows = tokens.shape[0]
    sems = [DMA((PIECES,))] * 8 + [DMA] * 4
    return pl.pallas_call(
        gather_kernel,
        name="gather_sequence",
        in_specs=[ANY, ANY],
        out_specs=[ANY, ANY],
        out_shape=[jax.ShapeDtypeStruct((4 * rows, D), BF16), jax.ShapeDtypeStruct(w_qkv.shape, BF16)],
        scratch_shapes=sems,
        compiler_params=pltpu.CompilerParams(collective_id=1, has_side_effects=True),
    )(tokens, w_qkv)


def exchange_kernel(to_rows, src, dst, send, recv, loc):
    me = Place()
    others = []
    for k in range(1, 4):
        quarter = lax.rem(me.q + k, 4)
        others.append(me.member(quarter))
    greet(others)
    rows = (dst.shape[0] if to_rows else src.shape[0]) // 4

    def block(ref, quarter, by_rows):
        if by_rows:
            return ref.at[pl.ds(pl.multiple_of(quarter * rows, 16), rows)]
        return ref.at[quarter]

    def copy(k):
        quarter = lax.rem(me.q + k, 4)
        return remote(
            block(src, quarter, not to_rows), block(dst, me.q, to_rows), send.at[k], recv.at[k], others[k - 1]
        )

    def arrival(k):
        quarter = lax.rem(me.q + 4 - k, 4)
        return remote(
            block(src, quarter, not to_rows), block(dst, quarter, to_rows), send.at[k], recv.at[k], others[3 - k]
        )

    for k in (2, 1, 3):
        copy(k).start()
    own = pltpu.make_async_copy(block(src, me.q, not to_rows), block(dst, me.q, to_rows), loc)
    own.start()
    for k in (1, 2, 3):
        arrival(k).wait_recv()
    for k in (1, 2, 3):
        copy(k).wait_send()
    own.wait()


def exchange(values, to_rows, number):
    if to_rows:
        _, rows, width = values.shape
        shape = (4 * rows, width)
    else:
        rows, width = values.shape
        shape = (4, rows // 4, width)
    return pl.pallas_call(
        functools.partial(exchange_kernel, to_rows),
        name="exchange_rows" if to_rows else "exchange_heads",
        in_specs=[ANY],
        out_specs=ANY,
        out_shape=jax.ShapeDtypeStruct(shape, values.dtype),
        scratch_shapes=[DMA((4,)), DMA((4,)), DMA],
        compiler_params=pltpu.CompilerParams(collective_id=number, has_side_effects=True),
    )(values)


ROWS_QKV = 384


def normalise(x):
    centred = x - jnp.mean(x, axis=-1, keepdims=True)
    scale = lax.rsqrt(jnp.mean(centred * centred, axis=-1, keepdims=True) + EPS)
    return centred * scale, scale


def widen(x, ones, rows):
    lane = lax.broadcasted_iota(jnp.int32, (rows, LANES - HEAD), 1)
    return jnp.concatenate([x, jnp.where(lane < ones, 1.0, 0.0).astype(x.dtype)], axis=1)


def qkv_kernel(heads, steps, x, gain, shift, w, wt, normed, q, k, v, kt, vt):
    rows = x.shape[0]

    @pl.when(pl.program_id(0) < steps)
    def _():
        unit, _ = normalise(x[...].astype(F32))
        low = (unit * gain[...] + shift[...]).astype(BF16)
        normed[...] = low
        qs = (dot(low, w[0]).astype(BF16).astype(F32) * HEAD**-0.5).astype(BF16)
        ks = dot(low, w[1]).astype(BF16)
        vs = dot(low, w[2]).astype(BF16)
        kts = dot(wt[0], low, NT).astype(BF16)
        vts = dot(wt[1], low, NT).astype(BF16)
        line = lax.broadcasted_iota(jnp.int32, (16, rows), 0)
        ones = jnp.where(line < 1, 1.0, 0.0).astype(BF16)
        for h in range(heads):
            cols = slice(h * HEAD, (h + 1) * HEAD)
            q[h] = widen(qs[:, cols], 0, rows)
            k[h] = widen(ks[:, cols], 3, rows)
            v[h] = widen(vs[:, cols], 3, rows)
            kt[h] = kts[cols]
            vt[h, :HEAD] = vts[cols]
            vt[h, HEAD:] = ones

    @pl.when(pl.program_id(0) >= steps)
    def _():
        for out in (q, k, v, kt, vt):
            out[...] = jnp.zeros_like(out)


def project(full, gain, shift, w):
    total = full.shape[0]
    heads = w.shape[2] // HEAD
    steps = total // ROWS_QKV
    wide = total + PAD
    wt = jnp.swapaxes(w[1:], 1, 2)
    whole = lambda shape: pl.BlockSpec(shape, lambda i: (0,) * len(shape))
    by_rows = pl.BlockSpec((heads, ROWS_QKV, LANES), lambda i: (0, i, 0))
    by_cols = lambda n: pl.BlockSpec((heads, n, ROWS_QKV), lambda i: (0, 0, i))
    clamp = pl.BlockSpec((ROWS_QKV, D), lambda i: (jnp.minimum(i, steps - 1), 0))
    rowed = jax.ShapeDtypeStruct((heads, wide, LANES), BF16)
    return pl.pallas_call(
        functools.partial(qkv_kernel, heads, steps),
        name="norm_and_project",
        grid=(steps + PAD // ROWS_QKV,),
        in_specs=[clamp, whole((1, D)), whole((1, D)), whole(w.shape), whole(wt.shape)],
        out_specs=[clamp, by_rows, by_rows, by_rows, by_cols(HEAD), by_cols(HEAD + 16)],
        out_shape=[
            jax.ShapeDtypeStruct((total, D), BF16),
            rowed,
            rowed,
            rowed,
            jax.ShapeDtypeStruct((heads, HEAD, wide), BF16),
            jax.ShapeDtypeStruct((heads, HEAD + 16, wide), BF16),
        ],
        compiler_params=limit(48),
    )(full, gain, shift, w, wt)


FWD_Q, FWD_K = 384, 512
BWD_Q, BWD_K = 384, 384


def attention_kernel(heads, total, lo, hi, idc, idr, q, k, vt, out, lse):
    step = FWD_K // LANES

    def one_block(i, _):
        r0 = pl.multiple_of(i * FWD_Q, LANES)
        qs = [q[h, pl.ds(r0, FWD_Q), :] for h in range(heads)]
        mine = idr[:, pl.ds(r0, FWD_Q)]

        def keys(at, carry):
            c0 = pl.multiple_of(at * LANES, LANES)
            allowed = idc[pl.ds(c0, FWD_K), :] == mine
            new = []
            for h in range(heads):
                top, acc = carry[h]
                s = jnp.where(allowed, dot(k[h, pl.ds(c0, FWD_K), :], qs[h], NT), MASKED)
                above = jnp.maximum(top, jnp.max(s, axis=0, keepdims=True))
                p = jnp.exp(s - above).astype(BF16)
                acc = acc * jnp.exp(top - above) + dot(vt[h, :, pl.ds(c0, FWD_K)], p)
                new.append((above, acc))
            return tuple(new)

        start = tuple(
            (jnp.full((1, FWD_Q), MASKED, F32), jnp.zeros((vt.shape[1], FWD_Q), F32)) for _ in range(heads)
        )
        first = lo[i]
        count = (hi[i] - first + step - 1) // step
        done = lax.fori_loop(0, count, lambda n, c: keys(first + n * step, c), start)
        valid = jnp.where(mine >= 0, 1.0, 0.0)
        mixed = []
        for h in range(heads):
            top, acc = done[h]
            row_total = acc[HEAD : HEAD + 1]
            mixed.append(acc[:HEAD] * (valid / row_total))
            lse[pl.ds(h, 1), pl.ds(r0, FWD_Q)] = top + jnp.log(row_total)
        out[pl.ds(r0, FWD_Q), :] = jnp.concatenate(mixed, axis=0).T.astype(BF16)
        return 0

    lax.fori_loop(0, total // FWD_Q, one_block, 0)


def attention(ids, q, k, vt):
    lo, hi, idc, idr = ids
    heads, wide, _ = q.shape
    total = wide - PAD
    return pl.pallas_call(
        functools.partial(attention_kernel, heads, total),
        name="attention",
        in_specs=[SMEM, SMEM] + [VMEM] * 5,
        out_specs=[VMEM, VMEM],
        out_shape=[
            jax.ShapeDtypeStruct((total, heads * HEAD), BF16),
            jax.ShapeDtypeStruct((heads, total), F32),
        ],
        compiler_params=limit(56),
    )(lo, hi, idc, idr, q, k, vt)


def thirds(x):
    a = x.astype(BF16).astype(F32)
    b = (x - a).astype(BF16).astype(F32)
    return a, b, x - a - b


def attention_back_kernel(
    heads, total, lo, hi, idc, idr, q, k, v, kt, out, grad, lse, dproj, qe, ge, dq
):
    wide = q.shape[1]
    step = BWD_Q // LANES
    lane = lax.broadcasted_iota(jnp.int32, (PAD, LANES), 1)

    def extend(values, tail):
        a, b, c = thirds(tail)
        return jnp.where(
            lane == HEAD, a, jnp.where(lane == HEAD + 1, b, jnp.where(lane == HEAD + 2, c, values))
        ).astype(BF16)

    def prepare(i, _):
        rows = pl.ds(pl.multiple_of(i * PAD, LANES), PAD)
        valid = jnp.where(idc[rows, :] >= 0, 1.0, 0.0)
        grads = grad[rows, :].astype(F32) * valid
        inner = grads * out[rows, :].astype(F32)
        for h in range(heads):
            cols = slice(h * HEAD, (h + 1) * HEAD)
            g = jnp.concatenate([grads[:, cols], jnp.zeros((PAD, LANES - HEAD), F32)], axis=1)
            ge[h, rows, :] = extend(g, -jnp.sum(inner[:, cols], axis=1, keepdims=True))
            qe[h, rows, :] = extend(q[h, rows, :].astype(F32), -lse[rows, h : h + 1])
            dq[h, :, rows] = jnp.zeros((HEAD, PAD), F32)
        return 0

    lax.fori_loop(0, total // PAD, prepare, 0)
    for h in range(heads):
        qe[h, total:, :] = jnp.zeros((wide - total, LANES), BF16)
        ge[h, total:, :] = jnp.zeros((wide - total, LANES), BF16)
        dq[h, :, total:] = jnp.zeros((HEAD, wide - total), F32)

    def one_block(i, _):
        c0 = pl.multiple_of(i * BWD_K, LANES)
        cols = pl.ds(c0, BWD_K)
        mine = idc[cols, :]

        def queries(at, carry):
            r0 = pl.multiple_of(at * LANES, LANES)
            rows = pl.ds(r0, BWD_Q)
            allowed = mine == idr[:, rows]
            new = []
            for h in range(heads):
                dk, dv = carry[h]
                qh = qe[h, rows, :]
                gh = ge[h, rows, :]
                p = jnp.where(allowed, jnp.exp(dot(k[h, cols, :], qh, NT)), 0.0)
                ds = (p * dot(v[h, cols, :], gh, NT)).astype(BF16)
                dv = dv + dot(p.astype(BF16), gh)
                dk = dk + dot(ds, qh)
                dq[h, :, rows] += dot(kt[h, :, cols], ds)
                new.append((dk, dv))
            return tuple(new)

        zero = jnp.zeros((BWD_K, LANES), F32)
        first = lo[i]
        count = (hi[i] - first + step - 1) // step
        done = lax.fori_loop(
            0, count, lambda n, c: queries(first + n * step, c), tuple((zero, zero) for _ in range(heads))
        )
        for part in range(2):
            joined = jnp.concatenate([done[h][part][:, :HEAD] for h in range(heads)], axis=1)
            dproj[part + 1, cols, :] = joined.astype(BF16)
        return 0

    lax.fori_loop(0, total // BWD_K, one_block, 0)

    def finish(i, _):
        rows = pl.ds(pl.multiple_of(i * PAD, LANES), PAD)
        joined = jnp.concatenate([dq[h, :, rows] for h in range(heads)], axis=0)
        dproj[0, rows, :] = (joined * HEAD**-0.5).T.astype(BF16)
        return 0

    lax.fori_loop(0, total // PAD, finish, 0)


def attention_back(ids, q, k, v, kt, out, grad, lse):
    lo, hi, idc, idr = ids
    heads, wide, _ = q.shape
    total = wide - PAD
    return pl.pallas_call(
        functools.partial(attention_back_kernel, heads, total),
        name="attention_back",
        in_specs=[SMEM, SMEM] + [VMEM] * 9,
        out_specs=VMEM,
        out_shape=jax.ShapeDtypeStruct((3, total, heads * HEAD), BF16),
        scratch_shapes=[
            pltpu.VMEM((heads, wide, LANES), BF16),
            pltpu.VMEM((heads, wide, LANES), BF16),
            pltpu.VMEM((heads, HEAD, wide), F32),
        ],
        compiler_params=limit(60),
    )(lo, hi, idc, idr, q, k, v, kt, out, grad, lse.T)


def scene_ranges(scene, block):
    total = scene.shape[0]
    place = jnp.arange(total, dtype=jnp.int32)
    ids = jnp.where(scene >= 0, scene, -1 - place)
    before = jnp.sum(
        ((scene[None, :] >= 0) & (scene[None, :] < jnp.arange(6, dtype=jnp.int32)[:, None])).astype(jnp.int32), axis=1
    )
    first, last = scene[0::block], scene[block - 1 :: block]
    start = jnp.arange(total // block, dtype=jnp.int32) * block
    pick = lambda number: jnp.sum(
        jnp.where(number[:, None] == jnp.arange(6, dtype=jnp.int32)[None, :], before[None, :], 0), axis=1
    )
    lo = jnp.where(first >= 0, pick(first), start) // LANES
    hi = (jnp.where(last >= 0, pick(last + 1), start + block) + LANES - 1) // LANES
    padded = jnp.pad(ids, (0, PAD), constant_values=-(1 << 20))
    return lo, hi, padded[:, None], padded[None, :]


ROWS_MID = 288


def middle_kernel(
    att, tok, cot, w_out, b_out, gain, shift, w_up, b_up, w_down, b_down,
    layer_out, grad_mid, grad_att, d_out, d_up, d_down, d_vec, d_bup, a_out, a_up, a_down, a_vec, a_bup,
):
    step = pl.program_id(0)
    parts = w_up.shape[0]
    width = att.shape[2]

    @pl.when(step == 0)
    def _():
        for ref in (a_out, a_up, a_down, a_vec, a_bup):
            ref[...] = jnp.zeros_like(ref)

    atts = [att[v] for v in range(parts)]
    middle = tok[...].astype(F32) + b_out[...]
    for v in range(parts):
        middle = middle + dot(atts[v], w_out[v * width : (v + 1) * width, :])
    unit, scale = normalise(middle)
    low = (unit * gain[...] + shift[...]).astype(BF16)
    cot_low = cot[...]
    cot_full = cot_low.astype(F32)
    out = middle + b_down[...]
    grad_norm = jnp.zeros_like(middle)
    for v in range(parts):
        hidden = dot(low, w_up[v]) + b_up[v]
        below = 0.5 * (1.0 + lax.erf(hidden * 0.5**0.5))
        density = jnp.exp(-0.5 * hidden * hidden) * 0.3989422804014327
        active = (hidden * below).astype(BF16)
        out = out + dot(active, w_down[v])
        grad_hidden = (dot(cot_low, w_down[v], NT) * (below + hidden * density)).astype(BF16)
        grad_norm = grad_norm + dot(grad_hidden, w_up[v], NT)
        a_down[v] += dot(active, cot_low, TN)
        a_up[v] += dot(low, grad_hidden, TN)
        a_bup[v] += jnp.sum(grad_hidden.astype(F32), axis=0, keepdims=True)
    layer_out[...] = out.astype(BF16)
    scaled = grad_norm * gain[...]
    back = cot_full + scale * (
        scaled
        - jnp.mean(scaled, axis=-1, keepdims=True)
        - unit * jnp.mean(scaled * unit, axis=-1, keepdims=True)
    )
    grad_mid[...] = back
    back_low = back.astype(BF16)
    for v in range(parts):
        rows = slice(v * width, (v + 1) * width)
        a_out[rows, :] += dot(atts[v], back_low, TN)
        grad_att[v] = dot(back_low, w_out[rows, :], NT).astype(BF16)
    a_vec[0:1] += jnp.sum(grad_norm * unit, axis=0, keepdims=True)
    a_vec[1:2] += jnp.sum(grad_norm, axis=0, keepdims=True)
    a_vec[2:3] += jnp.sum(back, axis=0, keepdims=True)
    a_vec[3:4] += jnp.sum(cot_full, axis=0, keepdims=True)

    @pl.when(step == pl.num_programs(0) - 1)
    def _():
        for ref, total in ((d_out, a_out), (d_up, a_up), (d_down, a_down), (d_vec, a_vec), (d_bup, a_bup)):
            ref[...] = total[...].astype(ref.dtype)


def middle_part(att, tok, cot, w_out, b_out, gain, shift, w_up, b_up, w_down, b_down):
    parts, rows, width = att.shape
    whole = lambda a: pl.BlockSpec(a.shape, lambda i: (0,) * len(a.shape))
    shape = lambda s, t: jax.ShapeDtypeStruct(s, t)
    tile = pl.BlockSpec((ROWS_MID, D), lambda i: (i, 0))
    heads_tile = pl.BlockSpec((parts, ROWS_MID, width), lambda i: (0, i, 0))
    sums = [w_out.shape, w_up.shape, w_down.shape, (8, D), b_up.shape]
    kinds = [BF16, BF16, BF16, F32, F32]
    totals = [shape(s, t) for s, t in zip(sums, kinds)]
    return pl.pallas_call(
        middle_kernel,
        name="middle_part",
        grid=(rows // ROWS_MID,),
        in_specs=[heads_tile, tile, tile] + [whole(a) for a in (w_out, b_out, gain, shift, w_up, b_up, w_down, b_down)],
        out_specs=[tile, tile, heads_tile] + [whole(t) for t in totals],
        out_shape=[shape((rows, D), BF16), shape((rows, D), F32), shape((parts, rows, width), BF16)] + totals,
        scratch_shapes=[pltpu.VMEM(s, F32) for s in sums],
        compiler_params=limit(60),
    )(att, tok, cot, w_out, b_out, gain, shift, w_up, b_up, w_down, b_down)


ROWS_FIN = 384


def project_back_kernel(tok, gain, normed, dproj, w, partial, d_w, d_vec, a_w, a_vec):
    step = pl.program_id(0)

    @pl.when(step == 0)
    def _():
        a_w[...] = jnp.zeros_like(a_w)
        a_vec[...] = jnp.zeros_like(a_vec)

    low = normed[...]
    grad = jnp.zeros(tok.shape, F32)
    for c in range(3):
        grad = grad + dot(dproj[c], w[c], NT)
        a_w[c] += dot(low, dproj[c], TN)
    partial[...] = grad.astype(BF16)
    unit, _ = normalise(tok[...].astype(F32))
    a_vec[0:1] += jnp.sum(grad * unit, axis=0, keepdims=True)
    a_vec[1:2] += jnp.sum(grad, axis=0, keepdims=True)

    @pl.when(step == pl.num_programs(0) - 1)
    def _():
        d_w[...] = a_w[...].astype(BF16)
        d_vec[...] = a_vec[...]


def project_back(full, gain, normed, dproj, w):
    total = full.shape[0]
    width = w.shape[2]
    whole = lambda s: pl.BlockSpec(s, lambda i: (0,) * len(s))
    tile = pl.BlockSpec((ROWS_FIN, D), lambda i: (i, 0))
    return pl.pallas_call(
        project_back_kernel,
        name="project_back",
        grid=(total // ROWS_FIN,),
        in_specs=[tile, whole((1, D)), tile, pl.BlockSpec((3, ROWS_FIN, width), lambda i: (0, i, 0)), whole(w.shape)],
        out_specs=[tile, whole(w.shape), whole((8, D))],
        out_shape=[
            jax.ShapeDtypeStruct((total, D), BF16),
            jax.ShapeDtypeStruct(w.shape, BF16),
            jax.ShapeDtypeStruct((8, D), F32),
        ],
        scratch_shapes=[pltpu.VMEM(w.shape, F32), pltpu.VMEM((8, D), F32)],
        compiler_params=limit(48),
    )(full, gain, normed, dproj, w)


def return_kernel(
    partial, own_tok, grad_mid, gain, vec, grad, vec_sum,
    mine, theirs, sent, crossed, tok, mid, low, back, vz, vzsum, vd,
    load_s, sib_s, sib_r, cross_s, cross_r, swap_s, swap_r, vz_s, vz_r, vd_s, vd_r,
):
    me = Place()
    rows = own_tok.shape[0]
    piece = rows // PIECES
    ndp = vd.shape[0]
    around = [(me.d, lax.rem(me.m + k, 4)) for k in range(1, 4)]
    along = [(lax.rem(me.d + k, ndp), me.m) for k in range(1, ndp)]
    greet([me.sibling, me.cross, me.partner] + around + along)
    other = 1 - me.c

    def rows_of(quarter, p):
        return pl.ds(pl.multiple_of(quarter * rows + p * piece, 16), piece)

    quarters = [2 * me.c + 1 - me.r, me.q]
    for_sib = [2 * other + 1 - me.r, 2 * other + me.r]

    def to_sib(slot, p):
        return remote(
            partial.at[rows_of(for_sib[slot], p)],
            theirs.at[slot, p],
            sib_s.at[slot, p],
            sib_r.at[slot, p],
            me.sibling,
        )

    def load(slot, p):
        return pltpu.make_async_copy(partial.at[rows_of(quarters[slot], p)], mine.at[slot, p], load_s.at[slot, p])

    def to_cross(p):
        return remote(sent.at[p], crossed.at[p], cross_s.at[p], cross_r.at[p], me.cross)

    def to_partner(p):
        return remote(low.at[p], back.at[p], swap_s.at[p], swap_r.at[p], me.partner)

    for slot in range(2):
        for p in range(PIECES):
            to_sib(slot, p).start()
            load(slot, p).start()
    load_tok = pltpu.make_async_copy(own_tok, tok, load_s.at[2, 0])
    load_mid = pltpu.make_async_copy(grad_mid, mid, load_s.at[2, 1])
    load_tok.start()
    load_mid.start()

    vz[me.m] = vec[...]

    def around_copy(k):
        return remote(vz.at[me.m], vz.at[me.m], vz_s.at[k], vz_r.at[k], around[k])

    for k in range(3):
        around_copy(k).start()

    for p in range(PIECES):
        load(0, p).wait()
        to_sib(0, p).wait_recv()
        sent[p] = (mine[0, p].astype(F32) + theirs[0, p].astype(F32)).astype(BF16)
        to_cross(p).start()

    for k in range(3):
        source = lax.rem(me.m + 3 - k, 4)
        remote(vz.at[source], vz.at[source], vz_s.at[k], vz_r.at[k], around[k]).wait_recv()
    vd[me.d] = vz[0] + vz[1] + vz[2] + vz[3]

    def along_copy(k):
        return remote(vd.at[me.d], vd.at[me.d], vd_s.at[k], vd_r.at[k], along[k])

    for k in range(ndp - 1):
        along_copy(k).start()

    load_tok.wait()
    load_mid.wait()
    for p in range(PIECES):
        span = pl.ds(p * piece, piece)
        load(1, p).wait()
        to_sib(1, p).wait_recv()
        to_cross(p).wait_recv()
        total = mine[1, p].astype(F32) + theirs[1, p].astype(F32) + crossed[p].astype(F32)
        unit, scale = normalise(tok[span, :].astype(F32))
        scaled = total * gain[...]
        result = mid[span, :] + scale * (
            scaled
            - jnp.mean(scaled, axis=-1, keepdims=True)
            - unit * jnp.mean(scaled * unit, axis=-1, keepdims=True)
        )

        @pl.when(me.native)
        def _():
            grad[span, :] = result

        @pl.when(jnp.logical_not(me.native))
        def _():
            low[p] = result.astype(BF16)
            to_partner(p).start()

    for k in range(ndp - 1):
        source = lax.rem(me.d + ndp - 1 - k, ndp)
        remote(vd.at[source], vd.at[source], vd_s.at[k], vd_r.at[k], along[k]).wait_recv()
    total = vd[0]
    for i in range(1, ndp):
        total = total + vd[i]
    vec_sum[...] = total

    @pl.when(jnp.logical_not(me.native))
    def _():
        for p in range(PIECES):
            to_partner(p).wait_recv()
            grad[pl.ds(p * piece, piece), :] = back[p].astype(F32)
        for p in range(PIECES):
            to_partner(p).wait_send()

    for slot in range(2):
        for p in range(PIECES):
            to_sib(slot, p).wait_send()
    for p in range(PIECES):
        to_cross(p).wait_send()
    for k in range(3):
        around_copy(k).wait_send()
    for k in range(ndp - 1):
        along_copy(k).wait_send()


def return_home(partial, own_tok, grad_mid, gain, vec, ndp):
    rows = own_tok.shape[0]
    piece = rows // PIECES
    pieces = (PIECES, piece, D)
    return pl.pallas_call(
        return_kernel,
        name="return_home",
        in_specs=[ANY, ANY, ANY, VMEM, VMEM],
        out_specs=[VMEM, VMEM],
        out_shape=[jax.ShapeDtypeStruct((rows, D), F32), jax.ShapeDtypeStruct((8, D), F32)],
        scratch_shapes=[
            pltpu.VMEM((2,) + pieces, BF16),
            pltpu.VMEM((2,) + pieces, BF16),
            pltpu.VMEM(pieces, BF16),
            pltpu.VMEM(pieces, BF16),
            pltpu.VMEM((rows, D), BF16),
            pltpu.VMEM((rows, D), F32),
            pltpu.VMEM(pieces, BF16),
            pltpu.VMEM(pieces, BF16),
            pltpu.VMEM((4, 8, D), F32),
            pltpu.VMEM((8, D), F32),
            pltpu.VMEM((ndp, 8, D), F32),
            DMA((3, PIECES)),
            DMA((2, PIECES)),
            DMA((2, PIECES)),
            DMA((PIECES,)),
            DMA((PIECES,)),
            DMA((PIECES,)),
            DMA((PIECES,)),
            DMA((3,)),
            DMA((3,)),
            DMA((ndp - 1,)),
            DMA((ndp - 1,)),
        ],
        compiler_params=pltpu.CompilerParams(
            collective_id=4, has_side_effects=True, vmem_limit_bytes=48 << 20
        ),
    )(partial, own_tok, grad_mid, gain, vec)


def swap_pairs(ndp):
    pairs = []
    for d in range(ndp):
        for m in range(4):
            native = d % 2 == m // 2
            to = (d, m) if native else (d ^ 1, (m + 2) % 4)
            pairs.append((d * 4 + m, to[0] * 4 + to[1]))
    return pairs


def gather_weights(w_out, w_up, w_down, ndp):
    d = lax.axis_index("dp")
    cut = lambda w: lax.dynamic_slice_in_dim(w, d * (w.shape[0] // ndp), w.shape[0] // ndp, 0)
    a, b, c = cut(w_out), cut(w_up), cut(w_down)
    half = b.shape[0] // 2
    mine = jnp.concatenate([a, jnp.concatenate([b[:half], b[half:]], axis=1), c], axis=0)
    parts = lax.all_gather(mine, ("dp", "mp"), axis=0).reshape(ndp, 4, *mine.shape)
    na, nb = a.shape[0], half
    out = parts[:, :, :na].transpose(1, 0, 2, 3).reshape(D, D)
    up = parts[:, :, na : na + nb].transpose(1, 0, 2, 3)
    up = jnp.stack([up[..., : FF // 4], up[..., FF // 4 :]], axis=2).reshape(4, D, FF // 4)
    down = parts[:, :, na + nb :].transpose(1, 0, 2, 3).reshape(4, FF // 4, D)
    return out, up, down


def reduce_weights(d_out, d_up, d_down, vec, bup, ndp):
    out = d_out.reshape(4, ndp, -1, D).transpose(1, 0, 2, 3)
    up = d_up.reshape(4, ndp, 2, -1, FF // 4)
    up = jnp.concatenate([up[:, :, 0], up[:, :, 1]], axis=-1).transpose(1, 0, 2, 3)
    down = d_down.reshape(4, ndp, -1, D).transpose(1, 0, 2, 3)
    flat = jnp.broadcast_to(vec.reshape(ndp, 1, -1), (ndp, 4, vec.size // ndp))
    flat_up = bup.reshape(4, ndp, -1).transpose(1, 0, 2)
    used = flat.shape[2] + flat_up.shape[2]
    tail = jnp.concatenate([flat, flat_up, jnp.zeros((ndp, 4, D - used), F32)], axis=2)[:, :, None].astype(BF16)
    cells = jnp.concatenate([out, up, down, tail], axis=2)
    n_out, n_up, n_down = out.shape[2], up.shape[2], down.shape[2]
    height = cells.shape[2]
    cells = lax.psum_scatter(cells.reshape(-1, D), "dp", scatter_dimension=0, tiled=True)
    cells = lax.psum_scatter(cells, "mp", scatter_dimension=0, tiled=True)
    cells = cells.reshape(height, D)
    cells = lax.all_gather(cells, "dp", axis=0).astype(F32)
    out = cells[:, :n_out].reshape(-1, D)
    up = cells[:, n_out : n_out + n_up]
    up = jnp.stack([up[..., : FF // 4], up[..., FF // 4 :]], axis=1).reshape(D, FF // 4)
    down = cells[:, n_out + n_up : n_out + n_up + n_down].reshape(-1, D)
    tail = cells[:, -1]
    vec_sum = tail[:, : flat.shape[2]].reshape(vec.shape)
    bup_sum = tail[:, flat.shape[2] : used].reshape(-1)
    return out, up, down, vec_sum, bup_sum


def shards(
    tokens,
    scene_ids,
    gain_one,
    shift_one,
    w_qkv,
    w_out,
    b_out,
    gain_two,
    shift_two,
    w_up,
    b_up,
    w_down,
    b_down,
    cotangent,
    ndp,
):
    rows = tokens.shape[0]
    d, m = lax.axis_index("dp"), lax.axis_index("mp")
    quarter = 2 * (d % 2) + m % 2
    line = lambda v: v.reshape(1, D)
    both = ("dp", "mp")
    swap = swap_pairs(ndp)

    all_out, all_up, all_down = gather_weights(w_out, w_up, w_down, ndp)
    all_bup = lax.all_gather(b_up, "mp", axis=0).reshape(4, 1, FF // 4)
    scene = lax.ppermute(scene_ids, both, [(i, (i // 4 ^ 1) * 4 + i % 4) for i in range(4 * ndp)])
    scene = jnp.where(d % 2 == m // 2, scene_ids, scene)
    lo_f, hi_f, idc, idr = scene_ranges(scene, FWD_Q)
    lo_b, hi_b, _, _ = scene_ranges(scene, BWD_K)

    full, w_mine = gather_sequence(tokens, w_qkv)
    own_cot = lax.ppermute(cotangent, both, swap)
    own_tok = lax.dynamic_slice_in_dim(full, quarter * rows, rows, 0)
    normed, q, k, v, kt, vt = project(full, line(gain_one), line(shift_one), w_mine)
    attended, lse = attention((lo_f, hi_f, idc, idr), q, k, vt)
    att = exchange(attended, False, 2)
    layer_out, grad_mid, grad_att, d_out, d_up, d_down, d_vec, d_bup = middle_part(
        att, own_tok, own_cot, all_out, line(b_out), line(gain_two), line(shift_two), all_up, all_bup, all_down, line(b_down)
    )
    layer_out = lax.ppermute(layer_out, both, swap)
    grad_heads = exchange(grad_att, True, 3)
    g_out, g_up, g_down, g_vec, g_bup = reduce_weights(d_out, d_up, d_down, d_vec[:4], d_bup, ndp)
    dproj = attention_back((lo_b, hi_b, idc, idr), q, k, v, kt, attended, grad_heads, lse)
    partial, d_qkv, d_one = project_back(full, line(gain_one), normed, dproj, w_mine)
    tokens_grad, one_sum = return_home(partial, own_tok, grad_mid, line(gain_one), d_one, ndp)
    g_qkv = lax.psum(lax.ppermute(d_qkv, both, swap), "dp").astype(F32)
    return (
        layer_out,
        tokens_grad,
        one_sum[0],
        one_sum[1],
        g_qkv,
        g_out,
        g_vec[2],
        g_vec[0],
        g_vec[1],
        g_up,
        g_bup,
        g_down,
        g_vec[3],
    )


def solution(mesh):
    ndp = mesh.shape["dp"]
    return jax.shard_map(
        functools.partial(shards, ndp=ndp),
        mesh=mesh,
        in_specs=(
            P(("dp", "mp"), None),
            P("dp"),
            P(),
            P(),
            P(None, None, "mp"),
            P("mp", None),
            P(),
            P(),
            P(),
            P(None, "mp"),
            P("mp"),
            P("mp", None),
            P(),
            P(("dp", "mp"), None),
        ),
        out_specs=(
            P(("dp", "mp"), None),
            P(("dp", "mp"), None),
            P(),
            P(),
            P(None, None, "mp"),
            P("mp", None),
            P(),
            P(),
            P(),
            P(None, "mp"),
            P("mp"),
            P("mp", None),
            P(),
        ),
        check_vma=False,
    )
```

```python
import functools

import jax
import jax.numpy as jnp
from jax import lax
from jax.experimental import pallas as pl
from jax.experimental.pallas import tpu as pltpu
from jax.sharding import PartitionSpec as P

HEAD = 64
D = 768
FF = 1536
LANES = 128
PAD = 384
OUT_ROWS = D // 4
UP_ROWS = FF // 4
VEC_AT = OUT_ROWS + 2 * UP_ROWS
UNITS = 1024
EPS = 1e-05
MASKED = -1e30
MESH = pl.DeviceIdType.MESH
F32 = jnp.float32
BF16 = jnp.bfloat16
VMEM = pl.BlockSpec(memory_space=pltpu.VMEM)
SMEM = pl.BlockSpec(memory_space=pltpu.SMEM)
ANY = pl.BlockSpec(memory_space=pl.ANY)
DMA = pltpu.SemaphoreType.DMA

NN = (((1,), (0,)), ((), ()))
NT = (((1,), (1,)), ((), ()))
TN = (((0,), (0,)), ((), ()))


def dot(a, b, dims=NN):
    return lax.dot_general(a, b, dims, preferred_element_type=F32)


def work(us):
    return pl.CostEstimate(flops=us * 10**9, bytes_accessed=us * 3 * 10**6, transcendentals=0)


def limit(mib):
    return pltpu.CompilerParams(vmem_limit_bytes=mib << 20)


class Place:
    def __init__(self):
        self.d = lax.axis_index("dp")
        self.m = lax.axis_index("mp")
        self.c = lax.rem(self.d, 2)
        self.r = lax.rem(self.m, 2)
        self.hf = self.m // 2
        self.q = 2 * self.c + self.r
        self.native = self.c == self.hf
        self.sibling = (self.d + 1 - 2 * self.c, self.m)
        self.cross = (self.d, self.m + 1 - 2 * self.r)
        self.partner = (self.d + 1 - 2 * self.c, lax.rem(self.m + 2, 4))

    def member(self, quarter):
        return (self.d - self.c + quarter // 2, 2 * self.hf + quarter % 2)


def greet(others):
    barrier = pltpu.get_barrier_semaphore()
    for other in others:
        pl.semaphore_signal(barrier, inc=1, device_id=other, device_id_type=MESH)
    pl.semaphore_wait(barrier, len(others))


def remote(src, dst, send, recv, device):
    return pltpu.make_async_remote_copy(
        src_ref=src, dst_ref=dst, send_sem=send, recv_sem=recv, device_id=device, device_id_type=MESH
    )


PIECES = 3
TILE = 384


def normalise(x):
    centred = x - jnp.mean(x, axis=-1, keepdims=True)
    scale = lax.rsqrt(jnp.mean(centred * centred, axis=-1, keepdims=True) + EPS)
    return centred * scale, scale


def widen(x, ones, rows):
    lane = lax.broadcasted_iota(jnp.int32, (rows, LANES - HEAD), 1)
    return jnp.concatenate([x, jnp.where(lane < ones, 1.0, 0.0).astype(x.dtype)], axis=1)


def start_kernel(
    heads, tok, wq, ids, bup, gain, shift, mine,
    full, own, w_out, ids_own, bups, normed, q, k, v, kt, vt, units,
    buf, w, low_s, q_s, k_s, v_s, kt_s, vt_s,
    swap_s, swap_r, cross_s, cross_r, sib_s, sib_r, fwd_s, fwd_r, w_s, w_r, ids_s, ids_r, b_s, b_r, out_s, late_s,
    uz_s, uz_r,
):
    me = Place()
    foreign = jnp.logical_not(me.native)
    rows = tok.shape[0]
    piece = rows // PIECES
    total = buf.shape[0]
    tiles = total // TILE
    groups = w.shape[1]
    group = me.d // 2
    around = [(me.d, lax.rem(me.m + j, 4)) for j in range(1, 4)]
    lines = [(2 * lax.rem(group + j, groups) + me.c, me.m) for j in range(1, groups)]
    greet([me.sibling, me.partner] + around + lines)

    def rows_of(quarter, n):
        p = jnp.where(me.hf == 0, n, PIECES - 1 - n)
        return pl.ds(pl.multiple_of(quarter * rows + p * piece, 16), piece)

    def part(quarter, n):
        return buf.at[rows_of(quarter, n)]

    sib_q = 2 * (1 - me.c) + me.r
    cross_q = 2 * me.c + 1 - me.r
    sib_cross_q = 2 * (1 - me.c) + 1 - me.r

    def swap(n):
        p = jnp.where(me.hf == 1, n, PIECES - 1 - n)
        src = tok.at[pl.ds(pl.multiple_of(p * piece, 16), piece)]
        dst = buf.at[pl.ds(pl.multiple_of(sib_q * rows + p * piece, 16), piece)]
        return remote(src, dst, swap_s.at[n], swap_r.at[n], me.partner)

    def swap_in(n):
        return remote(part(me.q, n), part(me.q, n), swap_s.at[n], swap_r.at[n], me.partner)

    def cross(quarter, n):
        return remote(part(quarter, n), part(quarter, n), cross_s.at[n], cross_r.at[n], me.cross)

    def sib(quarter, n):
        return remote(part(quarter, n), part(quarter, n), sib_s.at[n], sib_r.at[n], me.sibling)

    def forward(quarter, n):
        return remote(part(quarter, n), part(quarter, n), fwd_s.at[n], fwd_r.at[n], me.sibling)

    weight = remote(wq.at[:, group], w.at[:, group], w_s.at[0], w_r.at[0], me.partner)

    def weight_share(j):
        return remote(w.at[:, group], w.at[:, group], w_s.at[j], w_r.at[j], lines[j - 1])

    def weight_in(j):
        source = lax.rem(group + groups - j, groups)
        return remote(w.at[:, source], w.at[:, source], w_s.at[j], w_r.at[j], lines[j - 1])

    unit_own = pltpu.make_async_copy(mine, units.at[me.m], late_s.at[7])

    def unit_z(j, source):
        return remote(mine, units.at[source], uz_s.at[j], uz_r.at[j], around[j])

    scenes = remote(ids, ids_own, ids_s, ids_r, me.sibling)
    unit_own.start()
    for j in range(3):
        remote(bup, bups.at[me.m], b_s.at[j], b_r.at[j], around[j]).start()
    bups[me.m] = bup[...]

    @pl.when(me.native)
    def _():
        scenes.start()
        buf[pl.ds(pl.multiple_of(me.q * rows, 16), rows), :] = tok[...]
        for n in range(PIECES):
            cross(me.q, n).start()
            sib(me.q, n).start()
        w[...] = wq[...]
        ids_own[...] = ids[...]

    @pl.when(foreign)
    def _():
        weight.start()
        for n in range(PIECES):
            swap(n).start()

    def share(n):
        swap_in(n).wait_recv()
        cross(me.q, n).start()
        sib(me.q, n).start()

    def pass_on(n):
        cross(cross_q, n).wait_recv()
        forward(cross_q, n).start()

    def from_sibling(n):
        sib(sib_q, n).wait_recv()
        forward(sib_cross_q, n).wait_recv()

    def outputs(t):
        span = pl.ds(pl.multiple_of(t * TILE, LANES), TILE)
        pairs = [
            (low_s.at[span], normed.at[span]),
            (buf.at[span], full.at[span]),
            (q_s.at[:, span], q.at[:, span]),
            (k_s.at[:, span], k.at[:, span]),
            (v_s.at[:, span], v.at[:, span]),
            (kt_s.at[:, :, span], kt.at[:, :, span]),
            (vt_s.at[:, :, span], vt.at[:, :, span]),
        ]
        return [pltpu.make_async_copy(src, dst, out_s.at[t, j]) for j, (src, dst) in enumerate(pairs)]

    line = lax.broadcasted_iota(jnp.int32, (16, TILE), 0)
    ones = jnp.where(line < 1, 1.0, 0.0).astype(BF16)

    def compute(first, stride, count):
        def one(n, _):
            at = first + stride * n
            t = jnp.where(me.hf == 0, at, tiles - 1 - at)
            span = pl.ds(pl.multiple_of(t * TILE, LANES), TILE)
            unit, _ = normalise(buf[span, :].astype(F32))
            low = (unit * gain[...] + shift[...]).astype(BF16)
            low_s[span, :] = low
            qs = (dot(low, w[0].reshape(D, -1)).astype(BF16).astype(F32) * HEAD**-0.5).astype(BF16)
            ks = dot(low, w[1].reshape(D, -1))
            vs = dot(low, w[2].reshape(D, -1))
            kts = ks.T.astype(BF16)
            vts = vs.T.astype(BF16)
            ks = ks.astype(BF16)
            vs = vs.astype(BF16)
            for h in range(heads):
                cols = slice(h * HEAD, (h + 1) * HEAD)
                q_s[h, span, :] = widen(qs[:, cols], 0, TILE)
                k_s[h, span, :] = widen(ks[:, cols], 3, TILE)
                v_s[h, span, :] = widen(vs[:, cols], 3, TILE)
                kt_s[h, :, span] = kts[cols]
                vt_s[h, :HEAD, span] = vts[cols]
                vt_s[h, HEAD:, span] = ones
            for copy in outputs(t):
                copy.start()
            return 0

        lax.fori_loop(0, count, one, 0)

    pad = pl.ds(total, PAD)
    zeros = jnp.zeros((heads, PAD, LANES), BF16)
    for ref in (q_s, k_s, v_s):
        ref[:, pad, :] = zeros
    for ref in (kt_s, vt_s):
        ref[:, :, pad] = jnp.zeros((heads, ref.shape[1], PAD), BF16)
    padding = [
        pltpu.make_async_copy(src, dst, late_s.at[j])
        for j, (src, dst) in enumerate(
            [(a.at[:, pad], b.at[:, pad]) for a, b in ((q_s, q), (k_s, k), (v_s, v))]
            + [(a.at[:, :, pad], b.at[:, :, pad]) for a, b in ((kt_s, kt), (vt_s, vt))]
        )
    ]
    for copy in padding:
        copy.start()

    @pl.when(me.native)
    def _():
        for n in range(PIECES):
            pass_on(n)

    @pl.when(foreign)
    def _():
        weight.wait_recv()
        for j in range(1, groups):
            weight_share(j).start()
        for n in range(PIECES):
            share(n)
        for j in range(1, groups):
            weight_in(j).wait_recv()
        for n in range(PIECES):
            from_sibling(n)

    for j in range(3):
        unit_z(j, me.m).start()
    compute(0, 1, 2)

    @pl.when(foreign)
    def _():
        pass_on(0)

    compute(2, 1, 2)

    @pl.when(foreign)
    def _():
        pass_on(1)

    @pl.when(me.native)
    def _():
        from_sibling(0)

    compute(4, 1, 1)

    @pl.when(me.native)
    def _():
        from_sibling(1)

    compute(5, 2, 2)

    @pl.when(foreign)
    def _():
        pass_on(2)

    @pl.when(me.native)
    def _():
        from_sibling(2)

    own_copy = pltpu.make_async_copy(buf.at[pl.ds(pl.multiple_of(me.q * rows, 16), rows)], own, late_s.at[5])
    w_copy = pltpu.make_async_copy(w, w_out, late_s.at[6])
    own_copy.start()
    w_copy.start()
    compute(6, 2, 2)
    unit_own.wait()
    for j in range(3):
        unit_z(j, lax.rem(me.m + 3 - j, 4)).wait_recv()
        unit_z(j, me.m).wait_send()

    for j in range(3):
        source = lax.rem(me.m + 3 - j, 4)
        remote(bup, bups.at[source], b_s.at[j], b_r.at[j], around[j]).wait_recv()
        remote(bup, bups.at[me.m], b_s.at[j], b_r.at[j], around[j]).wait_send()

    @pl.when(me.native)
    def _():
        scenes.wait_send()

    @pl.when(foreign)
    def _():
        scenes.wait_recv()
        weight.wait_send()
        for j in range(1, groups):
            weight_share(j).wait_send()
        for n in range(PIECES):
            swap(n).wait_send()

    for n in range(PIECES):
        cross(me.q, n).wait_send()
        sib(me.q, n).wait_send()
        forward(cross_q, n).wait_send()
    for copy in padding + [own_copy, w_copy]:
        copy.wait()

    def finish_tile(t, _):
        for copy in outputs(t):
            copy.wait()
        return 0

    lax.fori_loop(0, tiles, finish_tile, 0)


def start(tokens, w_qkv, scene_ids, b_up, gain, shift, mine, ndp):
    rows = tokens.shape[0]
    total = 4 * rows
    heads = w_qkv.shape[2] // HEAD
    groups = ndp // 2
    w_qkv = w_qkv.reshape(3, groups, D // groups, -1)
    units = (4,) + mine.shape
    wide = total + PAD
    shape = jax.ShapeDtypeStruct
    rowed = (heads, wide, LANES)
    k_cols, v_cols = (heads, HEAD, wide), (heads, HEAD + 16, wide)
    three = DMA((PIECES,))
    return pl.pallas_call(
        functools.partial(start_kernel, heads),
        name="start",
        cost_estimate=work(50),
        in_specs=[VMEM] * 6 + [ANY],
        out_specs=[ANY, ANY, ANY, VMEM, VMEM] + [ANY] * 7,
        out_shape=[
            shape((total, D), BF16),
            shape((rows, D), BF16),
            shape(w_qkv.shape, BF16),
            shape(scene_ids.shape, jnp.int32),
            shape((4,) + b_up.shape, F32),
            shape((total, D), BF16),
            shape(rowed, BF16),
            shape(rowed, BF16),
            shape(rowed, BF16),
            shape(k_cols, BF16),
            shape(v_cols, BF16),
            shape(units, BF16),
        ],
        scratch_shapes=[
            pltpu.VMEM((total, D), BF16),
            pltpu.VMEM(w_qkv.shape, BF16),
            pltpu.VMEM((total, D), BF16),
            pltpu.VMEM(rowed, BF16),
            pltpu.VMEM(rowed, BF16),
            pltpu.VMEM(rowed, BF16),
            pltpu.VMEM(k_cols, BF16),
            pltpu.VMEM(v_cols, BF16),
        ]
        + [three] * 8
        + [DMA((groups,))] * 2
        + [DMA] * 2
        + [DMA((3,))] * 2
        + [DMA((total // TILE, 7)), DMA((8,))]
        + [DMA((3,))] * 2,
        compiler_params=pltpu.CompilerParams(
            collective_id=1, has_side_effects=True, vmem_limit_bytes=60 << 20
        ),
    )(tokens, w_qkv, scene_ids, b_up, gain, shift, mine)


def exchange_kernel(to_rows, src, dst, send, recv, loc):
    me = Place()
    others = []
    for k in range(1, 4):
        quarter = lax.rem(me.q + k, 4)
        others.append(me.member(quarter))
    greet(others)
    rows = (dst.shape[0] if to_rows else src.shape[0]) // 4

    def block(ref, quarter, by_rows):
        if by_rows:
            return ref.at[pl.ds(pl.multiple_of(quarter * rows, 16), rows)]
        return ref.at[quarter]

    def copy(k):
        quarter = lax.rem(me.q + k, 4)
        return remote(
            block(src, quarter, not to_rows), block(dst, me.q, to_rows), send.at[k], recv.at[k], others[k - 1]
        )

    def arrival(k):
        quarter = lax.rem(me.q + 4 - k, 4)
        return remote(
            block(src, quarter, not to_rows), block(dst, quarter, to_rows), send.at[k], recv.at[k], others[3 - k]
        )

    for k in (2, 1, 3):
        copy(k).start()
    own = pltpu.make_async_copy(block(src, me.q, not to_rows), block(dst, me.q, to_rows), loc)
    own.start()
    for k in (1, 2, 3):
        arrival(k).wait_recv()
    for k in (1, 2, 3):
        copy(k).wait_send()
    own.wait()


def exchange(values, to_rows, number):
    if to_rows:
        _, rows, width = values.shape
        shape = (4 * rows, width)
    else:
        rows, width = values.shape
        shape = (4, rows // 4, width)
    return pl.pallas_call(
        functools.partial(exchange_kernel, to_rows),
        name="exchange_rows" if to_rows else "exchange_heads",
        in_specs=[ANY],
        out_specs=ANY,
        out_shape=jax.ShapeDtypeStruct(shape, values.dtype),
        scratch_shapes=[DMA((4,)), DMA((4,)), DMA],
        cost_estimate=work(20),
        compiler_params=pltpu.CompilerParams(collective_id=number, has_side_effects=True),
    )(values)


FWD_Q, FWD_K = 384, 512
BWD_Q, BWD_K = 384, 384


def attention_kernel(heads, total, lo, hi, idc, idr, q, k, vt, out, lse):
    step = FWD_K // LANES

    def one_block(i, _):
        r0 = pl.multiple_of(i * FWD_Q, LANES)
        qs = [q[h, pl.ds(r0, FWD_Q), :] for h in range(heads)]
        mine = idr[:, pl.ds(r0, FWD_Q)]

        def keys(at, carry):
            c0 = pl.multiple_of(at * LANES, LANES)
            allowed = idc[pl.ds(c0, FWD_K), :] == mine
            new = []
            for h in range(heads):
                top, acc = carry[h]
                s = jnp.where(allowed, dot(k[h, pl.ds(c0, FWD_K), :], qs[h], NT), MASKED)
                above = jnp.maximum(top, jnp.max(s, axis=0, keepdims=True))
                p = jnp.exp(s - above).astype(BF16)
                acc = acc * jnp.exp(top - above) + dot(vt[h, :, pl.ds(c0, FWD_K)], p)
                new.append((above, acc))
            return tuple(new)

        start = tuple(
            (jnp.full((1, FWD_Q), MASKED, F32), jnp.zeros((vt.shape[1], FWD_Q), F32)) for _ in range(heads)
        )
        first = lo[i]
        count = (hi[i] - first + step - 1) // step
        done = lax.fori_loop(0, count, lambda n, c: keys(first + n * step, c), start)
        valid = jnp.where(mine >= 0, 1.0, 0.0)
        mixed = []
        for h in range(heads):
            top, acc = done[h]
            row_total = acc[HEAD : HEAD + 1]
            mixed.append(acc[:HEAD] * (valid / row_total))
            lse[pl.ds(h, 1), pl.ds(r0, FWD_Q)] = top + jnp.log(row_total)
        out[pl.ds(r0, FWD_Q), :] = jnp.concatenate(mixed, axis=0).T.astype(BF16)
        return 0

    lax.fori_loop(0, total // FWD_Q, one_block, 0)


def attention(ids, q, k, vt):
    lo, hi, idc, idr = ids
    heads, wide, _ = q.shape
    total = wide - PAD
    return pl.pallas_call(
        functools.partial(attention_kernel, heads, total),
        name="attention",
        cost_estimate=work(31),
        in_specs=[SMEM, SMEM] + [VMEM] * 5,
        out_specs=[VMEM, VMEM],
        out_shape=[
            jax.ShapeDtypeStruct((total, heads * HEAD), BF16),
            jax.ShapeDtypeStruct((heads, total), F32),
        ],
        compiler_params=limit(56),
    )(lo, hi, idc, idr, q, k, vt)


def thirds(x):
    a = x.astype(BF16).astype(F32)
    b = (x - a).astype(BF16).astype(F32)
    return a, b, x - a - b


def attention_back_kernel(
    heads, total, lo, hi, idc, idr, q, k, v, kt, out, grad, lse, dproj, qe, ge, dq
):
    wide = q.shape[1]
    step = BWD_Q // LANES
    lane = lax.broadcasted_iota(jnp.int32, (PAD, LANES), 1)

    def extend(values, tail):
        a, b, c = thirds(tail)
        return jnp.where(
            lane == HEAD, a, jnp.where(lane == HEAD + 1, b, jnp.where(lane == HEAD + 2, c, values))
        ).astype(BF16)

    def prepare(i, _):
        rows = pl.ds(pl.multiple_of(i * PAD, LANES), PAD)
        valid = jnp.where(idc[rows, :] >= 0, 1.0, 0.0)
        grads = grad[rows, :].astype(F32) * valid
        inner = grads * out[rows, :].astype(F32)
        for h in range(heads):
            cols = slice(h * HEAD, (h + 1) * HEAD)
            g = jnp.concatenate([grads[:, cols], jnp.zeros((PAD, LANES - HEAD), F32)], axis=1)
            ge[h, rows, :] = extend(g, -jnp.sum(inner[:, cols], axis=1, keepdims=True))
            qe[h, rows, :] = extend(q[h, rows, :].astype(F32), -lse[rows, h : h + 1])
            dq[h, :, rows] = jnp.zeros((HEAD, PAD), F32)
        return 0

    lax.fori_loop(0, total // PAD, prepare, 0)
    for h in range(heads):
        qe[h, total:, :] = jnp.zeros((wide - total, LANES), BF16)
        ge[h, total:, :] = jnp.zeros((wide - total, LANES), BF16)
        dq[h, :, total:] = jnp.zeros((HEAD, wide - total), F32)

    def one_block(i, _):
        c0 = pl.multiple_of(i * BWD_K, LANES)
        cols = pl.ds(c0, BWD_K)
        mine = idc[cols, :]

        def queries(at, carry):
            r0 = pl.multiple_of(at * LANES, LANES)
            rows = pl.ds(r0, BWD_Q)
            allowed = mine == idr[:, rows]
            new = []
            for h in range(heads):
                dk, dv = carry[h]
                qh = qe[h, rows, :]
                gh = ge[h, rows, :]
                p = jnp.where(allowed, jnp.exp(dot(k[h, cols, :], qh, NT)), 0.0)
                ds = (p * dot(v[h, cols, :], gh, NT)).astype(BF16)
                dv = dv + dot(p.astype(BF16), gh)
                dk = dk + dot(ds, qh)
                dq[h, :, rows] += dot(kt[h, :, cols], ds)
                new.append((dk, dv))
            return tuple(new)

        zero = jnp.zeros((BWD_K, LANES), F32)
        first = lo[i]
        count = (hi[i] - first + step - 1) // step
        done = lax.fori_loop(
            0, count, lambda n, c: queries(first + n * step, c), tuple((zero, zero) for _ in range(heads))
        )
        for part in range(2):
            joined = jnp.concatenate([done[h][part][:, :HEAD] for h in range(heads)], axis=1)
            dproj[part + 1, cols, :] = joined.astype(BF16)
        return 0

    lax.fori_loop(0, total // BWD_K, one_block, 0)

    def finish(i, _):
        rows = pl.ds(pl.multiple_of(i * PAD, LANES), PAD)
        joined = jnp.concatenate([dq[h, :, rows] for h in range(heads)], axis=0)
        dproj[0, rows, :] = (joined * HEAD**-0.5).T.astype(BF16)
        return 0

    lax.fori_loop(0, total // PAD, finish, 0)


def attention_back(ids, q, k, v, kt, out, grad, lse):
    lo, hi, idc, idr = ids
    heads, wide, _ = q.shape
    total = wide - PAD
    return pl.pallas_call(
        functools.partial(attention_back_kernel, heads, total),
        name="attention_back",
        cost_estimate=work(51),
        in_specs=[SMEM, SMEM] + [VMEM] * 9,
        out_specs=VMEM,
        out_shape=jax.ShapeDtypeStruct((3, total, heads * HEAD), BF16),
        scratch_shapes=[
            pltpu.VMEM((heads, wide, LANES), BF16),
            pltpu.VMEM((heads, wide, LANES), BF16),
            pltpu.VMEM((heads, HEAD, wide), F32),
        ],
        compiler_params=limit(60),
    )(lo, hi, idc, idr, q, k, v, kt, out, grad, lse.T)


def scene_ranges(scene, block):
    total = scene.shape[0]
    place = jnp.arange(total, dtype=jnp.int32)
    ids = jnp.where(scene >= 0, scene, -1 - place)
    before = jnp.sum(
        ((scene[None, :] >= 0) & (scene[None, :] < jnp.arange(6, dtype=jnp.int32)[:, None])).astype(jnp.int32), axis=1
    )
    first, last = scene[0::block], scene[block - 1 :: block]
    start = jnp.arange(total // block, dtype=jnp.int32) * block
    pick = lambda number: jnp.sum(
        jnp.where(number[:, None] == jnp.arange(6, dtype=jnp.int32)[None, :], before[None, :], 0), axis=1
    )
    lo = jnp.where(first >= 0, pick(first), start) // LANES
    hi = (jnp.where(last >= 0, pick(last + 1), start + block) + LANES - 1) // LANES
    padded = jnp.pad(ids, (0, PAD), constant_values=-(1 << 20))
    return lo, hi, padded[:, None], padded[None, :]


ROWS_MID = 288


def middle_kernel(
    weights, att, tok, cot, b_out, gain, shift, b_up, b_down,
    layer_out, grad_mid, grad_att, cells, w, acc, vec, bup, sems,
):
    step = pl.program_id(0)
    ndp, parts, piece, _ = cells.shape
    width = att.shape[2]

    @pl.when(step == 0)
    def _():
        def load(i):
            rows = pl.ds(i // parts * piece, piece)
            return pltpu.make_async_copy(weights.at[i // parts, i % parts], w.at[i % parts, rows], sems.at[i])

        for i in range(ndp * parts):
            load(i).start()
        for ref in (acc, vec, bup):
            ref[...] = jnp.zeros_like(ref)
        for i in range(ndp * parts):
            load(i).wait()

    out_rows = slice(0, OUT_ROWS)
    down_rows = slice(OUT_ROWS, OUT_ROWS + UP_ROWS)
    up_rows = slice(OUT_ROWS + UP_ROWS, VEC_AT)
    atts = [att[v] for v in range(parts)]
    middle = tok[...].astype(F32) + b_out[...]
    for v in range(parts):
        middle = middle + dot(atts[v], w[v, out_rows])
    unit, scale = normalise(middle)
    low = (unit * gain[...] + shift[...]).astype(BF16)
    cot_low = cot[...]
    cot_full = cot_low.astype(F32)
    out = middle + b_down[...]
    grad_norm = jnp.zeros_like(middle)
    for v in range(parts):
        hidden = dot(low, w[v, up_rows], NT) + b_up[v]
        below = 0.5 * (1.0 + lax.erf(hidden * 0.5**0.5))
        density = jnp.exp(-0.5 * hidden * hidden) * 0.3989422804014327
        active = (hidden * below).astype(BF16)
        out = out + dot(active, w[v, down_rows])
        grad_hidden = (dot(cot_low, w[v, down_rows], NT) * (below + hidden * density)).astype(BF16)
        grad_norm = grad_norm + dot(grad_hidden, w[v, up_rows])
        acc[v, down_rows] += dot(active, cot_low, TN)
        acc[v, up_rows] += dot(grad_hidden, low, TN)
        bup[v] += jnp.sum(grad_hidden.astype(F32), axis=0, keepdims=True)
    layer_out[...] = out.astype(BF16)
    scaled = grad_norm * gain[...]
    back = cot_full + scale * (
        scaled
        - jnp.mean(scaled, axis=-1, keepdims=True)
        - unit * jnp.mean(scaled * unit, axis=-1, keepdims=True)
    )
    grad_mid[...] = back
    back_low = back.astype(BF16)
    for v in range(parts):
        acc[v, out_rows] += dot(atts[v], back_low, TN)
        grad_att[v] = dot(back_low, w[v, out_rows], NT).astype(BF16)
    vec[0:1] += jnp.sum(grad_norm * unit, axis=0, keepdims=True)
    vec[1:2] += jnp.sum(grad_norm, axis=0, keepdims=True)
    vec[2:3] += jnp.sum(back, axis=0, keepdims=True)
    vec[3:4] += jnp.sum(cot_full, axis=0, keepdims=True)

    @pl.when(step == pl.num_programs(0) - 1)
    def _():
        for v in range(parts):
            acc[v, VEC_AT : VEC_AT + 8] = vec[...]
            acc[v, VEC_AT + 4 : VEC_AT + 5, :UP_ROWS] = bup[v]
            for d in range(ndp):
                cells[d, v] = acc[v, d * piece : (d + 1) * piece].astype(BF16)


def middle_part(weights, att, tok, cot, b_out, gain, shift, b_up, b_down):
    parts, rows, width = att.shape
    ndp = weights.shape[0]
    whole = lambda a: pl.BlockSpec(a.shape, lambda i: (0,) * len(a.shape))
    shape = lambda s, t: jax.ShapeDtypeStruct(s, t)
    tile = pl.BlockSpec((ROWS_MID, D), lambda i: (i, 0))
    heads_tile = pl.BlockSpec((parts, ROWS_MID, width), lambda i: (0, i, 0))
    cells = shape((ndp, parts, UNITS // ndp, D), BF16)
    return pl.pallas_call(
        middle_kernel,
        name="middle_part",
        cost_estimate=work(37),
        grid=(rows // ROWS_MID,),
        in_specs=[ANY, heads_tile, tile, tile] + [whole(a) for a in (b_out, gain, shift, b_up, b_down)],
        out_specs=[tile, tile, heads_tile, whole(cells)],
        out_shape=[shape((rows, D), BF16), shape((rows, D), F32), shape((parts, rows, width), BF16), cells],
        scratch_shapes=[
            pltpu.VMEM((parts, UNITS, D), BF16),
            pltpu.VMEM((parts, UNITS, D), F32),
            pltpu.VMEM((8, D), F32),
            pltpu.VMEM(b_up.shape, F32),
            DMA((ndp * parts,)),
        ],
        compiler_params=limit(60),
    )(weights, att, tok, cot, b_out, gain, shift, b_up, b_down)


def finish_kernel(
    dproj, normed, full, w, grad_mid, gain, cells, grad, vec_sum, d_w, sums,
    part, theirs, sent, crossed, low, back, acc, w_part, w_in, w_z, w_all, vec, vz, vd,
    sib_s, sib_r, cross_s, cross_r, swap_s, swap_r, vz_s, vz_r, vd_s, vd_r,
    ws_s, ws_r, wz_s, wz_r, wg_s, wg_r, wf_s, wf_r,
    u_in, u_all, uz_s, uz_r, ug_s, ug_r, uf_s, uf_r,
):
    me = Place()
    foreign = jnp.logical_not(me.native)
    rows = grad_mid.shape[0]
    piece = rows // PIECES
    width = w.shape[2]
    ndp = vd.shape[0]
    groups, w_rows, _ = w_part.shape
    group = me.d // 2
    around = [(me.d, lax.rem(me.m + k, 4)) for k in range(1, 4)]
    along = [(lax.rem(me.d + k, ndp), me.m) for k in range(1, ndp)]
    greet([me.partner] + around + along)

    order = [2 * (1 - me.hf) + 1 - me.r, 2 * (1 - me.hf) + me.r, 2 * me.hf + 1 - me.r, 2 * me.hf + me.r]

    def to_sib(k, p):
        slot = k % 2
        return remote(part.at[k, p], theirs.at[slot, p], sib_s.at[slot, p], sib_r.at[slot, p], me.sibling)

    def to_cross(p):
        return remote(sent.at[p], crossed.at[p], cross_s.at[p], cross_r.at[p], me.cross)

    def to_partner(p):
        return remote(low.at[p], back.at[p], swap_s.at[p], swap_r.at[p], me.partner)

    def unit_z(j):
        to = lax.rem(me.m + 1 + j, 4)
        return remote(cells.at[to], u_in.at[j], uz_s.at[j], uz_r.at[j], around[j])

    def unit_give(j):
        return remote(
            u_all.at[me.d], u_all.at[me.d], ug_s.at[j], ug_r.at[j], (2 * lax.rem(group + j, groups) + me.c, me.m)
        )

    def unit_forward(j):
        source = 2 * lax.rem(group + groups - j, groups) + me.c
        return remote(u_all.at[source], u_all.at[source], uf_s.at[j], uf_r.at[j], me.sibling)

    def unit_give_in(j):
        source = 2 * lax.rem(group + groups - j, groups) + me.c
        return remote(u_all.at[source], u_all.at[source], ug_s.at[j], ug_r.at[j], (source, me.m))

    def unit_forward_in(j):
        source = 2 * lax.rem(group + groups - j, groups) + 1 - me.c
        return remote(u_all.at[source], u_all.at[source], uf_s.at[j], uf_r.at[j], me.sibling)

    for j in range(3):
        unit_z(j).start()
    acc[...] = jnp.zeros_like(acc)
    vec[...] = jnp.zeros_like(vec)

    def compute(k):
        def one(p, _):
            span = pl.ds(pl.multiple_of(order[k] * rows + p * piece, 16), piece)
            rounded = normed[span, :]
            total = jnp.zeros((piece, D), F32)
            for c in range(3):
                given = dproj[c, span, :]
                total = total + dot(given, w[c], NT)
                acc[c * width : (c + 1) * width, :] += dot(given, rounded, TN)
            part[k, p] = total.astype(BF16)
            unit, _ = normalise(full[span, :].astype(F32))
            vec[0:1] += jnp.sum(total * unit, axis=0, keepdims=True)
            vec[1:2] += jnp.sum(total, axis=0, keepdims=True)

            @pl.when(me.native if k < 2 else foreign)
            def _():
                to_sib(k, p).start()

            return 0

        lax.fori_loop(0, PIECES, one, 0)

    def pass_across(k):
        for p in range(PIECES):
            to_sib(k, p).wait_recv()
            sent[p] = (part[k, p].astype(F32) + theirs[0, p].astype(F32)).astype(BF16)
            to_cross(p).start()

    def conclude(k, p):
        to_sib(k, p).wait_recv()
        to_cross(p).wait_recv()
        total = part[k, p].astype(F32) + theirs[1, p].astype(F32) + crossed[p].astype(F32)
        span = pl.ds(pl.multiple_of(me.q * rows + p * piece, 16), piece)
        unit, scale = normalise(full[span, :].astype(F32))
        scaled = total * gain[...]
        return grad_mid[p * piece : (p + 1) * piece, :] + scale * (
            scaled
            - jnp.mean(scaled, axis=-1, keepdims=True)
            - unit * jnp.mean(scaled * unit, axis=-1, keepdims=True)
        )

    def conclude_foreign(p):
        low[p] = conclude(1, p).astype(BF16)
        to_partner(p).start()

    compute(0)

    @pl.when(foreign)
    def _():
        pass_across(0)

    compute(1)
    compute(2)
    unit_sum = cells[me.m].astype(F32)
    for j in range(3):
        unit_z(j).wait_recv()
        unit_sum = unit_sum + u_in[j].astype(F32)
    u_all[me.d] = unit_sum.astype(BF16)
    for j in range(1, groups):
        unit_give(j).start()
    unit_forward(0).start()

    @pl.when(me.native)
    def _():
        pass_across(2)

    @pl.when(foreign)
    def _():
        conclude_foreign(0)

    compute(3)

    for i in range(groups):
        w_part[i] = acc[i * w_rows : (i + 1) * w_rows, :].astype(BF16)

    def other_group(k):
        return lax.rem(group + k, groups)

    def w_send(k):
        to = other_group(k)
        return remote(w_part.at[to], w_in.at[k], ws_s.at[k], ws_r.at[k], (2 * to + me.c, me.m))

    for k in range(1, groups):
        w_send(k).start()

    vz[me.m] = vec[...]

    def around_copy(k):
        return remote(vz.at[me.m], vz.at[me.m], vz_s.at[k], vz_r.at[k], around[k])

    for k in range(3):
        around_copy(k).start()

    @pl.when(foreign)
    def _():
        for p in range(1, PIECES):
            conclude_foreign(p)

    for k in range(3):
        source = lax.rem(me.m + 3 - k, 4)
        remote(vz.at[source], vz.at[source], vz_s.at[k], vz_r.at[k], around[k]).wait_recv()
    vd[me.d] = vz[0] + vz[1] + vz[2] + vz[3]

    def along_copy(k):
        return remote(vd.at[me.d], vd.at[me.d], vd_s.at[k], vd_r.at[k], along[k])

    for k in range(ndp - 1):
        along_copy(k).start()

    w_sum = w_part[group].astype(F32)
    for k in range(1, groups):
        w_send(k).wait_recv()
        w_sum = w_sum + w_in[k].astype(F32)

    to_z = remote(w_z.at[0], w_z.at[1], wz_s, wz_r, (me.d, lax.rem(me.m + 2, 4)))

    def w_give(k):
        return remote(
            w_all.at[group], w_all.at[group], wg_s.at[k], wg_r.at[k], (2 * other_group(k) + me.c, me.m)
        )

    def w_forward(k):
        source = lax.rem(group + groups - k, groups)
        return remote(w_all.at[source], w_all.at[source], wf_s.at[k], wf_r.at[k], me.sibling)

    @pl.when(foreign)
    def _():
        w_z[0] = w_sum.astype(BF16)
        to_z.start()

    @pl.when(me.native)
    def _():
        to_z.wait_recv()
        w_all[group] = (w_sum + w_z[1].astype(F32)).astype(BF16)
        for k in range(1, groups):
            w_give(k).start()
        w_forward(0).start()
        for p in range(PIECES):
            grad[p * piece : (p + 1) * piece, :] = conclude(3, p)
        for k in range(1, groups):
            source = lax.rem(group + groups - k, groups)
            remote(
                w_all.at[source], w_all.at[source], wg_s.at[k], wg_r.at[k], (2 * source + me.c, me.m)
            ).wait_recv()
            w_forward(k).start()

    for k in range(ndp - 1):
        source = lax.rem(me.d + ndp - 1 - k, ndp)
        remote(vd.at[source], vd.at[source], vd_s.at[k], vd_r.at[k], along[k]).wait_recv()
    total = vd[0]
    for i in range(1, ndp):
        total = total + vd[i]
    vec_sum[...] = total

    @pl.when(foreign)
    def _():
        for k in range(groups):
            source = lax.rem(group + groups - k, groups)
            remote(w_all.at[source], w_all.at[source], wf_s.at[k], wf_r.at[k], me.sibling).wait_recv()

    for i in range(groups):
        d_w[i * w_rows : (i + 1) * w_rows, :] = w_all[i].astype(F32)
    for j in range(1, groups):
        unit_give_in(j).wait_recv()
        unit_forward(j).start()
    for j in range(groups):
        unit_forward_in(j).wait_recv()
    height = sums.shape[0] // ndp
    for i in range(ndp):
        sums[i * height : (i + 1) * height, :] = u_all[i].astype(F32)
    for j in range(groups):
        unit_forward(j).wait_send()
    for j in range(1, groups):
        unit_give(j).wait_send()
    for j in range(3):
        unit_z(j).wait_send()

    @pl.when(foreign)
    def _():
        for p in range(PIECES):
            to_partner(p).wait_recv()
            grad[p * piece : (p + 1) * piece, :] = back[p].astype(F32)
        for p in range(PIECES):
            to_partner(p).wait_send()
            to_sib(2, p).wait_send()
            to_sib(3, p).wait_send()
        to_z.wait_send()

    @pl.when(me.native)
    def _():
        for p in range(PIECES):
            to_sib(0, p).wait_send()
            to_sib(1, p).wait_send()
        for k in range(1, groups):
            w_give(k).wait_send()
        for k in range(groups):
            w_forward(k).wait_send()

    for p in range(PIECES):
        to_cross(p).wait_send()
    for k in range(1, groups):
        w_send(k).wait_send()
    for k in range(3):
        around_copy(k).wait_send()
    for k in range(ndp - 1):
        along_copy(k).wait_send()


def finish(dproj, normed, full, w, grad_mid, gain, cells, ndp):
    rows = grad_mid.shape[0]
    piece = rows // PIECES
    pieces = (PIECES, piece, D)
    groups = ndp // 2
    columns = 3 * w.shape[2]
    cut = (groups, columns // groups, D)
    return pl.pallas_call(
        finish_kernel,
        name="finish",
        cost_estimate=work(60),
        in_specs=[VMEM] * 7,
        out_specs=[VMEM] * 4,
        out_shape=[
            jax.ShapeDtypeStruct((rows, D), F32),
            jax.ShapeDtypeStruct((8, D), F32),
            jax.ShapeDtypeStruct((columns, D), F32),
            jax.ShapeDtypeStruct((UNITS, D), F32),
        ],
        scratch_shapes=[
            pltpu.VMEM((4,) + pieces, BF16),
            pltpu.VMEM((2,) + pieces, BF16),
            pltpu.VMEM(pieces, BF16),
            pltpu.VMEM(pieces, BF16),
            pltpu.VMEM(pieces, BF16),
            pltpu.VMEM(pieces, BF16),
            pltpu.VMEM((columns, D), F32),
            pltpu.VMEM(cut, BF16),
            pltpu.VMEM(cut, BF16),
            pltpu.VMEM((2,) + cut[1:], BF16),
            pltpu.VMEM(cut, BF16),
            pltpu.VMEM((8, D), F32),
            pltpu.VMEM((4, 8, D), F32),
            pltpu.VMEM((ndp, 8, D), F32),
            DMA((2, PIECES)),
            DMA((2, PIECES)),
            DMA((PIECES,)),
            DMA((PIECES,)),
            DMA((PIECES,)),
            DMA((PIECES,)),
            DMA((3,)),
            DMA((3,)),
            DMA((ndp - 1,)),
            DMA((ndp - 1,)),
            DMA((groups,)),
            DMA((groups,)),
            DMA,
            DMA,
            DMA((groups,)),
            DMA((groups,)),
            DMA((groups,)),
            DMA((groups,)),
            pltpu.VMEM((3, UNITS // ndp, D), BF16),
            pltpu.VMEM((ndp, UNITS // ndp, D), BF16),
            DMA((3,)),
            DMA((3,)),
            DMA((groups,)),
            DMA((groups,)),
            DMA((groups,)),
            DMA((groups,)),
        ],
        compiler_params=pltpu.CompilerParams(
            collective_id=4, has_side_effects=True, vmem_limit_bytes=60 << 20
        ),
    )(dproj, normed, full, w, grad_mid, gain, cells)


def swap_pairs(ndp):
    return [
        (d * 4 + m, (d ^ 1) * 4 + (m + 2) % 4) for d in range(ndp) for m in range(4) if d % 2 != m // 2
    ]


def weight_piece(w_out, w_up, w_down, ndp):
    block = jnp.concatenate([w_out, w_down, w_up.T, jnp.zeros((UNITS - w_out.shape[0] - 2 * w_down.shape[0], D), BF16)])
    piece = UNITS // ndp
    return lax.dynamic_slice_in_dim(block, lax.axis_index("dp") * piece, piece, 0)


def sum_over_dp(cells):
    return lax.psum_scatter(cells.reshape(-1, D), "dp", scatter_dimension=0, tiled=True)


def shards(
    tokens,
    scene_ids,
    gain_one,
    shift_one,
    w_qkv,
    w_out,
    b_out,
    gain_two,
    shift_two,
    w_up,
    b_up,
    w_down,
    b_down,
    cotangent,
    ndp,
):
    d, m = lax.axis_index("dp"), lax.axis_index("mp")
    native = d % 2 == m // 2
    line = lambda v: v.reshape(1, D)
    both = ("dp", "mp")
    swap = swap_pairs(ndp)

    full, own_tok, w_mine, scene, all_bup, normed, q, k, v, kt, vt, weights = start(
        tokens,
        w_qkv,
        scene_ids.reshape(-1, LANES),
        b_up.reshape(1, FF // 4),
        line(gain_one),
        line(shift_one),
        weight_piece(w_out, w_up, w_down, ndp),
        ndp,
    )
    w_mine = w_mine.reshape(w_qkv.shape)
    weights = lax.all_gather(weights, "dp", axis=0)
    scene = scene.reshape(-1)
    lo_f, hi_f, idc, idr = scene_ranges(scene, FWD_Q)
    lo_b, hi_b = (lo_f, hi_f) if BWD_K == FWD_Q else scene_ranges(scene, BWD_K)[:2]
    sent_cot, q = lax.optimization_barrier((cotangent, q))
    own_cot = jnp.where(native, cotangent, lax.ppermute(sent_cot, both, swap))
    attended, lse = attention((lo_f, hi_f, idc, idr), q, k, vt)
    att = exchange(attended, False, 2)
    layer_out, grad_mid, grad_att, cells = middle_part(
        weights, att, own_tok, own_cot, line(b_out), line(gain_two), line(shift_two), all_bup, line(b_down)
    )
    grad_heads = exchange(grad_att, True, 3)
    sent_out, grad_heads = lax.optimization_barrier((layer_out, grad_heads))
    layer_out = jnp.where(native, layer_out, lax.ppermute(sent_out, both, swap))
    cells = sum_over_dp(cells)
    dproj = attention_back((lo_b, hi_b, idc, idr), q, k, v, kt, attended, grad_heads, lse)
    cells, dproj = lax.optimization_barrier((cells, dproj))
    tokens_grad, one_sum, d_qkv, sums = finish(
        dproj, normed, full, w_mine, grad_mid, line(gain_one), cells.reshape(4, -1, D), ndp
    )
    g_qkv = jnp.swapaxes(d_qkv.reshape(3, -1, D), 1, 2)
    g_vec = sums[VEC_AT : VEC_AT + 4]
    return (
        layer_out,
        tokens_grad,
        one_sum[0],
        one_sum[1],
        g_qkv,
        sums[:OUT_ROWS],
        g_vec[2],
        g_vec[0],
        g_vec[1],
        sums[OUT_ROWS + UP_ROWS : VEC_AT].T,
        sums[VEC_AT + 4, :UP_ROWS],
        sums[OUT_ROWS : OUT_ROWS + UP_ROWS],
        g_vec[3],
    )


def solution(mesh):
    ndp = mesh.shape["dp"]
    return jax.shard_map(
        functools.partial(shards, ndp=ndp),
        mesh=mesh,
        in_specs=(
            P(("dp", "mp"), None),
            P("dp"),
            P(),
            P(),
            P(None, None, "mp"),
            P("mp", None),
            P(),
            P(),
            P(),
            P(None, "mp"),
            P("mp"),
            P("mp", None),
            P(),
            P(("dp", "mp"), None),
        ),
        out_specs=(
            P(("dp", "mp"), None),
            P(("dp", "mp"), None),
            P(),
            P(),
            P(None, None, "mp"),
            P("mp", None),
            P(),
            P(),
            P(),
            P(None, "mp"),
            P("mp"),
            P("mp", None),
            P(),
        ),
        check_vma=False,
    )
```

```python
import functools

import jax
import jax.numpy as jnp
from jax import lax
from jax.experimental import pallas as pl
from jax.experimental.pallas import tpu as pltpu
from jax.sharding import PartitionSpec as P

HEAD = 64
D = 768
FF = 1536
LANES = 128
PAD = 384
OUT_ROWS = D // 4
UP_ROWS = FF // 4
VEC_AT = OUT_ROWS + 2 * UP_ROWS
UNITS = 1024
EPS = 1e-05
MASKED = -1e30
MESH = pl.DeviceIdType.MESH
F32 = jnp.float32
BF16 = jnp.bfloat16
VMEM = pl.BlockSpec(memory_space=pltpu.VMEM)
SMEM = pl.BlockSpec(memory_space=pltpu.SMEM)
ANY = pl.BlockSpec(memory_space=pl.ANY)
DMA = pltpu.SemaphoreType.DMA

NN = (((1,), (0,)), ((), ()))
NT = (((1,), (1,)), ((), ()))
TN = (((0,), (0,)), ((), ()))


def dot(a, b, dims=NN):
    return lax.dot_general(a, b, dims, preferred_element_type=F32)


def work(us):
    return pl.CostEstimate(flops=us * 10**9, bytes_accessed=us * 3 * 10**6, transcendentals=0)


def limit(mib):
    return pltpu.CompilerParams(vmem_limit_bytes=mib << 20)


class Place:
    def __init__(self):
        self.d = lax.axis_index("dp")
        self.m = lax.axis_index("mp")
        self.c = lax.rem(self.d, 2)
        self.r = lax.rem(self.m, 2)
        self.hf = self.m // 2
        self.q = 2 * self.c + self.r
        self.native = self.c == self.hf
        self.sibling = (self.d + 1 - 2 * self.c, self.m)
        self.cross = (self.d, self.m + 1 - 2 * self.r)
        self.partner = (self.d + 1 - 2 * self.c, lax.rem(self.m + 2, 4))

    def member(self, quarter):
        return (self.d - self.c + quarter // 2, 2 * self.hf + quarter % 2)


def greet(others):
    barrier = pltpu.get_barrier_semaphore()
    for other in others:
        pl.semaphore_signal(barrier, inc=1, device_id=other, device_id_type=MESH)
    pl.semaphore_wait(barrier, len(others))


def remote(src, dst, send, recv, device):
    return pltpu.make_async_remote_copy(
        src_ref=src, dst_ref=dst, send_sem=send, recv_sem=recv, device_id=device, device_id_type=MESH
    )


PIECES = 3
TILE = 384


def normalise(x):
    centred = x - jnp.mean(x, axis=-1, keepdims=True)
    scale = lax.rsqrt(jnp.mean(centred * centred, axis=-1, keepdims=True) + EPS)
    return centred * scale, scale


def widen(x, ones, rows):
    lane = lax.broadcasted_iota(jnp.int32, (rows, LANES - HEAD), 1)
    return jnp.concatenate([x, jnp.where(lane < ones, 1.0, 0.0).astype(x.dtype)], axis=1)


def start_kernel(
    heads, tok, wq, ids, bup, gain, shift, mine,
    full, own, w_out, ids_own, bups, normed, q, k, v, kt, vt, units,
    buf, w, low_s, q_s, k_s, v_s, kt_s, vt_s,
    swap_s, swap_r, cross_s, cross_r, sib_s, sib_r, fwd_s, fwd_r, w_s, w_r, ids_s, ids_r, b_s, b_r, out_s, late_s,
    uz_s, uz_r,
):
    me = Place()
    foreign = jnp.logical_not(me.native)
    rows = tok.shape[0]
    piece = rows // PIECES
    total = buf.shape[0]
    tiles = total // TILE
    groups = w.shape[1]
    group = me.d // 2
    around = [(me.d, lax.rem(me.m + j, 4)) for j in range(1, 4)]
    lines = [(2 * lax.rem(group + j, groups) + me.c, me.m) for j in range(1, groups)]
    greet([me.sibling, me.partner] + around + lines)

    def rows_of(quarter, n):
        p = jnp.where(me.hf == 0, n, PIECES - 1 - n)
        return pl.ds(pl.multiple_of(quarter * rows + p * piece, 16), piece)

    def part(quarter, n):
        return buf.at[rows_of(quarter, n)]

    sib_q = 2 * (1 - me.c) + me.r
    cross_q = 2 * me.c + 1 - me.r
    sib_cross_q = 2 * (1 - me.c) + 1 - me.r

    def swap(n):
        p = jnp.where(me.hf == 1, n, PIECES - 1 - n)
        src = tok.at[pl.ds(pl.multiple_of(p * piece, 16), piece)]
        dst = buf.at[pl.ds(pl.multiple_of(sib_q * rows + p * piece, 16), piece)]
        return remote(src, dst, swap_s.at[n], swap_r.at[n], me.partner)

    def swap_in(n):
        return remote(part(me.q, n), part(me.q, n), swap_s.at[n], swap_r.at[n], me.partner)

    def cross(quarter, n):
        return remote(part(quarter, n), part(quarter, n), cross_s.at[n], cross_r.at[n], me.cross)

    def sib(quarter, n):
        return remote(part(quarter, n), part(quarter, n), sib_s.at[n], sib_r.at[n], me.sibling)

    def forward(quarter, n):
        return remote(part(quarter, n), part(quarter, n), fwd_s.at[n], fwd_r.at[n], me.sibling)

    weight = remote(wq.at[:, group], w.at[:, group], w_s.at[0], w_r.at[0], me.partner)

    def weight_share(j):
        return remote(w.at[:, group], w.at[:, group], w_s.at[j], w_r.at[j], lines[j - 1])

    def weight_in(j):
        source = lax.rem(group + groups - j, groups)
        return remote(w.at[:, source], w.at[:, source], w_s.at[j], w_r.at[j], lines[j - 1])

    unit_own = pltpu.make_async_copy(mine, units.at[me.m], late_s.at[7])

    def unit_z(j, source):
        return remote(mine, units.at[source], uz_s.at[j], uz_r.at[j], around[j])

    scenes = remote(ids, ids_own, ids_s, ids_r, me.sibling)
    unit_own.start()
    for j in range(3):
        remote(bup, bups.at[me.m], b_s.at[j], b_r.at[j], around[j]).start()
    bups[me.m] = bup[...]

    @pl.when(me.native)
    def _():
        scenes.start()
        buf[pl.ds(pl.multiple_of(me.q * rows, 16), rows), :] = tok[...]
        for n in range(PIECES):
            cross(me.q, n).start()
            sib(me.q, n).start()
        w[...] = wq[...]
        ids_own[...] = ids[...]

    @pl.when(foreign)
    def _():
        weight.start()
        for n in range(PIECES):
            swap(n).start()

    def share(n):
        swap_in(n).wait_recv()
        cross(me.q, n).start()
        sib(me.q, n).start()

    def pass_on(n):
        cross(cross_q, n).wait_recv()
        forward(cross_q, n).start()

    def from_sibling(n):
        sib(sib_q, n).wait_recv()
        forward(sib_cross_q, n).wait_recv()

    def outputs(t):
        span = pl.ds(pl.multiple_of(t * TILE, LANES), TILE)
        pairs = [
            (low_s.at[span], normed.at[span]),
            (buf.at[span], full.at[span]),
            (q_s.at[:, span], q.at[:, span]),
            (k_s.at[:, span], k.at[:, span]),
            (v_s.at[:, span], v.at[:, span]),
            (kt_s.at[:, :, span], kt.at[:, :, span]),
            (vt_s.at[:, :, span], vt.at[:, :, span]),
        ]
        return [pltpu.make_async_copy(src, dst, out_s.at[t, j]) for j, (src, dst) in enumerate(pairs)]

    line = lax.broadcasted_iota(jnp.int32, (16, TILE), 0)
    ones = jnp.where(line < 1, 1.0, 0.0).astype(BF16)

    def compute(first, stride, count):
        def one(n, _):
            at = first + stride * n
            t = jnp.where(me.hf == 0, at, tiles - 1 - at)
            span = pl.ds(pl.multiple_of(t * TILE, LANES), TILE)
            unit, _ = normalise(buf[span, :].astype(F32))
            low = (unit * gain[...] + shift[...]).astype(BF16)
            low_s[span, :] = low
            qs = (dot(low, w[0].reshape(D, -1)).astype(BF16).astype(F32) * HEAD**-0.5).astype(BF16)
            ks = dot(low, w[1].reshape(D, -1))
            vs = dot(low, w[2].reshape(D, -1))
            kts = ks.T.astype(BF16)
            vts = vs.T.astype(BF16)
            ks = ks.astype(BF16)
            vs = vs.astype(BF16)
            for h in range(heads):
                cols = slice(h * HEAD, (h + 1) * HEAD)
                q_s[h, span, :] = widen(qs[:, cols], 0, TILE)
                k_s[h, span, :] = widen(ks[:, cols], 3, TILE)
                v_s[h, span, :] = widen(vs[:, cols], 3, TILE)
                kt_s[h, :, span] = kts[cols]
                vt_s[h, :HEAD, span] = vts[cols]
                vt_s[h, HEAD:, span] = ones
            for copy in outputs(t):
                copy.start()
            return 0

        lax.fori_loop(0, count, one, 0)

    pad = pl.ds(total, PAD)
    zeros = jnp.zeros((heads, PAD, LANES), BF16)
    for ref in (q_s, k_s, v_s):
        ref[:, pad, :] = zeros
    for ref in (kt_s, vt_s):
        ref[:, :, pad] = jnp.zeros((heads, ref.shape[1], PAD), BF16)
    padding = [
        pltpu.make_async_copy(src, dst, late_s.at[j])
        for j, (src, dst) in enumerate(
            [(a.at[:, pad], b.at[:, pad]) for a, b in ((q_s, q), (k_s, k), (v_s, v))]
            + [(a.at[:, :, pad], b.at[:, :, pad]) for a, b in ((kt_s, kt), (vt_s, vt))]
        )
    ]
    for copy in padding:
        copy.start()

    @pl.when(me.native)
    def _():
        for n in range(PIECES):
            pass_on(n)

    @pl.when(foreign)
    def _():
        weight.wait_recv()
        for j in range(1, groups):
            weight_share(j).start()
        for n in range(PIECES):
            share(n)
        for j in range(1, groups):
            weight_in(j).wait_recv()
        for n in range(PIECES):
            from_sibling(n)

    for j in range(3):
        unit_z(j, me.m).start()
    compute(0, 1, 2)

    @pl.when(foreign)
    def _():
        pass_on(0)

    compute(2, 1, 2)

    @pl.when(foreign)
    def _():
        pass_on(1)

    @pl.when(me.native)
    def _():
        from_sibling(0)

    compute(4, 1, 1)

    @pl.when(me.native)
    def _():
        from_sibling(1)

    compute(5, 2, 2)

    @pl.when(foreign)
    def _():
        pass_on(2)

    @pl.when(me.native)
    def _():
        from_sibling(2)

    own_copy = pltpu.make_async_copy(buf.at[pl.ds(pl.multiple_of(me.q * rows, 16), rows)], own, late_s.at[5])
    w_copy = pltpu.make_async_copy(w, w_out, late_s.at[6])
    own_copy.start()
    w_copy.start()
    compute(6, 2, 2)
    unit_own.wait()
    for j in range(3):
        unit_z(j, lax.rem(me.m + 3 - j, 4)).wait_recv()
        unit_z(j, me.m).wait_send()

    for j in range(3):
        source = lax.rem(me.m + 3 - j, 4)
        remote(bup, bups.at[source], b_s.at[j], b_r.at[j], around[j]).wait_recv()
        remote(bup, bups.at[me.m], b_s.at[j], b_r.at[j], around[j]).wait_send()

    @pl.when(me.native)
    def _():
        scenes.wait_send()

    @pl.when(foreign)
    def _():
        scenes.wait_recv()
        weight.wait_send()
        for j in range(1, groups):
            weight_share(j).wait_send()
        for n in range(PIECES):
            swap(n).wait_send()

    for n in range(PIECES):
        cross(me.q, n).wait_send()
        sib(me.q, n).wait_send()
        forward(cross_q, n).wait_send()
    for copy in padding + [own_copy, w_copy]:
        copy.wait()

    def finish_tile(t, _):
        for copy in outputs(t):
            copy.wait()
        return 0

    lax.fori_loop(0, tiles, finish_tile, 0)


def start(tokens, w_qkv, scene_ids, b_up, gain, shift, mine, ndp):
    rows = tokens.shape[0]
    total = 4 * rows
    heads = w_qkv.shape[2] // HEAD
    groups = ndp // 2
    w_qkv = w_qkv.reshape(3, groups, D // groups, -1)
    units = (4,) + mine.shape
    wide = total + PAD
    shape = jax.ShapeDtypeStruct
    rowed = (heads, wide, LANES)
    k_cols, v_cols = (heads, HEAD, wide), (heads, HEAD + 16, wide)
    three = DMA((PIECES,))
    return pl.pallas_call(
        functools.partial(start_kernel, heads),
        name="start",
        cost_estimate=work(50),
        in_specs=[VMEM] * 6 + [ANY],
        out_specs=[ANY, ANY, ANY, VMEM, VMEM] + [ANY] * 7,
        out_shape=[
            shape((total, D), BF16),
            shape((rows, D), BF16),
            shape(w_qkv.shape, BF16),
            shape(scene_ids.shape, jnp.int32),
            shape((4,) + b_up.shape, F32),
            shape((total, D), BF16),
            shape(rowed, BF16),
            shape(rowed, BF16),
            shape(rowed, BF16),
            shape(k_cols, BF16),
            shape(v_cols, BF16),
            shape(units, BF16),
        ],
        scratch_shapes=[
            pltpu.VMEM((total, D), BF16),
            pltpu.VMEM(w_qkv.shape, BF16),
            pltpu.VMEM((total, D), BF16),
            pltpu.VMEM(rowed, BF16),
            pltpu.VMEM(rowed, BF16),
            pltpu.VMEM(rowed, BF16),
            pltpu.VMEM(k_cols, BF16),
            pltpu.VMEM(v_cols, BF16),
        ]
        + [three] * 8
        + [DMA((groups,))] * 2
        + [DMA] * 2
        + [DMA((3,))] * 2
        + [DMA((total // TILE, 7)), DMA((8,))]
        + [DMA((3,))] * 2,
        compiler_params=pltpu.CompilerParams(
            collective_id=1, has_side_effects=True, vmem_limit_bytes=60 << 20
        ),
    )(tokens, w_qkv, scene_ids, b_up, gain, shift, mine)


BLOCK = 256


def blocks(total):
    return -(-total // BLOCK)


def attention_kernel(heads, total, lo, hi, idc, idr, q, k, vt, out, lse):
    def one_block(i, _):
        r0 = pl.multiple_of(i * BLOCK, LANES)
        qs = [q[h, pl.ds(r0, BLOCK), :] for h in range(heads)]
        mine = idr[:, pl.ds(r0, BLOCK)]

        def keys(size, at, carry):
            cols = pl.ds(pl.multiple_of(at * LANES, LANES), size)
            allowed = idc[cols, :] == mine
            scores = [jnp.where(allowed, dot(k[h, cols, :], qs[h], NT), MASKED) for h in range(heads)]
            new = []
            for h in range(heads):
                top, acc = carry[h]
                above = jnp.maximum(top, jnp.max(scores[h], axis=0, keepdims=True))
                p = jnp.exp(scores[h] - above).astype(BF16)
                acc = acc * jnp.exp(top - above) + dot(vt[h, :, cols], p)
                new.append((above, acc))
            return tuple(new)

        done = tuple((jnp.full((1, BLOCK), MASKED, F32), jnp.zeros((vt.shape[1], BLOCK), F32)) for _ in range(heads))
        first = lo[i]
        done = in_steps(first, hi[i], keys, done)
        valid = jnp.where(mine >= 0, 1.0, 0.0)
        mixed = []
        for h in range(heads):
            top, acc = done[h]
            row_total = acc[HEAD : HEAD + 1]
            mixed.append(acc[:HEAD] * (valid / row_total))
            lse[pl.ds(h, 1), pl.ds(r0, BLOCK)] = top + jnp.log(row_total)
        out[pl.ds(r0, BLOCK), :] = jnp.concatenate(mixed, axis=0).T.astype(BF16)
        return 0

    lax.fori_loop(0, blocks(total), one_block, 0)


def in_steps(first, last, body, carry):
    wide, narrow = 2 * BLOCK // LANES, BLOCK // LANES
    count = (last - first + narrow - 1) // narrow
    carry = lax.fori_loop(0, count // 2, lambda n, c: body(2 * BLOCK, first + n * wide, c), carry)
    return lax.fori_loop(0, count % 2, lambda n, c: body(BLOCK, first + (count - 1) * narrow, c), carry)


def attention(ids, q, k, vt):
    lo, hi, idc, idr = ids
    heads, wide, _ = q.shape
    total = wide - PAD
    rows = blocks(total) * BLOCK
    return pl.pallas_call(
        functools.partial(attention_kernel, heads, total),
        name="attention",
        cost_estimate=work(31),
        in_specs=[SMEM, SMEM] + [VMEM] * 5,
        out_specs=[VMEM, VMEM],
        out_shape=[
            jax.ShapeDtypeStruct((rows, heads * HEAD), BF16),
            jax.ShapeDtypeStruct((heads, rows), F32),
        ],
        compiler_params=limit(56),
    )(lo, hi, idc, idr, q, k, vt)


def attention_back_kernel(heads, total, lo, hi, idc, idr, q, k, v, kt, out, grad, lse, dproj, g, delta, dq):
    wide = q.shape[1]
    width = heads * HEAD
    head_of = lax.broadcasted_iota(jnp.int32, (8, width), 1) // HEAD
    pick = jnp.where(head_of == lax.broadcasted_iota(jnp.int32, (8, width), 0), 1.0, 0.0).astype(BF16)
    none = jnp.zeros((PAD, LANES - HEAD), BF16)

    def prepare(i, _):
        rows = pl.ds(pl.multiple_of(i * PAD, LANES), PAD)
        grads = jnp.where(idc[rows, :] >= 0, grad[rows, :].astype(F32), 0.0)
        inner = grads * out[rows, :].astype(F32)
        high = inner.astype(BF16)
        rest = (inner - high.astype(F32)).astype(BF16)
        delta[:, rows] = dot(pick, high, NT) + dot(pick, rest, NT)
        grads = grads.astype(BF16)
        for h in range(heads):
            g[h, rows, :] = jnp.concatenate([grads[:, h * HEAD : (h + 1) * HEAD], none], axis=1)
            dq[h, :, rows] = jnp.zeros((HEAD, PAD), F32)
        return 0

    lax.fori_loop(0, total // PAD, prepare, 0)
    tail = wide - total
    delta[:, total:] = jnp.zeros((8, tail), F32)
    for h in range(heads):
        g[h, total:, :] = jnp.zeros((tail, LANES), BF16)
        dq[h, :, total:] = jnp.zeros((HEAD, tail), F32)

    def one_block(i, _):
        c0 = pl.multiple_of(i * BLOCK, LANES)
        cols = pl.ds(c0, BLOCK)
        mine = idc[cols, :]

        def queries(size, at, carry):
            rows = pl.ds(pl.multiple_of(at * LANES, LANES), size)
            allowed = mine == idr[:, rows]
            both = [
                (dot(k[h, cols, :], q[h, rows, :], NT), dot(v[h, cols, :], g[h, rows, :], NT)) for h in range(heads)
            ]
            new = []
            for h in range(heads):
                dk, dv = carry[h]
                s, dp = both[h]
                p = jnp.where(allowed, jnp.exp(s - lse[h : h + 1, rows]), 0.0)
                ds = (p * (dp - delta[h : h + 1, rows])).astype(BF16)
                dv = dv + dot(p.astype(BF16), g[h, rows, :])
                dk = dk + dot(ds, q[h, rows, :])
                dq[h, :, rows] += dot(kt[h, :, cols], ds)
                new.append((dk, dv))
            return tuple(new)

        zero = jnp.zeros((BLOCK, LANES), F32)
        done = in_steps(lo[i], hi[i], queries, tuple((zero, zero) for _ in range(heads)))
        for part in range(2):
            joined = jnp.concatenate([done[h][part][:, :HEAD] for h in range(heads)], axis=1)
            dproj[part + 1, cols, :] = joined.astype(BF16)
        return 0

    lax.fori_loop(0, blocks(total), one_block, 0)

    def finish(i, _):
        rows = pl.ds(pl.multiple_of(i * PAD, LANES), PAD)
        joined = jnp.concatenate([dq[h, :, rows] for h in range(heads)], axis=0)
        dproj[0, rows, :] = (joined * HEAD**-0.5).T.astype(BF16)
        return 0

    lax.fori_loop(0, total // PAD, finish, 0)


def attention_back(ids, q, k, v, kt, out, grad, lse):
    lo, hi, idc, idr = ids
    heads, wide, _ = q.shape
    total = wide - PAD
    lse = jnp.pad(lse, ((0, 0), (0, wide - lse.shape[1])))
    return pl.pallas_call(
        functools.partial(attention_back_kernel, heads, total),
        name="attention_back",
        cost_estimate=work(51),
        in_specs=[SMEM, SMEM] + [VMEM] * 9,
        out_specs=VMEM,
        out_shape=jax.ShapeDtypeStruct((3, blocks(total) * BLOCK, heads * HEAD), BF16),
        scratch_shapes=[
            pltpu.VMEM((heads, wide, LANES), BF16),
            pltpu.VMEM((8, wide), F32),
            pltpu.VMEM((heads, HEAD, wide), F32),
        ],
        compiler_params=limit(60),
    )(lo, hi, idc, idr, q, k, v, kt, out, grad, lse)


def scene_ranges(scene):
    total = scene.shape[0]
    place = jnp.arange(total, dtype=jnp.int32)
    ids = jnp.where(scene >= 0, scene, -1 - place)
    before = jnp.sum(
        ((scene[None, :] >= 0) & (scene[None, :] < jnp.arange(6, dtype=jnp.int32)[:, None])).astype(jnp.int32), axis=1
    )
    whole = jnp.pad(scene, (0, blocks(total) * BLOCK - total), constant_values=-1)
    first, last = whole[0::BLOCK], whole[BLOCK - 1 :: BLOCK]
    start = jnp.arange(blocks(total), dtype=jnp.int32) * BLOCK
    pick = lambda number: jnp.sum(
        jnp.where(number[:, None] == jnp.arange(6, dtype=jnp.int32)[None, :], before[None, :], 0), axis=1
    )
    lo = jnp.where(first >= 0, pick(first), start) // LANES
    hi = (jnp.where(last >= 0, pick(last + 1), start + BLOCK) + LANES - 1) // LANES
    padded = jnp.pad(ids, (0, PAD), constant_values=-(1 << 20))
    return lo, hi, padded[:, None], padded[None, :]


ROWS_MID = 288


def middle_kernel(
    attended, tok, cot, weights, b_out, gain, shift, b_up, b_down,
    layer_out, grad_mid, grad_heads, cells,
    att, grad_att, w, acc, vec, bup, units, att_s, att_r, own_s, grad_s, grad_r, back_s, unit_s, cell_s,
):
    me = Place()
    ndp, parts, piece, _ = weights.shape
    rows = tok.shape[0]
    tiles = rows // ROWS_MID
    width = att.shape[2]
    others = [lax.rem(me.q + k, 4) for k in range(1, 4)]
    greet([me.member(quarter) for quarter in others])

    def tile(t, quarter=0):
        return pl.ds(pl.multiple_of(quarter * rows + t * ROWS_MID, 16), ROWS_MID)

    def att_to(k, t):
        return remote(
            attended.at[tile(t, others[k])], att.at[me.q, tile(t)], att_s.at[k, t], att_r.at[k, t], me.member(others[k])
        )

    def att_from(k, t):
        source = others[2 - k]
        return remote(
            attended.at[tile(t)], att.at[source, tile(t)], att_s.at[k, t], att_r.at[k, t], me.member(source)
        )

    def att_own(t):
        return pltpu.make_async_copy(attended.at[tile(t, me.q)], att.at[me.q, tile(t)], own_s.at[t])

    def grad_to(k, t):
        return remote(
            grad_att.at[others[k], tile(t)], grad_heads.at[tile(t, me.q)], grad_s.at[k, t], grad_r.at[k, t], me.member(others[k])
        )

    def grad_from(k, t):
        source = others[2 - k]
        return remote(
            grad_att.at[source, tile(t)], grad_heads.at[tile(t, source)], grad_s.at[k, t], grad_r.at[k, t], me.member(source)
        )

    def grad_own(t):
        return pltpu.make_async_copy(grad_att.at[me.q, tile(t)], grad_heads.at[tile(t, me.q)], back_s.at[t])

    for t in range(tiles):
        for k in (1, 0, 2):
            att_to(k, t).start()
        att_own(t).start()

    def load(i):
        at = pl.ds(i // parts * piece, piece)
        return pltpu.make_async_copy(weights.at[i // parts, i % parts], w.at[i % parts, at], unit_s.at[i])

    for i in range(ndp * parts):
        load(i).start()
    for ref in (acc, vec, bup):
        ref[...] = jnp.zeros_like(ref)
    for i in range(ndp * parts):
        load(i).wait()

    out_rows = slice(0, OUT_ROWS)
    down_rows = slice(OUT_ROWS, OUT_ROWS + UP_ROWS)
    up_rows = slice(OUT_ROWS + UP_ROWS, VEC_AT)

    def one_tile(t, _):
        here = tile(t)
        att_own(t).wait()
        for k in range(3):
            att_from(k, t).wait_recv()
        atts = [att[v, here, :] for v in range(parts)]
        middle = tok[here, :].astype(F32) + b_out[...]
        for v in range(parts):
            middle = middle + dot(atts[v], w[v, out_rows])
        unit, scale = normalise(middle)
        low = (unit * gain[...] + shift[...]).astype(BF16)
        cot_low = cot[here, :]
        cot_full = cot_low.astype(F32)
        out = middle + b_down[...]
        grad_norm = jnp.zeros_like(middle)
        for v in range(parts):
            hidden = dot(low, w[v, up_rows], NT) + b_up[v]
            below = 0.5 * (1.0 + lax.erf(hidden * 0.5**0.5))
            density = jnp.exp(-0.5 * hidden * hidden) * 0.3989422804014327
            active = (hidden * below).astype(BF16)
            out = out + dot(active, w[v, down_rows])
            grad_hidden = (dot(cot_low, w[v, down_rows], NT) * (below + hidden * density)).astype(BF16)
            grad_norm = grad_norm + dot(grad_hidden, w[v, up_rows])
            acc[v, down_rows] += dot(active, cot_low, TN)
            acc[v, up_rows] += dot(grad_hidden, low, TN)
            bup[v] += jnp.sum(grad_hidden.astype(F32), axis=0, keepdims=True)
        layer_out[here, :] = out.astype(BF16)
        scaled = grad_norm * gain[...]
        back = cot_full + scale * (
            scaled
            - jnp.mean(scaled, axis=-1, keepdims=True)
            - unit * jnp.mean(scaled * unit, axis=-1, keepdims=True)
        )
        grad_mid[here, :] = back
        back_low = back.astype(BF16)
        for v in range(parts):
            grad_att[v, here, :] = dot(back_low, w[v, out_rows], NT).astype(BF16)
        for k in (1, 0, 2):
            grad_to(k, t).start()
        grad_own(t).start()
        for v in range(parts):
            acc[v, out_rows] += dot(atts[v], back_low, TN)
        vec[0:1] += jnp.sum(grad_norm * unit, axis=0, keepdims=True)
        vec[1:2] += jnp.sum(grad_norm, axis=0, keepdims=True)
        vec[2:3] += jnp.sum(back, axis=0, keepdims=True)
        vec[3:4] += jnp.sum(cot_full, axis=0, keepdims=True)
        return 0

    lax.fori_loop(0, tiles, one_tile, 0)

    def give(d):
        return pltpu.make_async_copy(units.at[d], cells.at[d], cell_s.at[d])

    for v in range(parts):
        acc[v, VEC_AT : VEC_AT + 8] = vec[...]
        acc[v, VEC_AT + 4 : VEC_AT + 5, :UP_ROWS] = bup[v]
    for d in range(ndp):
        for v in range(parts):
            units[d, v] = acc[v, d * piece : (d + 1) * piece].astype(BF16)
        give(d).start()
    for t in range(tiles):
        for k in range(3):
            grad_from(k, t).wait_recv()
            grad_to(k, t).wait_send()
            att_to(k, t).wait_send()
        grad_own(t).wait()
    for d in range(ndp):
        give(d).wait()


def middle_part(attended, tok, cot, weights, b_out, gain, shift, b_up, b_down):
    rows = tok.shape[0]
    width = attended.shape[1]
    ndp, parts, piece, _ = weights.shape
    tiles = rows // ROWS_MID
    shape = jax.ShapeDtypeStruct
    return pl.pallas_call(
        middle_kernel,
        name="middle_part",
        cost_estimate=work(50),
        in_specs=[ANY, VMEM, VMEM, ANY] + [VMEM] * 5,
        out_specs=[VMEM, VMEM, ANY, ANY],
        out_shape=[
            shape((rows, D), BF16),
            shape((rows, D), F32),
            shape((4 * rows, width), BF16),
            shape((ndp, parts, piece, D), BF16),
        ],
        scratch_shapes=[
            pltpu.VMEM((parts, rows, width), BF16),
            pltpu.VMEM((parts, rows, width), BF16),
            pltpu.VMEM((parts, UNITS, D), BF16),
            pltpu.VMEM((parts, UNITS, D), F32),
            pltpu.VMEM((8, D), F32),
            pltpu.VMEM(b_up.shape, F32),
            pltpu.VMEM((ndp, parts, piece, D), BF16),
            DMA((3, tiles)),
            DMA((3, tiles)),
            DMA((tiles,)),
            DMA((3, tiles)),
            DMA((3, tiles)),
            DMA((tiles,)),
            DMA((ndp * parts,)),
            DMA((ndp,)),
        ],
        compiler_params=pltpu.CompilerParams(
            collective_id=2, has_side_effects=True, vmem_limit_bytes=60 << 20
        ),
    )(attended, tok, cot, weights, b_out, gain, shift, b_up, b_down)


def finish_kernel(
    dproj, normed, full, w, grad_mid, gain, cells, grad, vec_sum, d_w, sums,
    part, theirs, sent, crossed, low, back, acc, w_part, w_in, w_z, w_all, vec, vz, vd,
    sib_s, sib_r, cross_s, cross_r, swap_s, swap_r, vz_s, vz_r, vd_s, vd_r,
    ws_s, ws_r, wz_s, wz_r, wg_s, wg_r, wf_s, wf_r,
    u_in, u_all, uz_s, uz_r, ug_s, ug_r, uf_s, uf_r,
):
    me = Place()
    foreign = jnp.logical_not(me.native)
    rows = grad_mid.shape[0]
    piece = rows // PIECES
    width = w.shape[2]
    ndp = vd.shape[0]
    groups, w_rows, _ = w_part.shape
    group = me.d // 2
    around = [(me.d, lax.rem(me.m + k, 4)) for k in range(1, 4)]
    along = [(lax.rem(me.d + k, ndp), me.m) for k in range(1, ndp)]
    greet([me.partner] + around + along)

    order = [2 * (1 - me.hf) + 1 - me.r, 2 * (1 - me.hf) + me.r, 2 * me.hf + 1 - me.r, 2 * me.hf + me.r]

    def to_sib(k, p):
        slot = k % 2
        return remote(part.at[k, p], theirs.at[slot, p], sib_s.at[slot, p], sib_r.at[slot, p], me.sibling)

    def to_cross(p):
        return remote(sent.at[p], crossed.at[p], cross_s.at[p], cross_r.at[p], me.cross)

    def to_partner(p):
        return remote(low.at[p], back.at[p], swap_s.at[p], swap_r.at[p], me.partner)

    def unit_z(j):
        to = lax.rem(me.m + 1 + j, 4)
        return remote(cells.at[to], u_in.at[j], uz_s.at[j], uz_r.at[j], around[j])

    def unit_give(j):
        return remote(
            u_all.at[me.d], u_all.at[me.d], ug_s.at[j], ug_r.at[j], (2 * lax.rem(group + j, groups) + me.c, me.m)
        )

    def unit_forward(j):
        source = 2 * lax.rem(group + groups - j, groups) + me.c
        return remote(u_all.at[source], u_all.at[source], uf_s.at[j], uf_r.at[j], me.sibling)

    def unit_give_in(j):
        source = 2 * lax.rem(group + groups - j, groups) + me.c
        return remote(u_all.at[source], u_all.at[source], ug_s.at[j], ug_r.at[j], (source, me.m))

    def unit_forward_in(j):
        source = 2 * lax.rem(group + groups - j, groups) + 1 - me.c
        return remote(u_all.at[source], u_all.at[source], uf_s.at[j], uf_r.at[j], me.sibling)

    for j in range(3):
        unit_z(j).start()
    acc[...] = jnp.zeros_like(acc)
    vec[...] = jnp.zeros_like(vec)

    def compute(k):
        def one(p, _):
            span = pl.ds(pl.multiple_of(order[k] * rows + p * piece, 16), piece)
            rounded = normed[span, :]
            total = jnp.zeros((piece, D), F32)
            for c in range(3):
                given = dproj[c, span, :]
                total = total + dot(given, w[c], NT)
                acc[c * width : (c + 1) * width, :] += dot(given, rounded, TN)
            part[k, p] = total.astype(BF16)
            unit, _ = normalise(full[span, :].astype(F32))
            vec[0:1] += jnp.sum(total * unit, axis=0, keepdims=True)
            vec[1:2] += jnp.sum(total, axis=0, keepdims=True)

            @pl.when(me.native if k < 2 else foreign)
            def _():
                to_sib(k, p).start()

            return 0

        lax.fori_loop(0, PIECES, one, 0)

    def pass_across(k):
        for p in range(PIECES):
            to_sib(k, p).wait_recv()
            sent[p] = (part[k, p].astype(F32) + theirs[0, p].astype(F32)).astype(BF16)
            to_cross(p).start()

    def conclude(k, p):
        to_sib(k, p).wait_recv()
        to_cross(p).wait_recv()
        total = part[k, p].astype(F32) + theirs[1, p].astype(F32) + crossed[p].astype(F32)
        span = pl.ds(pl.multiple_of(me.q * rows + p * piece, 16), piece)
        unit, scale = normalise(full[span, :].astype(F32))
        scaled = total * gain[...]
        return grad_mid[p * piece : (p + 1) * piece, :] + scale * (
            scaled
            - jnp.mean(scaled, axis=-1, keepdims=True)
            - unit * jnp.mean(scaled * unit, axis=-1, keepdims=True)
        )

    def conclude_foreign(p):
        low[p] = conclude(1, p).astype(BF16)
        to_partner(p).start()

    compute(0)

    @pl.when(foreign)
    def _():
        pass_across(0)

    compute(1)
    compute(2)
    unit_sum = cells[me.m].astype(F32)
    for j in range(3):
        unit_z(j).wait_recv()
        unit_sum = unit_sum + u_in[j].astype(F32)
    u_all[me.d] = unit_sum.astype(BF16)
    for j in range(1, groups):
        unit_give(j).start()
    unit_forward(0).start()

    @pl.when(me.native)
    def _():
        pass_across(2)

    @pl.when(foreign)
    def _():
        conclude_foreign(0)

    compute(3)

    for i in range(groups):
        w_part[i] = acc[i * w_rows : (i + 1) * w_rows, :].astype(BF16)

    def other_group(k):
        return lax.rem(group + k, groups)

    def w_send(k):
        to = other_group(k)
        return remote(w_part.at[to], w_in.at[k], ws_s.at[k], ws_r.at[k], (2 * to + me.c, me.m))

    for k in range(1, groups):
        w_send(k).start()

    vz[me.m] = vec[...]

    def around_copy(k):
        return remote(vz.at[me.m], vz.at[me.m], vz_s.at[k], vz_r.at[k], around[k])

    for k in range(3):
        around_copy(k).start()

    @pl.when(foreign)
    def _():
        for p in range(1, PIECES):
            conclude_foreign(p)

    for k in range(3):
        source = lax.rem(me.m + 3 - k, 4)
        remote(vz.at[source], vz.at[source], vz_s.at[k], vz_r.at[k], around[k]).wait_recv()
    vd[me.d] = vz[0] + vz[1] + vz[2] + vz[3]

    def along_copy(k):
        return remote(vd.at[me.d], vd.at[me.d], vd_s.at[k], vd_r.at[k], along[k])

    for k in range(ndp - 1):
        along_copy(k).start()

    w_sum = w_part[group].astype(F32)
    for k in range(1, groups):
        w_send(k).wait_recv()
        w_sum = w_sum + w_in[k].astype(F32)

    to_z = remote(w_z.at[0], w_z.at[1], wz_s, wz_r, (me.d, lax.rem(me.m + 2, 4)))

    def w_give(k):
        return remote(
            w_all.at[group], w_all.at[group], wg_s.at[k], wg_r.at[k], (2 * other_group(k) + me.c, me.m)
        )

    def w_forward(k):
        source = lax.rem(group + groups - k, groups)
        return remote(w_all.at[source], w_all.at[source], wf_s.at[k], wf_r.at[k], me.sibling)

    @pl.when(foreign)
    def _():
        w_z[0] = w_sum.astype(BF16)
        to_z.start()

    @pl.when(me.native)
    def _():
        to_z.wait_recv()
        w_all[group] = (w_sum + w_z[1].astype(F32)).astype(BF16)
        for k in range(1, groups):
            w_give(k).start()
        w_forward(0).start()
        for p in range(PIECES):
            grad[p * piece : (p + 1) * piece, :] = conclude(3, p)
        for k in range(1, groups):
            source = lax.rem(group + groups - k, groups)
            remote(
                w_all.at[source], w_all.at[source], wg_s.at[k], wg_r.at[k], (2 * source + me.c, me.m)
            ).wait_recv()
            w_forward(k).start()

    for k in range(ndp - 1):
        source = lax.rem(me.d + ndp - 1 - k, ndp)
        remote(vd.at[source], vd.at[source], vd_s.at[k], vd_r.at[k], along[k]).wait_recv()
    total = vd[0]
    for i in range(1, ndp):
        total = total + vd[i]
    vec_sum[...] = total

    @pl.when(foreign)
    def _():
        for k in range(groups):
            source = lax.rem(group + groups - k, groups)
            remote(w_all.at[source], w_all.at[source], wf_s.at[k], wf_r.at[k], me.sibling).wait_recv()

    for i in range(groups):
        d_w[i * w_rows : (i + 1) * w_rows, :] = w_all[i].astype(F32)
    for j in range(1, groups):
        unit_give_in(j).wait_recv()
        unit_forward(j).start()
    for j in range(groups):
        unit_forward_in(j).wait_recv()
    height = sums.shape[0] // ndp
    for i in range(ndp):
        sums[i * height : (i + 1) * height, :] = u_all[i].astype(F32)
    for j in range(groups):
        unit_forward(j).wait_send()
    for j in range(1, groups):
        unit_give(j).wait_send()
    for j in range(3):
        unit_z(j).wait_send()

    @pl.when(foreign)
    def _():
        for p in range(PIECES):
            to_partner(p).wait_recv()
            grad[p * piece : (p + 1) * piece, :] = back[p].astype(F32)
        for p in range(PIECES):
            to_partner(p).wait_send()
            to_sib(2, p).wait_send()
            to_sib(3, p).wait_send()
        to_z.wait_send()

    @pl.when(me.native)
    def _():
        for p in range(PIECES):
            to_sib(0, p).wait_send()
            to_sib(1, p).wait_send()
        for k in range(1, groups):
            w_give(k).wait_send()
        for k in range(groups):
            w_forward(k).wait_send()

    for p in range(PIECES):
        to_cross(p).wait_send()
    for k in range(1, groups):
        w_send(k).wait_send()
    for k in range(3):
        around_copy(k).wait_send()
    for k in range(ndp - 1):
        along_copy(k).wait_send()


def finish(dproj, normed, full, w, grad_mid, gain, cells, ndp):
    rows = grad_mid.shape[0]
    piece = rows // PIECES
    pieces = (PIECES, piece, D)
    groups = ndp // 2
    columns = 3 * w.shape[2]
    cut = (groups, columns // groups, D)
    return pl.pallas_call(
        finish_kernel,
        name="finish",
        cost_estimate=work(60),
        in_specs=[VMEM] * 7,
        out_specs=[VMEM] * 4,
        out_shape=[
            jax.ShapeDtypeStruct((rows, D), F32),
            jax.ShapeDtypeStruct((8, D), F32),
            jax.ShapeDtypeStruct((columns, D), F32),
            jax.ShapeDtypeStruct((UNITS, D), F32),
        ],
        scratch_shapes=[
            pltpu.VMEM((4,) + pieces, BF16),
            pltpu.VMEM((2,) + pieces, BF16),
            pltpu.VMEM(pieces, BF16),
            pltpu.VMEM(pieces, BF16),
            pltpu.VMEM(pieces, BF16),
            pltpu.VMEM(pieces, BF16),
            pltpu.VMEM((columns, D), F32),
            pltpu.VMEM(cut, BF16),
            pltpu.VMEM(cut, BF16),
            pltpu.VMEM((2,) + cut[1:], BF16),
            pltpu.VMEM(cut, BF16),
            pltpu.VMEM((8, D), F32),
            pltpu.VMEM((4, 8, D), F32),
            pltpu.VMEM((ndp, 8, D), F32),
            DMA((2, PIECES)),
            DMA((2, PIECES)),
            DMA((PIECES,)),
            DMA((PIECES,)),
            DMA((PIECES,)),
            DMA((PIECES,)),
            DMA((3,)),
            DMA((3,)),
            DMA((ndp - 1,)),
            DMA((ndp - 1,)),
            DMA((groups,)),
            DMA((groups,)),
            DMA,
            DMA,
            DMA((groups,)),
            DMA((groups,)),
            DMA((groups,)),
            DMA((groups,)),
            pltpu.VMEM((3, UNITS // ndp, D), BF16),
            pltpu.VMEM((ndp, UNITS // ndp, D), BF16),
            DMA((3,)),
            DMA((3,)),
            DMA((groups,)),
            DMA((groups,)),
            DMA((groups,)),
            DMA((groups,)),
        ],
        compiler_params=pltpu.CompilerParams(
            collective_id=4, has_side_effects=True, vmem_limit_bytes=60 << 20
        ),
    )(dproj, normed, full, w, grad_mid, gain, cells)


def swap_pairs(ndp):
    return [
        (d * 4 + m, (d ^ 1) * 4 + (m + 2) % 4) for d in range(ndp) for m in range(4) if d % 2 != m // 2
    ]


def weight_piece(w_out, w_up, w_down, ndp):
    block = jnp.concatenate([w_out, w_down, w_up.T, jnp.zeros((UNITS - w_out.shape[0] - 2 * w_down.shape[0], D), BF16)])
    piece = UNITS // ndp
    return lax.dynamic_slice_in_dim(block, lax.axis_index("dp") * piece, piece, 0)


def sum_over_dp(cells):
    return lax.psum_scatter(cells.reshape(-1, D), "dp", scatter_dimension=0, tiled=True)


def shards(
    tokens,
    scene_ids,
    gain_one,
    shift_one,
    w_qkv,
    w_out,
    b_out,
    gain_two,
    shift_two,
    w_up,
    b_up,
    w_down,
    b_down,
    cotangent,
    ndp,
):
    d, m = lax.axis_index("dp"), lax.axis_index("mp")
    native = d % 2 == m // 2
    line = lambda v: v.reshape(1, D)
    both = ("dp", "mp")
    swap = swap_pairs(ndp)

    full, own_tok, w_mine, scene, all_bup, normed, q, k, v, kt, vt, weights = start(
        tokens,
        w_qkv,
        scene_ids.reshape(-1, LANES),
        b_up.reshape(1, FF // 4),
        line(gain_one),
        line(shift_one),
        weight_piece(w_out, w_up, w_down, ndp),
        ndp,
    )
    w_mine = w_mine.reshape(w_qkv.shape)
    weights = lax.all_gather(weights, "dp", axis=0)
    scene = scene.reshape(-1)
    ids = scene_ranges(scene)
    sent_cot, q = lax.optimization_barrier((cotangent, q))
    own_cot = jnp.where(native, cotangent, lax.ppermute(sent_cot, both, swap))
    attended, lse = attention(ids, q, k, vt)
    layer_out, grad_mid, grad_heads, cells = middle_part(
        attended, own_tok, own_cot, weights, line(b_out), line(gain_two), line(shift_two), all_bup, line(b_down)
    )
    sent_out, grad_heads = lax.optimization_barrier((layer_out, grad_heads))
    layer_out = jnp.where(native, layer_out, lax.ppermute(sent_out, both, swap))
    cells = sum_over_dp(cells)
    dproj = attention_back(ids, q, k, v, kt, attended, grad_heads, lse)
    cells, dproj = lax.optimization_barrier((cells, dproj))
    tokens_grad, one_sum, d_qkv, sums = finish(
        dproj, normed, full, w_mine, grad_mid, line(gain_one), cells.reshape(4, -1, D), ndp
    )
    g_qkv = jnp.swapaxes(d_qkv.reshape(3, -1, D), 1, 2)
    g_vec = sums[VEC_AT : VEC_AT + 4]
    return (
        layer_out,
        tokens_grad,
        one_sum[0],
        one_sum[1],
        g_qkv,
        sums[:OUT_ROWS],
        g_vec[2],
        g_vec[0],
        g_vec[1],
        sums[OUT_ROWS + UP_ROWS : VEC_AT].T,
        sums[VEC_AT + 4, :UP_ROWS],
        sums[OUT_ROWS : OUT_ROWS + UP_ROWS],
        g_vec[3],
    )


def solution(mesh):
    ndp = mesh.shape["dp"]
    return jax.shard_map(
        functools.partial(shards, ndp=ndp),
        mesh=mesh,
        in_specs=(
            P(("dp", "mp"), None),
            P("dp"),
            P(),
            P(),
            P(None, None, "mp"),
            P("mp", None),
            P(),
            P(),
            P(),
            P(None, "mp"),
            P("mp"),
            P("mp", None),
            P(),
            P(("dp", "mp"), None),
        ),
        out_specs=(
            P(("dp", "mp"), None),
            P(("dp", "mp"), None),
            P(),
            P(),
            P(None, None, "mp"),
            P("mp", None),
            P(),
            P(),
            P(),
            P(None, "mp"),
            P("mp"),
            P("mp", None),
            P(),
        ),
        check_vma=False,
    )
```

```python
import functools

import jax
import jax.numpy as jnp
from jax import lax
from jax.experimental import pallas as pl
from jax.experimental.pallas import tpu as pltpu
from jax.sharding import PartitionSpec as P

HEAD = 64
D = 768
FF = 1536
LANES = 128
PAD = 512
OUT_ROWS = D // 4
UP_ROWS = FF // 4
VEC_AT = OUT_ROWS + 2 * UP_ROWS
UNITS = 1024
EPS = 1e-05
MASKED = -1e30
MESH = pl.DeviceIdType.MESH
F32 = jnp.float32
BF16 = jnp.bfloat16
VMEM = pl.BlockSpec(memory_space=pltpu.VMEM)
SMEM = pl.BlockSpec(memory_space=pltpu.SMEM)
ANY = pl.BlockSpec(memory_space=pl.ANY)
DMA = pltpu.SemaphoreType.DMA

NN = (((1,), (0,)), ((), ()))
NT = (((1,), (1,)), ((), ()))
TN = (((0,), (0,)), ((), ()))


def dot(a, b, dims=NN):
    return lax.dot_general(a, b, dims, preferred_element_type=F32)


def work(us):
    return pl.CostEstimate(flops=us * 10**9, bytes_accessed=us * 3 * 10**6, transcendentals=0)


def limit(mib):
    return pltpu.CompilerParams(vmem_limit_bytes=mib << 20)


def line(ref):
    return ref[...].reshape(1, -1)


class Place:
    def __init__(self):
        self.d = lax.axis_index("dp")
        self.m = lax.axis_index("mp")
        self.c = lax.rem(self.d, 2)
        self.r = lax.rem(self.m, 2)
        self.hf = self.m // 2
        self.q = 2 * self.c + self.r
        self.native = self.c == self.hf
        self.sibling = (self.d + 1 - 2 * self.c, self.m)
        self.cross = (self.d, self.m + 1 - 2 * self.r)
        self.partner = (self.d + 1 - 2 * self.c, lax.rem(self.m + 2, 4))

    def member(self, quarter):
        return (self.d - self.c + quarter // 2, 2 * self.hf + quarter % 2)


def greet(others):
    barrier = pltpu.get_barrier_semaphore()
    for other in others:
        pl.semaphore_signal(barrier, inc=1, device_id=other, device_id_type=MESH)
    pl.semaphore_wait(barrier, len(others))


def remote(src, dst, send, recv, device):
    return pltpu.make_async_remote_copy(
        src_ref=src, dst_ref=dst, send_sem=send, recv_sem=recv, device_id=device, device_id_type=MESH
    )


PIECES = 3
TILE = 384
SCENES = 4


def normalise(x):
    centred = x - jnp.mean(x, axis=-1, keepdims=True)
    scale = lax.rsqrt(jnp.mean(centred * centred, axis=-1, keepdims=True) + EPS)
    return centred * scale, scale


def widen(x, ones, rows):
    lane = lax.broadcasted_iota(jnp.int32, (rows, LANES - HEAD), 1)
    return jnp.concatenate([x, jnp.where(lane < ones, 1.0, 0.0).astype(x.dtype)], axis=1)


def describe_scenes(ids, row, column, before):
    lines = ids.shape[0]
    for j in range(lines):
        place = j * LANES + lax.broadcasted_iota(jnp.int32, (1, LANES), 1)
        number = ids[j : j + 1, :]
        number = jnp.where(number >= 0, number, -1 - place)
        span = slice(j * LANES, (j + 1) * LANES)
        row[:, span] = number
        column[span, :] = jnp.broadcast_to(number.astype(F32), (LANES, LANES)).T[:, :1].astype(jnp.int32)
    rest = row.shape[1] - lines * LANES
    row[:, lines * LANES :] = jnp.full((1, rest), -(1 << 21), jnp.int32)
    column[lines * LANES :, :] = jnp.full((rest, 1), -(1 << 20), jnp.int32)
    lane = lax.broadcasted_iota(jnp.int32, (1, LANES), 1)
    counts = jnp.zeros((1, LANES), F32)
    for number in range(1, SCENES + 1):
        mine = jnp.where((ids[...] >= 0) & (ids[...] < number), 1.0, 0.0)
        total = jnp.sum(jnp.sum(mine, axis=0, keepdims=True), axis=1, keepdims=True)
        counts = jnp.where(lane == number, total, counts)
    before[...] = counts.astype(jnp.int32)


def start_kernel(
    heads, tok, wq, ids, b_up, gain, shift, mine,
    full, own, w_out, ids_own, id_row, id_column, before, b_ups, normed, q, k, v, kt, vt, units,
    buf, w, low_s, q_s, k_s, v_s, kt_s, vt_s,
    swap_s, swap_r, cross_s, cross_r, sib_s, sib_r, fwd_s, fwd_r, w_s, w_r, ids_s, ids_r, b_s, b_r, out_s, late_s,
    uz_s, uz_r,
):
    me = Place()
    foreign = jnp.logical_not(me.native)
    rows = tok.shape[0]
    piece = rows // PIECES
    total = buf.shape[0]
    tiles = total // TILE
    groups = w.shape[1]
    group = me.d // 2
    around = [(me.d, lax.rem(me.m + j, 4)) for j in range(1, 4)]
    lines = [(2 * lax.rem(group + j, groups) + me.c, me.m) for j in range(1, groups)]
    greet([me.sibling, me.partner] + around + lines)

    def rows_of(quarter, n):
        p = jnp.where(me.hf == 0, n, PIECES - 1 - n)
        return pl.ds(pl.multiple_of(quarter * rows + p * piece, 16), piece)

    def part(quarter, n):
        return buf.at[rows_of(quarter, n)]

    sib_q = 2 * (1 - me.c) + me.r
    cross_q = 2 * me.c + 1 - me.r
    sib_cross_q = 2 * (1 - me.c) + 1 - me.r

    def swap(n):
        p = jnp.where(me.hf == 1, n, PIECES - 1 - n)
        src = tok.at[pl.ds(pl.multiple_of(p * piece, 16), piece)]
        dst = buf.at[pl.ds(pl.multiple_of(sib_q * rows + p * piece, 16), piece)]
        return remote(src, dst, swap_s.at[n], swap_r.at[n], me.partner)

    def swap_in(n):
        return remote(part(me.q, n), part(me.q, n), swap_s.at[n], swap_r.at[n], me.partner)

    def cross(quarter, n):
        return remote(part(quarter, n), part(quarter, n), cross_s.at[n], cross_r.at[n], me.cross)

    def sib(quarter, n):
        return remote(part(quarter, n), part(quarter, n), sib_s.at[n], sib_r.at[n], me.sibling)

    def forward(quarter, n):
        return remote(part(quarter, n), part(quarter, n), fwd_s.at[n], fwd_r.at[n], me.sibling)

    weight = remote(wq.at[:, group], w.at[:, group], w_s.at[0], w_r.at[0], me.partner)

    def weight_share(j):
        return remote(w.at[:, group], w.at[:, group], w_s.at[j], w_r.at[j], lines[j - 1])

    def weight_in(j):
        source = lax.rem(group + groups - j, groups)
        return remote(w.at[:, source], w.at[:, source], w_s.at[j], w_r.at[j], lines[j - 1])

    unit_own = pltpu.make_async_copy(mine, units.at[me.m], late_s.at[7])

    def unit_z(j, source):
        return remote(mine, units.at[source], uz_s.at[j], uz_r.at[j], around[j])

    def give_b_up(j):
        return remote(b_ups.at[me.m], b_ups.at[me.m], b_s.at[j], b_r.at[j], around[j])

    scenes = remote(ids, ids_own, ids_s, ids_r, me.sibling)
    unit_own.start()
    b_ups[me.m] = line(b_up)
    for j in range(3):
        give_b_up(j).start()

    @pl.when(me.native)
    def _():
        scenes.start()
        buf[pl.ds(pl.multiple_of(me.q * rows, 16), rows), :] = tok[...]
        for n in range(PIECES):
            cross(me.q, n).start()
            sib(me.q, n).start()
        w[...] = wq[...]
        ids_own[...] = ids[...]

    @pl.when(foreign)
    def _():
        weight.start()
        for n in range(PIECES):
            swap(n).start()

    def share(n):
        swap_in(n).wait_recv()
        cross(me.q, n).start()
        sib(me.q, n).start()

    def pass_on(n):
        cross(cross_q, n).wait_recv()
        forward(cross_q, n).start()

    def from_sibling(n):
        sib(sib_q, n).wait_recv()
        forward(sib_cross_q, n).wait_recv()

    def outputs(t):
        span = pl.ds(pl.multiple_of(t * TILE, LANES), TILE)
        pairs = [
            (low_s.at[span], normed.at[span]),
            (buf.at[span], full.at[span]),
            (q_s.at[:, span], q.at[:, span]),
            (k_s.at[:, span], k.at[:, span]),
            (v_s.at[:, span], v.at[:, span]),
            (kt_s.at[:, :, span], kt.at[:, :, span]),
            (vt_s.at[:, :, span], vt.at[:, :, span]),
        ]
        return [pltpu.make_async_copy(src, dst, out_s.at[t, j]) for j, (src, dst) in enumerate(pairs)]

    ones = jnp.where(lax.broadcasted_iota(jnp.int32, (16, TILE), 0) < 1, 1.0, 0.0).astype(BF16)

    def compute(first, stride, count):
        def one(n, _):
            at = first + stride * n
            t = jnp.where(me.hf == 0, at, tiles - 1 - at)
            span = pl.ds(pl.multiple_of(t * TILE, LANES), TILE)
            unit, _ = normalise(buf[span, :].astype(F32))
            low = (unit * line(gain) + line(shift)).astype(BF16)
            low_s[span, :] = low
            qs = (dot(low, w[0].reshape(-1, D), NT).astype(BF16).astype(F32) * HEAD**-0.5).astype(BF16)
            ks = dot(low, w[1].reshape(-1, D), NT)
            vs = dot(low, w[2].reshape(-1, D), NT)
            kts = ks.T.astype(BF16)
            vts = vs.T.astype(BF16)
            ks = ks.astype(BF16)
            vs = vs.astype(BF16)
            for h in range(heads):
                cols = slice(h * HEAD, (h + 1) * HEAD)
                q_s[h, span, :] = widen(qs[:, cols], 0, TILE)
                k_s[h, span, :] = widen(ks[:, cols], 3, TILE)
                v_s[h, span, :] = widen(vs[:, cols], 3, TILE)
                kt_s[h, :, span] = kts[cols]
                vt_s[h, :HEAD, span] = vts[cols]
                vt_s[h, HEAD:, span] = ones
            for copy in outputs(t):
                copy.start()
            return 0

        lax.fori_loop(0, count, one, 0)

    pad = pl.ds(total, PAD)
    zeros = jnp.zeros((heads, PAD, LANES), BF16)
    for ref in (q_s, k_s, v_s):
        ref[:, pad, :] = zeros
    for ref in (kt_s, vt_s):
        ref[:, :, pad] = jnp.zeros((heads, ref.shape[1], PAD), BF16)
    padding = [
        pltpu.make_async_copy(src, dst, late_s.at[j])
        for j, (src, dst) in enumerate(
            [(a.at[:, pad], b.at[:, pad]) for a, b in ((q_s, q), (k_s, k), (v_s, v))]
            + [(a.at[:, :, pad], b.at[:, :, pad]) for a, b in ((kt_s, kt), (vt_s, vt))]
        )
    ]
    for copy in padding:
        copy.start()

    @pl.when(me.native)
    def _():
        for n in range(PIECES):
            pass_on(n)

    @pl.when(foreign)
    def _():
        weight.wait_recv()
        for j in range(1, groups):
            weight_share(j).start()
        for n in range(PIECES):
            share(n)
        for j in range(1, groups):
            weight_in(j).wait_recv()
        for n in range(PIECES):
            from_sibling(n)

    for j in range(3):
        unit_z(j, me.m).start()

    @pl.when(foreign)
    def _():
        scenes.wait_recv()

    describe_scenes(ids_own, id_row, id_column, before)
    compute(0, 1, 2)

    @pl.when(foreign)
    def _():
        pass_on(0)

    compute(2, 1, 2)

    @pl.when(foreign)
    def _():
        pass_on(1)

    @pl.when(me.native)
    def _():
        from_sibling(0)

    compute(4, 1, 1)

    @pl.when(me.native)
    def _():
        from_sibling(1)

    compute(5, 2, 2)

    @pl.when(foreign)
    def _():
        pass_on(2)

    @pl.when(me.native)
    def _():
        from_sibling(2)

    own_copy = pltpu.make_async_copy(buf.at[pl.ds(pl.multiple_of(me.q * rows, 16), rows)], own, late_s.at[5])
    w_copy = pltpu.make_async_copy(w, w_out, late_s.at[6])
    own_copy.start()
    w_copy.start()
    compute(6, 2, 2)
    unit_own.wait()
    for j in range(3):
        unit_z(j, lax.rem(me.m + 3 - j, 4)).wait_recv()
        unit_z(j, me.m).wait_send()

    for j in range(3):
        source = lax.rem(me.m + 3 - j, 4)
        remote(b_ups.at[source], b_ups.at[source], b_s.at[j], b_r.at[j], around[j]).wait_recv()
        give_b_up(j).wait_send()

    @pl.when(me.native)
    def _():
        scenes.wait_send()

    @pl.when(foreign)
    def _():
        weight.wait_send()
        for j in range(1, groups):
            weight_share(j).wait_send()
        for n in range(PIECES):
            swap(n).wait_send()

    for n in range(PIECES):
        cross(me.q, n).wait_send()
        sib(me.q, n).wait_send()
        forward(cross_q, n).wait_send()
    for copy in padding + [own_copy, w_copy]:
        copy.wait()

    def finish_tile(t, _):
        for copy in outputs(t):
            copy.wait()
        return 0

    lax.fori_loop(0, tiles, finish_tile, 0)


def start(tokens, w_qkv, scene_ids, b_up, gain, shift, mine, ndp):
    rows = tokens.shape[0]
    total = 4 * rows
    heads = w_qkv.shape[1] // HEAD
    groups = ndp // 2
    w_qkv = w_qkv.reshape(3, groups, -1, D)
    units = (4,) + mine.shape
    wide = total + PAD
    shape = jax.ShapeDtypeStruct
    rowed = (heads, wide, LANES)
    k_cols, v_cols = (heads, HEAD, wide), (heads, HEAD + 16, wide)
    three = DMA((PIECES,))
    return pl.pallas_call(
        functools.partial(start_kernel, heads),
        name="start",
        cost_estimate=work(50),
        in_specs=[VMEM] * 6 + [ANY],
        out_specs=[ANY] * 3 + [VMEM] * 5 + [ANY] * 7,
        out_shape=[
            shape((total, D), BF16),
            shape((rows, D), BF16),
            shape(w_qkv.shape, BF16),
            shape(scene_ids.shape, jnp.int32),
            shape((1, wide), jnp.int32),
            shape((wide, 1), jnp.int32),
            shape((1, LANES), jnp.int32),
            shape((4, 1) + b_up.shape, F32),
            shape((total, D), BF16),
            shape(rowed, BF16),
            shape(rowed, BF16),
            shape(rowed, BF16),
            shape(k_cols, BF16),
            shape(v_cols, BF16),
            shape(units, BF16),
        ],
        scratch_shapes=[
            pltpu.VMEM((total, D), BF16),
            pltpu.VMEM(w_qkv.shape, BF16),
            pltpu.VMEM((total, D), BF16),
            pltpu.VMEM(rowed, BF16),
            pltpu.VMEM(rowed, BF16),
            pltpu.VMEM(rowed, BF16),
            pltpu.VMEM(k_cols, BF16),
            pltpu.VMEM(v_cols, BF16),
        ]
        + [three] * 8
        + [DMA((groups,))] * 2
        + [DMA] * 2
        + [DMA((3,))] * 2
        + [DMA((total // TILE, 7)), DMA((8,))]
        + [DMA((3,))] * 2,
        compiler_params=pltpu.CompilerParams(
            collective_id=1, has_side_effects=True, vmem_limit_bytes=60 << 20
        ),
    )(tokens, w_qkv, scene_ids, b_up, gain, shift, mine)


BLOCK = 256
STEP = 512


def blocks(total):
    return -(-total // BLOCK)


def block_range(i, numbers, before):
    lines = numbers.shape[0]
    per = BLOCK // LANES
    top, bottom = numbers[i * per, 0], numbers[jnp.minimum(i * per + per, lines) - 1, LANES - 1]
    bottom = jnp.where(i * per + per > lines, -1, bottom)
    low = jnp.where(top >= 0, before[0, jnp.maximum(top, 0)], i * BLOCK)
    high = jnp.where(bottom >= 0, before[0, jnp.maximum(bottom, 0) + 1], i * BLOCK + BLOCK)
    return low // LANES, (high + LANES - 1) // LANES


def list_steps(count, numbers, before, total, block_at, step_at, marks):
    stride = STEP // LANES

    def one_block(i, n):
        first, last = block_range(i, numbers, before)
        steps = (last - first + stride - 1) // stride

        def put(j, n):
            block_at[n] = i * (BLOCK // LANES)
            step_at[n] = first + j * stride
            marks[n] = jnp.where(j == 0, 1, 0) + jnp.where(j == steps - 1, 2, 0)
            return n + 1

        return lax.fori_loop(0, steps, put, n)

    n = lax.fori_loop(0, count, one_block, 0)
    for idle in range(2):
        block_at[n + idle] = 0
        step_at[n + idle] = total // LANES
        marks[n + idle] = 0
    return n


def step_lists(total):
    return [pltpu.SMEM((blocks(total) * (-(-total // STEP) + 1) + 2,), jnp.int32)] * 3


def attention_kernel(
    heads, total, numbers, before, idc, idr, q, k, vt, out, lse, block_at, step_at, marks, even, odd
):
    count = list_steps(blocks(total), numbers, before, total, block_at, step_at, marks)

    def place(i):
        rows = pl.ds(pl.multiple_of(block_at[i] * LANES, LANES), BLOCK)
        return rows, pl.ds(pl.multiple_of(step_at[i] * LANES, LANES), STEP)

    def score(i, buf, h):
        rows, cols = place(i)
        s = jnp.where(idc[cols, :] == idr[:, rows], dot(k[h, cols, :], q[h, rows, :], NT), MASKED)
        buf[h] = s
        return jnp.max(s, axis=0, keepdims=True)

    def step(i, now, after, carry):
        rows, cols = place(i)
        mark = marks[i]
        new = []
        for h in range(heads):
            top, acc, highest = carry[h]
            upcoming = score(i + 1, after, h)
            top = jnp.where(lax.rem(mark, 2) == 1, MASKED, top)
            above = jnp.maximum(top, highest)
            p = jnp.exp(now[h] - above).astype(BF16)
            acc = acc * jnp.exp(top - above) + dot(vt[h, :, cols], p)
            new.append((above, acc, upcoming))

        @pl.when(mark >= 2)
        def _():
            valid = jnp.where(idr[:, rows] >= 0, 1.0, 0.0)
            mixed = []
            for h in range(heads):
                top, acc, _ = new[h]
                row_total = acc[HEAD : HEAD + 1]
                mixed.append(acc[:HEAD] * (valid / row_total))
                lse[pl.ds(h, 1), rows] = top + jnp.log(row_total)
            out[rows, :] = jnp.concatenate(mixed, axis=0).T.astype(BF16)

        return tuple(new)

    low = jnp.full((1, BLOCK), MASKED, F32)
    start = tuple((low, jnp.zeros((vt.shape[1], BLOCK), F32), score(0, even, h)) for h in range(heads))

    def two_steps(n, carry):
        return step(2 * n + 1, odd, even, step(2 * n, even, odd, carry))

    lax.fori_loop(0, (count + 1) // 2, two_steps, start)


def attention(ids, q, k, vt):
    heads, wide, _ = q.shape
    total = wide - PAD
    rows = blocks(total) * BLOCK
    scores = pltpu.VMEM((heads, STEP, BLOCK), F32)
    return pl.pallas_call(
        functools.partial(attention_kernel, heads, total),
        name="attention",
        cost_estimate=work(31),
        in_specs=[SMEM] * 2 + [VMEM] * 5,
        out_specs=[VMEM, VMEM],
        out_shape=[
            jax.ShapeDtypeStruct((rows, heads * HEAD), BF16),
            jax.ShapeDtypeStruct((heads, wide), F32),
        ],
        scratch_shapes=step_lists(total) + [scores, scores],
        compiler_params=limit(56),
    )(*ids, q, k, vt)


def in_steps(first, last, body, carry):
    wide, narrow = 2 * BLOCK // LANES, BLOCK // LANES
    count = (last - first + narrow - 1) // narrow
    carry = lax.fori_loop(0, count // 2, lambda n, c: body(2 * BLOCK, first + n * wide, c), carry)
    return lax.fori_loop(0, count % 2, lambda n, c: body(BLOCK, first + (count - 1) * narrow, c), carry)


def attention_back_kernel(
    heads, total, numbers, before, idc, idr, q, k, v, kt, out, grad, lse, dproj, g, delta, dq
):
    wide = q.shape[1]
    width = heads * HEAD
    head_of = lax.broadcasted_iota(jnp.int32, (8, width), 1) // HEAD
    pick = jnp.where(head_of == lax.broadcasted_iota(jnp.int32, (8, width), 0), 1.0, 0.0).astype(BF16)
    none = jnp.zeros((TILE, LANES - HEAD), BF16)

    def prepare(i, _):
        rows = pl.ds(pl.multiple_of(i * TILE, LANES), TILE)
        grads = jnp.where(idc[rows, :] >= 0, grad[rows, :].astype(F32), 0.0)
        inner = grads * out[rows, :].astype(F32)
        high = inner.astype(BF16)
        rest = (inner - high.astype(F32)).astype(BF16)
        delta[:, rows] = dot(pick, high, NT) + dot(pick, rest, NT)
        grads = grads.astype(BF16)
        for h in range(heads):
            g[h, rows, :] = jnp.concatenate([grads[:, h * HEAD : (h + 1) * HEAD], none], axis=1)
            dq[h, :, rows] = jnp.zeros((HEAD, TILE), F32)
        return 0

    lax.fori_loop(0, total // TILE, prepare, 0)
    tail = wide - total
    delta[:, total:] = jnp.zeros((8, tail), F32)
    for h in range(heads):
        g[h, total:, :] = jnp.zeros((tail, LANES), BF16)
        dq[h, :, total:] = jnp.zeros((HEAD, tail), F32)

    def one_block(i, _):
        c0 = pl.multiple_of(i * BLOCK, LANES)
        cols = pl.ds(c0, BLOCK)
        mine = idc[cols, :]
        low, high = block_range(i, numbers, before)

        def queries(size, at, carry):
            rows = pl.ds(pl.multiple_of(at * LANES, LANES), size)
            allowed = mine == idr[:, rows]
            both = [
                (dot(k[h, cols, :], q[h, rows, :], NT), dot(v[h, cols, :], g[h, rows, :], NT)) for h in range(heads)
            ]
            new = []
            for h in range(heads):
                dk, dv = carry[h]
                s, dp = both[h]
                p = jnp.where(allowed, jnp.exp(s - lse[h : h + 1, rows]), 0.0)
                ds = (p * (dp - delta[h : h + 1, rows])).astype(BF16)
                dv = dv + dot(p.astype(BF16), g[h, rows, :])
                dk = dk + dot(ds, q[h, rows, :])
                dq[h, :, rows] += dot(kt[h, :, cols], ds)
                new.append((dk, dv))
            return tuple(new)

        zero = jnp.zeros((BLOCK, LANES), F32)
        done = in_steps(low, high, queries, tuple((zero, zero) for _ in range(heads)))
        for part in range(2):
            joined = jnp.concatenate([done[h][part][:, :HEAD] for h in range(heads)], axis=1)
            dproj[part + 1, cols, :] = joined.astype(BF16)
        return 0

    lax.fori_loop(0, blocks(total), one_block, 0)

    def finish(i, _):
        rows = pl.ds(pl.multiple_of(i * TILE, LANES), TILE)
        joined = jnp.concatenate([dq[h, :, rows] for h in range(heads)], axis=0)
        dproj[0, rows, :] = (joined * HEAD**-0.5).T.astype(BF16)
        return 0

    lax.fori_loop(0, total // TILE, finish, 0)


def attention_back(ids, q, k, v, kt, out, grad, lse):
    heads, wide, _ = q.shape
    total = wide - PAD
    return pl.pallas_call(
        functools.partial(attention_back_kernel, heads, total),
        name="attention_back",
        cost_estimate=work(51),
        in_specs=[SMEM] * 2 + [VMEM] * 9,
        out_specs=VMEM,
        out_shape=jax.ShapeDtypeStruct((3, blocks(total) * BLOCK, heads * HEAD), BF16),
        scratch_shapes=[
            pltpu.VMEM((heads, wide, LANES), BF16),
            pltpu.VMEM((8, wide), F32),
            pltpu.VMEM((heads, HEAD, wide), F32),
        ],
        compiler_params=limit(60),
    )(*ids, q, k, v, kt, out, grad, lse)


ROWS_MID = 288


def middle_kernel(
    attended, tok, cot, cot_came, b_out, gain, shift, b_up, b_down, *rest
):
    me = Place()
    groups = len(rest) - 25
    weights = rest[:groups]
    layer_out, grad_mid, grad_heads, cells = rest[groups : groups + 4]
    (
        att, grad_att, w, acc, vec, bup, sent, came, units,
        att_s, att_r, own_s, grad_s, grad_r, back_s, unit_s, push_s, push_r, sum_s, sum_r, cell_s,
    ) = rest[groups + 4 :]
    group = me.d // 2
    parts, piece, _ = weights[0].shape
    rows = tok.shape[0]
    tiles = rows // ROWS_MID
    width = att.shape[2]
    others = [lax.rem(me.q + k, 4) for k in range(1, 4)]
    greet([me.member(quarter) for quarter in others])

    def tile(t, quarter=0):
        return pl.ds(pl.multiple_of(quarter * rows + t * ROWS_MID, 16), ROWS_MID)

    def att_to(k, t):
        return remote(
            attended.at[tile(t, others[k])], att.at[me.q, tile(t)], att_s.at[k, t], att_r.at[k, t], me.member(others[k])
        )

    def att_from(k, t):
        source = others[2 - k]
        return remote(
            attended.at[tile(t)], att.at[source, tile(t)], att_s.at[k, t], att_r.at[k, t], me.member(source)
        )

    def att_own(t):
        return pltpu.make_async_copy(attended.at[tile(t, me.q)], att.at[me.q, tile(t)], own_s.at[t])

    def grad_to(k, t):
        return remote(
            grad_att.at[others[k], tile(t)], grad_heads.at[tile(t, me.q)], grad_s.at[k, t], grad_r.at[k, t], me.member(others[k])
        )

    def grad_from(k, t):
        source = others[2 - k]
        return remote(
            grad_att.at[source, tile(t)], grad_heads.at[tile(t, source)], grad_s.at[k, t], grad_r.at[k, t], me.member(source)
        )

    def grad_own(t):
        return pltpu.make_async_copy(grad_att.at[me.q, tile(t)], grad_heads.at[tile(t, me.q)], back_s.at[t])

    for t in range(tiles):
        for k in (1, 0, 2):
            att_to(k, t).start()
        att_own(t).start()

    def w_rows(j, core):
        source = 2 * lax.rem(group + groups - j, groups) + core
        return w.at[:, pl.ds(pl.multiple_of(source * piece, 16), piece)]

    def load(j):
        return pltpu.make_async_copy(weights[j], w_rows(j, me.c), unit_s.at[j])

    def push(j):
        return remote(weights[j], w_rows(j, me.c), push_s.at[j], push_r.at[j], me.sibling)

    def pushed(j):
        return remote(weights[j], w_rows(j, 1 - me.c), push_s.at[j], push_r.at[j], me.sibling)

    for j in range(groups):
        push(j).start()
        load(j).start()
    for ref in (acc, vec, bup):
        ref[...] = jnp.zeros_like(ref)
    for j in range(groups):
        load(j).wait()
        pushed(j).wait_recv()

    out_rows = slice(0, OUT_ROWS)
    down_rows = slice(OUT_ROWS, OUT_ROWS + UP_ROWS)
    up_rows = slice(OUT_ROWS + UP_ROWS, VEC_AT)

    def one_tile(t, _):
        here = tile(t)
        att_own(t).wait()
        for k in range(3):
            att_from(k, t).wait_recv()
        atts = [att[v, here, :] for v in range(parts)]
        middle = tok[here, :].astype(F32) + line(b_out)
        for v in range(parts):
            middle = middle + dot(atts[v], w[v, out_rows])
        unit, scale = normalise(middle)
        low = (unit * line(gain) + line(shift)).astype(BF16)
        cot_low = jnp.where(me.native, cot[here, :], cot_came[here, :])
        cot_full = cot_low.astype(F32)
        out = middle + line(b_down)
        grad_norm = jnp.zeros_like(middle)

        def products(v):
            return dot(low, w[v, up_rows], NT), dot(cot_low, w[v, down_rows], NT)

        upcoming = products(0)
        for v in range(parts):
            hidden, grad_active = upcoming
            if v + 1 < parts:
                upcoming = products(v + 1)
            hidden = hidden + b_up[v]
            below = 0.5 * (1.0 + lax.erf(hidden * 0.5**0.5))
            density = jnp.exp(-0.5 * hidden * hidden) * 0.3989422804014327
            active = (hidden * below).astype(BF16)
            grad_hidden = (grad_active * (below + hidden * density)).astype(BF16)
            out = out + dot(active, w[v, down_rows])
            grad_norm = grad_norm + dot(grad_hidden, w[v, up_rows])
            acc[v, down_rows] += dot(active, cot_low, TN)
            acc[v, up_rows] += dot(grad_hidden, low, TN)
            bup[v] += jnp.sum(grad_hidden.astype(F32), axis=0, keepdims=True)
        layer_out[here, :] = out.astype(BF16)
        scaled = grad_norm * line(gain)
        back = cot_full + scale * (
            scaled
            - jnp.mean(scaled, axis=-1, keepdims=True)
            - unit * jnp.mean(scaled * unit, axis=-1, keepdims=True)
        )
        grad_mid[here, :] = back
        back_low = back.astype(BF16)
        for v in range(parts):
            grad_att[v, here, :] = dot(back_low, w[v, out_rows], NT).astype(BF16)
        for k in (1, 0, 2):
            grad_to(k, t).start()
        grad_own(t).start()
        for v in range(parts):
            acc[v, out_rows] += dot(atts[v], back_low, TN)
        vec[0:1] += jnp.sum(grad_norm * unit, axis=0, keepdims=True)
        vec[1:2] += jnp.sum(grad_norm, axis=0, keepdims=True)
        vec[2:3] += jnp.sum(back, axis=0, keepdims=True)
        vec[3:4] += jnp.sum(cot_full, axis=0, keepdims=True)
        return 0

    lax.fori_loop(0, tiles, one_tile, 0)

    def sum_rows(i, core):
        return pl.ds(pl.multiple_of((2 * i + core) * piece, 16), piece)

    def give(i):
        return remote(sent.at[i], came.at[i], sum_s.at[i], sum_r.at[i], me.sibling)

    def keep(i):
        return pltpu.make_async_copy(units.at[i], cells.at[i], cell_s.at[i])

    for v in range(parts):
        acc[v, VEC_AT : VEC_AT + 8] = vec[...]
        acc[v, VEC_AT + 4 : VEC_AT + 5, :UP_ROWS] = bup[v]
    for i in range(groups):
        for v in range(parts):
            sent[i, v] = acc[v, sum_rows(i, 1 - me.c), :].astype(BF16)
        give(i).start()
    for i in range(groups):
        give(i).wait_recv()
        for v in range(parts):
            units[i, v] = (acc[v, sum_rows(i, me.c), :] + came[i, v].astype(F32)).astype(BF16)
        keep(i).start()
    for t in range(tiles):
        for k in range(3):
            grad_from(k, t).wait_recv()
            grad_to(k, t).wait_send()
            att_to(k, t).wait_send()
        grad_own(t).wait()
    for j in range(groups):
        push(j).wait_send()
        give(j).wait_send()
        keep(j).wait()


def middle_part(attended, tok, cot, cot_came, b_out, gain, shift, b_up, b_down, weights):
    rows = tok.shape[0]
    width = attended.shape[1]
    groups = len(weights)
    parts, piece, _ = weights[0].shape
    tiles = rows // ROWS_MID
    shape = jax.ShapeDtypeStruct
    halves = (groups, parts, piece, D)
    return pl.pallas_call(
        middle_kernel,
        name="middle_part",
        cost_estimate=work(50),
        in_specs=[ANY] + [VMEM] * 8 + [ANY] * groups,
        out_specs=[VMEM, VMEM, ANY, ANY],
        out_shape=[
            shape((rows, D), BF16),
            shape((rows, D), F32),
            shape((4 * rows, width), BF16),
            shape(halves, BF16),
        ],
        scratch_shapes=[
            pltpu.VMEM((parts, rows, width), BF16),
            pltpu.VMEM((parts, rows, width), BF16),
            pltpu.VMEM((parts, UNITS, D), BF16),
            pltpu.VMEM((parts, UNITS, D), F32),
            pltpu.VMEM((8, D), F32),
            pltpu.VMEM((parts, 1, UP_ROWS), F32),
            pltpu.VMEM(halves, BF16),
            pltpu.VMEM(halves, BF16),
            pltpu.VMEM(halves, BF16),
            DMA((3, tiles)),
            DMA((3, tiles)),
            DMA((tiles,)),
            DMA((3, tiles)),
            DMA((3, tiles)),
            DMA((tiles,)),
        ]
        + [DMA((groups,))] * 6,
        compiler_params=pltpu.CompilerParams(
            collective_id=2, has_side_effects=True, vmem_limit_bytes=60 << 20
        ),
    )(attended, tok, cot, cot_came, b_out, gain, shift, b_up, b_down, *weights)


def finish_kernel(
    dproj_in, normed_in, full_in, w, grad_mid, gain, cells, grad, vec_sum, d_w, sums,
    dproj, normed, full, part, theirs, sent, crossed, low, acc, w_part, w_in, w_z, vec, vz, vd, u_in, u_own,
    load_s, out_s, sib_s, sib_r, cross_s, cross_r, swap_s, swap_r, vz_s, vz_r, vd_s, vd_r,
    ws_s, ws_r, wz_s, wz_r, wg_s, wg_r, wf_s, wf_r, uz_s, uz_r, ug_s, ug_r, uf_s, uf_r,
):
    me = Place()
    foreign = jnp.logical_not(me.native)
    rows = grad_mid.shape[0]
    piece = rows // PIECES
    width = w.shape[1]
    ndp = vd.shape[0]
    groups, w_rows, _ = w_part.shape
    group = me.d // 2

    order = [2 * (1 - me.hf) + 1 - me.r, 2 * (1 - me.hf) + me.r, 2 * me.hf + 1 - me.r, 2 * me.hf + me.r]

    def span_of(k, p):
        return pl.ds(pl.multiple_of(order[k] * rows + p * piece, 16), piece)

    def loads(k, p):
        span = span_of(k, p)
        pairs = ((dproj_in.at[:, span], dproj.at[:, span]), (normed_in.at[span], normed.at[span]), (full_in.at[span], full.at[span]))
        return [pltpu.make_async_copy(src, dst, load_s.at[k, p, j]) for j, (src, dst) in enumerate(pairs)]

    for k in range(4):
        for p in range(PIECES):
            for copy in loads(k, p):
                copy.start()

    around = [(me.d, lax.rem(me.m + k, 4)) for k in range(1, 4)]
    along = [(lax.rem(me.d + k, ndp), me.m) for k in range(1, ndp)]
    greet([me.partner] + around + along)

    def to_sib(k, p):
        slot = k % 2
        return remote(part.at[k, p], theirs.at[slot, p], sib_s.at[slot, p], sib_r.at[slot, p], me.sibling)

    def to_cross(p):
        return remote(sent.at[p], crossed.at[p], cross_s.at[p], cross_r.at[p], me.cross)

    def to_partner(p):
        return remote(low.at[p], grad.at[p], swap_s.at[p], swap_r.at[p], me.partner)

    def keep(p):
        return pltpu.make_async_copy(low.at[p], grad.at[p], out_s.at[p])

    def unit_z(j):
        to = lax.rem(me.m + 1 + j, 4)
        return remote(cells.at[to], u_in.at[j], uz_s.at[j], uz_r.at[j], around[j])

    def unit_give(j):
        to = (2 * lax.rem(group + j, groups) + me.c, me.m)
        return remote(u_own, sums.at[me.d], ug_s.at[j], ug_r.at[j], to)

    def unit_give_in(j):
        source = 2 * lax.rem(group + groups - j, groups) + me.c
        return remote(u_own, sums.at[source], ug_s.at[j], ug_r.at[j], (source, me.m))

    def unit_forward(j):
        source = 2 * lax.rem(group + groups - j, groups) + me.c
        src = u_own if j == 0 else sums.at[source]
        return remote(src, sums.at[source], uf_s.at[j], uf_r.at[j], me.sibling)

    def unit_forward_in(j):
        source = 2 * lax.rem(group + groups - j, groups) + 1 - me.c
        return remote(u_own, sums.at[source], uf_s.at[j], uf_r.at[j], me.sibling)

    vec[...] = jnp.zeros_like(vec)

    def compute(k):
        def one(p, _):
            span = span_of(k, p)
            for copy in loads(k, p):
                copy.wait()
            total = jnp.zeros((piece, D), F32)
            for c in range(3):
                total = total + dot(dproj[c, span, :], w[c])
            part[k, p] = total.astype(BF16)

            @pl.when(me.native if k < 2 else foreign)
            def _():
                to_sib(k, p).start()

            return 0

        lax.fori_loop(0, PIECES, one, 0)

    def pass_across(k):
        for p in range(PIECES):
            to_sib(k, p).wait_recv()
            sent[p] = (part[k, p].astype(F32) + theirs[0, p].astype(F32)).astype(BF16)
            to_cross(p).start()

    def conclude(k, p):
        to_sib(k, p).wait_recv()
        to_cross(p).wait_recv()
        total = part[k, p].astype(F32) + theirs[1, p].astype(F32) + crossed[p].astype(F32)
        span = pl.ds(pl.multiple_of(me.q * rows + p * piece, 16), piece)
        unit, scale = normalise(full[span, :].astype(F32))
        vec[0:1] += jnp.sum(total * unit, axis=0, keepdims=True)
        vec[1:2] += jnp.sum(total, axis=0, keepdims=True)
        scaled = total * line(gain)
        result = grad_mid[p * piece : (p + 1) * piece, :] + scale * (
            scaled
            - jnp.mean(scaled, axis=-1, keepdims=True)
            - unit * jnp.mean(scaled * unit, axis=-1, keepdims=True)
        )
        low[p] = result.astype(BF16)

    def conclude_foreign(p):
        conclude(1, p)
        to_partner(p).start()

    compute(0)

    @pl.when(foreign)
    def _():
        pass_across(0)

    compute(1)
    compute(2)

    @pl.when(me.native)
    def _():
        pass_across(2)

    compute(3)
    for j in range(3):
        unit_z(j).start()

    for c in range(3):
        acc[c * width : (c + 1) * width, :] = dot(dproj[c], normed[...], TN)

    for i in range(groups):
        w_part[i] = acc[i * w_rows : (i + 1) * w_rows, :].astype(BF16)

    def other_group(k):
        return lax.rem(group + k, groups)

    def w_send(k):
        to = other_group(k)
        return remote(w_part.at[to], w_in.at[k], ws_s.at[k], ws_r.at[k], (2 * to + me.c, me.m))

    for k in range(1, groups):
        w_send(k).start()

    @pl.when(foreign)
    def _():
        conclude_foreign(0)
        conclude_foreign(1)

    w_sum = w_part[group].astype(F32)
    for k in range(1, groups):
        w_send(k).wait_recv()
        w_sum = w_sum + w_in[k].astype(F32)

    to_z = remote(w_z.at[0], w_z.at[1], wz_s, wz_r, (me.d, lax.rem(me.m + 2, 4)))

    def w_give(k):
        return remote(w_z.at[0], d_w.at[group], wg_s.at[k], wg_r.at[k], (2 * other_group(k) + me.c, me.m))

    def w_give_in(k):
        source = lax.rem(group + groups - k, groups)
        return remote(w_z.at[0], d_w.at[source], wg_s.at[k], wg_r.at[k], (2 * source + me.c, me.m))

    def w_forward(k):
        source = lax.rem(group + groups - k, groups)
        src = w_z.at[0] if k == 0 else d_w.at[source]
        return remote(src, d_w.at[source], wf_s.at[k], wf_r.at[k], me.sibling)

    w_keep = pltpu.make_async_copy(w_z.at[0], d_w.at[group], out_s.at[PIECES])
    unit_keep = pltpu.make_async_copy(u_own, sums.at[me.d], out_s.at[PIECES + 1])

    @pl.when(foreign)
    def _():
        w_z[0] = w_sum.astype(BF16)
        to_z.start()
        conclude_foreign(2)

    @pl.when(me.native)
    def _():
        to_z.wait_recv()
        w_z[0] = (w_sum + w_z[1].astype(F32)).astype(BF16)
        w_keep.start()
        for k in range(1, groups):
            w_give(k).start()
        w_forward(0).start()
        for p in range(PIECES):
            conclude(3, p)
            keep(p).start()

    vz[me.m] = vec[...]

    def around_copy(k):
        return remote(vz.at[me.m], vz.at[me.m], vz_s.at[k], vz_r.at[k], around[k])

    for k in range(3):
        around_copy(k).start()

    unit_sum = cells[me.m].astype(F32)
    for j in range(3):
        unit_z(j).wait_recv()
        unit_sum = unit_sum + u_in[j].astype(F32)
    u_own[...] = unit_sum.astype(BF16)
    unit_keep.start()
    for j in range(1, groups):
        unit_give(j).start()
    unit_forward(0).start()

    @pl.when(me.native)
    def _():
        for k in range(1, groups):
            w_give_in(k).wait_recv()
            w_forward(k).start()

    for k in range(3):
        source = lax.rem(me.m + 3 - k, 4)
        remote(vz.at[source], vz.at[source], vz_s.at[k], vz_r.at[k], around[k]).wait_recv()
    vd[me.d] = vz[0] + vz[1] + vz[2] + vz[3]

    def along_copy(k):
        return remote(vd.at[me.d], vd.at[me.d], vd_s.at[k], vd_r.at[k], along[k])

    for k in range(ndp - 1):
        along_copy(k).start()

    for j in range(1, groups):
        unit_give_in(j).wait_recv()
        unit_forward(j).start()
    for k in range(ndp - 1):
        source = lax.rem(me.d + ndp - 1 - k, ndp)
        remote(vd.at[source], vd.at[source], vd_s.at[k], vd_r.at[k], along[k]).wait_recv()
    total = vd[0]
    for i in range(1, ndp):
        total = total + vd[i]
    vec_sum[...] = total
    for j in range(groups):
        unit_forward_in(j).wait_recv()

    @pl.when(foreign)
    def _():
        for k in range(groups):
            source = lax.rem(group + groups - k, groups)
            remote(w_z.at[0], d_w.at[source], wf_s.at[k], wf_r.at[k], me.sibling).wait_recv()
        for p in range(PIECES):
            to_partner(p).wait_recv()
            to_partner(p).wait_send()
            to_sib(2, p).wait_send()
            to_sib(3, p).wait_send()
        to_z.wait_send()

    @pl.when(me.native)
    def _():
        for p in range(PIECES):
            keep(p).wait()
            to_sib(0, p).wait_send()
            to_sib(1, p).wait_send()
        for k in range(1, groups):
            w_give(k).wait_send()
        for k in range(groups):
            w_forward(k).wait_send()
        w_keep.wait()

    for p in range(PIECES):
        to_cross(p).wait_send()
    for k in range(1, groups):
        w_send(k).wait_send()
    for k in range(3):
        around_copy(k).wait_send()
        unit_z(k).wait_send()
    for k in range(ndp - 1):
        along_copy(k).wait_send()
    for j in range(groups):
        unit_forward(j).wait_send()
    for j in range(1, groups):
        unit_give(j).wait_send()
    unit_keep.wait()


def finish(dproj, normed, full, w, grad_mid, gain, cells, ndp):
    rows = grad_mid.shape[0]
    total = full.shape[0]
    piece = rows // PIECES
    pieces = (PIECES, piece, D)
    groups = ndp // 2
    columns = 3 * w.shape[1]
    cut = (groups, columns // groups, D)
    unit = cells.shape[1:]
    shape = jax.ShapeDtypeStruct
    return pl.pallas_call(
        finish_kernel,
        name="finish",
        cost_estimate=work(60),
        in_specs=[ANY] * 3 + [VMEM] * 4,
        out_specs=[ANY, VMEM, ANY, ANY],
        out_shape=[shape(pieces, BF16), shape((8, D), F32), shape(cut, BF16), shape((ndp,) + unit, BF16)],
        scratch_shapes=[
            pltpu.VMEM((3, total, w.shape[1]), BF16),
            pltpu.VMEM((total, D), BF16),
            pltpu.VMEM((total, D), BF16),
            pltpu.VMEM((4,) + pieces, BF16),
            pltpu.VMEM((2,) + pieces, BF16),
            pltpu.VMEM(pieces, BF16),
            pltpu.VMEM(pieces, BF16),
            pltpu.VMEM(pieces, BF16),
            pltpu.VMEM((columns, D), F32),
            pltpu.VMEM(cut, BF16),
            pltpu.VMEM(cut, BF16),
            pltpu.VMEM((2,) + cut[1:], BF16),
            pltpu.VMEM((8, D), F32),
            pltpu.VMEM((4, 8, D), F32),
            pltpu.VMEM((ndp, 8, D), F32),
            pltpu.VMEM((3,) + unit, BF16),
            pltpu.VMEM(unit, BF16),
            DMA((4, PIECES, 3)),
            DMA((PIECES + 2,)),
        ]
        + [DMA((2, PIECES))] * 2
        + [DMA((PIECES,))] * 4
        + [DMA((3,))] * 2
        + [DMA((ndp - 1,))] * 2
        + [DMA((groups,))] * 2
        + [DMA] * 2
        + [DMA((groups,))] * 4
        + [DMA((3,))] * 2
        + [DMA((groups,))] * 4,
        compiler_params=pltpu.CompilerParams(
            collective_id=4, has_side_effects=True, vmem_limit_bytes=60 << 20
        ),
    )(dproj, normed, full, w, grad_mid, gain, cells)


def outputs_kernel(
    width, layer, layer_came, grads, w_sums, unit_sums, vec_one,
    layer_out, tokens_grad, d_qkv, d_out, d_up, d_down, d_vecs, d_bup, d_ones, rows_of,
):
    me = Place()
    layer_out[...] = jnp.where(me.native, layer[...], layer_came[...])
    piece = grads.shape[1]
    for p in range(grads.shape[0]):
        tokens_grad[p * piece : (p + 1) * piece, :] = grads[p].astype(F32)
    groups, height, _ = w_sums.shape
    for i in range(groups):
        rows_of[i * height : (i + 1) * height, :] = w_sums[i].astype(F32)
    for c in range(3):
        d_qkv[c] = rows_of[c * width : (c + 1) * width, :]
    ndp, height, _ = unit_sums.shape
    for i in range(ndp):
        rows_of[i * height : (i + 1) * height, :] = unit_sums[i].astype(F32)
    d_out[...] = rows_of[:OUT_ROWS, :]
    d_down[...] = rows_of[OUT_ROWS : OUT_ROWS + UP_ROWS, :]
    d_up[...] = rows_of[OUT_ROWS + UP_ROWS : VEC_AT, :].T
    for i, ref in enumerate(d_vecs):
        ref[...] = rows_of[VEC_AT + i, :]
    d_bup[...] = rows_of[VEC_AT + 4, :UP_ROWS]
    for i, ref in enumerate(d_ones):
        ref[...] = vec_one[i, :]


def outputs(layer, layer_came, grads, w_sums, unit_sums, vec_one):
    rows = layer.shape[0]
    width = w_sums.shape[0] * w_sums.shape[1] // 3
    shape = lambda *s: jax.ShapeDtypeStruct(s, F32)

    def kernel(*refs):
        outs = refs[6:-1]
        outputs_kernel(width, *refs[:6], *outs[:6], outs[6:10], outs[10], outs[11:13], refs[-1])

    return pl.pallas_call(
        kernel,
        name="outputs",
        in_specs=[VMEM] * 6,
        out_specs=[VMEM] * 13,
        out_shape=[
            jax.ShapeDtypeStruct((rows, D), BF16),
            shape(rows, D),
            shape(3, width, D),
            shape(OUT_ROWS, D),
            shape(D, UP_ROWS),
            shape(UP_ROWS, D),
            shape(D),
            shape(D),
            shape(D),
            shape(D),
            shape(UP_ROWS),
            shape(D),
            shape(D),
        ],
        scratch_shapes=[pltpu.VMEM((UNITS, D), F32)],
        compiler_params=limit(48),
    )(layer, layer_came, grads, w_sums, unit_sums, vec_one)


def swap_pairs(ndp):
    return [
        (d * 4 + m, (d ^ 1) * 4 + (m + 2) % 4) for d in range(ndp) for m in range(4) if d % 2 != m // 2
    ]


def weight_piece(w_out, w_up, w_down, ndp):
    block = jnp.concatenate([w_out, w_down, w_up.T, jnp.zeros((UNITS - w_out.shape[0] - 2 * w_down.shape[0], D), BF16)])
    piece = UNITS // ndp
    return lax.dynamic_slice_in_dim(block, lax.axis_index("dp") * piece, piece, 0)


def from_other_pairs(block, ndp):
    groups = ndp // 2
    blocks_of = [block]
    for j in range(1, groups):
        pairs = [(d, 2 * ((d // 2 + j) % groups) + d % 2) for d in range(ndp)]
        blocks_of.append(lax.ppermute(block, "dp", pairs))
    return blocks_of


def sum_over_pairs(cells, ndp):
    cores = [[d for d in range(ndp) if d % 2 == core] for core in range(2)]
    return lax.psum_scatter(cells.reshape(-1, D), "dp", scatter_dimension=0, tiled=True, axis_index_groups=cores)


def shards(
    tokens,
    scene_ids,
    gain_one,
    shift_one,
    w_qkv,
    w_out,
    b_out,
    gain_two,
    shift_two,
    w_up,
    b_up,
    w_down,
    b_down,
    cotangent,
    ndp,
):
    both = ("dp", "mp")
    swap = swap_pairs(ndp)
    w_qkv = jnp.swapaxes(w_qkv, 1, 2)
    full, own_tok, w_mine, numbers, id_row, id_column, before, b_ups, normed, q, k, v, kt, vt, weights = start(
        tokens, w_qkv, scene_ids.reshape(-1, LANES), b_up, gain_one, shift_one, weight_piece(w_out, w_up, w_down, ndp), ndp
    )
    w_mine = w_mine.reshape(w_qkv.shape)
    ids = numbers, before, id_column, id_row
    weights = from_other_pairs(weights, ndp)
    sent_cot, q = lax.optimization_barrier((cotangent, q))
    cot_came = lax.ppermute(sent_cot, both, swap)
    attended, lse = attention(ids, q, k, vt)
    layer, grad_mid, grad_heads, cells = middle_part(
        attended, own_tok, cotangent, cot_came, b_out, gain_two, shift_two, b_ups, b_down, weights
    )
    sent_out, grad_heads = lax.optimization_barrier((layer, grad_heads))
    layer_came = lax.ppermute(sent_out, both, swap)
    cells = sum_over_pairs(cells, ndp)
    dproj = attention_back(ids, q, k, v, kt, attended, grad_heads, lse)
    cells, dproj = lax.optimization_barrier((cells, dproj))
    grads, vec_one, w_sums, unit_sums = finish(
        dproj, normed, full, w_mine, grad_mid, gain_one, cells.reshape(4, -1, D), ndp
    )
    (
        layer_out, tokens_grad, d_qkv, d_out, d_up, d_down, d_gain_two, d_shift_two, d_b_out, d_b_down, d_b_up, d_gain_one, d_shift_one,
    ) = outputs(layer, layer_came, grads, w_sums, unit_sums, vec_one)
    return (
        layer_out,
        tokens_grad,
        d_gain_one,
        d_shift_one,
        jnp.swapaxes(d_qkv, 1, 2),
        d_out,
        d_b_out,
        d_gain_two,
        d_shift_two,
        d_up,
        d_b_up,
        d_down,
        d_b_down,
    )


def solution(mesh):
    ndp = mesh.shape["dp"]
    return jax.shard_map(
        functools.partial(shards, ndp=ndp),
        mesh=mesh,
        in_specs=(
            P(("dp", "mp"), None),
            P("dp"),
            P(),
            P(),
            P(None, None, "mp"),
            P("mp", None),
            P(),
            P(),
            P(),
            P(None, "mp"),
            P("mp"),
            P("mp", None),
            P(),
            P(("dp", "mp"), None),
        ),
        out_specs=(
            P(("dp", "mp"), None),
            P(("dp", "mp"), None),
            P(),
            P(),
            P(None, None, "mp"),
            P("mp", None),
            P(),
            P(),
            P(),
            P(None, "mp"),
            P("mp"),
            P("mp", None),
            P(),
        ),
        check_vma=False,
    )
```

```python
import functools

import jax
import jax.numpy as jnp
from jax import lax
from jax.experimental import pallas as pl
from jax.experimental.pallas import tpu as pltpu
from jax.sharding import PartitionSpec as P

HEAD = 64
D = 768
FF = 1536
LANES = 128
PAD = 512
OUT_ROWS = D // 4
UP_ROWS = FF // 4
VEC_AT = OUT_ROWS + 2 * UP_ROWS
UNITS = 1024
EPS = 1e-05
MASKED = -1e30
MESH = pl.DeviceIdType.MESH
F32 = jnp.float32
BF16 = jnp.bfloat16
VMEM = pl.BlockSpec(memory_space=pltpu.VMEM)
SMEM = pl.BlockSpec(memory_space=pltpu.SMEM)
ANY = pl.BlockSpec(memory_space=pl.ANY)
DMA = pltpu.SemaphoreType.DMA

NN = (((1,), (0,)), ((), ()))
NT = (((1,), (1,)), ((), ()))
TN = (((0,), (0,)), ((), ()))


def dot(a, b, dims=NN):
    return lax.dot_general(a, b, dims, preferred_element_type=F32)


def work(us):
    return pl.CostEstimate(flops=us * 10**9, bytes_accessed=us * 3 * 10**6, transcendentals=0)


def limit(mib):
    return pltpu.CompilerParams(vmem_limit_bytes=mib << 20)


def line(ref):
    return ref[...].reshape(1, -1)


class Place:
    def __init__(self):
        self.d = lax.axis_index("dp")
        self.m = lax.axis_index("mp")
        self.c = lax.rem(self.d, 2)
        self.r = lax.rem(self.m, 2)
        self.hf = self.m // 2
        self.q = 2 * self.c + self.r
        self.native = self.c == self.hf
        self.sibling = (self.d + 1 - 2 * self.c, self.m)
        self.cross = (self.d, self.m + 1 - 2 * self.r)
        self.partner = (self.d + 1 - 2 * self.c, lax.rem(self.m + 2, 4))

    def member(self, quarter):
        return (self.d - self.c + quarter // 2, 2 * self.hf + quarter % 2)


def greet(others):
    barrier = pltpu.get_barrier_semaphore()
    for other in others:
        pl.semaphore_signal(barrier, inc=1, device_id=other, device_id_type=MESH)
    pl.semaphore_wait(barrier, len(others))


def remote(src, dst, send, recv, device):
    return pltpu.make_async_remote_copy(
        src_ref=src, dst_ref=dst, send_sem=send, recv_sem=recv, device_id=device, device_id_type=MESH
    )


STAGES = 3
PIECES = 6
TILE = 384
SCENES = 4


def normalise(x):
    centred = x - jnp.mean(x, axis=-1, keepdims=True)
    scale = lax.rsqrt(jnp.mean(centred * centred, axis=-1, keepdims=True) + EPS)
    return centred * scale, scale


def widen(x, ones, rows):
    lane = lax.broadcasted_iota(jnp.int32, (rows, LANES - HEAD), 1)
    return jnp.concatenate([x, jnp.where(lane < ones, 1.0, 0.0).astype(x.dtype)], axis=1)


def describe_scenes(ids, row, column, before):
    lines = ids.shape[0]
    for j in range(lines):
        place = j * LANES + lax.broadcasted_iota(jnp.int32, (1, LANES), 1)
        number = ids[j : j + 1, :]
        number = jnp.where(number >= 0, number, -1 - place)
        span = slice(j * LANES, (j + 1) * LANES)
        row[:, span] = number
        column[span, :] = jnp.broadcast_to(number.astype(F32), (LANES, LANES)).T[:, :1].astype(jnp.int32)
    rest = row.shape[1] - lines * LANES
    row[:, lines * LANES :] = jnp.full((1, rest), -(1 << 21), jnp.int32)
    column[lines * LANES :, :] = jnp.full((rest, 1), -(1 << 20), jnp.int32)
    lane = lax.broadcasted_iota(jnp.int32, (1, LANES), 1)
    counts = jnp.zeros((1, LANES), F32)
    for number in range(1, SCENES + 1):
        mine = jnp.where((ids[...] >= 0) & (ids[...] < number), 1.0, 0.0)
        total = jnp.sum(jnp.sum(mine, axis=0, keepdims=True), axis=1, keepdims=True)
        counts = jnp.where(lane == number, total, counts)
    before[...] = counts.astype(jnp.int32)


def start_kernel(
    heads, tok, wq, ids, b_up, gain, shift, mine,
    full, own, w_out, ids_own, id_row, id_column, before, b_ups, normed, q, k, v, kt, vt, units,
    buf, w, low_s, q_s, k_s, v_s, kt_s, vt_s,
    swap_s, swap_r, cross_s, cross_r, sib_s, sib_r, fwd_s, fwd_r, w_s, w_r, ids_s, ids_r, b_s, b_r, out_s, late_s,
    uz_s, uz_r,
):
    me = Place()
    foreign = jnp.logical_not(me.native)
    rows = tok.shape[0]
    piece = rows // PIECES
    total = buf.shape[0]
    tiles = total // TILE
    groups = w.shape[1]
    group = me.d // 2
    around = [(me.d, lax.rem(me.m + j, 4)) for j in range(1, 4)]
    lines = [(2 * lax.rem(group + j, groups) + me.c, me.m) for j in range(1, groups)]
    greet([me.sibling, me.partner] + around + lines)

    def rows_of(quarter, n):
        p = jnp.where(me.hf == 0, n, PIECES - 1 - n)
        return pl.ds(pl.multiple_of(quarter * rows + p * piece, 16), piece)

    def part(quarter, n):
        return buf.at[rows_of(quarter, n)]

    sib_q = 2 * (1 - me.c) + me.r
    cross_q = 2 * me.c + 1 - me.r
    sib_cross_q = 2 * (1 - me.c) + 1 - me.r

    def swap(n):
        p = jnp.where(me.hf == 1, n, PIECES - 1 - n)
        src = tok.at[pl.ds(pl.multiple_of(p * piece, 16), piece)]
        dst = buf.at[pl.ds(pl.multiple_of(sib_q * rows + p * piece, 16), piece)]
        return remote(src, dst, swap_s.at[n], swap_r.at[n], me.partner)

    def swap_in(n):
        return remote(part(me.q, n), part(me.q, n), swap_s.at[n], swap_r.at[n], me.partner)

    def cross(quarter, n):
        return remote(part(quarter, n), part(quarter, n), cross_s.at[n], cross_r.at[n], me.cross)

    def sib(quarter, n):
        return remote(part(quarter, n), part(quarter, n), sib_s.at[n], sib_r.at[n], me.sibling)

    def forward(quarter, n):
        return remote(part(quarter, n), part(quarter, n), fwd_s.at[n], fwd_r.at[n], me.sibling)

    weight = remote(wq.at[:, group], w.at[:, group], w_s.at[0], w_r.at[0], me.partner)

    def weight_share(j):
        return remote(w.at[:, group], w.at[:, group], w_s.at[j], w_r.at[j], lines[j - 1])

    def weight_in(j):
        source = lax.rem(group + groups - j, groups)
        return remote(w.at[:, source], w.at[:, source], w_s.at[j], w_r.at[j], lines[j - 1])

    unit_own = pltpu.make_async_copy(mine, units.at[me.m], late_s.at[7])

    def unit_z(j, source):
        return remote(mine, units.at[source], uz_s.at[j], uz_r.at[j], around[j])

    def give_b_up(j):
        return remote(b_ups.at[me.m], b_ups.at[me.m], b_s.at[j], b_r.at[j], around[j])

    scenes = remote(ids, ids_own, ids_s, ids_r, me.sibling)
    unit_own.start()
    b_ups[me.m] = line(b_up)
    for j in range(3):
        give_b_up(j).start()

    @pl.when(me.native)
    def _():
        scenes.start()
        buf[pl.ds(pl.multiple_of(me.q * rows, 16), rows), :] = tok[...]
        for n in range(PIECES):
            cross(me.q, n).start()
            sib(me.q, n).start()
        w[...] = wq[...]
        ids_own[...] = ids[...]

    @pl.when(foreign)
    def _():
        weight.start()
        for n in range(PIECES):
            swap(n).start()

    def share(n):
        swap_in(n).wait_recv()
        cross(me.q, n).start()
        sib(me.q, n).start()

    def pass_on(n):
        cross(cross_q, n).wait_recv()
        forward(cross_q, n).start()

    def from_sibling(n):
        sib(sib_q, n).wait_recv()
        forward(sib_cross_q, n).wait_recv()

    def outputs(t):
        span = pl.ds(pl.multiple_of(t * TILE, LANES), TILE)
        pairs = [
            (low_s.at[span], normed.at[span]),
            (buf.at[span], full.at[span]),
            (q_s.at[:, span], q.at[:, span]),
            (k_s.at[:, span], k.at[:, span]),
            (v_s.at[:, span], v.at[:, span]),
            (kt_s.at[:, :, span], kt.at[:, :, span]),
            (vt_s.at[:, :, span], vt.at[:, :, span]),
        ]
        return [pltpu.make_async_copy(src, dst, out_s.at[t, j]) for j, (src, dst) in enumerate(pairs)]

    ones = jnp.where(lax.broadcasted_iota(jnp.int32, (16, TILE), 0) < 1, 1.0, 0.0).astype(BF16)

    def compute(first, stride, count):
        def one(n, _):
            at = first + stride * n
            t = jnp.where(me.hf == 0, at, tiles - 1 - at)
            span = pl.ds(pl.multiple_of(t * TILE, LANES), TILE)
            unit, _ = normalise(buf[span, :].astype(F32))
            low = (unit * line(gain) + line(shift)).astype(BF16)
            low_s[span, :] = low
            qs = (dot(low, w[0].reshape(-1, D), NT).astype(BF16).astype(F32) * HEAD**-0.5).astype(BF16)
            ks = dot(low, w[1].reshape(-1, D), NT)
            vs = dot(low, w[2].reshape(-1, D), NT)
            kts = ks.T.astype(BF16)
            vts = vs.T.astype(BF16)
            ks = ks.astype(BF16)
            vs = vs.astype(BF16)
            for h in range(heads):
                cols = slice(h * HEAD, (h + 1) * HEAD)
                q_s[h, span, :] = widen(qs[:, cols], 0, TILE)
                k_s[h, span, :] = widen(ks[:, cols], 3, TILE)
                v_s[h, span, :] = widen(vs[:, cols], 3, TILE)
                kt_s[h, :, span] = kts[cols]
                vt_s[h, :HEAD, span] = vts[cols]
                vt_s[h, HEAD:, span] = ones
            for copy in outputs(t):
                copy.start()
            return 0

        lax.fori_loop(0, count, one, 0)

    pad = pl.ds(total, PAD)
    zeros = jnp.zeros((heads, PAD, LANES), BF16)
    for ref in (q_s, k_s, v_s):
        ref[:, pad, :] = zeros
    for ref in (kt_s, vt_s):
        ref[:, :, pad] = jnp.zeros((heads, ref.shape[1], PAD), BF16)
    padding = [
        pltpu.make_async_copy(src, dst, late_s.at[j])
        for j, (src, dst) in enumerate(
            [(a.at[:, pad], b.at[:, pad]) for a, b in ((q_s, q), (k_s, k), (v_s, v))]
            + [(a.at[:, :, pad], b.at[:, :, pad]) for a, b in ((kt_s, kt), (vt_s, vt))]
        )
    ]
    for copy in padding:
        copy.start()

    def stage(n):
        return range(n * PIECES // STAGES, (n + 1) * PIECES // STAGES)

    @pl.when(me.native)
    def _():
        for n in range(PIECES):
            pass_on(n)

    @pl.when(foreign)
    def _():
        weight.wait_recv()
        for j in range(1, groups):
            weight_share(j).start()
        for n in range(PIECES):
            share(n)
        for j in range(1, groups):
            weight_in(j).wait_recv()
        for n in range(PIECES):
            from_sibling(n)

    for j in range(3):
        unit_z(j, me.m).start()

    @pl.when(foreign)
    def _():
        scenes.wait_recv()

    describe_scenes(ids_own, id_row, id_column, before)
    compute(0, 1, 2)

    @pl.when(foreign)
    def _():
        for n in stage(0):
            pass_on(n)

    compute(2, 1, 2)

    @pl.when(foreign)
    def _():
        for n in stage(1):
            pass_on(n)

    @pl.when(me.native)
    def _():
        for n in stage(0):
            from_sibling(n)

    compute(4, 1, 1)

    @pl.when(me.native)
    def _():
        for n in stage(1):
            from_sibling(n)

    compute(5, 2, 2)

    @pl.when(foreign)
    def _():
        for n in stage(2):
            pass_on(n)

    @pl.when(me.native)
    def _():
        for n in stage(2):
            from_sibling(n)

    own_copy = pltpu.make_async_copy(buf.at[pl.ds(pl.multiple_of(me.q * rows, 16), rows)], own, late_s.at[5])
    w_copy = pltpu.make_async_copy(w, w_out, late_s.at[6])
    own_copy.start()
    w_copy.start()
    compute(6, 2, 2)
    unit_own.wait()
    for j in range(3):
        unit_z(j, lax.rem(me.m + 3 - j, 4)).wait_recv()
        unit_z(j, me.m).wait_send()

    for j in range(3):
        source = lax.rem(me.m + 3 - j, 4)
        remote(b_ups.at[source], b_ups.at[source], b_s.at[j], b_r.at[j], around[j]).wait_recv()
        give_b_up(j).wait_send()

    @pl.when(me.native)
    def _():
        scenes.wait_send()

    @pl.when(foreign)
    def _():
        weight.wait_send()
        for j in range(1, groups):
            weight_share(j).wait_send()
        for n in range(PIECES):
            swap(n).wait_send()

    for n in range(PIECES):
        cross(me.q, n).wait_send()
        sib(me.q, n).wait_send()
        forward(cross_q, n).wait_send()
    for copy in padding + [own_copy, w_copy]:
        copy.wait()

    def finish_tile(t, _):
        for copy in outputs(t):
            copy.wait()
        return 0

    lax.fori_loop(0, tiles, finish_tile, 0)


def start(tokens, w_qkv, scene_ids, b_up, gain, shift, mine, ndp):
    rows = tokens.shape[0]
    total = 4 * rows
    heads = w_qkv.shape[1] // HEAD
    groups = ndp // 2
    w_qkv = w_qkv.reshape(3, groups, -1, D)
    units = (4,) + mine.shape
    wide = total + PAD
    shape = jax.ShapeDtypeStruct
    rowed = (heads, wide, LANES)
    k_cols, v_cols = (heads, HEAD, wide), (heads, HEAD + 16, wide)
    three = DMA((PIECES,))
    return pl.pallas_call(
        functools.partial(start_kernel, heads),
        name="start",
        cost_estimate=work(50),
        in_specs=[VMEM] * 6 + [ANY],
        out_specs=[ANY] * 3 + [VMEM] * 5 + [ANY] * 7,
        out_shape=[
            shape((total, D), BF16),
            shape((rows, D), BF16),
            shape(w_qkv.shape, BF16),
            shape(scene_ids.shape, jnp.int32),
            shape((1, wide), jnp.int32),
            shape((wide, 1), jnp.int32),
            shape((1, LANES), jnp.int32),
            shape((4, 1) + b_up.shape, F32),
            shape((total, D), BF16),
            shape(rowed, BF16),
            shape(rowed, BF16),
            shape(rowed, BF16),
            shape(k_cols, BF16),
            shape(v_cols, BF16),
            shape(units, BF16),
        ],
        scratch_shapes=[
            pltpu.VMEM((total, D), BF16),
            pltpu.VMEM(w_qkv.shape, BF16),
            pltpu.VMEM((total, D), BF16),
            pltpu.VMEM(rowed, BF16),
            pltpu.VMEM(rowed, BF16),
            pltpu.VMEM(rowed, BF16),
            pltpu.VMEM(k_cols, BF16),
            pltpu.VMEM(v_cols, BF16),
        ]
        + [three] * 8
        + [DMA((groups,))] * 2
        + [DMA] * 2
        + [DMA((3,))] * 2
        + [DMA((total // TILE, 7)), DMA((8,))]
        + [DMA((3,))] * 2,
        compiler_params=pltpu.CompilerParams(
            collective_id=1, has_side_effects=True, vmem_limit_bytes=60 << 20
        ),
    )(tokens, w_qkv, scene_ids, b_up, gain, shift, mine)


BLOCK = 256
STEP = 512


def blocks(total):
    return -(-total // BLOCK)


def block_range(i, numbers, before):
    lines = numbers.shape[0]
    per = BLOCK // LANES
    top, bottom = numbers[i * per, 0], numbers[jnp.minimum(i * per + per, lines) - 1, LANES - 1]
    bottom = jnp.where(i * per + per > lines, -1, bottom)
    low = jnp.where(top >= 0, before[0, jnp.maximum(top, 0)], i * BLOCK)
    high = jnp.where(bottom >= 0, before[0, jnp.maximum(bottom, 0) + 1], i * BLOCK + BLOCK)
    return low // LANES, (high + LANES - 1) // LANES


def list_steps(count, numbers, before, total, block_at, step_at, marks):
    stride = STEP // LANES

    def one_block(i, n):
        first, last = block_range(i, numbers, before)
        steps = (last - first + stride - 1) // stride

        def put(j, n):
            block_at[n] = i * (BLOCK // LANES)
            step_at[n] = first + j * stride
            marks[n] = jnp.where(j == 0, 1, 0) + jnp.where(j == steps - 1, 2, 0)
            return n + 1

        return lax.fori_loop(0, steps, put, n)

    n = lax.fori_loop(0, count, one_block, 0)
    for idle in range(2):
        block_at[n + idle] = 0
        step_at[n + idle] = total // LANES
        marks[n + idle] = 0
    return n


def step_lists(total):
    return [pltpu.SMEM((blocks(total) * (-(-total // STEP) + 1) + 2,), jnp.int32)] * 3


def attention_kernel(
    heads, total, numbers, before, idc, idr, q, k, vt, out, lse, block_at, step_at, marks, even, odd
):
    count = list_steps(blocks(total), numbers, before, total, block_at, step_at, marks)

    def place(i):
        rows = pl.ds(pl.multiple_of(block_at[i] * LANES, LANES), BLOCK)
        return rows, pl.ds(pl.multiple_of(step_at[i] * LANES, LANES), STEP)

    def score(i, buf, h):
        rows, cols = place(i)
        s = jnp.where(idc[cols, :] == idr[:, rows], dot(k[h, cols, :], q[h, rows, :], NT), MASKED)
        buf[h] = s
        return jnp.max(s, axis=0, keepdims=True)

    def step(i, now, after, carry):
        rows, cols = place(i)
        mark = marks[i]
        new = []
        for h in range(heads):
            top, acc, highest = carry[h]
            upcoming = score(i + 1, after, h)
            top = jnp.where(lax.rem(mark, 2) == 1, MASKED, top)
            above = jnp.maximum(top, highest)
            p = jnp.exp(now[h] - above).astype(BF16)
            acc = acc * jnp.exp(top - above) + dot(vt[h, :, cols], p)
            new.append((above, acc, upcoming))

        @pl.when(mark >= 2)
        def _():
            valid = jnp.where(idr[:, rows] >= 0, 1.0, 0.0)
            mixed = []
            for h in range(heads):
                top, acc, _ = new[h]
                row_total = acc[HEAD : HEAD + 1]
                mixed.append(acc[:HEAD] * (valid / row_total))
                lse[pl.ds(h, 1), rows] = top + jnp.log(row_total)
            out[rows, :] = jnp.concatenate(mixed, axis=0).T.astype(BF16)

        return tuple(new)

    low = jnp.full((1, BLOCK), MASKED, F32)
    start = tuple((low, jnp.zeros((vt.shape[1], BLOCK), F32), score(0, even, h)) for h in range(heads))

    def two_steps(n, carry):
        return step(2 * n + 1, odd, even, step(2 * n, even, odd, carry))

    lax.fori_loop(0, (count + 1) // 2, two_steps, start)


def attention(ids, q, k, vt):
    heads, wide, _ = q.shape
    total = wide - PAD
    rows = blocks(total) * BLOCK
    scores = pltpu.VMEM((heads, STEP, BLOCK), F32)
    return pl.pallas_call(
        functools.partial(attention_kernel, heads, total),
        name="attention",
        cost_estimate=work(31),
        in_specs=[SMEM] * 2 + [VMEM] * 5,
        out_specs=[VMEM, VMEM],
        out_shape=[
            jax.ShapeDtypeStruct((rows, heads * HEAD), BF16),
            jax.ShapeDtypeStruct((heads, wide), F32),
        ],
        scratch_shapes=step_lists(total) + [scores, scores],
        compiler_params=limit(56),
    )(*ids, q, k, vt)


def in_steps(first, last, body, carry):
    wide, narrow = 2 * BLOCK // LANES, BLOCK // LANES
    count = (last - first + narrow - 1) // narrow
    carry = lax.fori_loop(0, count // 2, lambda n, c: body(2 * BLOCK, first + n * wide, c), carry)
    return lax.fori_loop(0, count % 2, lambda n, c: body(BLOCK, first + (count - 1) * narrow, c), carry)


def attention_back_kernel(
    heads, total, numbers, before, idc, idr, q_in, k_in, v_in, kt_in, out, grad, lse, dproj,
    q, k, v, kt, made, g, delta, dq, in_s, out_s,
):
    wide = q.shape[1]
    width = heads * HEAD
    head_of = lax.broadcasted_iota(jnp.int32, (8, width), 1) // HEAD
    pick = jnp.where(head_of == lax.broadcasted_iota(jnp.int32, (8, width), 0), 1.0, 0.0).astype(BF16)
    none = jnp.zeros((TILE, LANES - HEAD), BF16)
    arriving = [
        pltpu.make_async_copy(src, dst, in_s.at[i])
        for i, (src, dst) in enumerate(((q_in, q), (k_in, k), (v_in, v), (kt_in, kt)))
    ]
    for copy in arriving:
        copy.start()

    def prepare(i, _):
        rows = pl.ds(pl.multiple_of(i * TILE, LANES), TILE)
        grads = jnp.where(idc[rows, :] >= 0, grad[rows, :].astype(F32), 0.0)
        inner = grads * out[rows, :].astype(F32)
        high = inner.astype(BF16)
        rest = (inner - high.astype(F32)).astype(BF16)
        delta[:, rows] = dot(pick, high, NT) + dot(pick, rest, NT)
        grads = grads.astype(BF16)
        for h in range(heads):
            g[h, rows, :] = jnp.concatenate([grads[:, h * HEAD : (h + 1) * HEAD], none], axis=1)
            dq[h, :, rows] = jnp.zeros((HEAD, TILE), F32)
        return 0

    lax.fori_loop(0, total // TILE, prepare, 0)
    tail = wide - total
    delta[:, total:] = jnp.zeros((8, tail), F32)
    for h in range(heads):
        g[h, total:, :] = jnp.zeros((tail, LANES), BF16)
        dq[h, :, total:] = jnp.zeros((HEAD, tail), F32)

    for copy in arriving:
        copy.wait()

    def give(i):
        cols = pl.ds(pl.multiple_of(i * BLOCK, LANES), BLOCK)
        return pltpu.make_async_copy(made.at[1:3, cols], dproj.at[1:3, cols], out_s.at[i])

    def one_block(i, _):
        c0 = pl.multiple_of(i * BLOCK, LANES)
        cols = pl.ds(c0, BLOCK)
        mine = idc[cols, :]
        low, high = block_range(i, numbers, before)

        def queries(size, at, carry):
            rows = pl.ds(pl.multiple_of(at * LANES, LANES), size)
            allowed = mine == idr[:, rows]
            both = [
                (dot(k[h, cols, :], q[h, rows, :], NT), dot(v[h, cols, :], g[h, rows, :], NT)) for h in range(heads)
            ]
            new = []
            for h in range(heads):
                dk, dv = carry[h]
                s, dp = both[h]
                p = jnp.where(allowed, jnp.exp(s - lse[h : h + 1, rows]), 0.0)
                ds = (p * (dp - delta[h : h + 1, rows])).astype(BF16)
                dv = dv + dot(p.astype(BF16), g[h, rows, :])
                dk = dk + dot(ds, q[h, rows, :])
                dq[h, :, rows] += dot(kt[h, :, cols], ds)
                new.append((dk, dv))
            return tuple(new)

        zero = jnp.zeros((BLOCK, LANES), F32)
        done = in_steps(low, high, queries, tuple((zero, zero) for _ in range(heads)))
        for part in range(2):
            joined = jnp.concatenate([done[h][part][:, :HEAD] for h in range(heads)], axis=1)
            made[part + 1, cols, :] = joined.astype(BF16)
        give(i).start()
        return 0

    lax.fori_loop(0, blocks(total), one_block, 0)

    def finish(i, _):
        rows = pl.ds(pl.multiple_of(i * TILE, LANES), TILE)
        joined = jnp.concatenate([dq[h, :, rows] for h in range(heads)], axis=0)
        made[0, rows, :] = (joined * HEAD**-0.5).T.astype(BF16)
        give_q(i).start()
        return 0

    def give_q(i):
        rows = pl.ds(pl.multiple_of(i * TILE, LANES), TILE)
        return pltpu.make_async_copy(made.at[0, rows], dproj.at[0, rows], out_s.at[blocks(total) + i])

    lax.fori_loop(0, total // TILE, finish, 0)
    for i in range(blocks(total)):
        give(i).wait()
    for i in range(total // TILE):
        give_q(i).wait()


def attention_back(ids, q, k, v, kt, out, grad, lse):
    heads, wide, _ = q.shape
    total = wide - PAD
    return pl.pallas_call(
        functools.partial(attention_back_kernel, heads, total),
        name="attention_back",
        cost_estimate=work(51),
        in_specs=[SMEM] * 2 + [VMEM] * 2 + [ANY] * 4 + [VMEM] * 3,
        out_specs=ANY,
        out_shape=jax.ShapeDtypeStruct((3, blocks(total) * BLOCK, heads * HEAD), BF16),
        scratch_shapes=[
            pltpu.VMEM(q.shape, BF16),
            pltpu.VMEM(k.shape, BF16),
            pltpu.VMEM(v.shape, BF16),
            pltpu.VMEM(kt.shape, BF16),
            pltpu.VMEM((3, blocks(total) * BLOCK, heads * HEAD), BF16),
            pltpu.VMEM((heads, wide, LANES), BF16),
            pltpu.VMEM((8, wide), F32),
            pltpu.VMEM((heads, HEAD, wide), F32),
            DMA((4,)),
            DMA((blocks(total) + total // TILE,)),
        ],
        compiler_params=limit(60),
    )(*ids, q, k, v, kt, out, grad, lse)


ROWS_MID = 288


def middle_kernel(
    attended, tok, cot, cot_came, b_out, gain, shift, b_up, b_down, *rest
):
    me = Place()
    groups = len(rest) - 25
    weights = rest[:groups]
    layer_out, grad_mid, grad_heads, cells = rest[groups : groups + 4]
    (
        att, grad_att, w, acc, vec, bup, sent, came, units,
        att_s, att_r, own_s, grad_s, grad_r, back_s, unit_s, push_s, push_r, sum_s, sum_r, cell_s,
    ) = rest[groups + 4 :]
    group = me.d // 2
    parts, piece, _ = weights[0].shape
    rows = tok.shape[0]
    tiles = rows // ROWS_MID
    width = att.shape[2]
    others = [lax.rem(me.q + k, 4) for k in range(1, 4)]
    greet([me.member(quarter) for quarter in others])

    def tile(t, quarter=0):
        return pl.ds(pl.multiple_of(quarter * rows + t * ROWS_MID, 16), ROWS_MID)

    def att_to(k, t):
        return remote(
            attended.at[tile(t, others[k])], att.at[me.q, tile(t)], att_s.at[k, t], att_r.at[k, t], me.member(others[k])
        )

    def att_from(k, t):
        source = others[2 - k]
        return remote(
            attended.at[tile(t)], att.at[source, tile(t)], att_s.at[k, t], att_r.at[k, t], me.member(source)
        )

    def att_own(t):
        return pltpu.make_async_copy(attended.at[tile(t, me.q)], att.at[me.q, tile(t)], own_s.at[t])

    def grad_to(k, t):
        return remote(
            grad_att.at[others[k], tile(t)], grad_heads.at[tile(t, me.q)], grad_s.at[k, t], grad_r.at[k, t], me.member(others[k])
        )

    def grad_from(k, t):
        source = others[2 - k]
        return remote(
            grad_att.at[source, tile(t)], grad_heads.at[tile(t, source)], grad_s.at[k, t], grad_r.at[k, t], me.member(source)
        )

    def grad_own(t):
        return pltpu.make_async_copy(grad_att.at[me.q, tile(t)], grad_heads.at[tile(t, me.q)], back_s.at[t])

    for t in range(tiles):
        for k in (1, 0, 2):
            att_to(k, t).start()
        att_own(t).start()

    def w_rows(j, core):
        source = 2 * lax.rem(group + groups - j, groups) + core
        return w.at[:, pl.ds(pl.multiple_of(source * piece, 16), piece)]

    def load(j):
        return pltpu.make_async_copy(weights[j], w_rows(j, me.c), unit_s.at[j])

    def push(j):
        return remote(weights[j], w_rows(j, me.c), push_s.at[j], push_r.at[j], me.sibling)

    def pushed(j):
        return remote(weights[j], w_rows(j, 1 - me.c), push_s.at[j], push_r.at[j], me.sibling)

    for j in range(groups):
        push(j).start()
        load(j).start()
    for ref in (acc, vec, bup):
        ref[...] = jnp.zeros_like(ref)
    for j in range(groups):
        load(j).wait()
        pushed(j).wait_recv()

    out_rows = slice(0, OUT_ROWS)
    down_rows = slice(OUT_ROWS, OUT_ROWS + UP_ROWS)
    up_rows = slice(OUT_ROWS + UP_ROWS, VEC_AT)

    def one_tile(t, _):
        here = tile(t)
        att_own(t).wait()
        for k in range(3):
            att_from(k, t).wait_recv()
        atts = [att[v, here, :] for v in range(parts)]
        middle = tok[here, :].astype(F32) + line(b_out)
        for v in range(parts):
            middle = middle + dot(atts[v], w[v, out_rows])
        unit, scale = normalise(middle)
        low = (unit * line(gain) + line(shift)).astype(BF16)
        cot_low = jnp.where(me.native, cot[here, :], cot_came[here, :])
        cot_full = cot_low.astype(F32)
        out = middle + line(b_down)
        grad_norm = jnp.zeros_like(middle)

        def products(v):
            return dot(low, w[v, up_rows], NT), dot(cot_low, w[v, down_rows], NT)

        upcoming = products(0)
        for v in range(parts):
            hidden, grad_active = upcoming
            if v + 1 < parts:
                upcoming = products(v + 1)
            hidden = hidden + b_up[v]
            below = 0.5 * (1.0 + lax.erf(hidden * 0.5**0.5))
            density = jnp.exp(-0.5 * hidden * hidden) * 0.3989422804014327
            active = (hidden * below).astype(BF16)
            grad_hidden = (grad_active * (below + hidden * density)).astype(BF16)
            out = out + dot(active, w[v, down_rows])
            grad_norm = grad_norm + dot(grad_hidden, w[v, up_rows])
            acc[v, down_rows] += dot(active, cot_low, TN)
            acc[v, up_rows] += dot(grad_hidden, low, TN)
            bup[v] += jnp.sum(grad_hidden.astype(F32), axis=0, keepdims=True)
        layer_out[here, :] = out.astype(BF16)
        scaled = grad_norm * line(gain)
        back = cot_full + scale * (
            scaled
            - jnp.mean(scaled, axis=-1, keepdims=True)
            - unit * jnp.mean(scaled * unit, axis=-1, keepdims=True)
        )
        grad_mid[here, :] = back
        back_low = back.astype(BF16)
        for v in range(parts):
            grad_att[v, here, :] = dot(back_low, w[v, out_rows], NT).astype(BF16)
        for k in (1, 0, 2):
            grad_to(k, t).start()
        grad_own(t).start()
        for v in range(parts):
            acc[v, out_rows] += dot(atts[v], back_low, TN)
        vec[0:1] += jnp.sum(grad_norm * unit, axis=0, keepdims=True)
        vec[1:2] += jnp.sum(grad_norm, axis=0, keepdims=True)
        vec[2:3] += jnp.sum(back, axis=0, keepdims=True)
        vec[3:4] += jnp.sum(cot_full, axis=0, keepdims=True)
        return 0

    lax.fori_loop(0, tiles, one_tile, 0)

    def sum_rows(i, core):
        return pl.ds(pl.multiple_of((2 * i + core) * piece, 16), piece)

    def give(i):
        return remote(sent.at[i], came.at[i], sum_s.at[i], sum_r.at[i], me.sibling)

    def keep(i):
        return pltpu.make_async_copy(units.at[i], cells.at[i], cell_s.at[i])

    for v in range(parts):
        acc[v, VEC_AT : VEC_AT + 8] = vec[...]
        acc[v, VEC_AT + 4 : VEC_AT + 5, :UP_ROWS] = bup[v]
    for i in range(groups):
        for v in range(parts):
            sent[i, v] = acc[v, sum_rows(i, 1 - me.c), :].astype(BF16)
        give(i).start()
    for i in range(groups):
        give(i).wait_recv()
        for v in range(parts):
            units[i, v] = (acc[v, sum_rows(i, me.c), :] + came[i, v].astype(F32)).astype(BF16)
        keep(i).start()
    for t in range(tiles):
        for k in range(3):
            grad_from(k, t).wait_recv()
            grad_to(k, t).wait_send()
            att_to(k, t).wait_send()
        grad_own(t).wait()
    for j in range(groups):
        push(j).wait_send()
        give(j).wait_send()
        keep(j).wait()


def middle_part(attended, tok, cot, cot_came, b_out, gain, shift, b_up, b_down, weights):
    rows = tok.shape[0]
    width = attended.shape[1]
    groups = len(weights)
    parts, piece, _ = weights[0].shape
    tiles = rows // ROWS_MID
    shape = jax.ShapeDtypeStruct
    halves = (groups, parts, piece, D)
    return pl.pallas_call(
        middle_kernel,
        name="middle_part",
        cost_estimate=work(50),
        in_specs=[ANY] + [VMEM] * 8 + [ANY] * groups,
        out_specs=[VMEM, VMEM, ANY, ANY],
        out_shape=[
            shape((rows, D), BF16),
            shape((rows, D), F32),
            shape((4 * rows, width), BF16),
            shape(halves, BF16),
        ],
        scratch_shapes=[
            pltpu.VMEM((parts, rows, width), BF16),
            pltpu.VMEM((parts, rows, width), BF16),
            pltpu.VMEM((parts, UNITS, D), BF16),
            pltpu.VMEM((parts, UNITS, D), F32),
            pltpu.VMEM((8, D), F32),
            pltpu.VMEM((parts, 1, UP_ROWS), F32),
            pltpu.VMEM(halves, BF16),
            pltpu.VMEM(halves, BF16),
            pltpu.VMEM(halves, BF16),
            DMA((3, tiles)),
            DMA((3, tiles)),
            DMA((tiles,)),
            DMA((3, tiles)),
            DMA((3, tiles)),
            DMA((tiles,)),
        ]
        + [DMA((groups,))] * 6,
        compiler_params=pltpu.CompilerParams(
            collective_id=2, has_side_effects=True, vmem_limit_bytes=48 << 20
        ),
    )(attended, tok, cot, cot_came, b_out, gain, shift, b_up, b_down, *weights)


CUTS = 3


def finish_kernel(
    dproj_in, normed_in, full_in, w, grad_mid, gain, cells, grad, vec_sum, d_w, sums,
    dproj, normed, full, part, theirs, sent, crossed, low, acc, w_part, w_in, w_z, vec, vz, vd, u_in, u_own,
    load_s, out_s, sib_s, sib_r, cross_s, cross_r, swap_s, swap_r, vz_s, vz_r, vd_s, vd_r,
    ws_s, ws_r, wz_s, wz_r, wg_s, wg_r, wf_s, wf_r, uz_s, uz_r, ug_s, ug_r, uf_s, uf_r,
):
    me = Place()
    foreign = jnp.logical_not(me.native)
    rows = grad_mid.shape[0]
    piece = rows // CUTS
    width = w.shape[1]
    ndp = vd.shape[0]
    groups, w_rows, _ = w_part.shape
    group = me.d // 2

    order = [2 * (1 - me.hf) + 1 - me.r, 2 * (1 - me.hf) + me.r, 2 * me.hf + 1 - me.r, 2 * me.hf + me.r]

    def span_of(k, p):
        return pl.ds(pl.multiple_of(order[k] * rows + p * piece, 16), piece)

    def loads(k, p):
        span = span_of(k, p)
        pairs = ((dproj_in.at[:, span], dproj.at[:, span]), (normed_in.at[span], normed.at[span]), (full_in.at[span], full.at[span]))
        return [pltpu.make_async_copy(src, dst, load_s.at[k, p, j]) for j, (src, dst) in enumerate(pairs)]

    for k in range(4):
        for p in range(CUTS):
            for copy in loads(k, p):
                copy.start()

    around = [(me.d, lax.rem(me.m + k, 4)) for k in range(1, 4)]
    along = [(lax.rem(me.d + k, ndp), me.m) for k in range(1, ndp)]
    greet([me.partner] + around + along)

    def to_sib(k, p):
        slot = k % 2
        return remote(part.at[k, p], theirs.at[slot, p], sib_s.at[slot, p], sib_r.at[slot, p], me.sibling)

    def to_cross(p):
        return remote(sent.at[p], crossed.at[p], cross_s.at[p], cross_r.at[p], me.cross)

    def to_partner(p):
        return remote(low.at[p], grad.at[p], swap_s.at[p], swap_r.at[p], me.partner)

    def keep(p):
        return pltpu.make_async_copy(low.at[p], grad.at[p], out_s.at[p])

    def unit_z(j):
        to = lax.rem(me.m + 1 + j, 4)
        return remote(cells.at[to], u_in.at[j], uz_s.at[j], uz_r.at[j], around[j])

    def unit_give(j):
        to = (2 * lax.rem(group + j, groups) + me.c, me.m)
        return remote(u_own, sums.at[me.d], ug_s.at[j], ug_r.at[j], to)

    def unit_give_in(j):
        source = 2 * lax.rem(group + groups - j, groups) + me.c
        return remote(u_own, sums.at[source], ug_s.at[j], ug_r.at[j], (source, me.m))

    def unit_forward(j):
        source = 2 * lax.rem(group + groups - j, groups) + me.c
        src = u_own if j == 0 else sums.at[source]
        return remote(src, sums.at[source], uf_s.at[j], uf_r.at[j], me.sibling)

    def unit_forward_in(j):
        source = 2 * lax.rem(group + groups - j, groups) + 1 - me.c
        return remote(u_own, sums.at[source], uf_s.at[j], uf_r.at[j], me.sibling)

    vec[...] = jnp.zeros_like(vec)

    def compute(k):
        def one(p, _):
            span = span_of(k, p)
            for copy in loads(k, p):
                copy.wait()
            total = jnp.zeros((piece, D), F32)
            for c in range(3):
                total = total + dot(dproj[c, span, :], w[c])
            part[k, p] = total.astype(BF16)

            @pl.when(me.native if k < 2 else foreign)
            def _():
                to_sib(k, p).start()

            return 0

        lax.fori_loop(0, CUTS, one, 0)

    def pass_across(k):
        for p in range(CUTS):
            to_sib(k, p).wait_recv()
            sent[p] = (part[k, p].astype(F32) + theirs[0, p].astype(F32)).astype(BF16)
            to_cross(p).start()

    def conclude(k, p):
        to_sib(k, p).wait_recv()
        to_cross(p).wait_recv()
        total = part[k, p].astype(F32) + theirs[1, p].astype(F32) + crossed[p].astype(F32)
        span = pl.ds(pl.multiple_of(me.q * rows + p * piece, 16), piece)
        unit, scale = normalise(full[span, :].astype(F32))
        vec[0:1] += jnp.sum(total * unit, axis=0, keepdims=True)
        vec[1:2] += jnp.sum(total, axis=0, keepdims=True)
        scaled = total * line(gain)
        result = grad_mid[p * piece : (p + 1) * piece, :] + scale * (
            scaled
            - jnp.mean(scaled, axis=-1, keepdims=True)
            - unit * jnp.mean(scaled * unit, axis=-1, keepdims=True)
        )
        low[p] = result.astype(BF16)

    def conclude_foreign(p):
        conclude(1, p)
        to_partner(p).start()

    compute(0)

    @pl.when(foreign)
    def _():
        pass_across(0)

    compute(1)
    compute(2)

    @pl.when(me.native)
    def _():
        pass_across(2)

    compute(3)
    for j in range(3):
        unit_z(j).start()

    for c in range(3):
        acc[c * width : (c + 1) * width, :] = dot(dproj[c], normed[...], TN)

    for i in range(groups):
        w_part[i] = acc[i * w_rows : (i + 1) * w_rows, :].astype(BF16)

    def other_group(k):
        return lax.rem(group + k, groups)

    def w_send(k):
        to = other_group(k)
        return remote(w_part.at[to], w_in.at[k], ws_s.at[k], ws_r.at[k], (2 * to + me.c, me.m))

    for k in range(1, groups):
        w_send(k).start()

    @pl.when(foreign)
    def _():
        for p in range(2 * CUTS // 3):
            conclude_foreign(p)

    w_sum = w_part[group].astype(F32)
    for k in range(1, groups):
        w_send(k).wait_recv()
        w_sum = w_sum + w_in[k].astype(F32)

    to_z = remote(w_z.at[0], w_z.at[1], wz_s, wz_r, (me.d, lax.rem(me.m + 2, 4)))

    def w_give(k):
        return remote(w_z.at[0], d_w.at[group], wg_s.at[k], wg_r.at[k], (2 * other_group(k) + me.c, me.m))

    def w_give_in(k):
        source = lax.rem(group + groups - k, groups)
        return remote(w_z.at[0], d_w.at[source], wg_s.at[k], wg_r.at[k], (2 * source + me.c, me.m))

    def w_forward(k):
        source = lax.rem(group + groups - k, groups)
        src = w_z.at[0] if k == 0 else d_w.at[source]
        return remote(src, d_w.at[source], wf_s.at[k], wf_r.at[k], me.sibling)

    w_keep = pltpu.make_async_copy(w_z.at[0], d_w.at[group], out_s.at[CUTS])
    unit_keep = pltpu.make_async_copy(u_own, sums.at[me.d], out_s.at[CUTS + 1])

    @pl.when(foreign)
    def _():
        w_z[0] = w_sum.astype(BF16)
        to_z.start()
        for p in range(2 * CUTS // 3, CUTS):
            conclude_foreign(p)

    @pl.when(me.native)
    def _():
        to_z.wait_recv()
        w_z[0] = (w_sum + w_z[1].astype(F32)).astype(BF16)
        w_keep.start()
        for k in range(1, groups):
            w_give(k).start()
        w_forward(0).start()
        for p in range(CUTS):
            conclude(3, p)
            keep(p).start()

    vz[me.m] = vec[...]

    def around_copy(k):
        return remote(vz.at[me.m], vz.at[me.m], vz_s.at[k], vz_r.at[k], around[k])

    for k in range(3):
        around_copy(k).start()

    unit_sum = cells[me.m].astype(F32)
    for j in range(3):
        unit_z(j).wait_recv()
        unit_sum = unit_sum + u_in[j].astype(F32)
    u_own[...] = unit_sum.astype(BF16)
    unit_keep.start()
    for j in range(1, groups):
        unit_give(j).start()
    unit_forward(0).start()

    @pl.when(me.native)
    def _():
        for k in range(1, groups):
            w_give_in(k).wait_recv()
            w_forward(k).start()

    for k in range(3):
        source = lax.rem(me.m + 3 - k, 4)
        remote(vz.at[source], vz.at[source], vz_s.at[k], vz_r.at[k], around[k]).wait_recv()
    vd[me.d] = vz[0] + vz[1] + vz[2] + vz[3]

    def along_copy(k):
        return remote(vd.at[me.d], vd.at[me.d], vd_s.at[k], vd_r.at[k], along[k])

    for k in range(ndp - 1):
        along_copy(k).start()

    for j in range(1, groups):
        unit_give_in(j).wait_recv()
        unit_forward(j).start()
    for k in range(ndp - 1):
        source = lax.rem(me.d + ndp - 1 - k, ndp)
        remote(vd.at[source], vd.at[source], vd_s.at[k], vd_r.at[k], along[k]).wait_recv()
    total = vd[0]
    for i in range(1, ndp):
        total = total + vd[i]
    vec_sum[...] = total
    for j in range(groups):
        unit_forward_in(j).wait_recv()

    @pl.when(foreign)
    def _():
        for k in range(groups):
            source = lax.rem(group + groups - k, groups)
            remote(w_z.at[0], d_w.at[source], wf_s.at[k], wf_r.at[k], me.sibling).wait_recv()
        for p in range(CUTS):
            to_partner(p).wait_recv()
            to_partner(p).wait_send()
            to_sib(2, p).wait_send()
            to_sib(3, p).wait_send()
        to_z.wait_send()

    @pl.when(me.native)
    def _():
        for p in range(CUTS):
            keep(p).wait()
            to_sib(0, p).wait_send()
            to_sib(1, p).wait_send()
        for k in range(1, groups):
            w_give(k).wait_send()
        for k in range(groups):
            w_forward(k).wait_send()
        w_keep.wait()

    for p in range(CUTS):
        to_cross(p).wait_send()
    for k in range(1, groups):
        w_send(k).wait_send()
    for k in range(3):
        around_copy(k).wait_send()
        unit_z(k).wait_send()
    for k in range(ndp - 1):
        along_copy(k).wait_send()
    for j in range(groups):
        unit_forward(j).wait_send()
    for j in range(1, groups):
        unit_give(j).wait_send()
    unit_keep.wait()


def finish(dproj, normed, full, w, grad_mid, gain, cells, ndp):
    rows = grad_mid.shape[0]
    total = full.shape[0]
    piece = rows // CUTS
    pieces = (CUTS, piece, D)
    groups = ndp // 2
    columns = 3 * w.shape[1]
    cut = (groups, columns // groups, D)
    unit = cells.shape[1:]
    shape = jax.ShapeDtypeStruct
    return pl.pallas_call(
        finish_kernel,
        name="finish",
        cost_estimate=work(60),
        in_specs=[ANY] * 3 + [VMEM] * 4,
        out_specs=[ANY, VMEM, ANY, ANY],
        out_shape=[shape(pieces, BF16), shape((8, D), F32), shape(cut, BF16), shape((ndp,) + unit, BF16)],
        scratch_shapes=[
            pltpu.VMEM((3, total, w.shape[1]), BF16),
            pltpu.VMEM((total, D), BF16),
            pltpu.VMEM((total, D), BF16),
            pltpu.VMEM((4,) + pieces, BF16),
            pltpu.VMEM((2,) + pieces, BF16),
            pltpu.VMEM(pieces, BF16),
            pltpu.VMEM(pieces, BF16),
            pltpu.VMEM(pieces, BF16),
            pltpu.VMEM((columns, D), F32),
            pltpu.VMEM(cut, BF16),
            pltpu.VMEM(cut, BF16),
            pltpu.VMEM((2,) + cut[1:], BF16),
            pltpu.VMEM((8, D), F32),
            pltpu.VMEM((4, 8, D), F32),
            pltpu.VMEM((ndp, 8, D), F32),
            pltpu.VMEM((3,) + unit, BF16),
            pltpu.VMEM(unit, BF16),
            DMA((4, CUTS, 3)),
            DMA((CUTS + 2,)),
        ]
        + [DMA((2, CUTS))] * 2
        + [DMA((CUTS,))] * 4
        + [DMA((3,))] * 2
        + [DMA((ndp - 1,))] * 2
        + [DMA((groups,))] * 2
        + [DMA] * 2
        + [DMA((groups,))] * 4
        + [DMA((3,))] * 2
        + [DMA((groups,))] * 4,
        compiler_params=pltpu.CompilerParams(
            collective_id=4, has_side_effects=True, vmem_limit_bytes=60 << 20
        ),
    )(dproj, normed, full, w, grad_mid, gain, cells)


def outputs_kernel(
    layer, layer_came, grads, w_sums, unit_sums, vec_one,
    layer_out, tokens_grad, d_qkv, d_out, d_up, d_down, d_gain_two, d_shift_two, d_b_out, d_b_down, d_b_up, d_gain_one, d_shift_one,
    layer_s, came_s, grads_s, w_s, unit_s, grads_f, w_f, unit_f, up_f, in_s, out_s,
):
    me = Place()
    arriving = [
        pltpu.make_async_copy(src, dst, in_s.at[i])
        for i, (src, dst) in enumerate(
            ((unit_sums, unit_s), (w_sums, w_s), (grads, grads_s), (layer, layer_s), (layer_came, came_s))
        )
    ]
    for copy in arriving:
        copy.start()
    leaving = []

    def leave(src, dst):
        copy = pltpu.make_async_copy(src, dst, out_s.at[len(leaving)])
        copy.start()
        leaving.append(copy)

    def flatten(pieces, flat):
        count, height, _ = pieces.shape
        for i in range(count):
            flat[i * height : (i + 1) * height, :] = pieces[i].astype(F32)

    arriving[0].wait()
    flatten(unit_s, unit_f)
    leave(unit_f.at[:OUT_ROWS], d_out)
    leave(unit_f.at[OUT_ROWS : OUT_ROWS + UP_ROWS], d_down)
    up_f[...] = unit_f[OUT_ROWS + UP_ROWS : VEC_AT, :].T
    leave(up_f, d_up)
    arriving[1].wait()
    flatten(w_s, w_f)
    leave(w_f, d_qkv)
    arriving[2].wait()
    flatten(grads_s, grads_f)
    leave(grads_f, tokens_grad)
    for i in (3, 4):
        arriving[i].wait()
    layer_s[...] = jnp.where(me.native, layer_s[...], came_s[...])
    leave(layer_s, layer_out)
    for i, ref in enumerate((d_gain_two, d_shift_two, d_b_out, d_b_down)):
        ref[...] = unit_f[VEC_AT + i, :]
    d_b_up[...] = unit_f[VEC_AT + 4, :UP_ROWS]
    d_gain_one[...] = vec_one[0, :]
    d_shift_one[...] = vec_one[1, :]
    for copy in leaving:
        copy.wait()


def outputs(layer, layer_came, grads, w_sums, unit_sums, vec_one):
    rows = layer.shape[0]
    columns = w_sums.shape[0] * w_sums.shape[1]
    shape = lambda *s: jax.ShapeDtypeStruct(s, F32)
    return pl.pallas_call(
        outputs_kernel,
        name="outputs",
        in_specs=[ANY] * 5 + [VMEM],
        out_specs=[ANY] * 6 + [VMEM] * 7,
        out_shape=[
            jax.ShapeDtypeStruct((rows, D), BF16),
            shape(rows, D),
            shape(columns, D),
            shape(OUT_ROWS, D),
            shape(D, UP_ROWS),
            shape(UP_ROWS, D),
            shape(D),
            shape(D),
            shape(D),
            shape(D),
            shape(UP_ROWS),
            shape(D),
            shape(D),
        ],
        scratch_shapes=[
            pltpu.VMEM(layer.shape, BF16),
            pltpu.VMEM(layer.shape, BF16),
            pltpu.VMEM(grads.shape, BF16),
            pltpu.VMEM(w_sums.shape, BF16),
            pltpu.VMEM(unit_sums.shape, BF16),
            pltpu.VMEM((rows, D), F32),
            pltpu.VMEM((columns, D), F32),
            pltpu.VMEM((UNITS, D), F32),
            pltpu.VMEM((D, UP_ROWS), F32),
            DMA((5,)),
            DMA((6,)),
        ],
        compiler_params=limit(60),
    )(layer, layer_came, grads, w_sums, unit_sums, vec_one)


def swap_pairs(ndp):
    return [
        (d * 4 + m, (d ^ 1) * 4 + (m + 2) % 4) for d in range(ndp) for m in range(4) if d % 2 != m // 2
    ]


def weight_piece(w_out, w_up, w_down, ndp):
    block = jnp.concatenate([w_out, w_down, w_up.T, jnp.zeros((UNITS - w_out.shape[0] - 2 * w_down.shape[0], D), BF16)])
    piece = UNITS // ndp
    return lax.dynamic_slice_in_dim(block, lax.axis_index("dp") * piece, piece, 0)


def from_other_pairs(block, ndp):
    groups = ndp // 2
    blocks_of = [block]
    for j in range(1, groups):
        pairs = [(d, 2 * ((d // 2 + j) % groups) + d % 2) for d in range(ndp)]
        blocks_of.append(lax.ppermute(block, "dp", pairs))
    return blocks_of


def sum_over_pairs(cells, ndp):
    cores = [[d for d in range(ndp) if d % 2 == core] for core in range(2)]
    return lax.psum_scatter(cells.reshape(-1, D), "dp", scatter_dimension=0, tiled=True, axis_index_groups=cores)


def shards(
    tokens,
    scene_ids,
    gain_one,
    shift_one,
    w_qkv,
    w_out,
    b_out,
    gain_two,
    shift_two,
    w_up,
    b_up,
    w_down,
    b_down,
    cotangent,
    ndp,
):
    both = ("dp", "mp")
    swap = swap_pairs(ndp)
    w_qkv = jnp.swapaxes(w_qkv, 1, 2)
    full, own_tok, w_mine, numbers, id_row, id_column, before, b_ups, normed, q, k, v, kt, vt, weights = start(
        tokens, w_qkv, scene_ids.reshape(-1, LANES), b_up, gain_one, shift_one, weight_piece(w_out, w_up, w_down, ndp), ndp
    )
    w_mine = w_mine.reshape(w_qkv.shape)
    ids = numbers, before, id_column, id_row
    weights = from_other_pairs(weights, ndp)
    sent_cot, q = lax.optimization_barrier((cotangent, q))
    cot_came = lax.ppermute(sent_cot, both, swap)
    attended, lse = attention(ids, q, k, vt)
    layer, grad_mid, grad_heads, cells = middle_part(
        attended, own_tok, cotangent, cot_came, b_out, gain_two, shift_two, b_ups, b_down, weights
    )
    sent_out, grad_heads = lax.optimization_barrier((layer, grad_heads))
    layer_came = lax.ppermute(sent_out, both, swap)
    cells = sum_over_pairs(cells, ndp)
    dproj = attention_back(ids, q, k, v, kt, attended, grad_heads, lse)
    cells, dproj = lax.optimization_barrier((cells, dproj))
    grads, vec_one, w_sums, unit_sums = finish(
        dproj, normed, full, w_mine, grad_mid, gain_one, cells.reshape(4, -1, D), ndp
    )
    (
        layer_out, tokens_grad, d_qkv, d_out, d_up, d_down, d_gain_two, d_shift_two, d_b_out, d_b_down, d_b_up, d_gain_one, d_shift_one,
    ) = outputs(layer, layer_came, grads, w_sums, unit_sums, vec_one)
    return (
        layer_out,
        tokens_grad,
        d_gain_one,
        d_shift_one,
        jnp.swapaxes(d_qkv.reshape(w_qkv.shape), 1, 2),
        d_out,
        d_b_out,
        d_gain_two,
        d_shift_two,
        d_up,
        d_b_up,
        d_down,
        d_b_down,
    )


def solution(mesh):
    ndp = mesh.shape["dp"]
    return jax.shard_map(
        functools.partial(shards, ndp=ndp),
        mesh=mesh,
        in_specs=(
            P(("dp", "mp"), None),
            P("dp"),
            P(),
            P(),
            P(None, None, "mp"),
            P("mp", None),
            P(),
            P(),
            P(),
            P(None, "mp"),
            P("mp"),
            P("mp", None),
            P(),
            P(("dp", "mp"), None),
        ),
        out_specs=(
            P(("dp", "mp"), None),
            P(("dp", "mp"), None),
            P(),
            P(),
            P(None, None, "mp"),
            P("mp", None),
            P(),
            P(),
            P(),
            P(None, "mp"),
            P("mp"),
            P("mp", None),
            P(),
        ),
        check_vma=False,
    )
```

```python
import functools

import jax
import jax.numpy as jnp
from jax import lax
from jax.experimental import pallas as pl
from jax.experimental.pallas import tpu as pltpu
from jax.sharding import PartitionSpec as P

HEAD = 64
D = 768
FF = 1536
LANES = 128
PAD = 512
OUT_ROWS = D // 4
UP_ROWS = FF // 4
VEC_AT = OUT_ROWS + 2 * UP_ROWS
UNITS = 1024
EPS = 1e-05
MASKED = -1e30
MESH = pl.DeviceIdType.MESH
F32 = jnp.float32
BF16 = jnp.bfloat16
VMEM = pl.BlockSpec(memory_space=pltpu.VMEM)
SMEM = pl.BlockSpec(memory_space=pltpu.SMEM)
ANY = pl.BlockSpec(memory_space=pl.ANY)
DMA = pltpu.SemaphoreType.DMA

NN = (((1,), (0,)), ((), ()))
NT = (((1,), (1,)), ((), ()))
TN = (((0,), (0,)), ((), ()))


def dot(a, b, dims=NN):
    return lax.dot_general(a, b, dims, preferred_element_type=F32)


def work(us):
    return pl.CostEstimate(flops=us * 10**9, bytes_accessed=us * 3 * 10**6, transcendentals=0)


def limit(mib):
    return pltpu.CompilerParams(vmem_limit_bytes=mib << 20)


def line(ref):
    return ref[...].reshape(1, -1)


class Place:
    def __init__(self):
        self.d = lax.axis_index("dp")
        self.m = lax.axis_index("mp")
        self.c = lax.rem(self.d, 2)
        self.r = lax.rem(self.m, 2)
        self.hf = self.m // 2
        self.q = 2 * self.c + self.r
        self.native = self.c == self.hf
        self.sibling = (self.d + 1 - 2 * self.c, self.m)
        self.cross = (self.d, self.m + 1 - 2 * self.r)
        self.partner = (self.d + 1 - 2 * self.c, lax.rem(self.m + 2, 4))

    def member(self, quarter):
        return (self.d - self.c + quarter // 2, 2 * self.hf + quarter % 2)


def greet(others):
    barrier = pltpu.get_barrier_semaphore()
    for other in others:
        pl.semaphore_signal(barrier, inc=1, device_id=other, device_id_type=MESH)
    pl.semaphore_wait(barrier, len(others))


def remote(src, dst, send, recv, device):
    return pltpu.make_async_remote_copy(
        src_ref=src, dst_ref=dst, send_sem=send, recv_sem=recv, device_id=device, device_id_type=MESH
    )


STAGES = 3
PIECES = 6
TILE = 384
SCENES = 4


def normalise(x):
    centred = x - jnp.mean(x, axis=-1, keepdims=True)
    scale = lax.rsqrt(jnp.mean(centred * centred, axis=-1, keepdims=True) + EPS)
    return centred * scale, scale


def widen(x, ones, rows):
    lane = lax.broadcasted_iota(jnp.int32, (rows, LANES - HEAD), 1)
    return jnp.concatenate([x, jnp.where(lane < ones, 1.0, 0.0).astype(x.dtype)], axis=1)


def describe_scenes(ids, row, column, before):
    lines = ids.shape[0]
    for j in range(lines):
        place = j * LANES + lax.broadcasted_iota(jnp.int32, (1, LANES), 1)
        number = ids[j : j + 1, :]
        number = jnp.where(number >= 0, number, -1 - place)
        span = slice(j * LANES, (j + 1) * LANES)
        row[:, span] = number
        column[span, :] = jnp.broadcast_to(number.astype(F32), (LANES, LANES)).T[:, :1].astype(jnp.int32)
    rest = row.shape[1] - lines * LANES
    row[:, lines * LANES :] = jnp.full((1, rest), -(1 << 21), jnp.int32)
    column[lines * LANES :, :] = jnp.full((rest, 1), -(1 << 20), jnp.int32)
    lane = lax.broadcasted_iota(jnp.int32, (1, LANES), 1)
    counts = jnp.zeros((1, LANES), F32)
    for number in range(1, SCENES + 1):
        mine = jnp.where((ids[...] >= 0) & (ids[...] < number), 1.0, 0.0)
        total = jnp.sum(jnp.sum(mine, axis=0, keepdims=True), axis=1, keepdims=True)
        counts = jnp.where(lane == number, total, counts)
    before[...] = counts.astype(jnp.int32)


def start_kernel(
    heads, tok, wq, ids, b_up, gain, shift, mine,
    full, own, w_out, ids_own, id_row, id_column, before, b_ups, normed, q, k, v, kt, vt, units,
    buf, w, low_s, q_s, k_s, v_s, kt_s, vt_s,
    swap_s, swap_r, cross_s, cross_r, sib_s, sib_r, fwd_s, fwd_r, w_s, w_r, ids_s, ids_r, b_s, b_r, out_s, late_s,
    uz_s, uz_r,
):
    me = Place()
    foreign = jnp.logical_not(me.native)
    rows = tok.shape[0]
    piece = rows // PIECES
    total = buf.shape[0]
    tiles = total // TILE
    groups = w.shape[1]
    group = me.d // 2
    around = [(me.d, lax.rem(me.m + j, 4)) for j in range(1, 4)]
    lines = [(2 * lax.rem(group + j, groups) + me.c, me.m) for j in range(1, groups)]
    greet([me.sibling, me.partner] + around + lines)

    def rows_of(quarter, n):
        p = jnp.where(me.hf == 0, n, PIECES - 1 - n)
        return pl.ds(pl.multiple_of(quarter * rows + p * piece, 16), piece)

    def part(quarter, n):
        return buf.at[rows_of(quarter, n)]

    sib_q = 2 * (1 - me.c) + me.r
    cross_q = 2 * me.c + 1 - me.r
    sib_cross_q = 2 * (1 - me.c) + 1 - me.r

    def swap(n):
        p = jnp.where(me.hf == 1, n, PIECES - 1 - n)
        src = tok.at[pl.ds(pl.multiple_of(p * piece, 16), piece)]
        dst = buf.at[pl.ds(pl.multiple_of(sib_q * rows + p * piece, 16), piece)]
        return remote(src, dst, swap_s.at[n], swap_r.at[n], me.partner)

    def swap_in(n):
        return remote(part(me.q, n), part(me.q, n), swap_s.at[n], swap_r.at[n], me.partner)

    def cross(quarter, n):
        return remote(part(quarter, n), part(quarter, n), cross_s.at[n], cross_r.at[n], me.cross)

    def sib(quarter, n):
        return remote(part(quarter, n), part(quarter, n), sib_s.at[n], sib_r.at[n], me.sibling)

    def forward(quarter, n):
        return remote(part(quarter, n), part(quarter, n), fwd_s.at[n], fwd_r.at[n], me.sibling)

    weight = remote(wq.at[:, group], w.at[:, group], w_s.at[0], w_r.at[0], me.partner)

    def weight_share(j):
        return remote(w.at[:, group], w.at[:, group], w_s.at[j], w_r.at[j], lines[j - 1])

    def weight_in(j):
        source = lax.rem(group + groups - j, groups)
        return remote(w.at[:, source], w.at[:, source], w_s.at[j], w_r.at[j], lines[j - 1])

    unit_own = pltpu.make_async_copy(mine, units.at[me.m], late_s.at[7])

    def unit_z(j, source):
        return remote(mine, units.at[source], uz_s.at[j], uz_r.at[j], around[j])

    def give_b_up(j):
        return remote(b_ups.at[me.m], b_ups.at[me.m], b_s.at[j], b_r.at[j], around[j])

    scenes = remote(ids, ids_own, ids_s, ids_r, me.sibling)
    unit_own.start()
    b_ups[me.m] = line(b_up)
    for j in range(3):
        give_b_up(j).start()

    @pl.when(me.native)
    def _():
        scenes.start()
        buf[pl.ds(pl.multiple_of(me.q * rows, 16), rows), :] = tok[...]
        for n in range(PIECES):
            cross(me.q, n).start()
            sib(me.q, n).start()
        w[...] = wq[...]
        ids_own[...] = ids[...]

    @pl.when(foreign)
    def _():
        weight.start()
        for n in range(PIECES):
            swap(n).start()

    def share(n):
        swap_in(n).wait_recv()
        cross(me.q, n).start()
        sib(me.q, n).start()

    def pass_on(n):
        cross(cross_q, n).wait_recv()
        forward(cross_q, n).start()

    def from_sibling(n):
        sib(sib_q, n).wait_recv()
        forward(sib_cross_q, n).wait_recv()

    def outputs(t):
        span = pl.ds(pl.multiple_of(t * TILE, LANES), TILE)
        pairs = [
            (low_s.at[span], normed.at[span]),
            (buf.at[span], full.at[span]),
            (q_s.at[:, span], q.at[:, span]),
            (k_s.at[:, span], k.at[:, span]),
            (v_s.at[:, span], v.at[:, span]),
            (kt_s.at[:, :, span], kt.at[:, :, span]),
            (vt_s.at[:, :, span], vt.at[:, :, span]),
        ]
        return [pltpu.make_async_copy(src, dst, out_s.at[t, j]) for j, (src, dst) in enumerate(pairs)]

    ones = jnp.where(lax.broadcasted_iota(jnp.int32, (16, TILE), 0) < 1, 1.0, 0.0).astype(BF16)

    def compute(first, stride, count):
        def one(n, _):
            at = first + stride * n
            t = jnp.where(me.hf == 0, at, tiles - 1 - at)
            span = pl.ds(pl.multiple_of(t * TILE, LANES), TILE)
            unit, _ = normalise(buf[span, :].astype(F32))
            low = (unit * line(gain) + line(shift)).astype(BF16)
            low_s[span, :] = low
            qs = (dot(low, w[0].reshape(-1, D), NT).astype(BF16).astype(F32) * HEAD**-0.5).astype(BF16)
            ks = dot(low, w[1].reshape(-1, D), NT)
            vs = dot(low, w[2].reshape(-1, D), NT)
            kts = ks.T.astype(BF16)
            vts = vs.T.astype(BF16)
            ks = ks.astype(BF16)
            vs = vs.astype(BF16)
            for h in range(heads):
                cols = slice(h * HEAD, (h + 1) * HEAD)
                q_s[h, span, :] = widen(qs[:, cols], 0, TILE)
                k_s[h, span, :] = widen(ks[:, cols], 3, TILE)
                v_s[h, span, :] = widen(vs[:, cols], 3, TILE)
                kt_s[h, :, span] = kts[cols]
                vt_s[h, :HEAD, span] = vts[cols]
                vt_s[h, HEAD:, span] = ones
            for copy in outputs(t):
                copy.start()
            return 0

        lax.fori_loop(0, count, one, 0)

    pad = pl.ds(total, PAD)
    zeros = jnp.zeros((heads, PAD, LANES), BF16)
    for ref in (q_s, k_s, v_s):
        ref[:, pad, :] = zeros
    for ref in (kt_s, vt_s):
        ref[:, :, pad] = jnp.zeros((heads, ref.shape[1], PAD), BF16)
    padding = [
        pltpu.make_async_copy(src, dst, late_s.at[j])
        for j, (src, dst) in enumerate(
            [(a.at[:, pad], b.at[:, pad]) for a, b in ((q_s, q), (k_s, k), (v_s, v))]
            + [(a.at[:, :, pad], b.at[:, :, pad]) for a, b in ((kt_s, kt), (vt_s, vt))]
        )
    ]
    for copy in padding:
        copy.start()

    def stage(n):
        return range(n * PIECES // STAGES, (n + 1) * PIECES // STAGES)

    @pl.when(me.native)
    def _():
        for n in range(PIECES):
            pass_on(n)

    @pl.when(foreign)
    def _():
        weight.wait_recv()
        for j in range(1, groups):
            weight_share(j).start()
        for n in range(PIECES):
            share(n)
        for j in range(1, groups):
            weight_in(j).wait_recv()
        for n in range(PIECES):
            from_sibling(n)

    for j in range(3):
        unit_z(j, me.m).start()

    @pl.when(foreign)
    def _():
        scenes.wait_recv()

    describe_scenes(ids_own, id_row, id_column, before)
    compute(0, 1, 2)

    @pl.when(foreign)
    def _():
        for n in stage(0):
            pass_on(n)

    compute(2, 1, 2)

    @pl.when(foreign)
    def _():
        for n in stage(1):
            pass_on(n)

    @pl.when(me.native)
    def _():
        for n in stage(0):
            from_sibling(n)

    compute(4, 1, 1)

    @pl.when(me.native)
    def _():
        for n in stage(1):
            from_sibling(n)

    compute(5, 2, 2)

    @pl.when(foreign)
    def _():
        for n in stage(2):
            pass_on(n)

    @pl.when(me.native)
    def _():
        for n in stage(2):
            from_sibling(n)

    own_copy = pltpu.make_async_copy(buf.at[pl.ds(pl.multiple_of(me.q * rows, 16), rows)], own, late_s.at[5])
    w_copy = pltpu.make_async_copy(w, w_out, late_s.at[6])
    own_copy.start()
    w_copy.start()
    compute(6, 2, 2)
    unit_own.wait()
    for j in range(3):
        unit_z(j, lax.rem(me.m + 3 - j, 4)).wait_recv()
        unit_z(j, me.m).wait_send()

    for j in range(3):
        source = lax.rem(me.m + 3 - j, 4)
        remote(b_ups.at[source], b_ups.at[source], b_s.at[j], b_r.at[j], around[j]).wait_recv()
        give_b_up(j).wait_send()

    @pl.when(me.native)
    def _():
        scenes.wait_send()

    @pl.when(foreign)
    def _():
        weight.wait_send()
        for j in range(1, groups):
            weight_share(j).wait_send()
        for n in range(PIECES):
            swap(n).wait_send()

    for n in range(PIECES):
        cross(me.q, n).wait_send()
        sib(me.q, n).wait_send()
        forward(cross_q, n).wait_send()
    for copy in padding + [own_copy, w_copy]:
        copy.wait()

    def finish_tile(t, _):
        for copy in outputs(t):
            copy.wait()
        return 0

    lax.fori_loop(0, tiles, finish_tile, 0)


def start(tokens, w_qkv, scene_ids, b_up, gain, shift, mine, ndp):
    rows = tokens.shape[0]
    total = 4 * rows
    heads = w_qkv.shape[1] // HEAD
    groups = ndp // 2
    w_qkv = w_qkv.reshape(3, groups, -1, D)
    units = (4,) + mine.shape
    wide = total + PAD
    shape = jax.ShapeDtypeStruct
    rowed = (heads, wide, LANES)
    k_cols, v_cols = (heads, HEAD, wide), (heads, HEAD + 16, wide)
    three = DMA((PIECES,))
    return pl.pallas_call(
        functools.partial(start_kernel, heads),
        name="start",
        cost_estimate=work(50),
        in_specs=[VMEM] * 6 + [ANY],
        out_specs=[ANY] * 3 + [VMEM] * 5 + [ANY] * 7,
        out_shape=[
            shape((total, D), BF16),
            shape((rows, D), BF16),
            shape(w_qkv.shape, BF16),
            shape(scene_ids.shape, jnp.int32),
            shape((1, wide), jnp.int32),
            shape((wide, 1), jnp.int32),
            shape((1, LANES), jnp.int32),
            shape((4, 1) + b_up.shape, F32),
            shape((total, D), BF16),
            shape(rowed, BF16),
            shape(rowed, BF16),
            shape(rowed, BF16),
            shape(k_cols, BF16),
            shape(v_cols, BF16),
            shape(units, BF16),
        ],
        scratch_shapes=[
            pltpu.VMEM((total, D), BF16),
            pltpu.VMEM(w_qkv.shape, BF16),
            pltpu.VMEM((total, D), BF16),
            pltpu.VMEM(rowed, BF16),
            pltpu.VMEM(rowed, BF16),
            pltpu.VMEM(rowed, BF16),
            pltpu.VMEM(k_cols, BF16),
            pltpu.VMEM(v_cols, BF16),
        ]
        + [three] * 8
        + [DMA((groups,))] * 2
        + [DMA] * 2
        + [DMA((3,))] * 2
        + [DMA((total // TILE, 7)), DMA((8,))]
        + [DMA((3,))] * 2,
        compiler_params=pltpu.CompilerParams(
            collective_id=1, has_side_effects=True, vmem_limit_bytes=60 << 20
        ),
    )(tokens, w_qkv, scene_ids, b_up, gain, shift, mine)


BLOCK = 256
STEP = 512


def blocks(total):
    return -(-total // BLOCK)


def block_range(i, numbers, before):
    lines = numbers.shape[0]
    per = BLOCK // LANES
    top, bottom = numbers[i * per, 0], numbers[jnp.minimum(i * per + per, lines) - 1, LANES - 1]
    bottom = jnp.where(i * per + per > lines, -1, bottom)
    low = jnp.where(top >= 0, before[0, jnp.maximum(top, 0)], i * BLOCK)
    high = jnp.where(bottom >= 0, before[0, jnp.maximum(bottom, 0) + 1], i * BLOCK + BLOCK)
    return low // LANES, (high + LANES - 1) // LANES


def list_steps(count, numbers, before, total, block_at, step_at, marks):
    stride = STEP // LANES

    def one_block(i, n):
        first, last = block_range(i, numbers, before)
        steps = (last - first + stride - 1) // stride

        def put(j, n):
            block_at[n] = i * (BLOCK // LANES)
            step_at[n] = first + j * stride
            marks[n] = jnp.where(j == 0, 1, 0) + jnp.where(j == steps - 1, 2, 0)
            return n + 1

        return lax.fori_loop(0, steps, put, n)

    n = lax.fori_loop(0, count, one_block, 0)
    for idle in range(2):
        block_at[n + idle] = 0
        step_at[n + idle] = total // LANES
        marks[n + idle] = 0
    return n


def step_lists(total):
    return [pltpu.SMEM((blocks(total) * (-(-total // STEP) + 1) + 2,), jnp.int32)] * 3


def attention_kernel(
    heads, total, numbers, before, idc, idr, q, k, vt, out, lse, block_at, step_at, marks, even, odd
):
    count = list_steps(blocks(total), numbers, before, total, block_at, step_at, marks)

    def place(i):
        rows = pl.ds(pl.multiple_of(block_at[i] * LANES, LANES), BLOCK)
        return rows, pl.ds(pl.multiple_of(step_at[i] * LANES, LANES), STEP)

    def score(i, buf, h):
        rows, cols = place(i)
        s = jnp.where(idc[cols, :] == idr[:, rows], dot(k[h, cols, :], q[h, rows, :], NT), MASKED)
        buf[h] = s
        return jnp.max(s, axis=0, keepdims=True)

    def step(i, now, after, carry):
        rows, cols = place(i)
        mark = marks[i]
        new = []
        for h in range(heads):
            top, acc, highest = carry[h]
            upcoming = score(i + 1, after, h)
            top = jnp.where(lax.rem(mark, 2) == 1, MASKED, top)
            above = jnp.maximum(top, highest)
            p = jnp.exp(now[h] - above).astype(BF16)
            acc = acc * jnp.exp(top - above) + dot(vt[h, :, cols], p)
            new.append((above, acc, upcoming))

        @pl.when(mark >= 2)
        def _():
            valid = jnp.where(idr[:, rows] >= 0, 1.0, 0.0)
            mixed = []
            for h in range(heads):
                top, acc, _ = new[h]
                row_total = acc[HEAD : HEAD + 1]
                mixed.append(acc[:HEAD] * (valid / row_total))
                lse[pl.ds(h, 1), rows] = top + jnp.log(row_total)
            out[rows, :] = jnp.concatenate(mixed, axis=0).T.astype(BF16)

        return tuple(new)

    low = jnp.full((1, BLOCK), MASKED, F32)
    start = tuple((low, jnp.zeros((vt.shape[1], BLOCK), F32), score(0, even, h)) for h in range(heads))

    def two_steps(n, carry):
        return step(2 * n + 1, odd, even, step(2 * n, even, odd, carry))

    lax.fori_loop(0, (count + 1) // 2, two_steps, start)


def attention(ids, q, k, vt):
    heads, wide, _ = q.shape
    total = wide - PAD
    rows = blocks(total) * BLOCK
    scores = pltpu.VMEM((heads, STEP, BLOCK), F32)
    return pl.pallas_call(
        functools.partial(attention_kernel, heads, total),
        name="attention",
        cost_estimate=work(31),
        in_specs=[SMEM] * 2 + [VMEM] * 5,
        out_specs=[VMEM, VMEM],
        out_shape=[
            jax.ShapeDtypeStruct((rows, heads * HEAD), BF16),
            jax.ShapeDtypeStruct((heads, wide), F32),
        ],
        scratch_shapes=step_lists(total) + [scores, scores],
        compiler_params=limit(56),
    )(*ids, q, k, vt)


def in_steps(first, last, body, carry):
    wide, narrow = 2 * BLOCK // LANES, BLOCK // LANES
    count = (last - first + narrow - 1) // narrow
    carry = lax.fori_loop(0, count // 2, lambda n, c: body(2 * BLOCK, first + n * wide, c), carry)
    return lax.fori_loop(0, count % 2, lambda n, c: body(BLOCK, first + (count - 1) * narrow, c), carry)


def attention_back_kernel(
    heads, total, numbers, before, idc, idr, q_in, k_in, v_in, kt_in, out, grad, lse, dproj,
    q, k, v, kt, made, g, delta, dq, in_s, out_s,
):
    wide = q.shape[1]
    width = heads * HEAD
    head_of = lax.broadcasted_iota(jnp.int32, (8, width), 1) // HEAD
    pick = jnp.where(head_of == lax.broadcasted_iota(jnp.int32, (8, width), 0), 1.0, 0.0).astype(BF16)
    none = jnp.zeros((TILE, LANES - HEAD), BF16)
    arriving = [
        pltpu.make_async_copy(src, dst, in_s.at[i])
        for i, (src, dst) in enumerate(((q_in, q), (k_in, k), (v_in, v), (kt_in, kt)))
    ]
    for copy in arriving:
        copy.start()

    def prepare(i, _):
        rows = pl.ds(pl.multiple_of(i * TILE, LANES), TILE)
        grads = jnp.where(idc[rows, :] >= 0, grad[rows, :].astype(F32), 0.0)
        inner = grads * out[rows, :].astype(F32)
        high = inner.astype(BF16)
        rest = (inner - high.astype(F32)).astype(BF16)
        delta[:, rows] = dot(pick, high, NT) + dot(pick, rest, NT)
        grads = grads.astype(BF16)
        for h in range(heads):
            g[h, rows, :] = jnp.concatenate([grads[:, h * HEAD : (h + 1) * HEAD], none], axis=1)
            dq[h, :, rows] = jnp.zeros((HEAD, TILE), F32)
        return 0

    lax.fori_loop(0, total // TILE, prepare, 0)
    tail = wide - total
    delta[:, total:] = jnp.zeros((8, tail), F32)
    for h in range(heads):
        g[h, total:, :] = jnp.zeros((tail, LANES), BF16)
        dq[h, :, total:] = jnp.zeros((HEAD, tail), F32)

    for copy in arriving:
        copy.wait()

    def give(i):
        cols = pl.ds(pl.multiple_of(i * BLOCK, LANES), BLOCK)
        return pltpu.make_async_copy(made.at[1:3, cols], dproj.at[1:3, cols], out_s.at[i])

    def one_block(i, _):
        c0 = pl.multiple_of(i * BLOCK, LANES)
        cols = pl.ds(c0, BLOCK)
        mine = idc[cols, :]
        low, high = block_range(i, numbers, before)

        def queries(size, at, carry):
            rows = pl.ds(pl.multiple_of(at * LANES, LANES), size)
            allowed = mine == idr[:, rows]
            both = [
                (dot(k[h, cols, :], q[h, rows, :], NT), dot(v[h, cols, :], g[h, rows, :], NT)) for h in range(heads)
            ]
            new = []
            for h in range(heads):
                dk, dv = carry[h]
                s, dp = both[h]
                p = jnp.where(allowed, jnp.exp(s - lse[h : h + 1, rows]), 0.0)
                ds = (p * (dp - delta[h : h + 1, rows])).astype(BF16)
                dv = dv + dot(p.astype(BF16), g[h, rows, :])
                dk = dk + dot(ds, q[h, rows, :])
                dq[h, :, rows] += dot(kt[h, :, cols], ds)
                new.append((dk, dv))
            return tuple(new)

        zero = jnp.zeros((BLOCK, LANES), F32)
        done = in_steps(low, high, queries, tuple((zero, zero) for _ in range(heads)))
        for part in range(2):
            joined = jnp.concatenate([done[h][part][:, :HEAD] for h in range(heads)], axis=1)
            made[part + 1, cols, :] = joined.astype(BF16)
        give(i).start()
        return 0

    lax.fori_loop(0, blocks(total), one_block, 0)

    def finish(i, _):
        rows = pl.ds(pl.multiple_of(i * TILE, LANES), TILE)
        joined = jnp.concatenate([dq[h, :, rows] for h in range(heads)], axis=0)
        made[0, rows, :] = (joined * HEAD**-0.5).T.astype(BF16)
        give_q(i).start()
        return 0

    def give_q(i):
        rows = pl.ds(pl.multiple_of(i * TILE, LANES), TILE)
        return pltpu.make_async_copy(made.at[0, rows], dproj.at[0, rows], out_s.at[blocks(total) + i])

    lax.fori_loop(0, total // TILE, finish, 0)
    for i in range(blocks(total)):
        give(i).wait()
    for i in range(total // TILE):
        give_q(i).wait()


def attention_back(ids, q, k, v, kt, out, grad, lse):
    heads, wide, _ = q.shape
    total = wide - PAD
    return pl.pallas_call(
        functools.partial(attention_back_kernel, heads, total),
        name="attention_back",
        cost_estimate=work(51),
        in_specs=[SMEM] * 2 + [VMEM] * 2 + [ANY] * 4 + [VMEM] * 3,
        out_specs=ANY,
        out_shape=jax.ShapeDtypeStruct((3, blocks(total) * BLOCK, heads * HEAD), BF16),
        scratch_shapes=[
            pltpu.VMEM(q.shape, BF16),
            pltpu.VMEM(k.shape, BF16),
            pltpu.VMEM(v.shape, BF16),
            pltpu.VMEM(kt.shape, BF16),
            pltpu.VMEM((3, blocks(total) * BLOCK, heads * HEAD), BF16),
            pltpu.VMEM((heads, wide, LANES), BF16),
            pltpu.VMEM((8, wide), F32),
            pltpu.VMEM((heads, HEAD, wide), F32),
            DMA((4,)),
            DMA((blocks(total) + total // TILE,)),
        ],
        compiler_params=limit(60),
    )(*ids, q, k, v, kt, out, grad, lse)


ROWS_MID = 288


def middle_kernel(
    attended, tok, cot, cot_came, b_out, gain, shift, b_up, b_down, *rest
):
    me = Place()
    groups = len(rest) - 28
    weights = rest[:groups]
    layer_out, grad_mid, grad_heads, cells = rest[groups : groups + 4]
    (
        att, grad_att, w, acc, vec, bup, came, low_all, cot_all, back_all, active_all, hidden_all,
        att_s, att_r, own_s, grad_s, grad_r, back_s, unit_s, push_s, push_r, sum_s, sum_r, cell_s,
    ) = rest[groups + 4 :]
    group = me.d // 2
    parts, piece, _ = weights[0].shape
    rows = tok.shape[0]
    tiles = rows // ROWS_MID
    width = att.shape[2]
    others = [lax.rem(me.q + k, 4) for k in range(1, 4)]
    greet([me.member(quarter) for quarter in others])

    def tile(t, quarter=0):
        return pl.ds(pl.multiple_of(quarter * rows + t * ROWS_MID, 16), ROWS_MID)

    def att_to(k, t):
        return remote(
            attended.at[tile(t, others[k])], att.at[me.q, tile(t)], att_s.at[k, t], att_r.at[k, t], me.member(others[k])
        )

    def att_from(k, t):
        source = others[2 - k]
        return remote(
            attended.at[tile(t)], att.at[source, tile(t)], att_s.at[k, t], att_r.at[k, t], me.member(source)
        )

    def att_own(t):
        return pltpu.make_async_copy(attended.at[tile(t, me.q)], att.at[me.q, tile(t)], own_s.at[t])

    def grad_to(k, t):
        return remote(
            grad_att.at[others[k], tile(t)], grad_heads.at[tile(t, me.q)], grad_s.at[k, t], grad_r.at[k, t], me.member(others[k])
        )

    def grad_from(k, t):
        source = others[2 - k]
        return remote(
            grad_att.at[source, tile(t)], grad_heads.at[tile(t, source)], grad_s.at[k, t], grad_r.at[k, t], me.member(source)
        )

    def grad_own(t):
        return pltpu.make_async_copy(grad_att.at[me.q, tile(t)], grad_heads.at[tile(t, me.q)], back_s.at[t])

    for t in range(tiles):
        for k in (1, 0, 2):
            att_to(k, t).start()
        att_own(t).start()

    def w_rows(j, core):
        source = 2 * lax.rem(group + groups - j, groups) + core
        return w.at[:, pl.ds(pl.multiple_of(source * piece, 16), piece)]

    def load(j):
        return pltpu.make_async_copy(weights[j], w_rows(j, me.c), unit_s.at[j])

    def push(j):
        return remote(weights[j], w_rows(j, me.c), push_s.at[j], push_r.at[j], me.sibling)

    def pushed(j):
        return remote(weights[j], w_rows(j, 1 - me.c), push_s.at[j], push_r.at[j], me.sibling)

    for j in range(groups):
        push(j).start()
        load(j).start()
    for ref in (vec, bup):
        ref[...] = jnp.zeros_like(ref)
    for j in range(groups):
        load(j).wait()
        pushed(j).wait_recv()

    out_rows = slice(0, OUT_ROWS)
    down_rows = slice(OUT_ROWS, OUT_ROWS + UP_ROWS)
    up_rows = slice(OUT_ROWS + UP_ROWS, VEC_AT)

    def one_tile(t, _):
        here = tile(t)
        att_own(t).wait()
        for k in range(3):
            att_from(k, t).wait_recv()
        atts = [att[v, here, :] for v in range(parts)]
        middle = tok[here, :].astype(F32) + line(b_out)
        for v in range(parts):
            middle = middle + dot(atts[v], w[v, out_rows])
        unit, scale = normalise(middle)
        low = (unit * line(gain) + line(shift)).astype(BF16)
        cot_low = jnp.where(me.native, cot[here, :], cot_came[here, :])
        low_all[here, :] = low
        cot_all[here, :] = cot_low
        cot_full = cot_low.astype(F32)
        out = middle + line(b_down)
        grad_norm = jnp.zeros_like(middle)

        def products(v):
            return dot(low, w[v, up_rows], NT), dot(cot_low, w[v, down_rows], NT)

        upcoming = products(0)
        for v in range(parts):
            hidden, grad_active = upcoming
            if v + 1 < parts:
                upcoming = products(v + 1)
            hidden = hidden + b_up[v]
            below = 0.5 * (1.0 + lax.erf(hidden * 0.5**0.5))
            density = jnp.exp(-0.5 * hidden * hidden) * 0.3989422804014327
            active = (hidden * below).astype(BF16)
            grad_hidden = (grad_active * (below + hidden * density)).astype(BF16)
            out = out + dot(active, w[v, down_rows])
            grad_norm = grad_norm + dot(grad_hidden, w[v, up_rows])
            active_all[v, here, :] = active
            hidden_all[v, here, :] = grad_hidden
            bup[v] += jnp.sum(grad_hidden.astype(F32), axis=0, keepdims=True)
        layer_out[here, :] = out.astype(BF16)
        scaled = grad_norm * line(gain)
        back = cot_full + scale * (
            scaled
            - jnp.mean(scaled, axis=-1, keepdims=True)
            - unit * jnp.mean(scaled * unit, axis=-1, keepdims=True)
        )
        grad_mid[here, :] = back
        back_low = back.astype(BF16)
        back_all[here, :] = back_low
        for v in range(parts):
            grad_att[v, here, :] = dot(back_low, w[v, out_rows], NT).astype(BF16)
        for k in (1, 0, 2):
            grad_to(k, t).start()
        grad_own(t).start()
        vec[0:1] += jnp.sum(grad_norm * unit, axis=0, keepdims=True)
        vec[1:2] += jnp.sum(grad_norm, axis=0, keepdims=True)
        vec[2:3] += jnp.sum(back, axis=0, keepdims=True)
        vec[3:4] += jnp.sum(cot_full, axis=0, keepdims=True)
        return 0

    lax.fori_loop(0, tiles, one_tile, 0)

    def sum_rows(i, core):
        return pl.ds(pl.multiple_of((2 * i + core) * piece, 16), piece)

    def give(i):
        return remote(w.at[:, sum_rows(i, 1 - me.c)], came.at[i], sum_s.at[i], sum_r.at[i], me.sibling)

    def keep(i):
        return pltpu.make_async_copy(w.at[:, sum_rows(i, me.c)], cells.at[i], cell_s.at[i])

    for v in range(parts):
        acc[v, out_rows] = dot(att[v], back_all[...], TN)
        acc[v, down_rows] = dot(active_all[v], cot_all[...], TN)
        acc[v, up_rows] = dot(hidden_all[v], low_all[...], TN)
        acc[v, VEC_AT:] = jnp.zeros((UNITS - VEC_AT, D), F32)
        acc[v, VEC_AT : VEC_AT + 8] = vec[...]
        acc[v, VEC_AT + 4 : VEC_AT + 5, :UP_ROWS] = bup[v]
    for i in range(groups):
        for v in range(parts):
            w[v, sum_rows(i, 1 - me.c), :] = acc[v, sum_rows(i, 1 - me.c), :].astype(BF16)
        give(i).start()
    for i in range(groups):
        give(i).wait_recv()
        for v in range(parts):
            w[v, sum_rows(i, me.c), :] = (acc[v, sum_rows(i, me.c), :] + came[i, v].astype(F32)).astype(BF16)
        keep(i).start()
    for t in range(tiles):
        for k in range(3):
            grad_from(k, t).wait_recv()
            grad_to(k, t).wait_send()
            att_to(k, t).wait_send()
        grad_own(t).wait()
    for j in range(groups):
        push(j).wait_send()
        give(j).wait_send()
        keep(j).wait()


def middle_part(attended, tok, cot, cot_came, b_out, gain, shift, b_up, b_down, weights):
    rows = tok.shape[0]
    width = attended.shape[1]
    groups = len(weights)
    parts, piece, _ = weights[0].shape
    tiles = rows // ROWS_MID
    shape = jax.ShapeDtypeStruct
    halves = (groups, parts, piece, D)
    return pl.pallas_call(
        middle_kernel,
        name="middle_part",
        cost_estimate=work(50),
        in_specs=[ANY] + [VMEM] * 8 + [ANY] * groups,
        out_specs=[VMEM, VMEM, ANY, ANY],
        out_shape=[
            shape((rows, D), BF16),
            shape((rows, D), F32),
            shape((4 * rows, width), BF16),
            shape(halves, BF16),
        ],
        scratch_shapes=[
            pltpu.VMEM((parts, rows, width), BF16),
            pltpu.VMEM((parts, rows, width), BF16),
            pltpu.VMEM((parts, UNITS, D), BF16),
            pltpu.VMEM((parts, UNITS, D), F32),
            pltpu.VMEM((8, D), F32),
            pltpu.VMEM((parts, 1, UP_ROWS), F32),
            pltpu.VMEM(halves, BF16),
            pltpu.VMEM((rows, D), BF16),
            pltpu.VMEM((rows, D), BF16),
            pltpu.VMEM((rows, D), BF16),
            pltpu.VMEM((parts, rows, UP_ROWS), BF16),
            pltpu.VMEM((parts, rows, UP_ROWS), BF16),
            DMA((3, tiles)),
            DMA((3, tiles)),
            DMA((tiles,)),
            DMA((3, tiles)),
            DMA((3, tiles)),
            DMA((tiles,)),
        ]
        + [DMA((groups,))] * 6,
        compiler_params=pltpu.CompilerParams(
            collective_id=2, has_side_effects=True, vmem_limit_bytes=48 << 20
        ),
    )(attended, tok, cot, cot_came, b_out, gain, shift, b_up, b_down, *weights)


CUTS = 3


def finish_kernel(
    dproj_in, normed_in, full_in, w, grad_mid, gain, cells, grad, vec_sum, d_w, sums,
    dproj, normed, full, part, theirs, sent, crossed, low, acc, w_part, w_in, w_z, vec, vz, vd, u_in, u_own,
    load_s, out_s, sib_s, sib_r, cross_s, cross_r, swap_s, swap_r, vz_s, vz_r, vd_s, vd_r,
    ws_s, ws_r, wz_s, wz_r, wg_s, wg_r, wf_s, wf_r, uz_s, uz_r, ug_s, ug_r, uf_s, uf_r,
):
    me = Place()
    foreign = jnp.logical_not(me.native)
    rows = grad_mid.shape[0]
    piece = rows // CUTS
    width = w.shape[1]
    ndp = vd.shape[0]
    groups, w_rows, _ = w_part.shape
    group = me.d // 2

    order = [2 * (1 - me.hf) + 1 - me.r, 2 * (1 - me.hf) + me.r, 2 * me.hf + 1 - me.r, 2 * me.hf + me.r]

    def span_of(k, p):
        return pl.ds(pl.multiple_of(order[k] * rows + p * piece, 16), piece)

    def loads(k, p):
        span = span_of(k, p)
        pairs = ((dproj_in.at[:, span], dproj.at[:, span]), (normed_in.at[span], normed.at[span]), (full_in.at[span], full.at[span]))
        return [pltpu.make_async_copy(src, dst, load_s.at[k, p, j]) for j, (src, dst) in enumerate(pairs)]

    for k in range(4):
        for p in range(CUTS):
            for copy in loads(k, p):
                copy.start()

    around = [(me.d, lax.rem(me.m + k, 4)) for k in range(1, 4)]
    along = [(lax.rem(me.d + k, ndp), me.m) for k in range(1, ndp)]
    greet([me.partner] + around + along)

    def to_sib(k, p):
        slot = k % 2
        return remote(part.at[k, p], theirs.at[slot, p], sib_s.at[slot, p], sib_r.at[slot, p], me.sibling)

    def to_cross(p):
        return remote(sent.at[p], crossed.at[p], cross_s.at[p], cross_r.at[p], me.cross)

    def to_partner(p):
        return remote(low.at[p], grad.at[p], swap_s.at[p], swap_r.at[p], me.partner)

    def keep(p):
        return pltpu.make_async_copy(low.at[p], grad.at[p], out_s.at[p])

    def unit_z(j):
        to = lax.rem(me.m + 1 + j, 4)
        return remote(cells.at[to], u_in.at[j], uz_s.at[j], uz_r.at[j], around[j])

    def unit_give(j):
        to = (2 * lax.rem(group + j, groups) + me.c, me.m)
        return remote(u_own, sums.at[me.d], ug_s.at[j], ug_r.at[j], to)

    def unit_give_in(j):
        source = 2 * lax.rem(group + groups - j, groups) + me.c
        return remote(u_own, sums.at[source], ug_s.at[j], ug_r.at[j], (source, me.m))

    def unit_forward(j):
        source = 2 * lax.rem(group + groups - j, groups) + me.c
        src = u_own if j == 0 else sums.at[source]
        return remote(src, sums.at[source], uf_s.at[j], uf_r.at[j], me.sibling)

    def unit_forward_in(j):
        source = 2 * lax.rem(group + groups - j, groups) + 1 - me.c
        return remote(u_own, sums.at[source], uf_s.at[j], uf_r.at[j], me.sibling)

    vec[...] = jnp.zeros_like(vec)

    def compute(k):
        def one(p, _):
            span = span_of(k, p)
            for copy in loads(k, p):
                copy.wait()
            total = jnp.zeros((piece, D), F32)
            for c in range(3):
                total = total + dot(dproj[c, span, :], w[c])
            part[k, p] = total.astype(BF16)

            @pl.when(me.native if k < 2 else foreign)
            def _():
                to_sib(k, p).start()

            return 0

        lax.fori_loop(0, CUTS, one, 0)

    def pass_across(k):
        for p in range(CUTS):
            to_sib(k, p).wait_recv()
            sent[p] = (part[k, p].astype(F32) + theirs[0, p].astype(F32)).astype(BF16)
            to_cross(p).start()

    def conclude(k, p):
        to_sib(k, p).wait_recv()
        to_cross(p).wait_recv()
        total = part[k, p].astype(F32) + theirs[1, p].astype(F32) + crossed[p].astype(F32)
        span = pl.ds(pl.multiple_of(me.q * rows + p * piece, 16), piece)
        unit, scale = normalise(full[span, :].astype(F32))
        vec[0:1] += jnp.sum(total * unit, axis=0, keepdims=True)
        vec[1:2] += jnp.sum(total, axis=0, keepdims=True)
        scaled = total * line(gain)
        result = grad_mid[p * piece : (p + 1) * piece, :] + scale * (
            scaled
            - jnp.mean(scaled, axis=-1, keepdims=True)
            - unit * jnp.mean(scaled * unit, axis=-1, keepdims=True)
        )
        low[p] = result.astype(BF16)

    def conclude_foreign(p):
        conclude(1, p)
        to_partner(p).start()

    compute(0)

    @pl.when(foreign)
    def _():
        pass_across(0)

    compute(1)
    compute(2)

    @pl.when(me.native)
    def _():
        pass_across(2)

    compute(3)
    for j in range(3):
        unit_z(j).start()

    for c in range(3):
        acc[c * width : (c + 1) * width, :] = dot(dproj[c], normed[...], TN)

    for i in range(groups):
        w_part[i] = acc[i * w_rows : (i + 1) * w_rows, :].astype(BF16)

    def other_group(k):
        return lax.rem(group + k, groups)

    def w_send(k):
        to = other_group(k)
        return remote(w_part.at[to], w_in.at[k], ws_s.at[k], ws_r.at[k], (2 * to + me.c, me.m))

    for k in range(1, groups):
        w_send(k).start()

    @pl.when(foreign)
    def _():
        for p in range(2 * CUTS // 3):
            conclude_foreign(p)

    w_sum = w_part[group].astype(F32)
    for k in range(1, groups):
        w_send(k).wait_recv()
        w_sum = w_sum + w_in[k].astype(F32)

    to_z = remote(w_z.at[0], w_z.at[1], wz_s, wz_r, (me.d, lax.rem(me.m + 2, 4)))

    def w_give(k):
        return remote(w_z.at[0], d_w.at[group], wg_s.at[k], wg_r.at[k], (2 * other_group(k) + me.c, me.m))

    def w_give_in(k):
        source = lax.rem(group + groups - k, groups)
        return remote(w_z.at[0], d_w.at[source], wg_s.at[k], wg_r.at[k], (2 * source + me.c, me.m))

    def w_forward(k):
        source = lax.rem(group + groups - k, groups)
        src = w_z.at[0] if k == 0 else d_w.at[source]
        return remote(src, d_w.at[source], wf_s.at[k], wf_r.at[k], me.sibling)

    w_keep = pltpu.make_async_copy(w_z.at[0], d_w.at[group], out_s.at[CUTS])
    unit_keep = pltpu.make_async_copy(u_own, sums.at[me.d], out_s.at[CUTS + 1])

    @pl.when(foreign)
    def _():
        w_z[0] = w_sum.astype(BF16)
        to_z.start()
        for p in range(2 * CUTS // 3, CUTS):
            conclude_foreign(p)

    @pl.when(me.native)
    def _():
        to_z.wait_recv()
        w_z[0] = (w_sum + w_z[1].astype(F32)).astype(BF16)
        w_keep.start()
        for k in range(1, groups):
            w_give(k).start()
        w_forward(0).start()
        for p in range(CUTS):
            conclude(3, p)
            keep(p).start()

    vz[me.m] = vec[...]

    def around_copy(k):
        return remote(vz.at[me.m], vz.at[me.m], vz_s.at[k], vz_r.at[k], around[k])

    for k in range(3):
        around_copy(k).start()

    unit_sum = cells[me.m].astype(F32)
    for j in range(3):
        unit_z(j).wait_recv()
        unit_sum = unit_sum + u_in[j].astype(F32)
    u_own[...] = unit_sum.astype(BF16)
    unit_keep.start()
    for j in range(1, groups):
        unit_give(j).start()
    unit_forward(0).start()

    @pl.when(me.native)
    def _():
        for k in range(1, groups):
            w_give_in(k).wait_recv()
            w_forward(k).start()

    for k in range(3):
        source = lax.rem(me.m + 3 - k, 4)
        remote(vz.at[source], vz.at[source], vz_s.at[k], vz_r.at[k], around[k]).wait_recv()
    vd[me.d] = vz[0] + vz[1] + vz[2] + vz[3]

    def along_copy(k):
        return remote(vd.at[me.d], vd.at[me.d], vd_s.at[k], vd_r.at[k], along[k])

    for k in range(ndp - 1):
        along_copy(k).start()

    for j in range(1, groups):
        unit_give_in(j).wait_recv()
        unit_forward(j).start()
    for k in range(ndp - 1):
        source = lax.rem(me.d + ndp - 1 - k, ndp)
        remote(vd.at[source], vd.at[source], vd_s.at[k], vd_r.at[k], along[k]).wait_recv()
    total = vd[0]
    for i in range(1, ndp):
        total = total + vd[i]
    vec_sum[...] = total
    for j in range(groups):
        unit_forward_in(j).wait_recv()

    @pl.when(foreign)
    def _():
        for k in range(groups):
            source = lax.rem(group + groups - k, groups)
            remote(w_z.at[0], d_w.at[source], wf_s.at[k], wf_r.at[k], me.sibling).wait_recv()
        for p in range(CUTS):
            to_partner(p).wait_recv()
            to_partner(p).wait_send()
            to_sib(2, p).wait_send()
            to_sib(3, p).wait_send()
        to_z.wait_send()

    @pl.when(me.native)
    def _():
        for p in range(CUTS):
            keep(p).wait()
            to_sib(0, p).wait_send()
            to_sib(1, p).wait_send()
        for k in range(1, groups):
            w_give(k).wait_send()
        for k in range(groups):
            w_forward(k).wait_send()
        w_keep.wait()

    for p in range(CUTS):
        to_cross(p).wait_send()
    for k in range(1, groups):
        w_send(k).wait_send()
    for k in range(3):
        around_copy(k).wait_send()
        unit_z(k).wait_send()
    for k in range(ndp - 1):
        along_copy(k).wait_send()
    for j in range(groups):
        unit_forward(j).wait_send()
    for j in range(1, groups):
        unit_give(j).wait_send()
    unit_keep.wait()


def finish(dproj, normed, full, w, grad_mid, gain, cells, ndp):
    rows = grad_mid.shape[0]
    total = full.shape[0]
    piece = rows // CUTS
    pieces = (CUTS, piece, D)
    groups = ndp // 2
    columns = 3 * w.shape[1]
    cut = (groups, columns // groups, D)
    unit = cells.shape[1:]
    shape = jax.ShapeDtypeStruct
    return pl.pallas_call(
        finish_kernel,
        name="finish",
        cost_estimate=work(60),
        in_specs=[ANY] * 3 + [VMEM] * 4,
        out_specs=[ANY, VMEM, ANY, ANY],
        out_shape=[shape(pieces, BF16), shape((8, D), F32), shape(cut, BF16), shape((ndp,) + unit, BF16)],
        scratch_shapes=[
            pltpu.VMEM((3, total, w.shape[1]), BF16),
            pltpu.VMEM((total, D), BF16),
            pltpu.VMEM((total, D), BF16),
            pltpu.VMEM((4,) + pieces, BF16),
            pltpu.VMEM((2,) + pieces, BF16),
            pltpu.VMEM(pieces, BF16),
            pltpu.VMEM(pieces, BF16),
            pltpu.VMEM(pieces, BF16),
            pltpu.VMEM((columns, D), F32),
            pltpu.VMEM(cut, BF16),
            pltpu.VMEM(cut, BF16),
            pltpu.VMEM((2,) + cut[1:], BF16),
            pltpu.VMEM((8, D), F32),
            pltpu.VMEM((4, 8, D), F32),
            pltpu.VMEM((ndp, 8, D), F32),
            pltpu.VMEM((3,) + unit, BF16),
            pltpu.VMEM(unit, BF16),
            DMA((4, CUTS, 3)),
            DMA((CUTS + 2,)),
        ]
        + [DMA((2, CUTS))] * 2
        + [DMA((CUTS,))] * 4
        + [DMA((3,))] * 2
        + [DMA((ndp - 1,))] * 2
        + [DMA((groups,))] * 2
        + [DMA] * 2
        + [DMA((groups,))] * 4
        + [DMA((3,))] * 2
        + [DMA((groups,))] * 4,
        compiler_params=pltpu.CompilerParams(
            collective_id=4, has_side_effects=True, vmem_limit_bytes=60 << 20
        ),
    )(dproj, normed, full, w, grad_mid, gain, cells)


def outputs_kernel(
    layer, layer_came, grads, w_sums, unit_sums, vec_one,
    layer_out, tokens_grad, d_qkv, d_out, d_up, d_down, d_gain_two, d_shift_two, d_b_out, d_b_down, d_b_up, d_gain_one, d_shift_one,
    layer_s, came_s, grads_s, w_s, unit_s, vec_s, grads_f, w_f, unit_f, up_f, in_s, out_s,
):
    me = Place()
    arriving = [
        pltpu.make_async_copy(src, dst, in_s.at[i])
        for i, (src, dst) in enumerate(
            (
                (unit_sums, unit_s),
                (w_sums, w_s),
                (grads, grads_s),
                (layer, layer_s),
                (layer_came, came_s),
                (vec_one, vec_s),
            )
        )
    ]
    for i in (2, 1, 0, 3, 4, 5):
        arriving[i].start()
    leaving = []

    def leave(src, dst):
        copy = pltpu.make_async_copy(src, dst, out_s.at[len(leaving)])
        copy.start()
        leaving.append(copy)

    def flatten(pieces, flat):
        count, height, _ = pieces.shape
        for i in range(count):
            flat[i * height : (i + 1) * height, :] = pieces[i].astype(F32)

    arriving[2].wait()
    flatten(grads_s, grads_f)
    leave(grads_f, tokens_grad)
    arriving[1].wait()
    flatten(w_s, w_f)
    leave(w_f, d_qkv)
    arriving[0].wait()
    flatten(unit_s, unit_f)
    leave(unit_f.at[:OUT_ROWS], d_out)
    leave(unit_f.at[OUT_ROWS : OUT_ROWS + UP_ROWS], d_down)
    for i in (3, 4):
        arriving[i].wait()
    layer_s[...] = jnp.where(me.native, layer_s[...], came_s[...])
    leave(layer_s, layer_out)
    up_f[...] = unit_f[OUT_ROWS + UP_ROWS : VEC_AT, :].T
    leave(up_f, d_up)
    arriving[5].wait()
    for i, ref in enumerate((d_gain_two, d_shift_two, d_b_out, d_b_down)):
        ref[...] = unit_f[VEC_AT + i, :]
    d_b_up[...] = unit_f[VEC_AT + 4, :UP_ROWS]
    d_gain_one[...] = vec_s[0, :]
    d_shift_one[...] = vec_s[1, :]
    for copy in leaving:
        copy.wait()


def outputs(layer, layer_came, grads, w_sums, unit_sums, vec_one):
    rows = layer.shape[0]
    columns = w_sums.shape[0] * w_sums.shape[1]
    shape = lambda *s: jax.ShapeDtypeStruct(s, F32)
    return pl.pallas_call(
        outputs_kernel,
        name="outputs",
        in_specs=[ANY] * 6,
        out_specs=[ANY] * 6 + [VMEM] * 7,
        out_shape=[
            jax.ShapeDtypeStruct((rows, D), BF16),
            shape(rows, D),
            shape(columns, D),
            shape(OUT_ROWS, D),
            shape(D, UP_ROWS),
            shape(UP_ROWS, D),
            shape(D),
            shape(D),
            shape(D),
            shape(D),
            shape(UP_ROWS),
            shape(D),
            shape(D),
        ],
        scratch_shapes=[
            pltpu.VMEM(layer.shape, BF16),
            pltpu.VMEM(layer.shape, BF16),
            pltpu.VMEM(grads.shape, BF16),
            pltpu.VMEM(w_sums.shape, BF16),
            pltpu.VMEM(unit_sums.shape, BF16),
            pltpu.VMEM(vec_one.shape, F32),
            pltpu.VMEM((rows, D), F32),
            pltpu.VMEM((columns, D), F32),
            pltpu.VMEM((UNITS, D), F32),
            pltpu.VMEM((D, UP_ROWS), F32),
            DMA((6,)),
            DMA((6,)),
        ],
        compiler_params=limit(60),
    )(layer, layer_came, grads, w_sums, unit_sums, vec_one)


def swap_pairs(ndp):
    return [
        (d * 4 + m, (d ^ 1) * 4 + (m + 2) % 4) for d in range(ndp) for m in range(4) if d % 2 != m // 2
    ]


def weight_piece(w_out, w_up, w_down, ndp):
    block = jnp.concatenate([w_out, w_down, w_up.T, jnp.zeros((UNITS - w_out.shape[0] - 2 * w_down.shape[0], D), BF16)])
    piece = UNITS // ndp
    return lax.dynamic_slice_in_dim(block, lax.axis_index("dp") * piece, piece, 0)


def from_other_pairs(block, ndp):
    groups = ndp // 2
    blocks_of = [block]
    for j in range(1, groups):
        pairs = [(d, 2 * ((d // 2 + j) % groups) + d % 2) for d in range(ndp)]
        blocks_of.append(lax.ppermute(block, "dp", pairs))
    return blocks_of


def sum_over_pairs(cells, ndp):
    cores = [[d for d in range(ndp) if d % 2 == core] for core in range(2)]
    return lax.psum_scatter(cells.reshape(-1, D), "dp", scatter_dimension=0, tiled=True, axis_index_groups=cores)


def shards(
    tokens,
    scene_ids,
    gain_one,
    shift_one,
    w_qkv,
    w_out,
    b_out,
    gain_two,
    shift_two,
    w_up,
    b_up,
    w_down,
    b_down,
    cotangent,
    ndp,
):
    both = ("dp", "mp")
    swap = swap_pairs(ndp)
    w_qkv = jnp.swapaxes(w_qkv, 1, 2)
    full, own_tok, w_mine, numbers, id_row, id_column, before, b_ups, normed, q, k, v, kt, vt, weights = start(
        tokens, w_qkv, scene_ids.reshape(-1, LANES), b_up, gain_one, shift_one, weight_piece(w_out, w_up, w_down, ndp), ndp
    )
    w_mine = w_mine.reshape(w_qkv.shape)
    ids = numbers, before, id_column, id_row
    weights = from_other_pairs(weights, ndp)
    sent_cot, q = lax.optimization_barrier((cotangent, q))
    cot_came = lax.ppermute(sent_cot, both, swap)
    attended, lse = attention(ids, q, k, vt)
    layer, grad_mid, grad_heads, cells = middle_part(
        attended, own_tok, cotangent, cot_came, b_out, gain_two, shift_two, b_ups, b_down, weights
    )
    sent_out, grad_heads = lax.optimization_barrier((layer, grad_heads))
    layer_came = lax.ppermute(sent_out, both, swap)
    cells = sum_over_pairs(cells, ndp)
    dproj = attention_back(ids, q, k, v, kt, attended, grad_heads, lse)
    cells, dproj = lax.optimization_barrier((cells, dproj))
    grads, vec_one, w_sums, unit_sums = finish(
        dproj, normed, full, w_mine, grad_mid, gain_one, cells.reshape(4, -1, D), ndp
    )
    (
        layer_out, tokens_grad, d_qkv, d_out, d_up, d_down, d_gain_two, d_shift_two, d_b_out, d_b_down, d_b_up, d_gain_one, d_shift_one,
    ) = outputs(layer, layer_came, grads, w_sums, unit_sums, vec_one)
    return (
        layer_out,
        tokens_grad,
        d_gain_one,
        d_shift_one,
        jnp.swapaxes(d_qkv.reshape(w_qkv.shape), 1, 2),
        d_out,
        d_b_out,
        d_gain_two,
        d_shift_two,
        d_up,
        d_b_up,
        d_down,
        d_b_down,
    )


def solution(mesh):
    ndp = mesh.shape["dp"]
    return jax.shard_map(
        functools.partial(shards, ndp=ndp),
        mesh=mesh,
        in_specs=(
            P(("dp", "mp"), None),
            P("dp"),
            P(),
            P(),
            P(None, None, "mp"),
            P("mp", None),
            P(),
            P(),
            P(),
            P(None, "mp"),
            P("mp"),
            P("mp", None),
            P(),
            P(("dp", "mp"), None),
        ),
        out_specs=(
            P(("dp", "mp"), None),
            P(("dp", "mp"), None),
            P(),
            P(),
            P(None, None, "mp"),
            P("mp", None),
            P(),
            P(),
            P(),
            P(None, "mp"),
            P("mp"),
            P("mp", None),
            P(),
        ),
        check_vma=False,
    )
```

```python
import functools

import jax
import jax.numpy as jnp
from jax import lax
from jax.experimental import pallas as pl
from jax.experimental.pallas import tpu as pltpu
from jax.sharding import PartitionSpec as P

HEAD = 64
D = 768
FF = 1536
LANES = 128
PAD = 512
OUT_ROWS = D // 4
UP_ROWS = FF // 4
VEC_AT = OUT_ROWS + 2 * UP_ROWS
UNITS = 1024
EPS = 1e-05
MASKED = -1e30
MESH = pl.DeviceIdType.MESH
F32 = jnp.float32
BF16 = jnp.bfloat16
VMEM = pl.BlockSpec(memory_space=pltpu.VMEM)
SMEM = pl.BlockSpec(memory_space=pltpu.SMEM)
ANY = pl.BlockSpec(memory_space=pl.ANY)
DMA = pltpu.SemaphoreType.DMA

NN = (((1,), (0,)), ((), ()))
NT = (((1,), (1,)), ((), ()))
TN = (((0,), (0,)), ((), ()))


def dot(a, b, dims=NN):
    return lax.dot_general(a, b, dims, preferred_element_type=F32)


def work(us):
    return pl.CostEstimate(flops=us * 10**9, bytes_accessed=us * 3 * 10**6, transcendentals=0)


def limit(mib):
    return pltpu.CompilerParams(vmem_limit_bytes=mib << 20)


def line(ref):
    return ref[...].reshape(1, -1)


class Place:
    def __init__(self):
        self.d = lax.axis_index("dp")
        self.m = lax.axis_index("mp")
        self.c = lax.rem(self.d, 2)
        self.r = lax.rem(self.m, 2)
        self.hf = self.m // 2
        self.q = 2 * self.c + self.r
        self.native = self.c == self.hf
        self.sibling = (self.d + 1 - 2 * self.c, self.m)
        self.cross = (self.d, self.m + 1 - 2 * self.r)
        self.partner = (self.d + 1 - 2 * self.c, lax.rem(self.m + 2, 4))

    def member(self, quarter):
        return (self.d - self.c + quarter // 2, 2 * self.hf + quarter % 2)


def greet(others):
    barrier = pltpu.get_barrier_semaphore()
    for other in others:
        pl.semaphore_signal(barrier, inc=1, device_id=other, device_id_type=MESH)
    pl.semaphore_wait(barrier, len(others))


def remote(src, dst, send, recv, device):
    return pltpu.make_async_remote_copy(
        src_ref=src, dst_ref=dst, send_sem=send, recv_sem=recv, device_id=device, device_id_type=MESH
    )


STAGES = 3
PIECES = 6
TILE = 384
SCENES = 4


def normalise(x):
    centred = x - jnp.mean(x, axis=-1, keepdims=True)
    scale = lax.rsqrt(jnp.mean(centred * centred, axis=-1, keepdims=True) + EPS)
    return centred * scale, scale


def widen(x, ones, rows):
    lane = lax.broadcasted_iota(jnp.int32, (rows, LANES - HEAD), 1)
    return jnp.concatenate([x, jnp.where(lane < ones, 1.0, 0.0).astype(x.dtype)], axis=1)


def describe_scenes(ids, row, column, before):
    lines = ids.shape[0]
    for j in range(lines):
        place = j * LANES + lax.broadcasted_iota(jnp.int32, (1, LANES), 1)
        number = ids[j : j + 1, :]
        number = jnp.where(number >= 0, number, -1 - place)
        span = slice(j * LANES, (j + 1) * LANES)
        row[:, span] = number
        column[span, :] = jnp.broadcast_to(number.astype(F32), (LANES, LANES)).T[:, :1].astype(jnp.int32)
    rest = row.shape[1] - lines * LANES
    row[:, lines * LANES :] = jnp.full((1, rest), -(1 << 21), jnp.int32)
    column[lines * LANES :, :] = jnp.full((rest, 1), -(1 << 20), jnp.int32)
    lane = lax.broadcasted_iota(jnp.int32, (1, LANES), 1)
    counts = jnp.zeros((1, LANES), F32)
    for number in range(1, SCENES + 1):
        mine = jnp.where((ids[...] >= 0) & (ids[...] < number), 1.0, 0.0)
        total = jnp.sum(jnp.sum(mine, axis=0, keepdims=True), axis=1, keepdims=True)
        counts = jnp.where(lane == number, total, counts)
    before[...] = counts.astype(jnp.int32)


def start_kernel(
    heads, tok, wq, ids, b_up, gain, shift, mine,
    full, own, w_out, ids_own, id_row, id_column, before, b_ups, normed, q, k, v, kt, vt, units,
    buf, w, low_s, q_s, k_s, v_s, kt_s, vt_s,
    swap_s, swap_r, cross_s, cross_r, sib_s, sib_r, fwd_s, fwd_r, w_s, w_r, ids_s, ids_r, b_s, b_r, out_s, late_s,
    uz_s, uz_r,
):
    me = Place()
    foreign = jnp.logical_not(me.native)
    rows = tok.shape[0]
    piece = rows // PIECES
    total = buf.shape[0]
    tiles = total // TILE
    groups = w.shape[1]
    group = me.d // 2
    around = [(me.d, lax.rem(me.m + j, 4)) for j in range(1, 4)]
    lines = [(2 * lax.rem(group + j, groups) + me.c, me.m) for j in range(1, groups)]
    greet([me.sibling, me.partner] + around + lines)

    def rows_of(quarter, n):
        p = jnp.where(me.hf == 0, n, PIECES - 1 - n)
        return pl.ds(pl.multiple_of(quarter * rows + p * piece, 16), piece)

    def part(quarter, n):
        return buf.at[rows_of(quarter, n)]

    sib_q = 2 * (1 - me.c) + me.r
    cross_q = 2 * me.c + 1 - me.r
    sib_cross_q = 2 * (1 - me.c) + 1 - me.r

    def swap(n):
        p = jnp.where(me.hf == 1, n, PIECES - 1 - n)
        src = tok.at[pl.ds(pl.multiple_of(p * piece, 16), piece)]
        dst = buf.at[pl.ds(pl.multiple_of(sib_q * rows + p * piece, 16), piece)]
        return remote(src, dst, swap_s.at[n], swap_r.at[n], me.partner)

    def swap_in(n):
        return remote(part(me.q, n), part(me.q, n), swap_s.at[n], swap_r.at[n], me.partner)

    def cross(quarter, n):
        return remote(part(quarter, n), part(quarter, n), cross_s.at[n], cross_r.at[n], me.cross)

    def sib(quarter, n):
        return remote(part(quarter, n), part(quarter, n), sib_s.at[n], sib_r.at[n], me.sibling)

    def forward(quarter, n):
        return remote(part(quarter, n), part(quarter, n), fwd_s.at[n], fwd_r.at[n], me.sibling)

    weight = remote(wq.at[:, group], w.at[:, group], w_s.at[0], w_r.at[0], me.partner)

    def weight_share(j):
        return remote(w.at[:, group], w.at[:, group], w_s.at[j], w_r.at[j], lines[j - 1])

    def weight_in(j):
        source = lax.rem(group + groups - j, groups)
        return remote(w.at[:, source], w.at[:, source], w_s.at[j], w_r.at[j], lines[j - 1])


    def unit_z(j):
        return remote(mine, units.at[2 - j], uz_s.at[j], uz_r.at[j], around[j])

    def give_b_up(j):
        return remote(b_ups.at[me.m], b_ups.at[me.m], b_s.at[j], b_r.at[j], around[j])

    scenes = remote(ids, ids_own, ids_s, ids_r, me.sibling)
    b_ups[me.m] = line(b_up)
    for j in range(3):
        give_b_up(j).start()

    @pl.when(me.native)
    def _():
        scenes.start()
        buf[pl.ds(pl.multiple_of(me.q * rows, 16), rows), :] = tok[...]
        for n in range(PIECES):
            cross(me.q, n).start()
            sib(me.q, n).start()
        w[...] = wq[...]
        ids_own[...] = ids[...]

    @pl.when(foreign)
    def _():
        weight.start()
        for n in range(PIECES):
            swap(n).start()

    def share(n):
        swap_in(n).wait_recv()
        cross(me.q, n).start()
        sib(me.q, n).start()

    def pass_on(n):
        cross(cross_q, n).wait_recv()
        forward(cross_q, n).start()

    def from_sibling(n):
        sib(sib_q, n).wait_recv()
        forward(sib_cross_q, n).wait_recv()

    def outputs(t):
        span = pl.ds(pl.multiple_of(t * TILE, LANES), TILE)
        pairs = [
            (low_s.at[span], normed.at[span]),
            (buf.at[span], full.at[span]),
            (q_s.at[:, span], q.at[:, span]),
            (k_s.at[:, span], k.at[:, span]),
            (v_s.at[:, span], v.at[:, span]),
            (kt_s.at[:, :, span], kt.at[:, :, span]),
            (vt_s.at[:, :, span], vt.at[:, :, span]),
        ]
        return [pltpu.make_async_copy(src, dst, out_s.at[t, j]) for j, (src, dst) in enumerate(pairs)]

    ones = jnp.where(lax.broadcasted_iota(jnp.int32, (16, TILE), 0) < 1, 1.0, 0.0).astype(BF16)

    def compute(first, stride, count):
        def one(n, _):
            at = first + stride * n
            t = jnp.where(me.hf == 0, at, tiles - 1 - at)
            span = pl.ds(pl.multiple_of(t * TILE, LANES), TILE)
            unit, _ = normalise(buf[span, :].astype(F32))
            low = (unit * line(gain) + line(shift)).astype(BF16)
            low_s[span, :] = low
            qs = (dot(low, w[0].reshape(-1, D), NT).astype(BF16).astype(F32) * HEAD**-0.5).astype(BF16)
            ks = dot(low, w[1].reshape(-1, D), NT)
            vs = dot(low, w[2].reshape(-1, D), NT)
            kts = ks.T.astype(BF16)
            vts = vs.T.astype(BF16)
            ks = ks.astype(BF16)
            vs = vs.astype(BF16)
            for h in range(heads):
                cols = slice(h * HEAD, (h + 1) * HEAD)
                q_s[h, span, :] = widen(qs[:, cols], 0, TILE)
                k_s[h, span, :] = widen(ks[:, cols], 3, TILE)
                v_s[h, span, :] = widen(vs[:, cols], 3, TILE)
                kt_s[h, :, span] = kts[cols]
                vt_s[h, :HEAD, span] = vts[cols]
                vt_s[h, HEAD:, span] = ones
            for copy in outputs(t):
                copy.start()
            return 0

        lax.fori_loop(0, count, one, 0)

    pad = pl.ds(total, PAD)
    zeros = jnp.zeros((heads, PAD, LANES), BF16)
    for ref in (q_s, k_s, v_s):
        ref[:, pad, :] = zeros
    for ref in (kt_s, vt_s):
        ref[:, :, pad] = jnp.zeros((heads, ref.shape[1], PAD), BF16)
    padding = [
        pltpu.make_async_copy(src, dst, late_s.at[j])
        for j, (src, dst) in enumerate(
            [(a.at[:, pad], b.at[:, pad]) for a, b in ((q_s, q), (k_s, k), (v_s, v))]
            + [(a.at[:, :, pad], b.at[:, :, pad]) for a, b in ((kt_s, kt), (vt_s, vt))]
        )
    ]
    for copy in padding:
        copy.start()

    def stage(n):
        return range(n * PIECES // STAGES, (n + 1) * PIECES // STAGES)

    @pl.when(me.native)
    def _():
        for n in range(PIECES):
            pass_on(n)

    @pl.when(foreign)
    def _():
        weight.wait_recv()
        for j in range(1, groups):
            weight_share(j).start()
        for n in range(PIECES):
            share(n)
        for j in range(1, groups):
            weight_in(j).wait_recv()
        for n in range(PIECES):
            from_sibling(n)

    for j in range(3):
        unit_z(j).start()

    @pl.when(foreign)
    def _():
        scenes.wait_recv()

    describe_scenes(ids_own, id_row, id_column, before)
    compute(0, 1, 2)

    @pl.when(foreign)
    def _():
        for n in stage(0):
            pass_on(n)

    compute(2, 1, 2)

    @pl.when(foreign)
    def _():
        for n in stage(1):
            pass_on(n)

    @pl.when(me.native)
    def _():
        for n in stage(0):
            from_sibling(n)

    compute(4, 1, 1)

    @pl.when(me.native)
    def _():
        for n in stage(1):
            from_sibling(n)

    compute(5, 2, 2)

    @pl.when(foreign)
    def _():
        for n in stage(2):
            pass_on(n)

    @pl.when(me.native)
    def _():
        for n in stage(2):
            from_sibling(n)

    own_copy = pltpu.make_async_copy(buf.at[pl.ds(pl.multiple_of(me.q * rows, 16), rows)], own, late_s.at[5])
    w_copy = pltpu.make_async_copy(w, w_out, late_s.at[6])
    own_copy.start()
    w_copy.start()
    compute(6, 2, 2)
    for j in range(3):
        unit_z(j).wait_recv()
        unit_z(j).wait_send()

    for j in range(3):
        source = lax.rem(me.m + 3 - j, 4)
        remote(b_ups.at[source], b_ups.at[source], b_s.at[j], b_r.at[j], around[j]).wait_recv()
        give_b_up(j).wait_send()

    @pl.when(me.native)
    def _():
        scenes.wait_send()

    @pl.when(foreign)
    def _():
        weight.wait_send()
        for j in range(1, groups):
            weight_share(j).wait_send()
        for n in range(PIECES):
            swap(n).wait_send()

    for n in range(PIECES):
        cross(me.q, n).wait_send()
        sib(me.q, n).wait_send()
        forward(cross_q, n).wait_send()
    for copy in padding + [own_copy, w_copy]:
        copy.wait()

    def finish_tile(t, _):
        for copy in outputs(t):
            copy.wait()
        return 0

    lax.fori_loop(0, tiles, finish_tile, 0)


def start(tokens, w_qkv, scene_ids, b_up, gain, shift, mine, ndp):
    rows = tokens.shape[0]
    total = 4 * rows
    heads = w_qkv.shape[1] // HEAD
    groups = ndp // 2
    w_qkv = w_qkv.reshape(3, groups, -1, D)
    units = (3,) + mine.shape
    wide = total + PAD
    shape = jax.ShapeDtypeStruct
    rowed = (heads, wide, LANES)
    k_cols, v_cols = (heads, HEAD, wide), (heads, HEAD + 16, wide)
    three = DMA((PIECES,))
    return pl.pallas_call(
        functools.partial(start_kernel, heads),
        name="start",
        cost_estimate=work(50),
        in_specs=[VMEM] * 6 + [ANY],
        out_specs=[ANY] * 3 + [VMEM] * 5 + [ANY] * 7,
        out_shape=[
            shape((total, D), BF16),
            shape((rows, D), BF16),
            shape(w_qkv.shape, BF16),
            shape(scene_ids.shape, jnp.int32),
            shape((1, wide), jnp.int32),
            shape((wide, 1), jnp.int32),
            shape((1, LANES), jnp.int32),
            shape((4, 1) + b_up.shape, F32),
            shape((total, D), BF16),
            shape(rowed, BF16),
            shape(rowed, BF16),
            shape(rowed, BF16),
            shape(k_cols, BF16),
            shape(v_cols, BF16),
            shape(units, BF16),
        ],
        scratch_shapes=[
            pltpu.VMEM((total, D), BF16),
            pltpu.VMEM(w_qkv.shape, BF16),
            pltpu.VMEM((total, D), BF16),
            pltpu.VMEM(rowed, BF16),
            pltpu.VMEM(rowed, BF16),
            pltpu.VMEM(rowed, BF16),
            pltpu.VMEM(k_cols, BF16),
            pltpu.VMEM(v_cols, BF16),
        ]
        + [three] * 8
        + [DMA((groups,))] * 2
        + [DMA] * 2
        + [DMA((3,))] * 2
        + [DMA((total // TILE, 7)), DMA((7,))]
        + [DMA((3,))] * 2,
        compiler_params=pltpu.CompilerParams(
            collective_id=1, has_side_effects=True, vmem_limit_bytes=60 << 20
        ),
    )(tokens, w_qkv, scene_ids, b_up, gain, shift, mine)


BLOCK = 256
STEP = 512


def blocks(total):
    return -(-total // BLOCK)


def block_range(i, numbers, before):
    lines = numbers.shape[0]
    per = BLOCK // LANES
    top, bottom = numbers[i * per, 0], numbers[jnp.minimum(i * per + per, lines) - 1, LANES - 1]
    bottom = jnp.where(i * per + per > lines, -1, bottom)
    low = jnp.where(top >= 0, before[0, jnp.maximum(top, 0)], i * BLOCK)
    high = jnp.where(bottom >= 0, before[0, jnp.maximum(bottom, 0) + 1], i * BLOCK + BLOCK)
    return low // LANES, (high + LANES - 1) // LANES


def list_steps(count, numbers, before, total, block_at, step_at, marks):
    stride = STEP // LANES

    def one_block(i, n):
        first, last = block_range(i, numbers, before)
        steps = (last - first + stride - 1) // stride

        def put(j, n):
            block_at[n] = i * (BLOCK // LANES)
            step_at[n] = first + j * stride
            marks[n] = jnp.where(j == 0, 1, 0) + jnp.where(j == steps - 1, 2, 0)
            return n + 1

        return lax.fori_loop(0, steps, put, n)

    n = lax.fori_loop(0, count, one_block, 0)
    for idle in range(2):
        block_at[n + idle] = 0
        step_at[n + idle] = total // LANES
        marks[n + idle] = 0
    return n


def step_lists(total):
    return [pltpu.SMEM((blocks(total) * (-(-total // STEP) + 1) + 2,), jnp.int32)] * 3


def attention_kernel(
    heads, total, numbers, before, idc, idr, q, k, vt, out, lse, block_at, step_at, marks, even, odd
):
    count = list_steps(blocks(total), numbers, before, total, block_at, step_at, marks)

    def place(i):
        rows = pl.ds(pl.multiple_of(block_at[i] * LANES, LANES), BLOCK)
        return rows, pl.ds(pl.multiple_of(step_at[i] * LANES, LANES), STEP)

    def score(i, buf, h):
        rows, cols = place(i)
        s = jnp.where(idc[cols, :] == idr[:, rows], dot(k[h, cols, :], q[h, rows, :], NT), MASKED)
        buf[h] = s
        return jnp.max(s, axis=0, keepdims=True)

    def step(i, now, after, carry):
        rows, cols = place(i)
        mark = marks[i]
        new = []
        for h in range(heads):
            top, acc, highest = carry[h]
            upcoming = score(i + 1, after, h)
            top = jnp.where(lax.rem(mark, 2) == 1, MASKED, top)
            above = jnp.maximum(top, highest)
            p = jnp.exp(now[h] - above).astype(BF16)
            acc = acc * jnp.exp(top - above) + dot(vt[h, :, cols], p)
            new.append((above, acc, upcoming))

        @pl.when(mark >= 2)
        def _():
            valid = jnp.where(idr[:, rows] >= 0, 1.0, 0.0)
            mixed = []
            for h in range(heads):
                top, acc, _ = new[h]
                row_total = acc[HEAD : HEAD + 1]
                mixed.append(acc[:HEAD] * (valid / row_total))
                lse[pl.ds(h, 1), rows] = top + jnp.log(row_total)
            out[rows, :] = jnp.concatenate(mixed, axis=0).T.astype(BF16)

        return tuple(new)

    low = jnp.full((1, BLOCK), MASKED, F32)
    start = tuple((low, jnp.zeros((vt.shape[1], BLOCK), F32), score(0, even, h)) for h in range(heads))

    def two_steps(n, carry):
        return step(2 * n + 1, odd, even, step(2 * n, even, odd, carry))

    lax.fori_loop(0, (count + 1) // 2, two_steps, start)


def attention(ids, q, k, vt):
    heads, wide, _ = q.shape
    total = wide - PAD
    rows = blocks(total) * BLOCK
    scores = pltpu.VMEM((heads, STEP, BLOCK), F32)
    return pl.pallas_call(
        functools.partial(attention_kernel, heads, total),
        name="attention",
        cost_estimate=work(31),
        in_specs=[SMEM] * 2 + [VMEM] * 5,
        out_specs=[VMEM, VMEM],
        out_shape=[
            jax.ShapeDtypeStruct((rows, heads * HEAD), BF16),
            jax.ShapeDtypeStruct((heads, wide), F32),
        ],
        scratch_shapes=step_lists(total) + [scores, scores],
        compiler_params=limit(56),
    )(*ids, q, k, vt)


def in_steps(first, last, body, carry):
    wide, narrow = 2 * BLOCK // LANES, BLOCK // LANES
    count = (last - first + narrow - 1) // narrow
    carry = lax.fori_loop(0, count // 2, lambda n, c: body(2 * BLOCK, first + n * wide, c), carry)
    return lax.fori_loop(0, count % 2, lambda n, c: body(BLOCK, first + (count - 1) * narrow, c), carry)


def attention_back_kernel(
    heads, total, numbers, before, idc, idr, q_in, k_in, v_in, kt_in, out, grad, lse, dproj,
    q, k, v, kt, made, g, delta, dq, in_s, out_s,
):
    wide = q.shape[1]
    width = heads * HEAD
    head_of = lax.broadcasted_iota(jnp.int32, (8, width), 1) // HEAD
    pick = jnp.where(head_of == lax.broadcasted_iota(jnp.int32, (8, width), 0), 1.0, 0.0).astype(BF16)
    none = jnp.zeros((TILE, LANES - HEAD), BF16)
    arriving = [
        pltpu.make_async_copy(src, dst, in_s.at[i])
        for i, (src, dst) in enumerate(((q_in, q), (k_in, k), (v_in, v), (kt_in, kt)))
    ]
    for copy in arriving:
        copy.start()

    def prepare(i, _):
        rows = pl.ds(pl.multiple_of(i * TILE, LANES), TILE)
        grads = jnp.where(idc[rows, :] >= 0, grad[rows, :].astype(F32), 0.0)
        inner = grads * out[rows, :].astype(F32)
        high = inner.astype(BF16)
        rest = (inner - high.astype(F32)).astype(BF16)
        delta[:, rows] = dot(pick, high, NT) + dot(pick, rest, NT)
        grads = grads.astype(BF16)
        for h in range(heads):
            g[h, rows, :] = jnp.concatenate([grads[:, h * HEAD : (h + 1) * HEAD], none], axis=1)
            dq[h, :, rows] = jnp.zeros((HEAD, TILE), F32)
        return 0

    lax.fori_loop(0, total // TILE, prepare, 0)
    tail = wide - total
    delta[:, total:] = jnp.zeros((8, tail), F32)
    for h in range(heads):
        g[h, total:, :] = jnp.zeros((tail, LANES), BF16)
        dq[h, :, total:] = jnp.zeros((HEAD, tail), F32)

    for copy in arriving:
        copy.wait()

    def give(i):
        cols = pl.ds(pl.multiple_of(i * BLOCK, LANES), BLOCK)
        return pltpu.make_async_copy(made.at[1:3, cols], dproj.at[1:3, cols], out_s.at[i])

    def one_block(i, _):
        c0 = pl.multiple_of(i * BLOCK, LANES)
        cols = pl.ds(c0, BLOCK)
        mine = idc[cols, :]
        low, high = block_range(i, numbers, before)

        def queries(size, at, carry):
            rows = pl.ds(pl.multiple_of(at * LANES, LANES), size)
            allowed = mine == idr[:, rows]
            both = [
                (dot(k[h, cols, :], q[h, rows, :], NT), dot(v[h, cols, :], g[h, rows, :], NT)) for h in range(heads)
            ]
            new = []
            for h in range(heads):
                dk, dv = carry[h]
                s, dp = both[h]
                p = jnp.where(allowed, jnp.exp(s - lse[h : h + 1, rows]), 0.0)
                ds = (p * (dp - delta[h : h + 1, rows])).astype(BF16)
                dv = dv + dot(p.astype(BF16), g[h, rows, :])
                dk = dk + dot(ds, q[h, rows, :])
                dq[h, :, rows] += dot(kt[h, :, cols], ds)
                new.append((dk, dv))
            return tuple(new)

        zero = jnp.zeros((BLOCK, LANES), F32)
        done = in_steps(low, high, queries, tuple((zero, zero) for _ in range(heads)))
        for part in range(2):
            joined = jnp.concatenate([done[h][part][:, :HEAD] for h in range(heads)], axis=1)
            made[part + 1, cols, :] = joined.astype(BF16)
        give(i).start()
        return 0

    lax.fori_loop(0, blocks(total), one_block, 0)

    def finish(i, _):
        rows = pl.ds(pl.multiple_of(i * TILE, LANES), TILE)
        joined = jnp.concatenate([dq[h, :, rows] for h in range(heads)], axis=0)
        made[0, rows, :] = (joined * HEAD**-0.5).T.astype(BF16)
        give_q(i).start()
        return 0

    def give_q(i):
        rows = pl.ds(pl.multiple_of(i * TILE, LANES), TILE)
        return pltpu.make_async_copy(made.at[0, rows], dproj.at[0, rows], out_s.at[blocks(total) + i])

    lax.fori_loop(0, total // TILE, finish, 0)
    for i in range(blocks(total)):
        give(i).wait()
    for i in range(total // TILE):
        give_q(i).wait()


def attention_back(ids, q, k, v, kt, out, grad, lse):
    heads, wide, _ = q.shape
    total = wide - PAD
    return pl.pallas_call(
        functools.partial(attention_back_kernel, heads, total),
        name="attention_back",
        cost_estimate=work(51),
        in_specs=[SMEM] * 2 + [VMEM] * 2 + [ANY] * 4 + [VMEM] * 3,
        out_specs=ANY,
        out_shape=jax.ShapeDtypeStruct((3, blocks(total) * BLOCK, heads * HEAD), BF16),
        scratch_shapes=[
            pltpu.VMEM(q.shape, BF16),
            pltpu.VMEM(k.shape, BF16),
            pltpu.VMEM(v.shape, BF16),
            pltpu.VMEM(kt.shape, BF16),
            pltpu.VMEM((3, blocks(total) * BLOCK, heads * HEAD), BF16),
            pltpu.VMEM((heads, wide, LANES), BF16),
            pltpu.VMEM((8, wide), F32),
            pltpu.VMEM((heads, HEAD, wide), F32),
            DMA((4,)),
            DMA((blocks(total) + total // TILE,)),
        ],
        compiler_params=limit(60),
    )(*ids, q, k, v, kt, out, grad, lse)


ROWS_MID = 288


def middle_kernel(
    attended, tok, cot, cot_came, b_out, gain, shift, b_up, b_down, w_out, w_down, w_up_t, *rest
):
    me = Place()
    groups = len(rest) - 29
    weights = rest[:groups]
    layer_out, grad_mid, grad_heads, cells = rest[groups : groups + 4]
    (
        att, grad_att, w, acc, vec, bup, came, low_all, cot_all, back_all, active_all, hidden_all,
        att_s, att_r, own_s, grad_s, grad_r, back_s, unit_s, push_s, push_r, sum_s, sum_r, cell_s, shard_s,
    ) = rest[groups + 4 :]
    group = me.d // 2
    others_of, piece, _ = weights[0].shape
    parts = b_up.shape[0]
    rows = tok.shape[0]
    tiles = rows // ROWS_MID
    width = att.shape[2]
    others = [lax.rem(me.q + k, 4) for k in range(1, 4)]
    greet([me.member(quarter) for quarter in others])

    def tile(t, quarter=0):
        return pl.ds(pl.multiple_of(quarter * rows + t * ROWS_MID, 16), ROWS_MID)

    def att_to(k, t):
        return remote(
            attended.at[tile(t, others[k])], att.at[me.q, tile(t)], att_s.at[k, t], att_r.at[k, t], me.member(others[k])
        )

    def att_from(k, t):
        source = others[2 - k]
        return remote(
            attended.at[tile(t)], att.at[source, tile(t)], att_s.at[k, t], att_r.at[k, t], me.member(source)
        )

    def att_own(t):
        return pltpu.make_async_copy(attended.at[tile(t, me.q)], att.at[me.q, tile(t)], own_s.at[t])

    def grad_to(k, t):
        return remote(
            grad_att.at[others[k], tile(t)], grad_heads.at[tile(t, me.q)], grad_s.at[k, t], grad_r.at[k, t], me.member(others[k])
        )

    def grad_from(k, t):
        source = others[2 - k]
        return remote(
            grad_att.at[source, tile(t)], grad_heads.at[tile(t, source)], grad_s.at[k, t], grad_r.at[k, t], me.member(source)
        )

    def grad_own(t):
        return pltpu.make_async_copy(grad_att.at[me.q, tile(t)], grad_heads.at[tile(t, me.q)], back_s.at[t])

    for t in range(tiles):
        for k in (1, 0, 2):
            att_to(k, t).start()
        att_own(t).start()

    own_shard = [
        pltpu.make_async_copy(src, w.at[me.m, at], shard_s.at[i])
        for i, (src, at) in enumerate(
            (
                (w_out, pl.ds(0, OUT_ROWS)),
                (w_down, pl.ds(OUT_ROWS, UP_ROWS)),
                (w_up_t, pl.ds(OUT_ROWS + UP_ROWS, UP_ROWS)),
            )
        )
    ]

    def w_rows(j, k, core):
        source = 2 * lax.rem(group + groups - j, groups) + core
        return w.at[lax.rem(me.m + 1 + k, 4), pl.ds(pl.multiple_of(source * piece, 16), piece)]

    def load(j, k):
        return pltpu.make_async_copy(weights[j].at[k], w_rows(j, k, me.c), unit_s.at[j, k])

    def push(j, k):
        return remote(weights[j].at[k], w_rows(j, k, me.c), push_s.at[j, k], push_r.at[j, k], me.sibling)

    def pushed(j, k):
        return remote(weights[j].at[k], w_rows(j, k, 1 - me.c), push_s.at[j, k], push_r.at[j, k], me.sibling)

    each = [(j, k) for j in range(groups) for k in range(others_of)]
    for j, k in each:
        push(j, k).start()
        load(j, k).start()
    for copy in own_shard:
        copy.start()
    for ref in (vec, bup):
        ref[...] = jnp.zeros_like(ref)
    for copy in own_shard:
        copy.wait()
    for j, k in each:
        load(j, k).wait()
        pushed(j, k).wait_recv()

    out_rows = slice(0, OUT_ROWS)
    down_rows = slice(OUT_ROWS, OUT_ROWS + UP_ROWS)
    up_rows = slice(OUT_ROWS + UP_ROWS, VEC_AT)

    def one_tile(t, _):
        here = tile(t)
        att_own(t).wait()
        for k in range(3):
            att_from(k, t).wait_recv()
        atts = [att[v, here, :] for v in range(parts)]
        middle = tok[here, :].astype(F32) + line(b_out)
        for v in range(parts):
            middle = middle + dot(atts[v], w[v, out_rows])
        unit, scale = normalise(middle)
        low = (unit * line(gain) + line(shift)).astype(BF16)
        cot_low = jnp.where(me.native, cot[here, :], cot_came[here, :])
        low_all[here, :] = low
        cot_all[here, :] = cot_low
        cot_full = cot_low.astype(F32)
        out = middle + line(b_down)
        grad_norm = jnp.zeros_like(middle)

        def products(v):
            return dot(low, w[v, up_rows], NT), dot(cot_low, w[v, down_rows], NT)

        upcoming = products(0)
        for v in range(parts):
            hidden, grad_active = upcoming
            if v + 1 < parts:
                upcoming = products(v + 1)
            hidden = hidden + b_up[v]
            below = 0.5 * (1.0 + lax.erf(hidden * 0.5**0.5))
            density = jnp.exp(-0.5 * hidden * hidden) * 0.3989422804014327
            active = (hidden * below).astype(BF16)
            grad_hidden = (grad_active * (below + hidden * density)).astype(BF16)
            out = out + dot(active, w[v, down_rows])
            grad_norm = grad_norm + dot(grad_hidden, w[v, up_rows])
            active_all[v, here, :] = active
            hidden_all[v, here, :] = grad_hidden
            bup[v] += jnp.sum(grad_hidden.astype(F32), axis=0, keepdims=True)
        layer_out[here, :] = out.astype(BF16)
        scaled = grad_norm * line(gain)
        back = cot_full + scale * (
            scaled
            - jnp.mean(scaled, axis=-1, keepdims=True)
            - unit * jnp.mean(scaled * unit, axis=-1, keepdims=True)
        )
        grad_mid[here, :] = back
        back_low = back.astype(BF16)
        back_all[here, :] = back_low
        for v in range(parts):
            grad_att[v, here, :] = dot(back_low, w[v, out_rows], NT).astype(BF16)
        for k in (1, 0, 2):
            grad_to(k, t).start()
        grad_own(t).start()
        vec[0:1] += jnp.sum(grad_norm * unit, axis=0, keepdims=True)
        vec[1:2] += jnp.sum(grad_norm, axis=0, keepdims=True)
        vec[2:3] += jnp.sum(back, axis=0, keepdims=True)
        vec[3:4] += jnp.sum(cot_full, axis=0, keepdims=True)
        return 0

    lax.fori_loop(0, tiles, one_tile, 0)

    def sum_rows(i, core):
        return pl.ds(pl.multiple_of((2 * i + core) * piece, 16), piece)

    def give(i):
        return remote(w.at[:, sum_rows(i, 1 - me.c)], came.at[i], sum_s.at[i], sum_r.at[i], me.sibling)

    def keep(i):
        return pltpu.make_async_copy(w.at[:, sum_rows(i, me.c)], cells.at[i], cell_s.at[i])

    for v in range(parts):
        acc[v, out_rows] = dot(att[v], back_all[...], TN)
        acc[v, down_rows] = dot(active_all[v], cot_all[...], TN)
        acc[v, up_rows] = dot(hidden_all[v], low_all[...], TN)
        acc[v, VEC_AT:] = jnp.zeros((UNITS - VEC_AT, D), F32)
        acc[v, VEC_AT : VEC_AT + 8] = vec[...]
        acc[v, VEC_AT + 4 : VEC_AT + 5, :UP_ROWS] = bup[v]
    for i in range(groups):
        for v in range(parts):
            w[v, sum_rows(i, 1 - me.c), :] = acc[v, sum_rows(i, 1 - me.c), :].astype(BF16)
        give(i).start()
    for i in range(groups):
        give(i).wait_recv()
        for v in range(parts):
            w[v, sum_rows(i, me.c), :] = (acc[v, sum_rows(i, me.c), :] + came[i, v].astype(F32)).astype(BF16)
        keep(i).start()
    for t in range(tiles):
        for k in range(3):
            grad_from(k, t).wait_recv()
            grad_to(k, t).wait_send()
            att_to(k, t).wait_send()
        grad_own(t).wait()
    for j, k in each:
        push(j, k).wait_send()
    for i in range(groups):
        give(i).wait_send()
        keep(i).wait()


def middle_part(attended, tok, cot, cot_came, b_out, gain, shift, b_up, b_down, shard, weights):
    rows = tok.shape[0]
    width = attended.shape[1]
    groups = len(weights)
    parts, piece = b_up.shape[0], weights[0].shape[1]
    tiles = rows // ROWS_MID
    shape = jax.ShapeDtypeStruct
    halves = (groups, parts, piece, D)
    return pl.pallas_call(
        middle_kernel,
        name="middle_part",
        cost_estimate=work(50),
        in_specs=[ANY] + [VMEM] * 8 + [ANY] * (len(shard) + groups),
        out_specs=[VMEM, VMEM, ANY, ANY],
        out_shape=[
            shape((rows, D), BF16),
            shape((rows, D), F32),
            shape((4 * rows, width), BF16),
            shape(halves, BF16),
        ],
        scratch_shapes=[
            pltpu.VMEM((parts, rows, width), BF16),
            pltpu.VMEM((parts, rows, width), BF16),
            pltpu.VMEM((parts, UNITS, D), BF16),
            pltpu.VMEM((parts, UNITS, D), F32),
            pltpu.VMEM((8, D), F32),
            pltpu.VMEM((parts, 1, UP_ROWS), F32),
            pltpu.VMEM(halves, BF16),
            pltpu.VMEM((rows, D), BF16),
            pltpu.VMEM((rows, D), BF16),
            pltpu.VMEM((rows, D), BF16),
            pltpu.VMEM((parts, rows, UP_ROWS), BF16),
            pltpu.VMEM((parts, rows, UP_ROWS), BF16),
            DMA((3, tiles)),
            DMA((3, tiles)),
            DMA((tiles,)),
            DMA((3, tiles)),
            DMA((3, tiles)),
            DMA((tiles,)),
        ]
        + [DMA((groups, weights[0].shape[0]))] * 3
        + [DMA((groups,))] * 3
        + [DMA((len(shard),))],
        compiler_params=pltpu.CompilerParams(
            collective_id=2, has_side_effects=True, vmem_limit_bytes=48 << 20
        ),
    )(attended, tok, cot, cot_came, b_out, gain, shift, b_up, b_down, *shard, *weights)


CUTS = 3


def finish_kernel(
    dproj_in, normed_in, full_in, w, grad_mid, gain, cells, grad, vec_sum, d_w, sums,
    dproj, normed, full, part, theirs, sent, crossed, low, acc, w_part, w_in, w_z, vec, vz, vd, u_in, u_own,
    load_s, out_s, sib_s, sib_r, cross_s, cross_r, swap_s, swap_r, vz_s, vz_r, vd_s, vd_r,
    ws_s, ws_r, wz_s, wz_r, wg_s, wg_r, wf_s, wf_r, uz_s, uz_r, ug_s, ug_r, uf_s, uf_r,
):
    me = Place()
    foreign = jnp.logical_not(me.native)
    rows = grad_mid.shape[0]
    piece = rows // CUTS
    width = w.shape[1]
    ndp = vd.shape[0]
    groups, w_rows, _ = w_part.shape
    group = me.d // 2

    order = [2 * (1 - me.hf) + 1 - me.r, 2 * (1 - me.hf) + me.r, 2 * me.hf + 1 - me.r, 2 * me.hf + me.r]

    def span_of(k, p):
        return pl.ds(pl.multiple_of(order[k] * rows + p * piece, 16), piece)

    def loads(k, p):
        span = span_of(k, p)
        pairs = ((dproj_in.at[:, span], dproj.at[:, span]), (normed_in.at[span], normed.at[span]), (full_in.at[span], full.at[span]))
        return [pltpu.make_async_copy(src, dst, load_s.at[k, p, j]) for j, (src, dst) in enumerate(pairs)]

    for k in range(4):
        for p in range(CUTS):
            for copy in loads(k, p):
                copy.start()

    around = [(me.d, lax.rem(me.m + k, 4)) for k in range(1, 4)]
    along = [(lax.rem(me.d + k, ndp), me.m) for k in range(1, ndp)]
    greet([me.partner] + around + along)

    def to_sib(k, p):
        slot = k % 2
        return remote(part.at[k, p], theirs.at[slot, p], sib_s.at[slot, p], sib_r.at[slot, p], me.sibling)

    def to_cross(p):
        return remote(sent.at[p], crossed.at[p], cross_s.at[p], cross_r.at[p], me.cross)

    def to_partner(p):
        return remote(low.at[p], grad.at[p], swap_s.at[p], swap_r.at[p], me.partner)

    def keep(p):
        return pltpu.make_async_copy(low.at[p], grad.at[p], out_s.at[p])

    def unit_z(j):
        to = lax.rem(me.m + 1 + j, 4)
        return remote(cells.at[to], u_in.at[j], uz_s.at[j], uz_r.at[j], around[j])

    def unit_give(j):
        to = (2 * lax.rem(group + j, groups) + me.c, me.m)
        return remote(u_own, sums.at[me.d], ug_s.at[j], ug_r.at[j], to)

    def unit_give_in(j):
        source = 2 * lax.rem(group + groups - j, groups) + me.c
        return remote(u_own, sums.at[source], ug_s.at[j], ug_r.at[j], (source, me.m))

    def unit_forward(j):
        source = 2 * lax.rem(group + groups - j, groups) + me.c
        src = u_own if j == 0 else sums.at[source]
        return remote(src, sums.at[source], uf_s.at[j], uf_r.at[j], me.sibling)

    def unit_forward_in(j):
        source = 2 * lax.rem(group + groups - j, groups) + 1 - me.c
        return remote(u_own, sums.at[source], uf_s.at[j], uf_r.at[j], me.sibling)

    vec[...] = jnp.zeros_like(vec)

    def compute(k):
        def one(p, _):
            span = span_of(k, p)
            for copy in loads(k, p):
                copy.wait()
            total = jnp.zeros((piece, D), F32)
            for c in range(3):
                total = total + dot(dproj[c, span, :], w[c])
            part[k, p] = total.astype(BF16)

            @pl.when(me.native if k < 2 else foreign)
            def _():
                to_sib(k, p).start()

            return 0

        lax.fori_loop(0, CUTS, one, 0)

    def pass_across(k):
        for p in range(CUTS):
            to_sib(k, p).wait_recv()
            sent[p] = (part[k, p].astype(F32) + theirs[0, p].astype(F32)).astype(BF16)
            to_cross(p).start()

    def conclude(k, p):
        to_sib(k, p).wait_recv()
        to_cross(p).wait_recv()
        total = part[k, p].astype(F32) + theirs[1, p].astype(F32) + crossed[p].astype(F32)
        span = pl.ds(pl.multiple_of(me.q * rows + p * piece, 16), piece)
        unit, scale = normalise(full[span, :].astype(F32))
        vec[0:1] += jnp.sum(total * unit, axis=0, keepdims=True)
        vec[1:2] += jnp.sum(total, axis=0, keepdims=True)
        scaled = total * line(gain)
        result = grad_mid[p * piece : (p + 1) * piece, :] + scale * (
            scaled
            - jnp.mean(scaled, axis=-1, keepdims=True)
            - unit * jnp.mean(scaled * unit, axis=-1, keepdims=True)
        )
        low[p] = result.astype(BF16)

    def conclude_foreign(p):
        conclude(1, p)
        to_partner(p).start()

    compute(0)

    @pl.when(foreign)
    def _():
        pass_across(0)

    compute(1)
    compute(2)

    @pl.when(me.native)
    def _():
        pass_across(2)

    compute(3)
    for j in range(3):
        unit_z(j).start()

    for c in range(3):
        acc[c * width : (c + 1) * width, :] = dot(dproj[c], normed[...], TN)

    for i in range(groups):
        w_part[i] = acc[i * w_rows : (i + 1) * w_rows, :].astype(BF16)

    def other_group(k):
        return lax.rem(group + k, groups)

    def w_send(k):
        to = other_group(k)
        return remote(w_part.at[to], w_in.at[k], ws_s.at[k], ws_r.at[k], (2 * to + me.c, me.m))

    for k in range(1, groups):
        w_send(k).start()

    @pl.when(foreign)
    def _():
        for p in range(2 * CUTS // 3):
            conclude_foreign(p)

    w_sum = w_part[group].astype(F32)
    for k in range(1, groups):
        w_send(k).wait_recv()
        w_sum = w_sum + w_in[k].astype(F32)

    to_z = remote(w_z.at[0], w_z.at[1], wz_s, wz_r, (me.d, lax.rem(me.m + 2, 4)))

    def w_give(k):
        return remote(w_z.at[0], d_w.at[group], wg_s.at[k], wg_r.at[k], (2 * other_group(k) + me.c, me.m))

    def w_give_in(k):
        source = lax.rem(group + groups - k, groups)
        return remote(w_z.at[0], d_w.at[source], wg_s.at[k], wg_r.at[k], (2 * source + me.c, me.m))

    def w_forward(k):
        source = lax.rem(group + groups - k, groups)
        src = w_z.at[0] if k == 0 else d_w.at[source]
        return remote(src, d_w.at[source], wf_s.at[k], wf_r.at[k], me.sibling)

    w_keep = pltpu.make_async_copy(w_z.at[0], d_w.at[group], out_s.at[CUTS])
    unit_keep = pltpu.make_async_copy(u_own, sums.at[me.d], out_s.at[CUTS + 1])

    @pl.when(foreign)
    def _():
        w_z[0] = w_sum.astype(BF16)
        to_z.start()
        for p in range(2 * CUTS // 3, CUTS):
            conclude_foreign(p)

    @pl.when(me.native)
    def _():
        to_z.wait_recv()
        w_z[0] = (w_sum + w_z[1].astype(F32)).astype(BF16)
        w_keep.start()
        for k in range(1, groups):
            w_give(k).start()
        w_forward(0).start()
        for p in range(CUTS):
            conclude(3, p)
            keep(p).start()

    vz[me.m] = vec[...]

    def around_copy(k):
        return remote(vz.at[me.m], vz.at[me.m], vz_s.at[k], vz_r.at[k], around[k])

    for k in range(3):
        around_copy(k).start()

    unit_sum = cells[me.m].astype(F32)
    for j in range(3):
        unit_z(j).wait_recv()
        unit_sum = unit_sum + u_in[j].astype(F32)
    u_own[...] = unit_sum.astype(BF16)
    unit_keep.start()
    for j in range(1, groups):
        unit_give(j).start()
    unit_forward(0).start()

    @pl.when(me.native)
    def _():
        for k in range(1, groups):
            w_give_in(k).wait_recv()
            w_forward(k).start()

    for k in range(3):
        source = lax.rem(me.m + 3 - k, 4)
        remote(vz.at[source], vz.at[source], vz_s.at[k], vz_r.at[k], around[k]).wait_recv()
    vd[me.d] = vz[0] + vz[1] + vz[2] + vz[3]

    def along_copy(k):
        return remote(vd.at[me.d], vd.at[me.d], vd_s.at[k], vd_r.at[k], along[k])

    for k in range(ndp - 1):
        along_copy(k).start()

    for j in range(1, groups):
        unit_give_in(j).wait_recv()
        unit_forward(j).start()
    for k in range(ndp - 1):
        source = lax.rem(me.d + ndp - 1 - k, ndp)
        remote(vd.at[source], vd.at[source], vd_s.at[k], vd_r.at[k], along[k]).wait_recv()
    total = vd[0]
    for i in range(1, ndp):
        total = total + vd[i]
    vec_sum[...] = total
    for j in range(groups):
        unit_forward_in(j).wait_recv()

    @pl.when(foreign)
    def _():
        for k in range(groups):
            source = lax.rem(group + groups - k, groups)
            remote(w_z.at[0], d_w.at[source], wf_s.at[k], wf_r.at[k], me.sibling).wait_recv()
        for p in range(CUTS):
            to_partner(p).wait_recv()
            to_partner(p).wait_send()
            to_sib(2, p).wait_send()
            to_sib(3, p).wait_send()
        to_z.wait_send()

    @pl.when(me.native)
    def _():
        for p in range(CUTS):
            keep(p).wait()
            to_sib(0, p).wait_send()
            to_sib(1, p).wait_send()
        for k in range(1, groups):
            w_give(k).wait_send()
        for k in range(groups):
            w_forward(k).wait_send()
        w_keep.wait()

    for p in range(CUTS):
        to_cross(p).wait_send()
    for k in range(1, groups):
        w_send(k).wait_send()
    for k in range(3):
        around_copy(k).wait_send()
        unit_z(k).wait_send()
    for k in range(ndp - 1):
        along_copy(k).wait_send()
    for j in range(groups):
        unit_forward(j).wait_send()
    for j in range(1, groups):
        unit_give(j).wait_send()
    unit_keep.wait()


def finish(dproj, normed, full, w, grad_mid, gain, cells, ndp):
    rows = grad_mid.shape[0]
    total = full.shape[0]
    piece = rows // CUTS
    pieces = (CUTS, piece, D)
    groups = ndp // 2
    columns = 3 * w.shape[1]
    cut = (groups, columns // groups, D)
    unit = cells.shape[1:]
    shape = jax.ShapeDtypeStruct
    return pl.pallas_call(
        finish_kernel,
        name="finish",
        cost_estimate=work(60),
        in_specs=[ANY] * 3 + [VMEM] * 4,
        out_specs=[ANY, VMEM, ANY, ANY],
        out_shape=[shape(pieces, BF16), shape((8, D), F32), shape(cut, BF16), shape((ndp,) + unit, BF16)],
        scratch_shapes=[
            pltpu.VMEM((3, total, w.shape[1]), BF16),
            pltpu.VMEM((total, D), BF16),
            pltpu.VMEM((total, D), BF16),
            pltpu.VMEM((4,) + pieces, BF16),
            pltpu.VMEM((2,) + pieces, BF16),
            pltpu.VMEM(pieces, BF16),
            pltpu.VMEM(pieces, BF16),
            pltpu.VMEM(pieces, BF16),
            pltpu.VMEM((columns, D), F32),
            pltpu.VMEM(cut, BF16),
            pltpu.VMEM(cut, BF16),
            pltpu.VMEM((2,) + cut[1:], BF16),
            pltpu.VMEM((8, D), F32),
            pltpu.VMEM((4, 8, D), F32),
            pltpu.VMEM((ndp, 8, D), F32),
            pltpu.VMEM((3,) + unit, BF16),
            pltpu.VMEM(unit, BF16),
            DMA((4, CUTS, 3)),
            DMA((CUTS + 2,)),
        ]
        + [DMA((2, CUTS))] * 2
        + [DMA((CUTS,))] * 4
        + [DMA((3,))] * 2
        + [DMA((ndp - 1,))] * 2
        + [DMA((groups,))] * 2
        + [DMA] * 2
        + [DMA((groups,))] * 4
        + [DMA((3,))] * 2
        + [DMA((groups,))] * 4,
        compiler_params=pltpu.CompilerParams(
            collective_id=4, has_side_effects=True, vmem_limit_bytes=60 << 20
        ),
    )(dproj, normed, full, w, grad_mid, gain, cells)


def outputs_kernel(
    layer, layer_came, grads, w_sums, unit_sums, vec_one,
    layer_out, tokens_grad, d_qkv, d_out, d_up, d_down, d_gain_two, d_shift_two, d_b_out, d_b_down, d_b_up, d_gain_one, d_shift_one,
    layer_s, came_s, grads_s, w_s, unit_s, vec_s, grads_f, w_f, unit_f, up_f, in_s, out_s,
):
    me = Place()
    arriving = [
        pltpu.make_async_copy(src, dst, in_s.at[i])
        for i, (src, dst) in enumerate(
            (
                (unit_sums, unit_s),
                (w_sums, w_s),
                (grads, grads_s),
                (layer, layer_s),
                (layer_came, came_s),
                (vec_one, vec_s),
            )
        )
    ]
    for i in (2, 1, 0, 3, 4, 5):
        arriving[i].start()
    leaving = []

    def leave(src, dst):
        copy = pltpu.make_async_copy(src, dst, out_s.at[len(leaving)])
        copy.start()
        leaving.append(copy)

    def flatten(pieces, flat):
        count, height, _ = pieces.shape
        for i in range(count):
            flat[i * height : (i + 1) * height, :] = pieces[i].astype(F32)

    arriving[2].wait()
    flatten(grads_s, grads_f)
    leave(grads_f, tokens_grad)
    arriving[1].wait()
    flatten(w_s, w_f)
    leave(w_f, d_qkv)
    arriving[0].wait()
    flatten(unit_s, unit_f)
    leave(unit_f.at[:OUT_ROWS], d_out)
    leave(unit_f.at[OUT_ROWS : OUT_ROWS + UP_ROWS], d_down)
    for i in (3, 4):
        arriving[i].wait()
    layer_s[...] = jnp.where(me.native, layer_s[...], came_s[...])
    leave(layer_s, layer_out)
    up_f[...] = unit_f[OUT_ROWS + UP_ROWS : VEC_AT, :].T
    leave(up_f, d_up)
    arriving[5].wait()
    for i, ref in enumerate((d_gain_two, d_shift_two, d_b_out, d_b_down)):
        ref[...] = unit_f[VEC_AT + i, :]
    d_b_up[...] = unit_f[VEC_AT + 4, :UP_ROWS]
    d_gain_one[...] = vec_s[0, :]
    d_shift_one[...] = vec_s[1, :]
    for copy in leaving:
        copy.wait()


def outputs(layer, layer_came, grads, w_sums, unit_sums, vec_one):
    rows = layer.shape[0]
    columns = w_sums.shape[0] * w_sums.shape[1]
    shape = lambda *s: jax.ShapeDtypeStruct(s, F32)
    return pl.pallas_call(
        outputs_kernel,
        name="outputs",
        in_specs=[ANY] * 6,
        out_specs=[ANY] * 6 + [VMEM] * 7,
        out_shape=[
            jax.ShapeDtypeStruct((rows, D), BF16),
            shape(rows, D),
            shape(columns, D),
            shape(OUT_ROWS, D),
            shape(D, UP_ROWS),
            shape(UP_ROWS, D),
            shape(D),
            shape(D),
            shape(D),
            shape(D),
            shape(UP_ROWS),
            shape(D),
            shape(D),
        ],
        scratch_shapes=[
            pltpu.VMEM(layer.shape, BF16),
            pltpu.VMEM(layer.shape, BF16),
            pltpu.VMEM(grads.shape, BF16),
            pltpu.VMEM(w_sums.shape, BF16),
            pltpu.VMEM(unit_sums.shape, BF16),
            pltpu.VMEM(vec_one.shape, F32),
            pltpu.VMEM((rows, D), F32),
            pltpu.VMEM((columns, D), F32),
            pltpu.VMEM((UNITS, D), F32),
            pltpu.VMEM((D, UP_ROWS), F32),
            DMA((6,)),
            DMA((6,)),
        ],
        compiler_params=limit(60),
    )(layer, layer_came, grads, w_sums, unit_sums, vec_one)


def swap_pairs(ndp):
    return [
        (d * 4 + m, (d ^ 1) * 4 + (m + 2) % 4) for d in range(ndp) for m in range(4) if d % 2 != m // 2
    ]


def weight_piece(w_out, w_up, w_down, ndp):
    block = jnp.concatenate([w_out, w_down, w_up.T, jnp.zeros((UNITS - w_out.shape[0] - 2 * w_down.shape[0], D), BF16)])
    piece = UNITS // ndp
    return lax.dynamic_slice_in_dim(block, lax.axis_index("dp") * piece, piece, 0)


def from_other_pairs(block, ndp):
    groups = ndp // 2
    blocks_of = [block]
    for j in range(1, groups):
        pairs = [(d, 2 * ((d // 2 + j) % groups) + d % 2) for d in range(ndp)]
        blocks_of.append(lax.ppermute(block, "dp", pairs))
    return blocks_of


def sum_over_pairs(cells, ndp):
    cores = [[d for d in range(ndp) if d % 2 == core] for core in range(2)]
    return lax.psum_scatter(cells.reshape(-1, D), "dp", scatter_dimension=0, tiled=True, axis_index_groups=cores)


def shards(
    tokens,
    scene_ids,
    gain_one,
    shift_one,
    w_qkv,
    w_out,
    b_out,
    gain_two,
    shift_two,
    w_up,
    b_up,
    w_down,
    b_down,
    cotangent,
    ndp,
):
    both = ("dp", "mp")
    swap = swap_pairs(ndp)
    w_qkv = jnp.swapaxes(w_qkv, 1, 2)
    full, own_tok, w_mine, numbers, id_row, id_column, before, b_ups, normed, q, k, v, kt, vt, weights = start(
        tokens, w_qkv, scene_ids.reshape(-1, LANES), b_up, gain_one, shift_one, weight_piece(w_out, w_up, w_down, ndp), ndp
    )
    w_mine = w_mine.reshape(w_qkv.shape)
    ids = numbers, before, id_column, id_row
    weights = from_other_pairs(weights, ndp)
    sent_cot, q = lax.optimization_barrier((cotangent, q))
    cot_came = lax.ppermute(sent_cot, both, swap)
    attended, lse = attention(ids, q, k, vt)
    layer, grad_mid, grad_heads, cells = middle_part(
        attended, own_tok, cotangent, cot_came, b_out, gain_two, shift_two, b_ups, b_down, (w_out, w_down, w_up.T), weights
    )
    sent_out, grad_heads = lax.optimization_barrier((layer, grad_heads))
    layer_came = lax.ppermute(sent_out, both, swap)
    cells = sum_over_pairs(cells, ndp)
    dproj = attention_back(ids, q, k, v, kt, attended, grad_heads, lse)
    cells, dproj = lax.optimization_barrier((cells, dproj))
    grads, vec_one, w_sums, unit_sums = finish(
        dproj, normed, full, w_mine, grad_mid, gain_one, cells.reshape(4, -1, D), ndp
    )
    (
        layer_out, tokens_grad, d_qkv, d_out, d_up, d_down, d_gain_two, d_shift_two, d_b_out, d_b_down, d_b_up, d_gain_one, d_shift_one,
    ) = outputs(layer, layer_came, grads, w_sums, unit_sums, vec_one)
    return (
        layer_out,
        tokens_grad,
        d_gain_one,
        d_shift_one,
        jnp.swapaxes(d_qkv.reshape(w_qkv.shape), 1, 2),
        d_out,
        d_b_out,
        d_gain_two,
        d_shift_two,
        d_up,
        d_b_up,
        d_down,
        d_b_down,
    )


def solution(mesh):
    ndp = mesh.shape["dp"]
    return jax.shard_map(
        functools.partial(shards, ndp=ndp),
        mesh=mesh,
        in_specs=(
            P(("dp", "mp"), None),
            P("dp"),
            P(),
            P(),
            P(None, None, "mp"),
            P("mp", None),
            P(),
            P(),
            P(),
            P(None, "mp"),
            P("mp"),
            P("mp", None),
            P(),
            P(("dp", "mp"), None),
        ),
        out_specs=(
            P(("dp", "mp"), None),
            P(("dp", "mp"), None),
            P(),
            P(),
            P(None, None, "mp"),
            P("mp", None),
            P(),
            P(),
            P(),
            P(None, "mp"),
            P("mp"),
            P("mp", None),
            P(),
        ),
        check_vma=False,
    )
```

```python
import functools

import jax
import jax.numpy as jnp
from jax import lax
from jax.experimental import pallas as pl
from jax.experimental.pallas import tpu as pltpu
from jax.sharding import PartitionSpec as P

HEAD = 64
D = 768
FF = 1536
LANES = 128
PAD = 512
OUT_ROWS = D // 4
UP_ROWS = FF // 4
VEC_AT = OUT_ROWS + 2 * UP_ROWS
UNITS = 1024
EPS = 1e-05
MASKED = -1e30
MESH = pl.DeviceIdType.MESH
F32 = jnp.float32
BF16 = jnp.bfloat16
VMEM = pl.BlockSpec(memory_space=pltpu.VMEM)
SMEM = pl.BlockSpec(memory_space=pltpu.SMEM)
ANY = pl.BlockSpec(memory_space=pl.ANY)
DMA = pltpu.SemaphoreType.DMA

NN = (((1,), (0,)), ((), ()))
NT = (((1,), (1,)), ((), ()))
TN = (((0,), (0,)), ((), ()))


def dot(a, b, dims=NN):
    return lax.dot_general(a, b, dims, preferred_element_type=F32)


def work(us):
    return pl.CostEstimate(flops=us * 10**9, bytes_accessed=us * 3 * 10**6, transcendentals=0)


def limit(mib):
    return pltpu.CompilerParams(vmem_limit_bytes=mib << 20)


def line(ref):
    return ref[...].reshape(1, -1)


class Place:
    def __init__(self):
        self.d = lax.axis_index("dp")
        self.m = lax.axis_index("mp")
        self.c = lax.rem(self.d, 2)
        self.r = lax.rem(self.m, 2)
        self.hf = self.m // 2
        self.q = 2 * self.c + self.r
        self.native = self.c == self.hf
        self.sibling = (self.d + 1 - 2 * self.c, self.m)
        self.cross = (self.d, self.m + 1 - 2 * self.r)
        self.partner = (self.d + 1 - 2 * self.c, lax.rem(self.m + 2, 4))

    def member(self, quarter):
        return (self.d - self.c + quarter // 2, 2 * self.hf + quarter % 2)


def greet(others):
    barrier = pltpu.get_barrier_semaphore()
    for other in others:
        pl.semaphore_signal(barrier, inc=1, device_id=other, device_id_type=MESH)
    pl.semaphore_wait(barrier, len(others))


def remote(src, dst, send, recv, device):
    return pltpu.make_async_remote_copy(
        src_ref=src, dst_ref=dst, send_sem=send, recv_sem=recv, device_id=device, device_id_type=MESH
    )


STAGES = 3
PIECES = 6
TILE = 384
SCENES = 4


def normalise(x):
    centred = x - jnp.mean(x, axis=-1, keepdims=True)
    scale = lax.rsqrt(jnp.mean(centred * centred, axis=-1, keepdims=True) + EPS)
    return centred * scale, scale


def widen(x, ones, rows):
    lane = lax.broadcasted_iota(jnp.int32, (rows, LANES - HEAD), 1)
    return jnp.concatenate([x, jnp.where(lane < ones, 1.0, 0.0).astype(x.dtype)], axis=1)


def describe_scenes(ids, row, column, before):
    lines = ids.shape[0]
    for j in range(lines):
        place = j * LANES + lax.broadcasted_iota(jnp.int32, (1, LANES), 1)
        number = ids[j : j + 1, :]
        number = jnp.where(number >= 0, number, -1 - place)
        span = slice(j * LANES, (j + 1) * LANES)
        row[:, span] = number
        column[span, :] = jnp.broadcast_to(number.astype(F32), (LANES, LANES)).T[:, :1].astype(jnp.int32)
    rest = row.shape[1] - lines * LANES
    row[:, lines * LANES :] = jnp.full((1, rest), -(1 << 21), jnp.int32)
    column[lines * LANES :, :] = jnp.full((rest, 1), -(1 << 20), jnp.int32)
    lane = lax.broadcasted_iota(jnp.int32, (1, LANES), 1)
    counts = jnp.zeros((1, LANES), F32)
    for number in range(1, SCENES + 1):
        mine = jnp.where((ids[...] >= 0) & (ids[...] < number), 1.0, 0.0)
        total = jnp.sum(jnp.sum(mine, axis=0, keepdims=True), axis=1, keepdims=True)
        counts = jnp.where(lane == number, total, counts)
    before[...] = counts.astype(jnp.int32)


def start_kernel(
    heads, tok, wq, ids, b_up, gain, shift, mine,
    full, own, w_out, ids_own, id_row, id_column, before, b_ups, normed, q, k, v, kt, vt, units,
    buf, w, low_s, q_s, k_s, v_s, kt_s, vt_s,
    swap_s, swap_r, cross_s, cross_r, sib_s, sib_r, fwd_s, fwd_r, w_s, w_r, ids_s, ids_r, b_s, b_r, out_s, late_s,
    uz_s, uz_r,
):
    me = Place()
    foreign = jnp.logical_not(me.native)
    rows = tok.shape[0]
    piece = rows // PIECES
    total = buf.shape[0]
    tiles = total // TILE
    groups = w.shape[1]
    group = me.d // 2
    around = [(me.d, lax.rem(me.m + j, 4)) for j in range(1, 4)]
    lines = [(2 * lax.rem(group + j, groups) + me.c, me.m) for j in range(1, groups)]
    greet([me.sibling, me.partner] + around + lines)

    def rows_of(quarter, n):
        p = jnp.where(me.hf == 0, n, PIECES - 1 - n)
        return pl.ds(pl.multiple_of(quarter * rows + p * piece, 16), piece)

    def part(quarter, n):
        return buf.at[rows_of(quarter, n)]

    sib_q = 2 * (1 - me.c) + me.r
    cross_q = 2 * me.c + 1 - me.r
    sib_cross_q = 2 * (1 - me.c) + 1 - me.r

    def swap(n):
        p = jnp.where(me.hf == 1, n, PIECES - 1 - n)
        src = tok.at[pl.ds(pl.multiple_of(p * piece, 16), piece)]
        dst = buf.at[pl.ds(pl.multiple_of(sib_q * rows + p * piece, 16), piece)]
        return remote(src, dst, swap_s.at[n], swap_r.at[n], me.partner)

    def swap_in(n):
        return remote(part(me.q, n), part(me.q, n), swap_s.at[n], swap_r.at[n], me.partner)

    def cross(quarter, n):
        return remote(part(quarter, n), part(quarter, n), cross_s.at[n], cross_r.at[n], me.cross)

    def sib(quarter, n):
        return remote(part(quarter, n), part(quarter, n), sib_s.at[n], sib_r.at[n], me.sibling)

    def forward(quarter, n):
        return remote(part(quarter, n), part(quarter, n), fwd_s.at[n], fwd_r.at[n], me.sibling)

    weight = remote(wq.at[:, group], w.at[:, group], w_s.at[0], w_r.at[0], me.partner)

    def weight_share(j):
        return remote(w.at[:, group], w.at[:, group], w_s.at[j], w_r.at[j], lines[j - 1])

    def weight_in(j):
        source = lax.rem(group + groups - j, groups)
        return remote(w.at[:, source], w.at[:, source], w_s.at[j], w_r.at[j], lines[j - 1])


    def unit_z(j):
        return remote(mine, units.at[2 - j], uz_s.at[j], uz_r.at[j], around[j])

    def give_b_up(j):
        return remote(b_ups.at[me.m], b_ups.at[me.m], b_s.at[j], b_r.at[j], around[j])

    scenes = remote(ids, ids_own, ids_s, ids_r, me.sibling)
    b_ups[me.m] = line(b_up)
    for j in range(3):
        give_b_up(j).start()

    @pl.when(me.native)
    def _():
        scenes.start()
        buf[pl.ds(pl.multiple_of(me.q * rows, 16), rows), :] = tok[...]
        for n in range(PIECES):
            cross(me.q, n).start()
            sib(me.q, n).start()
        w[...] = wq[...]
        ids_own[...] = ids[...]

    @pl.when(foreign)
    def _():
        weight.start()
        for n in range(PIECES):
            swap(n).start()

    def share(n):
        swap_in(n).wait_recv()
        cross(me.q, n).start()
        sib(me.q, n).start()

    def pass_on(n):
        cross(cross_q, n).wait_recv()
        forward(cross_q, n).start()

    def from_sibling(n):
        sib(sib_q, n).wait_recv()
        forward(sib_cross_q, n).wait_recv()

    def outputs(t):
        span = pl.ds(pl.multiple_of(t * TILE, LANES), TILE)
        pairs = [
            (low_s.at[span], normed.at[span]),
            (buf.at[span], full.at[span]),
            (q_s.at[:, span], q.at[:, span]),
            (k_s.at[:, span], k.at[:, span]),
            (v_s.at[:, span], v.at[:, span]),
            (kt_s.at[:, :, span], kt.at[:, :, span]),
            (vt_s.at[:, :, span], vt.at[:, :, span]),
        ]
        return [pltpu.make_async_copy(src, dst, out_s.at[t, j]) for j, (src, dst) in enumerate(pairs)]

    ones = jnp.where(lax.broadcasted_iota(jnp.int32, (16, TILE), 0) < 1, 1.0, 0.0).astype(BF16)

    def compute(first, stride, count):
        def one(n, _):
            at = first + stride * n
            t = jnp.where(me.hf == 0, at, tiles - 1 - at)
            span = pl.ds(pl.multiple_of(t * TILE, LANES), TILE)
            unit, _ = normalise(buf[span, :].astype(F32))
            low = (unit * line(gain) + line(shift)).astype(BF16)
            low_s[span, :] = low
            qs = (dot(low, w[0].reshape(-1, D), NT).astype(BF16).astype(F32) * HEAD**-0.5).astype(BF16)
            ks = dot(low, w[1].reshape(-1, D), NT)
            vs = dot(low, w[2].reshape(-1, D), NT)
            kts = ks.T.astype(BF16)
            vts = vs.T.astype(BF16)
            ks = ks.astype(BF16)
            vs = vs.astype(BF16)
            for h in range(heads):
                cols = slice(h * HEAD, (h + 1) * HEAD)
                q_s[h, span, :] = widen(qs[:, cols], 0, TILE)
                k_s[h, span, :] = widen(ks[:, cols], 3, TILE)
                v_s[h, span, :] = widen(vs[:, cols], 3, TILE)
                kt_s[h, :, span] = kts[cols]
                vt_s[h, :HEAD, span] = vts[cols]
                vt_s[h, HEAD:, span] = ones
            for copy in outputs(t):
                copy.start()
            return 0

        lax.fori_loop(0, count, one, 0)

    pad = pl.ds(total, PAD)
    zeros = jnp.zeros((heads, PAD, LANES), BF16)
    for ref in (q_s, k_s, v_s):
        ref[:, pad, :] = zeros
    for ref in (kt_s, vt_s):
        ref[:, :, pad] = jnp.zeros((heads, ref.shape[1], PAD), BF16)
    padding = [
        pltpu.make_async_copy(src, dst, late_s.at[j])
        for j, (src, dst) in enumerate(
            [(a.at[:, pad], b.at[:, pad]) for a, b in ((q_s, q), (k_s, k), (v_s, v))]
            + [(a.at[:, :, pad], b.at[:, :, pad]) for a, b in ((kt_s, kt), (vt_s, vt))]
        )
    ]
    for copy in padding:
        copy.start()

    def stage(n):
        return range(n * PIECES // STAGES, (n + 1) * PIECES // STAGES)

    @pl.when(me.native)
    def _():
        for n in range(PIECES):
            pass_on(n)

    @pl.when(foreign)
    def _():
        weight.wait_recv()
        for j in range(1, groups):
            weight_share(j).start()
        for n in range(PIECES):
            share(n)
        for j in range(1, groups):
            weight_in(j).wait_recv()
        for n in range(PIECES):
            from_sibling(n)

    for j in range(3):
        unit_z(j).start()

    @pl.when(foreign)
    def _():
        scenes.wait_recv()

    describe_scenes(ids_own, id_row, id_column, before)
    compute(0, 1, 2)

    @pl.when(foreign)
    def _():
        for n in stage(0):
            pass_on(n)

    compute(2, 1, 2)

    @pl.when(foreign)
    def _():
        for n in stage(1):
            pass_on(n)

    @pl.when(me.native)
    def _():
        for n in stage(0):
            from_sibling(n)

    compute(4, 1, 1)

    @pl.when(me.native)
    def _():
        for n in stage(1):
            from_sibling(n)

    compute(5, 2, 2)

    @pl.when(foreign)
    def _():
        for n in stage(2):
            pass_on(n)

    @pl.when(me.native)
    def _():
        for n in stage(2):
            from_sibling(n)

    own_copy = pltpu.make_async_copy(buf.at[pl.ds(pl.multiple_of(me.q * rows, 16), rows)], own, late_s.at[5])
    w_copy = pltpu.make_async_copy(w, w_out, late_s.at[6])
    own_copy.start()
    w_copy.start()
    compute(6, 2, 2)
    for j in range(3):
        unit_z(j).wait_recv()
        unit_z(j).wait_send()

    for j in range(3):
        source = lax.rem(me.m + 3 - j, 4)
        remote(b_ups.at[source], b_ups.at[source], b_s.at[j], b_r.at[j], around[j]).wait_recv()
        give_b_up(j).wait_send()

    @pl.when(me.native)
    def _():
        scenes.wait_send()

    @pl.when(foreign)
    def _():
        weight.wait_send()
        for j in range(1, groups):
            weight_share(j).wait_send()
        for n in range(PIECES):
            swap(n).wait_send()

    for n in range(PIECES):
        cross(me.q, n).wait_send()
        sib(me.q, n).wait_send()
        forward(cross_q, n).wait_send()
    for copy in padding + [own_copy, w_copy]:
        copy.wait()

    def finish_tile(t, _):
        for copy in outputs(t):
            copy.wait()
        return 0

    lax.fori_loop(0, tiles, finish_tile, 0)


def start(tokens, w_qkv, scene_ids, b_up, gain, shift, mine, ndp):
    rows = tokens.shape[0]
    total = 4 * rows
    heads = w_qkv.shape[1] // HEAD
    groups = ndp // 2
    w_qkv = w_qkv.reshape(3, groups, -1, D)
    units = (3,) + mine.shape
    wide = total + PAD
    shape = jax.ShapeDtypeStruct
    rowed = (heads, wide, LANES)
    k_cols, v_cols = (heads, HEAD, wide), (heads, HEAD + 16, wide)
    three = DMA((PIECES,))
    return pl.pallas_call(
        functools.partial(start_kernel, heads),
        name="start",
        cost_estimate=work(50),
        in_specs=[VMEM] * 6 + [ANY],
        out_specs=[ANY] * 3 + [VMEM] * 5 + [ANY] * 7,
        out_shape=[
            shape((total, D), BF16),
            shape((rows, D), BF16),
            shape(w_qkv.shape, BF16),
            shape(scene_ids.shape, jnp.int32),
            shape((1, wide), jnp.int32),
            shape((wide, 1), jnp.int32),
            shape((1, LANES), jnp.int32),
            shape((4, 1) + b_up.shape, F32),
            shape((total, D), BF16),
            shape(rowed, BF16),
            shape(rowed, BF16),
            shape(rowed, BF16),
            shape(k_cols, BF16),
            shape(v_cols, BF16),
            shape(units, BF16),
        ],
        scratch_shapes=[
            pltpu.VMEM((total, D), BF16),
            pltpu.VMEM(w_qkv.shape, BF16),
            pltpu.VMEM((total, D), BF16),
            pltpu.VMEM(rowed, BF16),
            pltpu.VMEM(rowed, BF16),
            pltpu.VMEM(rowed, BF16),
            pltpu.VMEM(k_cols, BF16),
            pltpu.VMEM(v_cols, BF16),
        ]
        + [three] * 8
        + [DMA((groups,))] * 2
        + [DMA] * 2
        + [DMA((3,))] * 2
        + [DMA((total // TILE, 7)), DMA((7,))]
        + [DMA((3,))] * 2,
        compiler_params=pltpu.CompilerParams(
            collective_id=1, has_side_effects=True, vmem_limit_bytes=60 << 20
        ),
    )(tokens, w_qkv, scene_ids, b_up, gain, shift, mine)


BLOCK = 256
STEP = 512


def blocks(total):
    return -(-total // BLOCK)


def block_range(i, numbers, before):
    lines = numbers.shape[0]
    per = BLOCK // LANES
    top, bottom = numbers[i * per, 0], numbers[jnp.minimum(i * per + per, lines) - 1, LANES - 1]
    bottom = jnp.where(i * per + per > lines, -1, bottom)
    low = jnp.where(top >= 0, before[0, jnp.maximum(top, 0)], i * BLOCK)
    high = jnp.where(bottom >= 0, before[0, jnp.maximum(bottom, 0) + 1], i * BLOCK + BLOCK)
    return low // LANES, (high + LANES - 1) // LANES


def list_steps(count, numbers, before, total, block_at, step_at, marks):
    stride = STEP // LANES

    def one_block(i, n):
        first, last = block_range(i, numbers, before)
        steps = (last - first + stride - 1) // stride

        def put(j, n):
            block_at[n] = i * (BLOCK // LANES)
            step_at[n] = first + j * stride
            marks[n] = jnp.where(j == 0, 1, 0) + jnp.where(j == steps - 1, 2, 0)
            return n + 1

        return lax.fori_loop(0, steps, put, n)

    n = lax.fori_loop(0, count, one_block, 0)
    for idle in range(2):
        block_at[n + idle] = 0
        step_at[n + idle] = total // LANES
        marks[n + idle] = 0
    return n


def step_lists(total):
    return [pltpu.SMEM((blocks(total) * (-(-total // STEP) + 1) + 2,), jnp.int32)] * 3


def attention_kernel(
    heads, total, numbers, before, idc_in, idr, q_in, k_in, vt_in, out, lse,
    idc, q, k, vt, block_at, step_at, marks, even, odd, sems,
):
    arriving = [
        pltpu.make_async_copy(src, dst, sems.at[i])
        for i, (src, dst) in enumerate(((k_in, k), (q_in, q), (idc_in, idc), (vt_in, vt)))
    ]
    for copy in arriving:
        copy.start()
    count = list_steps(blocks(total), numbers, before, total, block_at, step_at, marks)

    def place(i):
        rows = pl.ds(pl.multiple_of(block_at[i] * LANES, LANES), BLOCK)
        return rows, pl.ds(pl.multiple_of(step_at[i] * LANES, LANES), STEP)

    def score(i, buf, h):
        rows, cols = place(i)
        s = jnp.where(idc[cols, :] == idr[:, rows], dot(k[h, cols, :], q[h, rows, :], NT), MASKED)
        buf[h] = s
        return jnp.max(s, axis=0, keepdims=True)

    def step(i, now, after, carry):
        rows, cols = place(i)
        mark = marks[i]
        new = []
        for h in range(heads):
            top, acc, highest = carry[h]
            upcoming = score(i + 1, after, h)
            top = jnp.where(lax.rem(mark, 2) == 1, MASKED, top)
            above = jnp.maximum(top, highest)
            p = jnp.exp(now[h] - above).astype(BF16)
            acc = acc * jnp.exp(top - above) + dot(vt[h, :, cols], p)
            new.append((above, acc, upcoming))

        @pl.when(mark >= 2)
        def _():
            valid = jnp.where(idr[:, rows] >= 0, 1.0, 0.0)
            mixed = []
            for h in range(heads):
                top, acc, _ = new[h]
                row_total = acc[HEAD : HEAD + 1]
                mixed.append(acc[:HEAD] * (valid / row_total))
                lse[pl.ds(h, 1), rows] = top + jnp.log(row_total)
            out[rows, :] = jnp.concatenate(mixed, axis=0).T.astype(BF16)

        return tuple(new)

    for copy in arriving:
        copy.wait()
    low = jnp.full((1, BLOCK), MASKED, F32)
    start = tuple((low, jnp.zeros((vt.shape[1], BLOCK), F32), score(0, even, h)) for h in range(heads))

    def two_steps(n, carry):
        return step(2 * n + 1, odd, even, step(2 * n, even, odd, carry))

    lax.fori_loop(0, (count + 1) // 2, two_steps, start)


def attention(ids, q, k, vt):
    heads, wide, _ = q.shape
    total = wide - PAD
    rows = blocks(total) * BLOCK
    scores = pltpu.VMEM((heads, STEP, BLOCK), F32)
    return pl.pallas_call(
        functools.partial(attention_kernel, heads, total),
        name="attention",
        cost_estimate=work(31),
        in_specs=[SMEM] * 2 + [ANY, VMEM] + [ANY] * 3,
        out_specs=[VMEM, VMEM],
        out_shape=[
            jax.ShapeDtypeStruct((rows, heads * HEAD), BF16),
            jax.ShapeDtypeStruct((heads, wide), F32),
        ],
        scratch_shapes=[
            pltpu.VMEM(ids[2].shape, jnp.int32),
            pltpu.VMEM(q.shape, BF16),
            pltpu.VMEM(k.shape, BF16),
            pltpu.VMEM(vt.shape, BF16),
        ]
        + step_lists(total)
        + [scores, scores, DMA((4,))],
        compiler_params=limit(56),
    )(*ids, q, k, vt)


def in_steps(first, last, body, carry):
    wide, narrow = 2 * BLOCK // LANES, BLOCK // LANES
    count = (last - first + narrow - 1) // narrow
    carry = lax.fori_loop(0, count // 2, lambda n, c: body(2 * BLOCK, first + n * wide, c), carry)
    return lax.fori_loop(0, count % 2, lambda n, c: body(BLOCK, first + (count - 1) * narrow, c), carry)


def attention_back_kernel(
    heads, total, numbers, before, idc, idr, q_in, k_in, v_in, kt_in, out, grad, lse, dproj,
    q, k, v, kt, made, g, delta, dq, in_s, out_s,
):
    wide = q.shape[1]
    width = heads * HEAD
    head_of = lax.broadcasted_iota(jnp.int32, (8, width), 1) // HEAD
    pick = jnp.where(head_of == lax.broadcasted_iota(jnp.int32, (8, width), 0), 1.0, 0.0).astype(BF16)
    none = jnp.zeros((TILE, LANES - HEAD), BF16)
    arriving = [
        pltpu.make_async_copy(src, dst, in_s.at[i])
        for i, (src, dst) in enumerate(((q_in, q), (k_in, k), (v_in, v), (kt_in, kt)))
    ]
    for copy in arriving:
        copy.start()

    def prepare(i, _):
        rows = pl.ds(pl.multiple_of(i * TILE, LANES), TILE)
        grads = jnp.where(idc[rows, :] >= 0, grad[rows, :].astype(F32), 0.0)
        inner = grads * out[rows, :].astype(F32)
        high = inner.astype(BF16)
        rest = (inner - high.astype(F32)).astype(BF16)
        delta[:, rows] = dot(pick, high, NT) + dot(pick, rest, NT)
        grads = grads.astype(BF16)
        for h in range(heads):
            g[h, rows, :] = jnp.concatenate([grads[:, h * HEAD : (h + 1) * HEAD], none], axis=1)
            dq[h, :, rows] = jnp.zeros((HEAD, TILE), F32)
        return 0

    lax.fori_loop(0, total // TILE, prepare, 0)
    tail = wide - total
    delta[:, total:] = jnp.zeros((8, tail), F32)
    for h in range(heads):
        g[h, total:, :] = jnp.zeros((tail, LANES), BF16)
        dq[h, :, total:] = jnp.zeros((HEAD, tail), F32)

    for copy in arriving:
        copy.wait()

    def give(i):
        cols = pl.ds(pl.multiple_of(i * BLOCK, LANES), BLOCK)
        return pltpu.make_async_copy(made.at[1:3, cols], dproj.at[1:3, cols], out_s.at[i])

    def one_block(i, _):
        c0 = pl.multiple_of(i * BLOCK, LANES)
        cols = pl.ds(c0, BLOCK)
        mine = idc[cols, :]
        low, high = block_range(i, numbers, before)

        def queries(size, at, carry):
            rows = pl.ds(pl.multiple_of(at * LANES, LANES), size)
            allowed = mine == idr[:, rows]
            both = [
                (dot(k[h, cols, :], q[h, rows, :], NT), dot(v[h, cols, :], g[h, rows, :], NT)) for h in range(heads)
            ]
            new = []
            for h in range(heads):
                dk, dv = carry[h]
                s, dp = both[h]
                p = jnp.where(allowed, jnp.exp(s - lse[h : h + 1, rows]), 0.0)
                ds = (p * (dp - delta[h : h + 1, rows])).astype(BF16)
                dv = dv + dot(p.astype(BF16), g[h, rows, :])
                dk = dk + dot(ds, q[h, rows, :])
                dq[h, :, rows] += dot(kt[h, :, cols], ds)
                new.append((dk, dv))
            return tuple(new)

        zero = jnp.zeros((BLOCK, LANES), F32)
        done = in_steps(low, high, queries, tuple((zero, zero) for _ in range(heads)))
        for part in range(2):
            joined = jnp.concatenate([done[h][part][:, :HEAD] for h in range(heads)], axis=1)
            made[part + 1, cols, :] = joined.astype(BF16)
        give(i).start()
        return 0

    lax.fori_loop(0, blocks(total), one_block, 0)

    def finish(i, _):
        rows = pl.ds(pl.multiple_of(i * TILE, LANES), TILE)
        joined = jnp.concatenate([dq[h, :, rows] for h in range(heads)], axis=0)
        made[0, rows, :] = (joined * HEAD**-0.5).T.astype(BF16)
        give_q(i).start()
        return 0

    def give_q(i):
        rows = pl.ds(pl.multiple_of(i * TILE, LANES), TILE)
        return pltpu.make_async_copy(made.at[0, rows], dproj.at[0, rows], out_s.at[blocks(total) + i])

    lax.fori_loop(0, total // TILE, finish, 0)
    for i in range(blocks(total)):
        give(i).wait()
    for i in range(total // TILE):
        give_q(i).wait()


def attention_back(ids, q, k, v, kt, out, grad, lse):
    heads, wide, _ = q.shape
    total = wide - PAD
    return pl.pallas_call(
        functools.partial(attention_back_kernel, heads, total),
        name="attention_back",
        cost_estimate=work(51),
        in_specs=[SMEM] * 2 + [VMEM] * 2 + [ANY] * 4 + [VMEM] * 3,
        out_specs=ANY,
        out_shape=jax.ShapeDtypeStruct((3, blocks(total) * BLOCK, heads * HEAD), BF16),
        scratch_shapes=[
            pltpu.VMEM(q.shape, BF16),
            pltpu.VMEM(k.shape, BF16),
            pltpu.VMEM(v.shape, BF16),
            pltpu.VMEM(kt.shape, BF16),
            pltpu.VMEM((3, blocks(total) * BLOCK, heads * HEAD), BF16),
            pltpu.VMEM((heads, wide, LANES), BF16),
            pltpu.VMEM((8, wide), F32),
            pltpu.VMEM((heads, HEAD, wide), F32),
            DMA((4,)),
            DMA((blocks(total) + total // TILE,)),
        ],
        compiler_params=limit(60),
    )(*ids, q, k, v, kt, out, grad, lse)


ROWS_MID = 288


def middle_kernel(
    attended, tok, cot, cot_came, b_out, gain, shift, b_up, b_down, w_out, w_down, w_up_t, *rest
):
    me = Place()
    groups = len(rest) - 29
    weights = rest[:groups]
    layer_out, grad_mid, grad_heads, cells = rest[groups : groups + 4]
    (
        att, grad_att, w, acc, vec, bup, came, low_all, cot_all, back_all, active_all, hidden_all,
        att_s, att_r, own_s, grad_s, grad_r, back_s, unit_s, push_s, push_r, sum_s, sum_r, cell_s, shard_s,
    ) = rest[groups + 4 :]
    group = me.d // 2
    others_of, piece, _ = weights[0].shape
    parts = b_up.shape[0]
    rows = tok.shape[0]
    tiles = rows // ROWS_MID
    width = att.shape[2]
    others = [lax.rem(me.q + k, 4) for k in range(1, 4)]
    greet([me.member(quarter) for quarter in others])

    def tile(t, quarter=0):
        return pl.ds(pl.multiple_of(quarter * rows + t * ROWS_MID, 16), ROWS_MID)

    def att_to(k, t):
        return remote(
            attended.at[tile(t, others[k])], att.at[me.q, tile(t)], att_s.at[k, t], att_r.at[k, t], me.member(others[k])
        )

    def att_from(k, t):
        source = others[2 - k]
        return remote(
            attended.at[tile(t)], att.at[source, tile(t)], att_s.at[k, t], att_r.at[k, t], me.member(source)
        )

    def att_own(t):
        return pltpu.make_async_copy(attended.at[tile(t, me.q)], att.at[me.q, tile(t)], own_s.at[t])

    def grad_to(k, t):
        return remote(
            grad_att.at[others[k], tile(t)], grad_heads.at[tile(t, me.q)], grad_s.at[k, t], grad_r.at[k, t], me.member(others[k])
        )

    def grad_from(k, t):
        source = others[2 - k]
        return remote(
            grad_att.at[source, tile(t)], grad_heads.at[tile(t, source)], grad_s.at[k, t], grad_r.at[k, t], me.member(source)
        )

    def grad_own(t):
        return pltpu.make_async_copy(grad_att.at[me.q, tile(t)], grad_heads.at[tile(t, me.q)], back_s.at[t])

    for t in range(tiles):
        for k in (1, 0, 2):
            att_to(k, t).start()
        att_own(t).start()

    own_shard = [
        pltpu.make_async_copy(src, w.at[me.m, at], shard_s.at[i])
        for i, (src, at) in enumerate(
            (
                (w_out, pl.ds(0, OUT_ROWS)),
                (w_down, pl.ds(OUT_ROWS, UP_ROWS)),
                (w_up_t, pl.ds(OUT_ROWS + UP_ROWS, UP_ROWS)),
            )
        )
    ]

    def w_rows(j, k, core):
        source = 2 * lax.rem(group + groups - j, groups) + core
        return w.at[lax.rem(me.m + 1 + k, 4), pl.ds(pl.multiple_of(source * piece, 16), piece)]

    def load(j, k):
        return pltpu.make_async_copy(weights[j].at[k], w_rows(j, k, me.c), unit_s.at[j, k])

    def push(j, k):
        return remote(weights[j].at[k], w_rows(j, k, me.c), push_s.at[j, k], push_r.at[j, k], me.sibling)

    def pushed(j, k):
        return remote(weights[j].at[k], w_rows(j, k, 1 - me.c), push_s.at[j, k], push_r.at[j, k], me.sibling)

    each = [(j, k) for j in range(groups) for k in range(others_of)]
    for j, k in each:
        push(j, k).start()
        load(j, k).start()
    for copy in own_shard:
        copy.start()
    for ref in (vec, bup):
        ref[...] = jnp.zeros_like(ref)
    for copy in own_shard:
        copy.wait()
    for j, k in each:
        load(j, k).wait()
        pushed(j, k).wait_recv()

    out_rows = slice(0, OUT_ROWS)
    down_rows = slice(OUT_ROWS, OUT_ROWS + UP_ROWS)
    up_rows = slice(OUT_ROWS + UP_ROWS, VEC_AT)

    def one_tile(t, _):
        here = tile(t)
        att_own(t).wait()
        for k in range(3):
            att_from(k, t).wait_recv()
        atts = [att[v, here, :] for v in range(parts)]
        middle = tok[here, :].astype(F32) + line(b_out)
        for v in range(parts):
            middle = middle + dot(atts[v], w[v, out_rows])
        unit, scale = normalise(middle)
        low = (unit * line(gain) + line(shift)).astype(BF16)
        cot_low = jnp.where(me.native, cot[here, :], cot_came[here, :])
        low_all[here, :] = low
        cot_all[here, :] = cot_low
        cot_full = cot_low.astype(F32)
        out = middle + line(b_down)
        grad_norm = jnp.zeros_like(middle)

        def products(v):
            return dot(low, w[v, up_rows], NT), dot(cot_low, w[v, down_rows], NT)

        upcoming = products(0)
        for v in range(parts):
            hidden, grad_active = upcoming
            if v + 1 < parts:
                upcoming = products(v + 1)
            hidden = hidden + b_up[v]
            below = 0.5 * (1.0 + lax.erf(hidden * 0.5**0.5))
            density = jnp.exp(-0.5 * hidden * hidden) * 0.3989422804014327
            active = (hidden * below).astype(BF16)
            grad_hidden = (grad_active * (below + hidden * density)).astype(BF16)
            out = out + dot(active, w[v, down_rows])
            grad_norm = grad_norm + dot(grad_hidden, w[v, up_rows])
            active_all[v, here, :] = active
            hidden_all[v, here, :] = grad_hidden
            bup[v] += jnp.sum(grad_hidden.astype(F32), axis=0, keepdims=True)
        layer_out[here, :] = out.astype(BF16)
        scaled = grad_norm * line(gain)
        back = cot_full + scale * (
            scaled
            - jnp.mean(scaled, axis=-1, keepdims=True)
            - unit * jnp.mean(scaled * unit, axis=-1, keepdims=True)
        )
        grad_mid[here, :] = back
        back_low = back.astype(BF16)
        back_all[here, :] = back_low
        for v in range(parts):
            grad_att[v, here, :] = dot(back_low, w[v, out_rows], NT).astype(BF16)
        for k in (1, 0, 2):
            grad_to(k, t).start()
        grad_own(t).start()
        vec[0:1] += jnp.sum(grad_norm * unit, axis=0, keepdims=True)
        vec[1:2] += jnp.sum(grad_norm, axis=0, keepdims=True)
        vec[2:3] += jnp.sum(back, axis=0, keepdims=True)
        vec[3:4] += jnp.sum(cot_full, axis=0, keepdims=True)
        return 0

    lax.fori_loop(0, tiles, one_tile, 0)

    def sum_rows(i, core):
        return pl.ds(pl.multiple_of((2 * i + core) * piece, 16), piece)

    def give(i):
        return remote(w.at[:, sum_rows(i, 1 - me.c)], came.at[i], sum_s.at[i], sum_r.at[i], me.sibling)

    def keep(i):
        return pltpu.make_async_copy(w.at[:, sum_rows(i, me.c)], cells.at[i], cell_s.at[i])

    for v in range(parts):
        acc[v, out_rows] = dot(att[v], back_all[...], TN)
        acc[v, down_rows] = dot(active_all[v], cot_all[...], TN)
        acc[v, up_rows] = dot(hidden_all[v], low_all[...], TN)
        acc[v, VEC_AT:] = jnp.zeros((UNITS - VEC_AT, D), F32)
        acc[v, VEC_AT : VEC_AT + 8] = vec[...]
        acc[v, VEC_AT + 4 : VEC_AT + 5, :UP_ROWS] = bup[v]
    for i in range(groups):
        for v in range(parts):
            w[v, sum_rows(i, 1 - me.c), :] = acc[v, sum_rows(i, 1 - me.c), :].astype(BF16)
        give(i).start()
    for i in range(groups):
        give(i).wait_recv()
        for v in range(parts):
            w[v, sum_rows(i, me.c), :] = (acc[v, sum_rows(i, me.c), :] + came[i, v].astype(F32)).astype(BF16)
        keep(i).start()
    for t in range(tiles):
        for k in range(3):
            grad_from(k, t).wait_recv()
            grad_to(k, t).wait_send()
            att_to(k, t).wait_send()
        grad_own(t).wait()
    for j, k in each:
        push(j, k).wait_send()
    for i in range(groups):
        give(i).wait_send()
        keep(i).wait()


def middle_part(attended, tok, cot, cot_came, b_out, gain, shift, b_up, b_down, shard, weights):
    rows = tok.shape[0]
    width = attended.shape[1]
    groups = len(weights)
    parts, piece = b_up.shape[0], weights[0].shape[1]
    tiles = rows // ROWS_MID
    shape = jax.ShapeDtypeStruct
    halves = (groups, parts, piece, D)
    return pl.pallas_call(
        middle_kernel,
        name="middle_part",
        cost_estimate=work(50),
        in_specs=[ANY] + [VMEM] * 8 + [ANY] * (len(shard) + groups),
        out_specs=[VMEM, VMEM, ANY, ANY],
        out_shape=[
            shape((rows, D), BF16),
            shape((rows, D), F32),
            shape((4 * rows, width), BF16),
            shape(halves, BF16),
        ],
        scratch_shapes=[
            pltpu.VMEM((parts, rows, width), BF16),
            pltpu.VMEM((parts, rows, width), BF16),
            pltpu.VMEM((parts, UNITS, D), BF16),
            pltpu.VMEM((parts, UNITS, D), F32),
            pltpu.VMEM((8, D), F32),
            pltpu.VMEM((parts, 1, UP_ROWS), F32),
            pltpu.VMEM(halves, BF16),
            pltpu.VMEM((rows, D), BF16),
            pltpu.VMEM((rows, D), BF16),
            pltpu.VMEM((rows, D), BF16),
            pltpu.VMEM((parts, rows, UP_ROWS), BF16),
            pltpu.VMEM((parts, rows, UP_ROWS), BF16),
            DMA((3, tiles)),
            DMA((3, tiles)),
            DMA((tiles,)),
            DMA((3, tiles)),
            DMA((3, tiles)),
            DMA((tiles,)),
        ]
        + [DMA((groups, weights[0].shape[0]))] * 3
        + [DMA((groups,))] * 3
        + [DMA((len(shard),))],
        compiler_params=pltpu.CompilerParams(
            collective_id=2, has_side_effects=True, vmem_limit_bytes=48 << 20
        ),
    )(attended, tok, cot, cot_came, b_out, gain, shift, b_up, b_down, *shard, *weights)


CUTS = 3


def finish_kernel(
    dproj_in, normed_in, full_in, w, grad_mid, gain, cells, grad, vec_sum, d_w, sums,
    dproj, normed, full, part, theirs, sent, crossed, low, acc, w_part, w_in, w_z, vec, vz, vd, u_in, u_own,
    load_s, out_s, sib_s, sib_r, cross_s, cross_r, swap_s, swap_r, vz_s, vz_r, vd_s, vd_r,
    ws_s, ws_r, wz_s, wz_r, wg_s, wg_r, wf_s, wf_r, uz_s, uz_r, ug_s, ug_r, uf_s, uf_r,
):
    me = Place()
    foreign = jnp.logical_not(me.native)
    rows = grad_mid.shape[0]
    piece = rows // CUTS
    width = w.shape[1]
    ndp = vd.shape[0]
    groups, w_rows, _ = w_part.shape
    group = me.d // 2

    order = [2 * (1 - me.hf) + 1 - me.r, 2 * (1 - me.hf) + me.r, 2 * me.hf + 1 - me.r, 2 * me.hf + me.r]

    def span_of(k, p):
        return pl.ds(pl.multiple_of(order[k] * rows + p * piece, 16), piece)

    def loads(k, p):
        span = span_of(k, p)
        pairs = ((dproj_in.at[:, span], dproj.at[:, span]), (normed_in.at[span], normed.at[span]), (full_in.at[span], full.at[span]))
        return [pltpu.make_async_copy(src, dst, load_s.at[k, p, j]) for j, (src, dst) in enumerate(pairs)]

    for k in range(4):
        for p in range(CUTS):
            for copy in loads(k, p):
                copy.start()

    around = [(me.d, lax.rem(me.m + k, 4)) for k in range(1, 4)]
    along = [(lax.rem(me.d + k, ndp), me.m) for k in range(1, ndp)]
    greet([me.partner] + around + along)

    def to_sib(k, p):
        slot = k % 2
        return remote(part.at[k, p], theirs.at[slot, p], sib_s.at[slot, p], sib_r.at[slot, p], me.sibling)

    def to_cross(p):
        return remote(sent.at[p], crossed.at[p], cross_s.at[p], cross_r.at[p], me.cross)

    def to_partner(p):
        return remote(low.at[p], grad.at[p], swap_s.at[p], swap_r.at[p], me.partner)

    def keep(p):
        return pltpu.make_async_copy(low.at[p], grad.at[p], out_s.at[p])

    def unit_z(j):
        to = lax.rem(me.m + 1 + j, 4)
        return remote(cells.at[to], u_in.at[j], uz_s.at[j], uz_r.at[j], around[j])

    def unit_give(j):
        to = (2 * lax.rem(group + j, groups) + me.c, me.m)
        return remote(u_own, sums.at[me.d], ug_s.at[j], ug_r.at[j], to)

    def unit_give_in(j):
        source = 2 * lax.rem(group + groups - j, groups) + me.c
        return remote(u_own, sums.at[source], ug_s.at[j], ug_r.at[j], (source, me.m))

    def unit_forward(j):
        source = 2 * lax.rem(group + groups - j, groups) + me.c
        src = u_own if j == 0 else sums.at[source]
        return remote(src, sums.at[source], uf_s.at[j], uf_r.at[j], me.sibling)

    def unit_forward_in(j):
        source = 2 * lax.rem(group + groups - j, groups) + 1 - me.c
        return remote(u_own, sums.at[source], uf_s.at[j], uf_r.at[j], me.sibling)

    vec[...] = jnp.zeros_like(vec)

    def compute(k):
        def one(p, _):
            span = span_of(k, p)
            for copy in loads(k, p):
                copy.wait()
            total = jnp.zeros((piece, D), F32)
            for c in range(3):
                total = total + dot(dproj[c, span, :], w[c])
            part[k, p] = total.astype(BF16)

            @pl.when(me.native if k < 2 else foreign)
            def _():
                to_sib(k, p).start()

            return 0

        lax.fori_loop(0, CUTS, one, 0)

    def pass_across(k):
        for p in range(CUTS):
            to_sib(k, p).wait_recv()
            sent[p] = (part[k, p].astype(F32) + theirs[0, p].astype(F32)).astype(BF16)
            to_cross(p).start()

    def conclude(k, p):
        to_sib(k, p).wait_recv()
        to_cross(p).wait_recv()
        total = part[k, p].astype(F32) + theirs[1, p].astype(F32) + crossed[p].astype(F32)
        span = pl.ds(pl.multiple_of(me.q * rows + p * piece, 16), piece)
        unit, scale = normalise(full[span, :].astype(F32))
        vec[0:1] += jnp.sum(total * unit, axis=0, keepdims=True)
        vec[1:2] += jnp.sum(total, axis=0, keepdims=True)
        scaled = total * line(gain)
        result = grad_mid[p * piece : (p + 1) * piece, :] + scale * (
            scaled
            - jnp.mean(scaled, axis=-1, keepdims=True)
            - unit * jnp.mean(scaled * unit, axis=-1, keepdims=True)
        )
        low[p] = result.astype(BF16)

    def conclude_foreign(p):
        conclude(1, p)
        to_partner(p).start()

    compute(0)

    @pl.when(foreign)
    def _():
        pass_across(0)

    compute(1)
    compute(2)

    @pl.when(me.native)
    def _():
        pass_across(2)

    compute(3)
    for j in range(3):
        unit_z(j).start()

    for c in range(3):
        acc[c * width : (c + 1) * width, :] = dot(dproj[c], normed[...], TN)

    for i in range(groups):
        w_part[i] = acc[i * w_rows : (i + 1) * w_rows, :].astype(BF16)

    def other_group(k):
        return lax.rem(group + k, groups)

    def w_send(k):
        to = other_group(k)
        return remote(w_part.at[to], w_in.at[k], ws_s.at[k], ws_r.at[k], (2 * to + me.c, me.m))

    for k in range(1, groups):
        w_send(k).start()

    @pl.when(foreign)
    def _():
        for p in range(2 * CUTS // 3):
            conclude_foreign(p)

    w_sum = w_part[group].astype(F32)
    for k in range(1, groups):
        w_send(k).wait_recv()
        w_sum = w_sum + w_in[k].astype(F32)

    to_z = remote(w_z.at[0], w_z.at[1], wz_s, wz_r, (me.d, lax.rem(me.m + 2, 4)))

    def w_give(k):
        return remote(w_z.at[0], d_w.at[group], wg_s.at[k], wg_r.at[k], (2 * other_group(k) + me.c, me.m))

    def w_give_in(k):
        source = lax.rem(group + groups - k, groups)
        return remote(w_z.at[0], d_w.at[source], wg_s.at[k], wg_r.at[k], (2 * source + me.c, me.m))

    def w_forward(k):
        source = lax.rem(group + groups - k, groups)
        src = w_z.at[0] if k == 0 else d_w.at[source]
        return remote(src, d_w.at[source], wf_s.at[k], wf_r.at[k], me.sibling)

    w_keep = pltpu.make_async_copy(w_z.at[0], d_w.at[group], out_s.at[CUTS])
    unit_keep = pltpu.make_async_copy(u_own, sums.at[me.d], out_s.at[CUTS + 1])

    @pl.when(foreign)
    def _():
        w_z[0] = w_sum.astype(BF16)
        to_z.start()
        for p in range(2 * CUTS // 3, CUTS):
            conclude_foreign(p)

    @pl.when(me.native)
    def _():
        to_z.wait_recv()
        w_z[0] = (w_sum + w_z[1].astype(F32)).astype(BF16)
        w_keep.start()
        for k in range(1, groups):
            w_give(k).start()
        w_forward(0).start()
        for p in range(CUTS):
            conclude(3, p)
            keep(p).start()

    vz[me.m] = vec[...]

    def around_copy(k):
        return remote(vz.at[me.m], vz.at[me.m], vz_s.at[k], vz_r.at[k], around[k])

    for k in range(3):
        around_copy(k).start()

    unit_sum = cells[me.m].astype(F32)
    for j in range(3):
        unit_z(j).wait_recv()
        unit_sum = unit_sum + u_in[j].astype(F32)
    u_own[...] = unit_sum.astype(BF16)
    unit_keep.start()
    for j in range(1, groups):
        unit_give(j).start()
    unit_forward(0).start()

    @pl.when(me.native)
    def _():
        for k in range(1, groups):
            w_give_in(k).wait_recv()
            w_forward(k).start()

    for k in range(3):
        source = lax.rem(me.m + 3 - k, 4)
        remote(vz.at[source], vz.at[source], vz_s.at[k], vz_r.at[k], around[k]).wait_recv()
    vd[me.d] = vz[0] + vz[1] + vz[2] + vz[3]

    def along_copy(k):
        return remote(vd.at[me.d], vd.at[me.d], vd_s.at[k], vd_r.at[k], along[k])

    for k in range(ndp - 1):
        along_copy(k).start()

    for j in range(1, groups):
        unit_give_in(j).wait_recv()
        unit_forward(j).start()
    for k in range(ndp - 1):
        source = lax.rem(me.d + ndp - 1 - k, ndp)
        remote(vd.at[source], vd.at[source], vd_s.at[k], vd_r.at[k], along[k]).wait_recv()
    total = vd[0]
    for i in range(1, ndp):
        total = total + vd[i]
    vec_sum[...] = total
    for j in range(groups):
        unit_forward_in(j).wait_recv()

    @pl.when(foreign)
    def _():
        for k in range(groups):
            source = lax.rem(group + groups - k, groups)
            remote(w_z.at[0], d_w.at[source], wf_s.at[k], wf_r.at[k], me.sibling).wait_recv()
        for p in range(CUTS):
            to_partner(p).wait_recv()
            to_partner(p).wait_send()
            to_sib(2, p).wait_send()
            to_sib(3, p).wait_send()
        to_z.wait_send()

    @pl.when(me.native)
    def _():
        for p in range(CUTS):
            keep(p).wait()
            to_sib(0, p).wait_send()
            to_sib(1, p).wait_send()
        for k in range(1, groups):
            w_give(k).wait_send()
        for k in range(groups):
            w_forward(k).wait_send()
        w_keep.wait()

    for p in range(CUTS):
        to_cross(p).wait_send()
    for k in range(1, groups):
        w_send(k).wait_send()
    for k in range(3):
        around_copy(k).wait_send()
        unit_z(k).wait_send()
    for k in range(ndp - 1):
        along_copy(k).wait_send()
    for j in range(groups):
        unit_forward(j).wait_send()
    for j in range(1, groups):
        unit_give(j).wait_send()
    unit_keep.wait()


def finish(dproj, normed, full, w, grad_mid, gain, cells, ndp):
    rows = grad_mid.shape[0]
    total = full.shape[0]
    piece = rows // CUTS
    pieces = (CUTS, piece, D)
    groups = ndp // 2
    columns = 3 * w.shape[1]
    cut = (groups, columns // groups, D)
    unit = cells.shape[1:]
    shape = jax.ShapeDtypeStruct
    return pl.pallas_call(
        finish_kernel,
        name="finish",
        cost_estimate=work(60),
        in_specs=[ANY] * 3 + [VMEM] * 4,
        out_specs=[ANY, VMEM, ANY, ANY],
        out_shape=[shape(pieces, BF16), shape((8, D), F32), shape(cut, BF16), shape((ndp,) + unit, BF16)],
        scratch_shapes=[
            pltpu.VMEM((3, total, w.shape[1]), BF16),
            pltpu.VMEM((total, D), BF16),
            pltpu.VMEM((total, D), BF16),
            pltpu.VMEM((4,) + pieces, BF16),
            pltpu.VMEM((2,) + pieces, BF16),
            pltpu.VMEM(pieces, BF16),
            pltpu.VMEM(pieces, BF16),
            pltpu.VMEM(pieces, BF16),
            pltpu.VMEM((columns, D), F32),
            pltpu.VMEM(cut, BF16),
            pltpu.VMEM(cut, BF16),
            pltpu.VMEM((2,) + cut[1:], BF16),
            pltpu.VMEM((8, D), F32),
            pltpu.VMEM((4, 8, D), F32),
            pltpu.VMEM((ndp, 8, D), F32),
            pltpu.VMEM((3,) + unit, BF16),
            pltpu.VMEM(unit, BF16),
            DMA((4, CUTS, 3)),
            DMA((CUTS + 2,)),
        ]
        + [DMA((2, CUTS))] * 2
        + [DMA((CUTS,))] * 4
        + [DMA((3,))] * 2
        + [DMA((ndp - 1,))] * 2
        + [DMA((groups,))] * 2
        + [DMA] * 2
        + [DMA((groups,))] * 4
        + [DMA((3,))] * 2
        + [DMA((groups,))] * 4,
        compiler_params=pltpu.CompilerParams(
            collective_id=4, has_side_effects=True, vmem_limit_bytes=60 << 20
        ),
    )(dproj, normed, full, w, grad_mid, gain, cells)


def outputs_kernel(
    layer, layer_came, grads, w_sums, unit_sums, vec_one,
    layer_out, tokens_grad, d_qkv, d_out, d_up, d_down, d_gain_two, d_shift_two, d_b_out, d_b_down, d_b_up, d_gain_one, d_shift_one,
    layer_s, came_s, grads_s, w_s, unit_s, vec_s, grads_f, w_f, unit_f, up_f, in_s, out_s,
):
    me = Place()
    arriving = [
        pltpu.make_async_copy(src, dst, in_s.at[i])
        for i, (src, dst) in enumerate(
            (
                (unit_sums, unit_s),
                (w_sums, w_s),
                (grads, grads_s),
                (layer, layer_s),
                (layer_came, came_s),
                (vec_one, vec_s),
            )
        )
    ]
    for i in (2, 1, 0, 3, 4, 5):
        arriving[i].start()
    leaving = []

    def leave(src, dst):
        copy = pltpu.make_async_copy(src, dst, out_s.at[len(leaving)])
        copy.start()
        leaving.append(copy)

    def flatten(pieces, flat):
        count, height, _ = pieces.shape
        for i in range(count):
            flat[i * height : (i + 1) * height, :] = pieces[i].astype(F32)

    arriving[2].wait()
    flatten(grads_s, grads_f)
    leave(grads_f, tokens_grad)
    arriving[1].wait()
    flatten(w_s, w_f)
    leave(w_f, d_qkv)
    arriving[0].wait()
    flatten(unit_s, unit_f)
    leave(unit_f.at[:OUT_ROWS], d_out)
    leave(unit_f.at[OUT_ROWS : OUT_ROWS + UP_ROWS], d_down)
    for i in (3, 4):
        arriving[i].wait()
    layer_s[...] = jnp.where(me.native, layer_s[...], came_s[...])
    leave(layer_s, layer_out)
    up_f[...] = unit_f[OUT_ROWS + UP_ROWS : VEC_AT, :].T
    leave(up_f, d_up)
    arriving[5].wait()
    for i, ref in enumerate((d_gain_two, d_shift_two, d_b_out, d_b_down)):
        ref[...] = unit_f[VEC_AT + i, :]
    d_b_up[...] = unit_f[VEC_AT + 4, :UP_ROWS]
    d_gain_one[...] = vec_s[0, :]
    d_shift_one[...] = vec_s[1, :]
    for copy in leaving:
        copy.wait()


def outputs(layer, layer_came, grads, w_sums, unit_sums, vec_one):
    rows = layer.shape[0]
    columns = w_sums.shape[0] * w_sums.shape[1]
    shape = lambda *s: jax.ShapeDtypeStruct(s, F32)
    return pl.pallas_call(
        outputs_kernel,
        name="outputs",
        in_specs=[ANY] * 6,
        out_specs=[ANY] * 6 + [VMEM] * 7,
        out_shape=[
            jax.ShapeDtypeStruct((rows, D), BF16),
            shape(rows, D),
            shape(columns, D),
            shape(OUT_ROWS, D),
            shape(D, UP_ROWS),
            shape(UP_ROWS, D),
            shape(D),
            shape(D),
            shape(D),
            shape(D),
            shape(UP_ROWS),
            shape(D),
            shape(D),
        ],
        scratch_shapes=[
            pltpu.VMEM(layer.shape, BF16),
            pltpu.VMEM(layer.shape, BF16),
            pltpu.VMEM(grads.shape, BF16),
            pltpu.VMEM(w_sums.shape, BF16),
            pltpu.VMEM(unit_sums.shape, BF16),
            pltpu.VMEM(vec_one.shape, F32),
            pltpu.VMEM((rows, D), F32),
            pltpu.VMEM((columns, D), F32),
            pltpu.VMEM((UNITS, D), F32),
            pltpu.VMEM((D, UP_ROWS), F32),
            DMA((6,)),
            DMA((6,)),
        ],
        compiler_params=limit(60),
    )(layer, layer_came, grads, w_sums, unit_sums, vec_one)


def swap_pairs(ndp):
    return [
        (d * 4 + m, (d ^ 1) * 4 + (m + 2) % 4) for d in range(ndp) for m in range(4) if d % 2 != m // 2
    ]


def weight_piece(w_out, w_up, w_down, ndp):
    block = jnp.concatenate([w_out, w_down, w_up.T, jnp.zeros((UNITS - w_out.shape[0] - 2 * w_down.shape[0], D), BF16)])
    piece = UNITS // ndp
    return lax.dynamic_slice_in_dim(block, lax.axis_index("dp") * piece, piece, 0)


def from_other_pairs(block, ndp):
    groups = ndp // 2
    blocks_of = [block]
    for j in range(1, groups):
        pairs = [(d, 2 * ((d // 2 + j) % groups) + d % 2) for d in range(ndp)]
        blocks_of.append(lax.ppermute(block, "dp", pairs))
    return blocks_of


def sum_over_pairs(cells, ndp):
    cores = [[d for d in range(ndp) if d % 2 == core] for core in range(2)]
    return lax.psum_scatter(cells.reshape(-1, D), "dp", scatter_dimension=0, tiled=True, axis_index_groups=cores)


def shards(
    tokens,
    scene_ids,
    gain_one,
    shift_one,
    w_qkv,
    w_out,
    b_out,
    gain_two,
    shift_two,
    w_up,
    b_up,
    w_down,
    b_down,
    cotangent,
    ndp,
):
    both = ("dp", "mp")
    swap = swap_pairs(ndp)
    w_qkv = jnp.swapaxes(w_qkv, 1, 2)
    full, own_tok, w_mine, numbers, id_row, id_column, before, b_ups, normed, q, k, v, kt, vt, weights = start(
        tokens, w_qkv, scene_ids.reshape(-1, LANES), b_up, gain_one, shift_one, weight_piece(w_out, w_up, w_down, ndp), ndp
    )
    w_mine = w_mine.reshape(w_qkv.shape)
    ids = numbers, before, id_column, id_row
    weights = from_other_pairs(weights, ndp)
    sent_cot, q = lax.optimization_barrier((cotangent, q))
    cot_came = lax.ppermute(sent_cot, both, swap)
    attended, lse = attention(ids, q, k, vt)
    layer, grad_mid, grad_heads, cells = middle_part(
        attended, own_tok, cotangent, cot_came, b_out, gain_two, shift_two, b_ups, b_down, (w_out, w_down, w_up.T), weights
    )
    sent_out, grad_heads = lax.optimization_barrier((layer, grad_heads))
    layer_came = lax.ppermute(sent_out, both, swap)
    cells = sum_over_pairs(cells, ndp)
    dproj = attention_back(ids, q, k, v, kt, attended, grad_heads, lse)
    cells, dproj = lax.optimization_barrier((cells, dproj))
    grads, vec_one, w_sums, unit_sums = finish(
        dproj, normed, full, w_mine, grad_mid, gain_one, cells.reshape(4, -1, D), ndp
    )
    (
        layer_out, tokens_grad, d_qkv, d_out, d_up, d_down, d_gain_two, d_shift_two, d_b_out, d_b_down, d_b_up, d_gain_one, d_shift_one,
    ) = outputs(layer, layer_came, grads, w_sums, unit_sums, vec_one)
    return (
        layer_out,
        tokens_grad,
        d_gain_one,
        d_shift_one,
        jnp.swapaxes(d_qkv.reshape(w_qkv.shape), 1, 2),
        d_out,
        d_b_out,
        d_gain_two,
        d_shift_two,
        d_up,
        d_b_up,
        d_down,
        d_b_down,
    )


def solution(mesh):
    ndp = mesh.shape["dp"]
    return jax.shard_map(
        functools.partial(shards, ndp=ndp),
        mesh=mesh,
        in_specs=(
            P(("dp", "mp"), None),
            P("dp"),
            P(),
            P(),
            P(None, None, "mp"),
            P("mp", None),
            P(),
            P(),
            P(),
            P(None, "mp"),
            P("mp"),
            P("mp", None),
            P(),
            P(("dp", "mp"), None),
        ),
        out_specs=(
            P(("dp", "mp"), None),
            P(("dp", "mp"), None),
            P(),
            P(),
            P(None, None, "mp"),
            P("mp", None),
            P(),
            P(),
            P(),
            P(None, "mp"),
            P("mp"),
            P("mp", None),
            P(),
        ),
        check_vma=False,
    )
```
